128 devices in a mesh: dp: 64 (over y_hi, x, z, core), fsdp: 2 (over y_lo).
Axes of the slice: x: 4, y: 4 (y_hi: 2, y_lo: 2; y = y_hi * 2 + y_lo), z: 4, core: 2. Of those that a mesh axis runs over, the one named last changes fastest.
Arguments:
- tokens: bfloat16 [128, 192, 1024], P(('dp', 'fsdp')), may hold values from -6 to 6
- memory: float32 [128, 192, 1024], P(('dp', 'fsdp')), may hold values from -6 to 6
- compressed: float32 [128, 192, 1024], P(('dp', 'fsdp')), may hold values from -6 to 6
- cotangent: bfloat16 [128, 192, 1024], P(('dp', 'fsdp')), may hold values from -6 to 6
- ln1_g: bfloat16 [1024], P('fsdp'), may hold values from 0.5 to 1.5
- ln1_b: bfloat16 [1024], P('fsdp'), may hold values from -1.75 to 1.75
- w_q: bfloat16 [1024, 1024], P('fsdp'), may hold values from -0.1875 to 0.1875
- w_kv: bfloat16 [1024, 2048], P('fsdp'), may hold values from -0.1875 to 0.1875
- w_r: bfloat16 [1024, 1024], P('fsdp'), may hold values from -0.1875 to 0.1875
- bias_u: bfloat16 [1024], P('fsdp'), may hold values from -3 to 3
- bias_v: bfloat16 [1024], P('fsdp'), may hold values from -3 to 3
- w_o: bfloat16 [1024, 1024], P('fsdp'), may hold values from -0.75 to 0.75
- ln2_g: bfloat16 [1024], P('fsdp'), may hold values from 0.5 to 1.5
- ln2_b: bfloat16 [1024], P('fsdp'), may hold values from -1.75 to 1.75
- w_in: bfloat16 [1024, 4096], P('fsdp'), may hold values from -0.1875 to 0.1875
- b_in: bfloat16 [4096], P('fsdp'), may hold values from -1.75 to 1.75
- w_out: bfloat16 [4096, 1024], P('fsdp'), may hold values from -0.09375 to 0.09375
- b_out: bfloat16 [1024], P('fsdp'), may hold values from -1.75 to 1.75
- conv_w: bfloat16 [3072, 1024], P('fsdp'), may hold values from -0.109375 to 0.109375
- conv_b: bfloat16 [1024], P('fsdp'), may hold values from -1.75 to 1.75
Outputs:
- mixed_out: bfloat16 [128, 192, 1024], P(('dp', 'fsdp'))
- compressed_next: float32 [128, 192, 1024], P(('dp', 'fsdp'))
- recon_loss: float32 [128], P(('dp', 'fsdp'))
- grad_tokens: float32 [128, 192, 1024], P(('dp', 'fsdp'))
- grad_ln1_g: float32 [1024], P('fsdp')
- grad_ln1_b: float32 [1024], P('fsdp')
- grad_w_q: float32 [1024, 1024], P('fsdp')
- grad_w_kv: float32 [1024, 2048], P('fsdp')
- grad_w_r: float32 [1024, 1024], P('fsdp')
- grad_bias_u: float32 [1024], P('fsdp')
- grad_bias_v: float32 [1024], P('fsdp')
- grad_w_o: float32 [1024, 1024], P('fsdp')
- grad_ln2_g: float32 [1024], P('fsdp')
- grad_ln2_b: float32 [1024], P('fsdp')
- grad_w_in: float32 [1024, 4096], P('fsdp')
- grad_b_in: float32 [4096], P('fsdp')
- grad_w_out: float32 [4096, 1024], P('fsdp')
- grad_b_out: float32 [1024], P('fsdp')
- grad_conv_w: float32 [3072, 1024], P('fsdp')
- grad_conv_b: float32 [1024], P('fsdp')
The draws below stay inside these ranges and needn't reach their ends.
All inputs are finite; a program needn't handle non-finite values.
Results may differ from the reference program's by a relative error of at most 0.015.
Values may be sent and summed in bfloat16 or wider, within the bound.
No kernel may reach another device: no remote copies, remote signals or barrier semaphores. Data moves between devices by JAX's collectives and lax.ppermute only.
A program may use at most 384 MiB of HBM per device.

```python
import jax
import jax.numpy as jnp
from jax import lax

D = 1024
H = 8
FF = 4096
HD = 128
SEGMENT_TOKENS = 192
MEM = 192
CMEM = 192
KEYS = 576
STREAMS = 128


def levels(own_key, dims, shards, low, high):
    gain, own = 1.0, jax.random.fold_in(own_key, 6)
    for position, shards_of in shards:
        draws = jnp.exp(jax.random.uniform(jax.random.fold_in(own, position), (shards_of,), jnp.float32, low / len(shards), high / len(shards)))
        gain = gain * jnp.repeat(draws, dims[position] // shards_of).reshape([-1 if axis == position else 1 for axis in range(len(dims))])
    return gain


def gaussian(rng, extent, width, limit, pieces=(), dtype=jnp.bfloat16):
    loudness = levels(rng, extent, pieces, -0.22, 0.18) if pieces else 1.0
    values = jax.random.normal(rng, extent, jnp.float32) * width * loudness
    return jnp.minimum(jnp.maximum(values, -limit), limit).astype(dtype)


def setup_inputs(seed: int = 0) -> dict:
    seeds = jax.random.split(jax.random.key(seed), 21)
    tokens = gaussian(seeds[0], (STREAMS, SEGMENT_TOKENS, D), 1.0, 6.0, ((0, 128),))
    memory = gaussian(seeds[1], (STREAMS, MEM, D), 1.0, 6.0, ((0, 128),), jnp.float32)
    compressed = gaussian(seeds[2], (STREAMS, CMEM, D), 1.0, 6.0, ((0, 128),), jnp.float32)
    cotangent = gaussian(seeds[3], (STREAMS, SEGMENT_TOKENS, D), 1.0, 6.0, ((0, 128),))
    ln1_g = jnp.clip(1.0 + 0.1 * jax.random.normal(seeds[4], (D,), jnp.float32), 0.5, 1.5).astype(jnp.bfloat16)
    ln1_b = gaussian(seeds[5], (D,), 0.3, 1.75, ((0, 2),))
    w_q = gaussian(seeds[6], (D, D), D ** -0.5, 0.1875, ((0, 2),))
    w_kv = gaussian(seeds[7], (D, 2 * D), D ** -0.5, 0.1875, ((0, 2),))
    w_r = gaussian(seeds[8], (D, D), D ** -0.5, 0.1875, ((0, 2),))
    bias_u = gaussian(seeds[9], (D,), 0.5, 3.0, ((0, 2),))
    bias_v = gaussian(seeds[10], (D,), 0.5, 3.0, ((0, 2),))
    w_o = gaussian(seeds[11], (D, D), (D // 16) ** -0.5, 0.75, ((0, 2),))
    ln2_g = jnp.clip(1.0 + 0.1 * jax.random.normal(seeds[12], (D,), jnp.float32), 0.5, 1.5).astype(jnp.bfloat16)
    ln2_b = gaussian(seeds[13], (D,), 0.3, 1.75, ((0, 2),))
    w_in = gaussian(seeds[14], (D, FF), D ** -0.5, 0.1875, ((0, 2),))
    b_in = gaussian(seeds[15], (FF,), 0.3, 1.75, ((0, 2),))
    w_out = gaussian(seeds[16], (FF, D), FF ** -0.5, 0.09375, ((0, 2),))
    b_out = gaussian(seeds[17], (D,), 0.3, 1.75, ((0, 2),))
    conv_w = gaussian(seeds[18], (3 * D, D), (3 * D) ** -0.5, 0.109375, ((0, 2),))
    conv_b = gaussian(seeds[19], (D,), 0.3, 1.75, ((0, 2),))
    return dict(tokens=tokens, memory=memory, compressed=compressed, cotangent=cotangent, ln1_g=ln1_g, ln1_b=ln1_b, w_q=w_q, w_kv=w_kv, w_r=w_r, bias_u=bias_u, bias_v=bias_v, w_o=w_o, ln2_g=ln2_g, ln2_b=ln2_b, w_in=w_in, b_in=b_in, w_out=w_out, b_out=b_out, conv_w=conv_w, conv_b=conv_b)


HIGHEST = lax.Precision.HIGHEST

@jax.custom_vjp
def low(v):
    return lax.optimization_barrier(v.astype(jnp.bfloat16)).astype(jnp.float32)

@jax.custom_vjp
def low_back(v):
    return v

def low_keep(v):
    return (low(v), None)

def low_pass(kept, grad):
    return (grad,)

def back_keep(v):
    return (v, None)

def back_low(kept, grad):
    return (low(grad),)
low.defvjp(low_keep, low_pass)
low_back.defvjp(back_keep, back_low)

def layer_norm(values, scaling, offset):
    center = values - lax.optimization_barrier(jnp.mean(values, axis=-1, keepdims=True))
    spread = lax.optimization_barrier(jnp.mean(center * center, axis=-1, keepdims=True))
    return center * lax.rsqrt(spread + 1e-05) * scaling + offset

def product(left, right):
    return jnp.dot(left, right, precision=HIGHEST)

def sinusoid(key_count, model_dim):
    distance = (key_count - 1 - jnp.arange(key_count)).astype(jnp.float32)
    inverse = 1.0 / 10000.0 ** (jnp.arange(0, model_dim, 2).astype(jnp.float32) / model_dim)
    angles = distance[:, None] * inverse[None, :]
    return jnp.concatenate([jnp.sin(angles), jnp.cos(angles)], axis=-1)

def rel_shift(scores):
    padded = jnp.pad(scores, ((0, 0), (0, 0), (1, 0)))
    padded = padded.reshape(scores.shape[0], scores.shape[2] + 1, scores.shape[1])
    return padded[:, 1:, :].reshape(scores.shape)

def softmax_rows(scores):
    largest = lax.optimization_barrier(jnp.max(scores, axis=-1, keepdims=True))
    exponent = jnp.exp(scores - largest)
    return exponent / lax.optimization_barrier(jnp.sum(exponent, axis=-1, keepdims=True))

def content_attend(asking, rows):
    key_count = rows.shape[0]
    keys_h = rows[:, :D].reshape(key_count, H, HD)
    values_h = rows[:, D:].reshape(key_count, H, HD)
    scores = low_back(jnp.einsum('ihd,jhd->hij', asking, keys_h, precision=HIGHEST))
    attn_probs = softmax_rows(scores)
    mixture = jnp.einsum('hij,jhd->ihd', low(attn_probs), values_h, precision=HIGHEST)
    return low_back(mixture.reshape(SEGMENT_TOKENS, D))

def stream_forward(params, tokens, memory, compressed):
    ln1_g, ln1_b, w_q, w_kv, w_r, bias_u, bias_v, w_o, ln2_g, ln2_b, w_in, b_in, w_out, b_out = params
    factor = HD ** (-0.5)
    joined = jnp.concatenate([compressed, memory, tokens], axis=0)
    normed = low(layer_norm(joined, ln1_g, ln1_b))
    queries = low_back(product(normed[KEYS - SEGMENT_TOKENS:], w_q))
    key_value = low(low_back(product(normed, w_kv)))
    relative = low(low_back(product(low(sinusoid(KEYS, D)), w_r)))
    content = low((queries + bias_u) * factor).reshape(SEGMENT_TOKENS, H, HD)
    located = low((queries + bias_v) * factor).reshape(SEGMENT_TOKENS, H, HD)
    keys_h = key_value[:, :D].reshape(KEYS, H, HD)
    values_h = key_value[:, D:].reshape(KEYS, H, HD)
    relative_h = relative.reshape(KEYS, H, HD)
    raw_scores = jnp.einsum('ihd,jhd->hij', located, relative_h, precision=HIGHEST)
    scores = low_back(jnp.einsum('ihd,jhd->hij', content, keys_h, precision=HIGHEST) + rel_shift(raw_scores))
    row_ids = jnp.arange(SEGMENT_TOKENS)[:, None]
    col_ids = jnp.arange(KEYS)[None, :]
    allowed = col_ids <= row_ids + (KEYS - SEGMENT_TOKENS)
    attn_probs = softmax_rows(jnp.where(allowed[None], scores, -1e+30))
    mixture = jnp.einsum('hij,jhd->ihd', low(attn_probs), values_h, precision=HIGHEST).reshape(SEGMENT_TOKENS, D)
    attended = low(low_back(mixture))
    residual = tokens + low_back(product(attended, w_o))
    normed2 = low(layer_norm(residual, ln2_g, ln2_b))
    hidden = low(jax.nn.gelu(low_back(product(normed2, w_in) + b_in)))
    result = residual + product(hidden, w_out) + b_out
    return (result, (queries, key_value))

def reconstruct(convolution_weights, queries, key_value, memory, ln1_g, ln1_b, w_kv):
    conv_w, conv_b = convolution_weights
    oldest = low(memory[:SEGMENT_TOKENS].reshape(SEGMENT_TOKENS // 3, 3 * D))
    compact = low_back(product(oldest, conv_w) + conv_b)
    comp_pair = low(low_back(product(low(layer_norm(compact, ln1_g, ln1_b)), w_kv)))
    asking = low(queries * HD ** (-0.5)).reshape(SEGMENT_TOKENS, H, HD)
    target = content_attend(asking, key_value[CMEM:CMEM + SEGMENT_TOKENS])
    guess = content_attend(asking, comp_pair)
    mismatch = target - guess
    return (jnp.mean(mismatch * mismatch), compact)

def reference(tokens, memory, compressed, cotangent, ln1_g, ln1_b, w_q, w_kv, w_r, bias_u, bias_v, w_o, ln2_g, ln2_b, w_in, b_in, w_out, b_out, conv_w, conv_b):
    main_params = tuple((weight.astype(jnp.float32) for weight in (ln1_g, ln1_b, w_q, w_kv, w_r, bias_u, bias_v, w_o, ln2_g, ln2_b, w_in, b_in, w_out, b_out)))
    convolution_weights = (conv_w.astype(jnp.float32), conv_b.astype(jnp.float32))
    tokens_all = tokens.astype(jnp.float32)
    memory_stacked = memory.astype(jnp.float32)
    compressed_stacked = compressed.astype(jnp.float32)

    def forward(params, token_rows):

        def single_segment_step(carried, element):
            result, kept_values = jax.checkpoint(stream_forward)(params, element[0], element[1], element[2])
            return (carried, (result, kept_values))
        unused_slot, (results, kept_values) = lax.scan(single_segment_step, jnp.zeros((), jnp.float32), (token_rows, memory_stacked, compressed_stacked))
        return (results, kept_values)
    results, pullback, kept_values = jax.vjp(forward, main_params, tokens_all, has_aux=True)
    grad_main, grad_tokens = pullback(cotangent.astype(jnp.float32))
    query_stacked, pair_stacked = kept_values
    ln1_gain = main_params[0]
    ln1_bias = main_params[1]
    kv_weight = main_params[3]

    def reconstruction_stacked(params):

        def single_segment_step(carried, element):
            loss_value, compact = jax.checkpoint(reconstruct)(params, element[0], element[1], element[2], ln1_gain, ln1_bias, kv_weight)
            return (carried, (loss_value, compact))
        unused_slot, (loss_values, compact_blocks) = lax.scan(single_segment_step, jnp.zeros((), jnp.float32), (query_stacked, pair_stacked, memory_stacked))
        return (jnp.sum(loss_values), (loss_values, compact_blocks))
    unused_slot, reconstruction_backward, (loss_values, compact_blocks) = jax.vjp(reconstruction_stacked, convolution_weights, has_aux=True)
    grad_conv = reconstruction_backward(jnp.ones((), jnp.float32))[0]
    compressed_next = jnp.concatenate([compressed_stacked[:, SEGMENT_TOKENS // 3:], compact_blocks], axis=1)
    return (results.astype(jnp.bfloat16), compressed_next, loss_values, grad_tokens, grad_main[0], grad_main[1], grad_main[2], grad_main[3], grad_main[4], grad_main[5], grad_main[6], grad_main[7], grad_main[8], grad_main[9], grad_main[10], grad_main[11], grad_main[12], grad_main[13], grad_conv[0], grad_conv[1])
```

```python
import jax
import jax.numpy as jnp
from jax import lax
from jax.sharding import Mesh, PartitionSpec as P

H = 8
f32 = jnp.float32
bf16 = jnp.bfloat16
AXES = ("yh", "x", "z", "c", "yl")


def layer_norm(values, scaling, offset):
    center = values - jnp.mean(values, axis=-1, keepdims=True)
    spread = jnp.mean(center * center, axis=-1, keepdims=True)
    return center * lax.rsqrt(spread + 1e-05) * scaling + offset


def sinusoid(key_count, model_dim):
    distance = (key_count - 1 - jnp.arange(key_count)).astype(jnp.float32)
    inverse = 1.0 / 10000.0 ** (jnp.arange(0, model_dim, 2).astype(jnp.float32) / model_dim)
    angles = distance[:, None] * inverse[None, :]
    return jnp.concatenate([jnp.sin(angles), jnp.cos(angles)], axis=-1)


def rel_shift(scores):
    padded = jnp.pad(scores, ((0, 0), (0, 0), (1, 0)))
    padded = padded.reshape(scores.shape[0], scores.shape[2] + 1, scores.shape[1])
    return padded[:, 1:, :].reshape(scores.shape)


def softmax_rows(scores):
    largest = jnp.max(scores, axis=-1, keepdims=True)
    exponent = jnp.exp(scores - largest)
    return exponent / jnp.sum(exponent, axis=-1, keepdims=True)


def split_heads(rows):
    model_dim = rows.shape[1] // 2
    head_size = model_dim // H
    keys_h = rows[:, :model_dim].reshape(rows.shape[0], H, head_size)
    values_h = rows[:, model_dim:].reshape(rows.shape[0], H, head_size)
    return (keys_h, values_h)


def content_attend(asking, rows):
    keys_h, values_h = split_heads(rows)
    scores = jnp.einsum("ihd,jhd->hij", asking, keys_h, preferred_element_type=f32)
    attn_probs = softmax_rows(scores)
    mixture = jnp.einsum(
        "hij,jhd->ihd", attn_probs.astype(bf16), values_h, preferred_element_type=f32
    )
    return (mixture.reshape(asking.shape[0], rows.shape[1] // 2), attn_probs)


def dot(a, b):
    return jnp.dot(a, b, preferred_element_type=f32)


def dot_t(a, b):
    return lax.dot_general(a, b, (((1,), (1,)), ((), ())), preferred_element_type=f32)


def core_swap(v):
    return lax.ppermute(v, "c", [(0, 1), (1, 0)])


RING = {"x": ("x", "c"), "z": ("z", "c"), "y": ("yh", "c", "yl")}


def exchange(v, ring, masks):
    def flat(i, c):
        return (i // 2 * 2 + c) * 2 + i % 2 if ring == "y" else 2 * i + c

    pairs = [(flat(i, c), flat(i ^ masks[c], c)) for i in range(4) for c in range(2)]
    return lax.ppermute(v, RING[ring], pairs)


def pick(v, index, axis):
    return lax.dynamic_index_in_dim(v, index, axis, keepdims=False)


def quarters(place, core):
    first = jnp.where(core == 0, 1, 3)
    second = jnp.where(core == 0, 3, 1)
    return place, place ^ first, place ^ 2, place ^ second


def halve(send, keep_own, keep_far, ring):
    got = exchange(send, ring, (1, 3))
    onward = (keep_far.astype(f32) + got[1].astype(f32)).astype(bf16)
    last = exchange(onward, ring, (3, 1))
    return keep_own.astype(f32) + got[0].astype(f32) + last.astype(f32)


def ring_stage(v, axis, ring, place, core):
    own, first, far, second = quarters(place, core)
    send = jnp.stack([pick(v, first, axis), pick(v, far, axis)]).astype(bf16)
    return halve(send, pick(v, own, axis), pick(v, second, axis), ring)


def per_device(
    tokens,
    memory,
    compressed,
    cotangent,
    ln1_g,
    ln1_b,
    w_q,
    w_kv,
    w_r,
    bias_u,
    bias_v,
    w_o,
    ln2_g,
    ln2_b,
    w_in,
    b_in,
    w_out,
    b_out,
    conv_w,
    conv_b,
):
    tokens, memory, compressed, cotangent = tokens[0], memory[0], compressed[0], cotangent[0]
    yl, core = lax.axis_index("yl"), lax.axis_index("c")
    place = {"x": lax.axis_index("x"), "z": lax.axis_index("z")}
    first_half = yl == 0

    def swap(v, axis=1):
        n = v.shape[axis] // 2
        low = lax.slice_in_dim(v, 0, n, axis=axis)
        high = lax.slice_in_dim(v, n, 2 * n, axis=axis)
        return jnp.where(first_half, v, jnp.concatenate([high, low], axis=axis))

    parts = [ln1_g, ln1_b, bias_u, bias_v, ln2_g, ln2_b, b_out, conv_b, b_in]
    flat = jnp.concatenate(parts)
    flat_other = lax.ppermute(flat.reshape(-1, 128), "yl", [(0, 1), (1, 0)]).reshape(-1)
    lows = jnp.where(first_half, flat, flat_other)
    highs = jnp.where(first_half, flat_other, flat)
    vectors, at = [], 0
    for part in parts:
        n = part.shape[0]
        vectors.append(jnp.concatenate([lows[at : at + n], highs[at : at + n]]).astype(f32))
        at += n
    ln1_g, ln1_b, bias_u, bias_v, ln2_g, ln2_b, b_out, conv_b, b_in = vectors

    def over_y(w):
        n = w.shape[0] // 2
        got = exchange(lax.dynamic_slice_in_dim(w, core * n, n, 0), "y", (1, 3))
        twin = core_swap(got)
        low = jnp.where(core == 0, got, twin)
        high = jnp.where(core == 0, twin, got)
        return jnp.concatenate([w, low, high], axis=0)

    w_kv = over_y(w_kv)
    w_q = over_y(w_q)
    w_r = over_y(w_r)
    w_o = over_y(w_o)
    conv_w = over_y(conv_w)

    spot = (place["x"] * 4 + place["z"]) * 2 + core
    n_in, n_out = w_in.shape[0] // 32, w_out.shape[0] // 32
    width = w_out.shape[1]
    chunks = w_in.shape[1] // width
    piece_in = lax.dynamic_slice_in_dim(w_in, spot * n_in, n_in, 0)
    piece_in = piece_in.reshape(n_in, chunks, width).transpose(1, 0, 2).reshape(-1, width)
    piece_out = lax.dynamic_slice_in_dim(w_out, spot * n_out, n_out, 0)
    piece = lax.ppermute(
        jnp.concatenate([piece_in, piece_out], axis=0), "yl", [(0, 1), (1, 0)]
    )
    spread = lax.all_gather(piece, ("x", "z", "c"), axis=0)
    got_in = spread[:, : n_in * chunks].reshape(32, chunks, n_in, width)
    got_in = got_in.transpose(0, 2, 1, 3).reshape(32 * n_in, chunks * width)
    w_in = jnp.concatenate([w_in, got_in], axis=0)
    w_out = jnp.concatenate([w_out, spread[:, n_in * chunks :].reshape(-1, width)], axis=0)

    seg_len = tokens.shape[0]
    model_dim = w_q.shape[0]
    head_size = model_dim // H
    key_count = compressed.shape[0] + memory.shape[0] + seg_len
    first_query = key_count - seg_len
    factor = head_size ** (-0.5)
    wide_tokens = tokens.astype(f32)
    joined = jnp.concatenate([compressed, memory, wide_tokens], axis=0)
    normed = layer_norm(joined, ln1_g, ln1_b).astype(bf16)
    normed_rel = swap(normed)
    queries = dot(normed_rel[first_query:], w_q)
    key_value = dot(normed_rel, w_kv).astype(bf16)
    sinus_table = sinusoid(key_count, model_dim).astype(bf16)
    relative = dot(swap(sinus_table), w_r).astype(bf16)
    content = ((queries + bias_u) * factor).astype(bf16).reshape(seg_len, H, head_size)
    located = ((queries + bias_v) * factor).astype(bf16).reshape(seg_len, H, head_size)
    keys_h, values_h = split_heads(key_value)
    relative_h = relative.reshape(key_count, H, head_size)
    raw_scores = jnp.einsum("ihd,jhd->hij", located, relative_h, preferred_element_type=f32)
    scores = jnp.einsum(
        "ihd,jhd->hij", content, keys_h, preferred_element_type=f32
    ) + rel_shift(raw_scores)
    row_ids = jnp.arange(seg_len)[:, None]
    col_ids = jnp.arange(key_count)[None, :]
    allowed = col_ids <= row_ids + first_query
    attn_probs = softmax_rows(jnp.where(allowed[None], scores, -1e30))
    probs_low = attn_probs.astype(bf16)
    mixture = jnp.einsum("hij,jhd->ihd", probs_low, values_h, preferred_element_type=f32)
    attended = mixture.reshape(seg_len, model_dim).astype(bf16)
    residual = wide_tokens + dot(swap(attended), w_o)
    normed2 = layer_norm(residual, ln2_g, ln2_b).astype(bf16)
    pre_act = dot(swap(normed2), w_in) + b_in
    hidden = jax.nn.gelu(pre_act).astype(bf16)
    mixed_out = (residual + dot(swap(hidden), w_out) + b_out).astype(bf16)

    oldest = memory.reshape(seg_len // 3, 3 * model_dim).astype(bf16)
    compact = dot(swap(oldest), conv_w) + conv_b
    comp_normed = layer_norm(compact, ln1_g, ln1_b).astype(bf16)
    comp_pair = dot(swap(comp_normed), w_kv).astype(bf16)
    asking = (queries * factor).astype(bf16).reshape(seg_len, H, head_size)
    start_old = compressed.shape[0]
    target = content_attend(asking, key_value[start_old : start_old + seg_len])[0]
    guess, guess_probs = content_attend(asking, comp_pair)
    mismatch = target - guess
    recon_loss = jnp.mean(mismatch * mismatch)
    compact_len = seg_len // 3
    compressed_next = jnp.concatenate([compressed[compact_len:], compact], axis=0)

    def rows_of(x, both=None):
        t = x.T.reshape(2, 2, 4, 4, x.shape[1] // 64, x.shape[0])
        return jnp.concatenate([pick(t, core, 1), core_swap(pick(t, 1 - core, 1))], axis=-1)

    def both(dy):
        return jnp.concatenate([dy, core_swap(dy)], axis=0)

    def reduce(rows, dy, ring):
        axis = 1 if ring == "x" else 2
        own, first, far, second = quarters(place[ring], core)

        def make(index):
            return jnp.einsum(
                "yauk,kc->yauc", pick(rows, index, axis), dy, preferred_element_type=f32
            ).astype(bf16)

        send = jnp.stack([make(first), make(far)])
        kept = halve(send, make(own), make(second), ring)
        other = "z" if ring == "x" else "x"
        return ring_stage(kept, 1, other, place[other], core)

    def finish(v):
        got = exchange(pick(v, 1 - yl, 0).astype(bf16), "y", (1, 3))
        mine = (pick(v, yl, 0) + got.astype(f32)).astype(bf16)
        far = lax.ppermute(mine, "yh", [(0, 1), (1, 0)])
        return (mine.astype(f32) + far.astype(f32)).astype(bf16)

    def rows1024(v):
        y, u, cols = v.shape
        return v.reshape(y, u, cols // width, width).transpose(0, 2, 1, 3).reshape(y, -1, width)

    def gather_sums(sums):
        counts = [v.shape[1] * v.shape[2] // width for v in sums]
        done = finish(jnp.concatenate([rows1024(v) for v in sums], axis=1))
        whole = lax.all_gather(done, ("c", "x", "z"), axis=0)
        outs, at = [], 0
        for v, n in zip(sums, counts):
            u, cols = v.shape[1], v.shape[2]
            part = whole[:, at : at + n].reshape(32, cols // width, u, width)
            outs.append(part.transpose(0, 2, 1, 3).reshape(32 * u, cols).astype(f32))
            at += n
        return outs

    d_guess = (
        (-2.0 / (seg_len * model_dim) * mismatch).astype(bf16).reshape(seg_len, H, head_size)
    )
    comp_keys, comp_values = split_heads(comp_pair)
    d_gprobs = jnp.einsum("ihd,jhd->hij", d_guess, comp_values, preferred_element_type=f32)
    d_comp_values = jnp.einsum(
        "hij,ihd->jhd", guess_probs.astype(bf16), d_guess, preferred_element_type=f32
    )
    d_gscores = (
        guess_probs * (d_gprobs - jnp.sum(guess_probs * d_gprobs, axis=-1, keepdims=True))
    ).astype(bf16)
    d_comp_keys = jnp.einsum("hij,ihd->jhd", d_gscores, asking, preferred_element_type=f32)
    d_comp_pair = jnp.concatenate(
        [
            d_comp_keys.reshape(compact_len, model_dim),
            d_comp_values.reshape(compact_len, model_dim),
        ],
        axis=1,
    ).astype(bf16)
    d_comp_normed = swap(dot_t(d_comp_pair, w_kv))
    unused, norm_back3 = jax.vjp(lambda values: layer_norm(values, ln1_g, ln1_b), compact)
    d_compact = norm_back3(d_comp_normed)[0].astype(bf16)
    d_conv_b = jnp.sum(d_compact.astype(f32), axis=0)
    part_conv = reduce(rows_of(oldest), both(d_compact), "z")

    cot_wide = cotangent.astype(f32)
    d_b_out = jnp.sum(cot_wide, axis=0)
    d_hidden = swap(dot_t(cotangent, w_out))
    part_w_out = reduce(rows_of(hidden), both(cotangent), "x")
    unused, gelu_back = jax.vjp(jax.nn.gelu, pre_act)
    d_pre = gelu_back(d_hidden)[0].astype(bf16)
    d_b_in = jnp.sum(d_pre.astype(f32), axis=0)
    part_w_in = reduce(rows_of(normed2), both(d_pre), "z")
    d_normed2 = swap(dot_t(d_pre, w_in))
    unused, norm_back2 = jax.vjp(layer_norm, residual, ln2_g, ln2_b)
    d_mid_norm, d_ln2_g, d_ln2_b = norm_back2(d_normed2)
    d_residual = cot_wide + d_mid_norm
    d_branch = d_residual.astype(bf16)
    part_w_o = reduce(rows_of(attended), both(d_branch), "x")
    d_attended = swap(dot_t(d_branch, w_o)).astype(bf16).reshape(seg_len, H, head_size)
    d_probs = jnp.einsum("ihd,jhd->hij", d_attended, values_h, preferred_element_type=f32)
    d_values = jnp.einsum("hij,ihd->jhd", probs_low, d_attended, preferred_element_type=f32)
    d_scores = (
        attn_probs * (d_probs - jnp.sum(attn_probs * d_probs, axis=-1, keepdims=True))
    ).astype(bf16)
    d_content = jnp.einsum("hij,jhd->ihd", d_scores, keys_h, preferred_element_type=f32)
    d_keys = jnp.einsum("hij,ihd->jhd", d_scores, content, preferred_element_type=f32)
    unused, shift_back = jax.vjp(rel_shift, raw_scores)
    d_raw = shift_back(d_scores.astype(f32))[0].astype(bf16)
    d_located = jnp.einsum("hij,jhd->ihd", d_raw, relative_h, preferred_element_type=f32)
    d_relative = jnp.einsum("hij,ihd->jhd", d_raw, located, preferred_element_type=f32)
    d_relative = d_relative.reshape(key_count, model_dim).astype(bf16)
    d_content = d_content.reshape(seg_len, model_dim) * factor
    d_located = d_located.reshape(seg_len, model_dim) * factor
    d_bias_u = jnp.sum(d_content, axis=0)
    d_bias_v = jnp.sum(d_located, axis=0)
    d_queries = (d_content + d_located).astype(bf16)
    part_w_q = reduce(rows_of(normed[first_query:]), both(d_queries), "z")
    part_w_r = reduce(rows_of(sinus_table), both(d_relative), "x")
    d_pair = jnp.concatenate(
        [d_keys.reshape(key_count, model_dim), d_values.reshape(key_count, model_dim)], axis=1
    ).astype(bf16)
    part_w_kv = reduce(rows_of(normed), both(d_pair), "x")
    d_normed = swap(dot_t(d_pair, w_kv))
    d_normed_q = swap(dot_t(d_queries, w_q))
    d_normed = jnp.concatenate(
        [d_normed[:first_query], d_normed[first_query:] + d_normed_q], axis=0
    )
    unused, norm_back1 = jax.vjp(layer_norm, joined, ln1_g, ln1_b)
    d_joined, d_ln1_g, d_ln1_b = norm_back1(d_normed)
    d_tokens = d_residual + d_joined[first_query:]

    g_conv, g_out, g_in = gather_sums([part_conv, part_w_out, part_w_in])
    g_o, g_q, g_r, g_kv = gather_sums([part_w_o, part_w_q, part_w_r, part_w_kv])

    small = [d_ln1_g, d_ln1_b, d_bias_u, d_bias_v, d_ln2_g, d_ln2_b, d_b_out, d_conv_b, d_b_in]
    total = jnp.concatenate(small).reshape(-1, 128)
    total = total + core_swap(total)
    for ring in ("x", "z", "y"):
        total = total + exchange(total, ring, (1, 1))
        total = total + exchange(total, ring, (2, 2) if ring == "y" else (3, 3))
    total = total.reshape(-1)
    halves, at = [], 0
    for v in small:
        n = v.shape[0]
        halves.append(lax.dynamic_slice_in_dim(total[at : at + n], yl * (n // 2), n // 2, 0))
        at += n
    t_ln1_g, t_ln1_b, t_bu, t_bv, t_ln2_g, t_ln2_b, t_bout, t_convb, t_bin = halves
    return (
        mixed_out[None],
        compressed_next[None],
        recon_loss[None],
        d_tokens[None],
        t_ln1_g,
        t_ln1_b,
        g_q,
        g_kv,
        g_r,
        t_bu,
        t_bv,
        g_o,
        t_ln2_g,
        t_ln2_b,
        g_in,
        t_bin,
        g_out,
        t_bout,
        g_conv,
        t_convb,
    )


def solution(mesh):
    fine = Mesh(mesh.devices.reshape(2, 4, 4, 2, 2), AXES)
    stream = P(AXES, None, None)
    vec, mat = P("yl"), P("yl", None)
    weights = (vec, vec, mat, mat, mat, vec, vec, mat, vec, vec, mat, vec, mat, vec, mat, vec)
    return jax.shard_map(
        per_device,
        mesh=fine,
        in_specs=(stream,) * 4 + weights,
        out_specs=(stream, stream, P(AXES), stream) + weights,
        check_vma=False,
    )
```

```python
import jax
import jax.numpy as jnp
from jax import lax
from jax.experimental import pallas as pl
from jax.experimental.pallas import tpu as pltpu
from jax.sharding import Mesh, PartitionSpec as P

H = 8
HD = 128
D = 1024
T = 192
KEYS = 576
PAD = 640
FF = 4096
FACTOR = HD ** (-0.5)
f32 = jnp.float32
bf16 = jnp.bfloat16
AXES = ("yh", "x", "z", "c", "yl")
RING = {"x": ("x", "c"), "z": ("z", "c"), "y": ("yh", "c", "yl")}


def sinusoid(key_count, model_dim):
    distance = (key_count - 1 - jnp.arange(key_count)).astype(f32)
    inverse = 1.0 / 10000.0 ** (jnp.arange(0, model_dim, 2).astype(f32) / model_dim)
    angles = distance[:, None] * inverse[None, :]
    return jnp.concatenate([jnp.sin(angles), jnp.cos(angles)], axis=-1)


def dot(a, b):
    return jnp.dot(a, b, preferred_element_type=f32)


def dot_t(a, b):
    return lax.dot_general(a, b, (((1,), (1,)), ((), ())), preferred_element_type=f32)


def t_dot(a, b):
    return lax.dot_general(a, b, (((0,), (0,)), ((), ())), preferred_element_type=f32)


def call(kernel, out, grid, in_specs, out_specs, scalars, args, scratch=()):
    return pl.pallas_call(
        kernel,
        out_shape=out,
        grid_spec=pltpu.PrefetchScalarGridSpec(
            num_scalar_prefetch=1,
            grid=grid,
            in_specs=in_specs,
            out_specs=out_specs,
            scratch_shapes=list(scratch),
        ),
        compiler_params=pltpu.CompilerParams(vmem_limit_bytes=56 << 20),
    )(scalars, *args)


def whole(a):
    zeros = (0,) * a.ndim
    return pl.BlockSpec(a.shape, lambda *_: zeros)


def shape(dims, dtype):
    return jax.ShapeDtypeStruct(dims, dtype)


def at(offset):
    return pl.multiple_of(offset, 128)


def center_scale(v):
    mid = v - jnp.mean(v, axis=-1, keepdims=True)
    r = lax.rsqrt(jnp.mean(mid * mid, axis=-1, keepdims=True) + 1e-5)
    return mid * r, r


def norm_back(xhat, r, g, dn):
    gd = dn * g
    return r * (
        gd
        - jnp.mean(gd, axis=-1, keepdims=True)
        - xhat * jnp.mean(gd * xhat, axis=-1, keepdims=True)
    )


def softmax(s):
    e = jnp.exp(s - jnp.max(s, axis=-1, keepdims=True))
    return e / jnp.sum(e, axis=-1, keepdims=True)


def first_norm(compressed, memory, tokens, g, b, none):
    def kernel(_, comp, mem, tok, g, b, out, old):
        gain, bias = g[...], b[...]

        def part(ref, base):
            for i in range(0, T, 32):
                xhat, r = center_scale(ref[i : i + 32, :].astype(f32))
                out[base + i : base + i + 32, :] = (xhat * gain + bias).astype(bf16)

        part(comp, 0)
        part(mem, T)
        part(tok, 2 * T)
        row = lax.broadcasted_iota(jnp.int32, (T // 3, T), 0)
        col = lax.broadcasted_iota(jnp.int32, (T // 3, T), 1)
        low = mem[...].astype(bf16)
        for tap in range(3):
            take = jnp.where(col == 3 * row + tap, 1.0, 0.0).astype(bf16)
            old[:, tap * D : (tap + 1) * D] = dot(take, low).astype(bf16)

    args = (compressed, memory, tokens, g, b)
    out = (shape((KEYS, D), bf16), shape((T // 3, 3 * D), bf16))
    return call(
        kernel, out, (1,), [whole(a) for a in args], [whole(o) for o in out], none, args
    )


def project(x, pieces, offsets, block, dtype, rows=None, row_block=0):
    rows = rows or x.shape[0]
    depth, n = x.shape[1], pieces[0].shape[1]

    def kernel(s, x_ref, *refs):
        total = None
        for i, w in enumerate(refs[:-1]):
            part = dot(x_ref[:, pl.ds(at(s[i]), w.shape[0])], w[...])
            total = part if total is None else total + part
        refs[-1][...] = total.astype(dtype)

    return call(
        kernel,
        shape((rows, n), dtype),
        (n // block,),
        [pl.BlockSpec((rows, depth), lambda j, s: (row_block, 0))]
        + [pl.BlockSpec((w.shape[0], block), lambda j, s: (0, j)) for w in pieces],
        pl.BlockSpec((rows, block), lambda j, s: (0, j)),
        offsets,
        (x, *pieces),
    )


def head(rows, row_block=0, first=0):
    return pl.BlockSpec((rows, HD), lambda h, s: (row_block, first + h))


def vec_head():
    return pl.BlockSpec((1, HD), lambda h, s: (0, h))


def attend(queries, key_value, relative, bias_u, bias_v, none):
    def kernel(_, q, k, v, rel, bu, bv, probs, out):
        pad = jnp.zeros((PAD - KEYS, HD), bf16)
        content = ((q[...] + bu[...]) * FACTOR).astype(bf16)
        located = ((q[...] + bv[...]) * FACTOR).astype(bf16)
        raw = dot_t(located, jnp.concatenate([rel[...], pad], axis=0))
        raw = pltpu.roll(raw, PAD - T + 1, 1, stride=1, stride_axis=0)
        s = dot_t(content, jnp.concatenate([k[...], pad], axis=0)) + raw
        row = lax.broadcasted_iota(jnp.int32, (T, PAD), 0)
        col = lax.broadcasted_iota(jnp.int32, (T, PAD), 1)
        p = softmax(jnp.where(col <= row + (KEYS - T), s, -1e30))
        probs[0] = p
        low = p.astype(bf16)
        out[...] = dot(low, jnp.concatenate([v[...], pad], axis=0)).astype(bf16)

    return call(
        kernel,
        (shape((H, T, PAD), f32), shape((T, D), bf16)),
        (H,),
        [head(T), head(KEYS), head(KEYS, 0, H), head(KEYS), vec_head(), vec_head()],
        [pl.BlockSpec((1, T, PAD), lambda h, s: (h, 0, 0)), head(T)],
        none,
        (queries, key_value, key_value, relative, bias_u, bias_v),
    )


def attend_back(queries, key_value, relative, bias_u, bias_v, probs, d_attended, none):
    def kernel(_, q, k, v, rel, bu, bv, probs, d_att, d_kv, d_rel, d_q, d_bu, d_bv):
        pad = jnp.zeros((PAD - KEYS, HD), bf16)
        content = ((q[...] + bu[...]) * FACTOR).astype(bf16)
        located = ((q[...] + bv[...]) * FACTOR).astype(bf16)
        p, da = probs[0], d_att[...]
        d_p = dot_t(da, jnp.concatenate([v[...], pad], axis=0))
        d_kv[1] = t_dot(p.astype(bf16), da)[:KEYS].astype(bf16)
        d_s = (p * (d_p - jnp.sum(p * d_p, axis=-1, keepdims=True))).astype(bf16)
        d_c = dot(d_s, jnp.concatenate([k[...], pad], axis=0)) * FACTOR
        d_kv[0] = t_dot(d_s, content)[:KEYS].astype(bf16)
        row = lax.broadcasted_iota(jnp.int32, (T, T), 0)
        col = lax.broadcasted_iota(jnp.int32, (T, T), 1)
        flip = jnp.where(row + col == T - 1, 1.0, 0.0).astype(bf16)
        d_raw = pltpu.roll(dot(flip, d_s), 0, 1, stride=1, stride_axis=0)
        d_raw = dot(flip, d_raw.astype(bf16)).astype(bf16)
        d_l = dot(d_raw, jnp.concatenate([rel[...], pad], axis=0)) * FACTOR
        d_rel[...] = t_dot(d_raw, located)[:KEYS].astype(bf16)
        d_q[...] = (d_c + d_l).astype(bf16)
        d_bu[...] = jnp.sum(d_c, axis=0, keepdims=True)
        d_bv[...] = jnp.sum(d_l, axis=0, keepdims=True)

    return call(
        kernel,
        (
            shape((2, KEYS, D), bf16),
            shape((KEYS, D), bf16),
            shape((T, D), bf16),
            shape((1, D), f32),
            shape((1, D), f32),
        ),
        (H,),
        [
            head(T),
            head(KEYS),
            head(KEYS, 0, H),
            head(KEYS),
            vec_head(),
            vec_head(),
            pl.BlockSpec((1, T, PAD), lambda h, s: (h, 0, 0)),
            head(T),
        ],
        [
            pl.BlockSpec((2, KEYS, HD), lambda h, s: (0, 0, h)),
            head(KEYS),
            head(T),
            vec_head(),
            vec_head(),
        ],
        none,
        (queries, key_value, key_value, relative, bias_u, bias_v, probs, d_attended),
    )


def out_and_norm(attended, pieces, offsets, tokens, g, b):
    def kernel(s, att, w0, w1, w2, tok, g, b, res, n2):
        total = tok[...].astype(f32)
        for i, w in enumerate((w0, w1, w2)):
            total = total + dot(att[:, pl.ds(at(s[i]), w.shape[0])], w[...])
        res[...] = total
        xhat, r = center_scale(total)
        n2[...] = (xhat * g[...] + b[...]).astype(bf16)

    args = (attended, *pieces, tokens, g, b)
    out = (shape((T, D), f32), shape((T, D), bf16))
    return call(
        kernel, out, (1,), [whole(a) for a in args], [whole(o) for o in out], offsets, args
    )


STEP = 512
HALF = FF // 2 // STEP


def feed_forward(n2, residual, cotangent, w_in, w_out, spread, b_in, b_out, scalars):
    n_in = w_in.shape[0] // 32
    n_out = w_out.shape[0] // 32
    skip = FF // D * n_in
    per = STEP // n_out
    K_NORM = 0.7978845608028654

    def natural(j, s):
        return lax.rem(j + s[0] * HALF, 2 * HALF)

    def kernel(s, n2, res, cot, wi0, wi1, wo0, wo1, bi, bo, hid, dpre, mixed, dn2, dbi, acc):
        j = pl.program_id(0)
        n = natural(j, s)
        mine = at(s[0] * (D // 2))
        theirs = at((1 - s[0]) * (D // 2))

        @pl.when(j == 0)
        def _():
            acc[...] = jnp.zeros_like(acc)
            dn2[...] = jnp.zeros_like(dn2)

        win0 = wi0[...]
        win1 = wi1[...].reshape(D // 2, STEP)
        pre = (
            dot(n2[:, pl.ds(mine, D // 2)], win0)
            + dot(n2[:, pl.ds(theirs, D // 2)], win1)
            + bi[pl.ds(n, 1), :]
        )
        cube = K_NORM * (pre + 0.044715 * (pre * pre * pre))
        t = jnp.tanh(cube)
        hidden = (0.5 * pre * (1.0 + t)).astype(bf16)
        slope = 0.5 * (1.0 + t) + (0.5 * K_NORM) * pre * (1.0 - t * t) * (
            1.0 + (3 * 0.044715) * (pre * pre)
        )
        hid[...] = hidden

        def rest(wo):
            d_pre = (dot_t(cot[...], wo) * slope).astype(bf16)
            dpre[...] = d_pre
            dbi[pl.ds(n, 1), :] = jnp.sum(d_pre.astype(f32), axis=0, keepdims=True)
            acc[...] += dot(hidden, wo)
            dn2[:, pl.ds(mine, D // 2)] += dot_t(d_pre, win0)
            dn2[:, pl.ds(theirs, D // 2)] += dot_t(d_pre, win1)

        @pl.when(j < HALF)
        def _():
            rest(wo0[...])

        @pl.when(j >= HALF)
        def _():
            rest(wo1[...].reshape(STEP, D))

        @pl.when(j == 2 * HALF - 1)
        def _():
            mixed[...] = (res[...] + acc[...] + bo[...]).astype(bf16)

    sub = D // STEP

    def in_other(j, s):
        n = natural(j, s)
        return (0, n // sub, lax.rem(n, sub))

    out = (
        shape((T, FF), bf16),
        shape((T, FF), bf16),
        shape((T, D), bf16),
        shape((T, D), f32),
        shape((2 * HALF, STEP), f32),
    )
    by_unit = pl.BlockSpec((T, STEP), lambda j, s: (0, natural(j, s)))
    return call(
        kernel,
        out,
        (2 * HALF,),
        [
            whole(n2),
            whole(residual),
            whole(cotangent),
            pl.BlockSpec((D // 2, STEP), lambda j, s: (0, natural(j, s))),
            pl.BlockSpec((32, n_in, STEP), in_other),
            pl.BlockSpec((STEP, D), lambda j, s: (jnp.minimum(j, HALF - 1), 0)),
            pl.BlockSpec(
                (per, n_out, D), lambda j, s: (jnp.maximum(j - HALF, 0), skip // n_out, 0)
            ),
            whole(b_in),
            whole(b_out),
        ],
        [by_unit, by_unit, whole(out[2]), whole(out[3]), whole(out[4])],
        scalars,
        (n2, residual, cotangent, w_in, spread, w_out, spread, b_in, b_out),
        [pltpu.VMEM((T, D), f32)],
    )


def second_norm_back(cotangent, d_n2, residual, g, pieces, offsets):
    def kernel(s, cot, dn, res, g, w0, w1, w2, d_res, d_br, d_att, dg, db, dbo):
        xhat, r = center_scale(res[...])
        dn, wide = dn[...], cot[...].astype(f32)
        dg[...] = jnp.sum(dn * xhat, axis=0, keepdims=True)
        db[...] = jnp.sum(dn, axis=0, keepdims=True)
        dbo[...] = jnp.sum(wide, axis=0, keepdims=True)
        total = wide + norm_back(xhat, r, g[...], dn)
        d_res[...] = total
        low = total.astype(bf16)
        d_br[...] = low
        for i, w in enumerate((w0, w1, w2)):
            d_att[:, pl.ds(at(s[i]), w.shape[0])] = dot_t(low, w[...]).astype(bf16)

    args = (cotangent, d_n2, residual, g, *pieces)
    out = (
        shape((T, D), f32),
        shape((T, D), bf16),
        shape((T, D), bf16),
        shape((1, D), f32),
        shape((1, D), f32),
        shape((1, D), f32),
    )
    return call(
        kernel, out, (1,), [whole(a) for a in args], [whole(o) for o in out], offsets, args
    )


def first_norm_back(d_kv, d_q, kv_pieces, q_pieces, compressed, memory, tokens, g, d_res, offsets):
    steps = 8
    wide, slim = 2 * D // steps, D // steps

    def kernel(s, dkv, dq, k0, k1, k2, q0, q1, q2, comp, mem, tok, g, dres, dtok, dg, db, acc):
        j = pl.program_id(0)

        @pl.when(j == 0)
        def _():
            acc[...] = jnp.zeros_like(acc)

        for i, (kw, qw) in enumerate(((k0, q0), (k1, q1), (k2, q2))):
            columns = pl.ds(at(s[i]), kw.shape[0])
            acc[:, columns] += dot_t(dkv[0], kw[...])
            acc[2 * T :, columns] += dot_t(dq[...], qw[...])

        @pl.when(j == steps - 1)
        def _():
            gain = g[...]
            sum_g = jnp.zeros((1, D), f32)
            sum_b = jnp.zeros((1, D), f32)
            for block, ref in enumerate((comp, mem, tok)):
                for i in range(0, T, 32):
                    xhat, r = center_scale(ref[i : i + 32, :].astype(f32))
                    dn = acc[block * T + i : block * T + i + 32, :]
                    sum_g += jnp.sum(dn * xhat, axis=0, keepdims=True)
                    sum_b += jnp.sum(dn, axis=0, keepdims=True)
                    if block == 2:
                        dtok[i : i + 32, :] = dres[i : i + 32, :] + norm_back(xhat, r, gain, dn)
            dg[...] = sum_g
            db[...] = sum_b

    rest = (compressed, memory, tokens, g, d_res)
    out = (shape((T, D), f32), shape((1, D), f32), shape((1, D), f32))
    return call(
        kernel,
        out,
        (steps,),
        [
            pl.BlockSpec((1, KEYS, wide), lambda j, s: (j // (steps // 2), 0, lax.rem(j, steps // 2))),
            pl.BlockSpec((T, slim), lambda j, s: (0, j)),
        ]
        + [pl.BlockSpec((w.shape[0], wide), lambda j, s: (0, j)) for w in kv_pieces]
        + [pl.BlockSpec((w.shape[0], slim), lambda j, s: (0, j)) for w in q_pieces]
        + [whole(a) for a in rest],
        [whole(o) for o in out],
        offsets,
        (d_kv, d_q, *kv_pieces, *q_pieces, *rest),
        [pltpu.VMEM((KEYS, D), f32)],
    )


def compress(oldest, pieces, offsets, bias, g, b):
    block = 256
    rows = T // 3

    def kernel(s, x, w0, w1, w2, bias, g, b, compact, normed):
        j = pl.program_id(0)
        total = bias[:, pl.ds(at(j * block), block)]
        for i, w in enumerate((w0, w1, w2)):
            total = total + dot(x[:, pl.ds(at(s[i]), w.shape[0])], w[...])
        compact[:, pl.ds(at(j * block), block)] = total

        @pl.when(j == D // block - 1)
        def _():
            xhat, r = center_scale(compact[...])
            normed[...] = (xhat * g[...] + b[...]).astype(bf16)

    rest = (bias, g, b)
    out = (shape((rows, D), f32), shape((rows, D), bf16))
    return call(
        kernel,
        out,
        (D // block,),
        [whole(oldest)]
        + [pl.BlockSpec((w.shape[0], block), lambda j, s: (0, j)) for w in pieces]
        + [whole(a) for a in rest],
        [whole(o) for o in out],
        offsets,
        (oldest, *pieces, *rest),
    )


def reconstruct(queries, key_value, comp_pair, none):
    rows = T // 3

    def kernel(_, q, k, v, ck, cv, loss, dck, dcv):
        h = pl.program_id(0)
        asking = (q[...] * FACTOR).astype(bf16)
        p = softmax(dot_t(asking, k[...])).astype(bf16)
        gp = softmax(dot_t(asking, ck[...]))
        low = gp.astype(bf16)
        miss = dot(p, v[...]) - dot(low, cv[...])

        @pl.when(h == 0)
        def _():
            loss[...] = jnp.zeros_like(loss)

        loss[...] += jnp.sum(miss * miss, axis=0, keepdims=True)
        d_guess = ((-2.0 / (T * D)) * miss).astype(bf16)
        d_gp = dot_t(d_guess, cv[...])
        dcv[...] = t_dot(low, d_guess).astype(bf16)
        d_gs = (gp * (d_gp - jnp.sum(gp * d_gp, axis=-1, keepdims=True))).astype(bf16)
        dck[...] = t_dot(d_gs, asking).astype(bf16)

    return call(
        kernel,
        (shape((1, HD), f32), shape((rows, D), bf16), shape((rows, D), bf16)),
        (H,),
        [head(T), head(T, 1), head(T, 1, H), head(rows), head(rows, 0, H)],
        [pl.BlockSpec((1, HD), lambda h, s: (0, 0)), head(rows), head(rows)],
        none,
        (queries, key_value, key_value, comp_pair, comp_pair),
    )


def compress_back(dck, dcv, pieces, offsets, compact, g):
    rows = T // 3

    def kernel(s, dck, dcv, w0, w1, w2, compact, g, d_compact, d_bias, dn):
        for i, w in enumerate((w0, w1, w2)):
            dn[:, pl.ds(at(s[i]), w.shape[0])] = dot_t(dck[...], w[:, :D]) + dot_t(
                dcv[...], w[:, D:]
            )
        xhat, r = center_scale(compact[...])
        low = norm_back(xhat, r, g[...], dn[...]).astype(bf16)
        d_compact[...] = low
        d_bias[...] = jnp.sum(low.astype(f32), axis=0, keepdims=True)

    args = (dck, dcv, *pieces, compact, g)
    out = (shape((rows, D), bf16), shape((1, D), f32))
    return call(
        kernel,
        out,
        (1,),
        [whole(a) for a in args],
        [whole(o) for o in out],
        offsets,
        args,
        [pltpu.VMEM((rows, D), f32)],
    )


def weight_grad(jobs, scalars):
    total = sum(j[3][0].shape[1] // (1 if j[4] else 2) for j in jobs)
    block = jobs[0][0][0].shape[1] // 8
    in_specs, args, widths = [], [], []
    for xs, row_block, rows, dys, ready in jobs:
        width = dys[0].shape[1] // (1 if ready else 2)
        widths.append(width)
        for x in xs:
            in_specs.append(
                pl.BlockSpec((rows, block), lambda q, y, s, r=row_block: (r, y * 4 + s[q]))
            )
        for dy in dys:
            in_specs.append(
                pl.BlockSpec((rows, width), lambda q, y, s, r=ready: (0, 0 if r else s[2]))
            )
        args += [*xs, *dys]

    def kernel(s, *refs):
        out = refs[-1]
        start = 0
        for i, width in enumerate(widths):
            xa, xb, da, db = refs[4 * i : 4 * i + 4]
            out[0, 0, :, start : start + width] = (
                t_dot(xa[...], da[...]) + t_dot(xb[...], db[...])
            ).astype(bf16)
            start += width

    return call(
        kernel,
        shape((2, 2, block, total), bf16),
        (2, 2),
        in_specs,
        pl.BlockSpec((1, 1, block, total), lambda q, y, s: (q, y, 0, 0)),
        scalars,
        args,
    )


def widen(gathered, start, rows, columns, swapped, none):
    u = rows // 16
    sub = u // 32
    chunks = columns // 2 // STEP
    order = [x * 4 + z for z in range(4) for x in range(4)] if swapped else list(range(16))

    def kernel(_, src, out):
        for to, frm in enumerate(order):
            out[to] = src[frm].astype(f32)

    return call(
        kernel,
        shape((16, u, columns), f32),
        (sub, 2, chunks),
        [
            pl.BlockSpec(
                (16, 32, STEP), lambda i, c, k, s: (c, start // 32 + k * sub + i, 0)
            )
        ],
        pl.BlockSpec((16, 32, STEP), lambda i, c, k, s: (0, i, c * chunks + k)),
        none,
        (gathered,),
    ).reshape(rows, columns)


def core_swap(v):
    return lax.ppermute(v, "c", [(0, 1), (1, 0)])


def pair_swap(v):
    return lax.ppermute(v, "yl", [(0, 1), (1, 0)])


def exchange(v, ring, masks):
    def flat(i, c):
        return (i // 2 * 2 + c) * 2 + i % 2 if ring == "y" else 2 * i + c

    pairs = [(flat(i, c), flat(i ^ masks[c], c)) for i in range(4) for c in range(2)]
    return lax.ppermute(v, RING[ring], pairs)


def pick(v, index, axis):
    return lax.dynamic_index_in_dim(v, index, axis, keepdims=False)


def quarters(place, core):
    first = jnp.where(core == 0, 1, 3)
    second = jnp.where(core == 0, 3, 1)
    return place, place ^ first, place ^ 2, place ^ second


def halve(send, keep, ring):
    got = exchange(send, ring, (1, 3))
    onward = (keep[1].astype(f32) + got[1].astype(f32)).astype(bf16)
    last = exchange(onward, ring, (3, 1))
    return keep[0].astype(f32) + got[0].astype(f32) + last.astype(f32)


def ring_stage(v, axis, ring, place, core):
    own, first, far, second = quarters(place, core)
    send = jnp.stack([pick(v, first, axis), pick(v, far, axis)]).astype(bf16)
    return halve(send, (pick(v, own, axis), pick(v, second, axis)), ring)


def per_device(
    tokens,
    memory,
    compressed,
    cotangent,
    ln1_g,
    ln1_b,
    w_q,
    w_kv,
    w_r,
    bias_u,
    bias_v,
    w_o,
    ln2_g,
    ln2_b,
    w_in,
    b_in,
    w_out,
    b_out,
    conv_w,
    conv_b,
):
    tokens, memory, compressed, cotangent = tokens[0], memory[0], compressed[0], cotangent[0]
    yl, core = lax.axis_index("yl"), lax.axis_index("c")
    place = {"x": lax.axis_index("x"), "z": lax.axis_index("z")}
    none = jnp.zeros((1,), jnp.int32)
    ints = lambda *v: jnp.stack([jnp.asarray(i, jnp.int32) for i in v])

    def thirds(rows):
        half = rows // 2
        other = (1 - yl) * half
        return ints(yl * half, other + core * (half // 2), other + (1 - core) * (half // 2))

    flat = jnp.concatenate(
        [ln1_g, ln1_b, bias_u, bias_v, ln2_g, ln2_b, b_out, conv_b, b_in]
    ).reshape(-1, STEP)
    flat_other = pair_swap(flat)
    low = jnp.where(yl == 0, flat, flat_other).astype(f32)
    high = jnp.where(yl == 0, flat_other, flat).astype(f32)
    full = jnp.concatenate([low[:8], high[:8]], axis=1)
    ln1_g, ln1_b, bias_u, bias_v, ln2_g, ln2_b, b_out, conv_b = [full[i : i + 1] for i in range(8)]
    b_in = jnp.concatenate([low[8:], high[8:]], axis=0)

    def over_y(w):
        n = w.shape[0] // 2
        got = exchange(lax.dynamic_slice_in_dim(w, core * n, n, 0), "y", (1, 3))
        return w, got, core_swap(got)

    kv_pieces = over_y(w_kv)
    q_pieces = over_y(w_q)
    r_pieces = over_y(w_r)
    o_pieces = over_y(w_o)
    conv_pieces = over_y(conv_w)
    thirds_d, thirds_c = thirds(D), thirds(3 * D)

    spot = (place["x"] * 4 + place["z"]) * 2 + core
    n_in, n_out = w_in.shape[0] // 32, w_out.shape[0] // 32
    piece_in = lax.dynamic_slice_in_dim(w_in, spot * n_in, n_in, 0)
    piece_out = lax.dynamic_slice_in_dim(w_out, spot * n_out, n_out, 0)
    piece = pair_swap(
        jnp.concatenate(
            [piece_in[:, i * D : (i + 1) * D] for i in range(FF // D)] + [piece_out], axis=0
        )
    )
    spread = lax.all_gather(piece, ("x", "z", "c"), axis=0)

    normed, oldest = first_norm(compressed, memory, tokens, ln1_g, ln1_b, none)
    key_value = project(normed, kv_pieces, thirds_d, 512, bf16)
    queries = project(normed, q_pieces, thirds_d, 512, f32, T, 2)
    sinus_table = sinusoid(KEYS, D).astype(bf16)
    relative = project(sinus_table, r_pieces, thirds_d, 512, bf16)
    probs, attended = attend(queries, key_value, relative, bias_u, bias_v, none)
    residual, normed2 = out_and_norm(attended, o_pieces, thirds_d, tokens, ln2_g, ln2_b)

    compact, comp_normed = compress(oldest, conv_pieces, thirds_c, conv_b, ln1_g, ln1_b)
    comp_pair = project(comp_normed, kv_pieces, thirds_d, 512, bf16)
    loss, d_ck, d_cv = reconstruct(queries, key_value, comp_pair, none)
    recon_loss = jnp.sum(loss) / (T * D)
    compressed_next = jnp.concatenate([compressed[T // 3 :], compact], axis=0)
    d_compact, d_conv_b = compress_back(d_ck, d_cv, kv_pieces, thirds_d, compact, ln1_g)

    def both(v):
        return (v, core_swap(v))

    def reduce(jobs, ring):
        own, first, far, second = quarters(place[ring], core)
        send = weight_grad(jobs, ints(first, far, core))
        keep = weight_grad(jobs, ints(own, second, core))
        kept = halve(send, keep, ring)
        other = "z" if ring == "x" else "x"
        y, rows, columns = kept.shape
        kept = kept.reshape(y, 4, rows // 4, columns)
        return ring_stage(kept, 1, other, place[other], core)

    def finish(sums):
        flat = [
            v.reshape(2, v.shape[1], -1, STEP).transpose(0, 2, 1, 3).reshape(2, -1, STEP)
            for v in sums
        ]
        v = jnp.concatenate(flat, axis=1)
        got = exchange(pick(v, 1 - yl, 0).astype(bf16), "y", (1, 3))
        mine = (pick(v, yl, 0) + got.astype(f32)).astype(bf16)
        far = lax.ppermute(mine, "yh", [(0, 1), (1, 0)])
        done = (mine.astype(f32) + far.astype(f32)).astype(bf16)
        return lax.all_gather(done, ("c", "x", "z"), axis=0)

    both_normed = both(normed)
    both_cot = both(cotangent)
    sum_conv = reduce([(both(oldest), 0, T // 3, both(d_compact), False)], "z")

    hidden, d_pre, mixed_out, d_normed2, d_b_in = feed_forward(
        normed2, residual, cotangent, w_in, w_out, spread, b_in, b_out, ints(yl)
    )
    sum_out = reduce([(both(hidden), 0, T, both_cot, False)], "x")
    sum_in = reduce([(both(normed2), 0, T, both(d_pre), False)], "z")
    d_residual, d_branch, d_attended, d_ln2_g, d_ln2_b, d_b_out = second_norm_back(
        cotangent, d_normed2, residual, ln2_g, o_pieces, thirds_d
    )
    sum_o = reduce([(both(attended), 0, T, both(d_branch), False)], "x")
    d_kv, d_relative, d_queries, d_bias_u, d_bias_v = attend_back(
        queries, key_value, relative, bias_u, bias_v, probs, d_attended, none
    )
    both_kv = (pick(d_kv, core, 0), core_swap(pick(d_kv, 1 - core, 0)))
    sum_kv = reduce([(both_normed, 0, KEYS, both_kv, True)], "x")
    sum_qr = reduce(
        [
            (both_normed, 2, T, both(d_queries), False),
            ((sinus_table, sinus_table), 0, KEYS, both(d_relative), False),
        ],
        "z",
    )
    d_tokens, d_ln1_g, d_ln1_b = first_norm_back(
        d_kv, d_queries, kv_pieces, q_pieces, compressed, memory, tokens, ln1_g, d_residual,
        thirds_d,
    )

    early = finish([sum_out, sum_in, sum_conv, sum_o])
    late = finish([sum_kv, sum_qr])
    g_out = widen(early, 0, FF // 2, D, False, none)
    g_in = widen(early, 128, D // 2, FF, True, none)
    g_conv = widen(early, 256, 3 * D // 2, D, True, none)
    g_o = widen(early, 352, D // 2, D, False, none)
    g_kv = widen(late, 0, D // 2, 2 * D, False, none)
    g_q = widen(late, 64, D // 2, D, True, none)
    g_r = widen(late, 96, D // 2, D, True, none)

    total = jnp.concatenate(
        [d_ln1_g, d_ln1_b, d_bias_u, d_bias_v, d_ln2_g, d_ln2_b, d_b_out, d_conv_b]
        + [d_b_in.reshape(4, D), jnp.zeros((4, D), f32)]
    )
    total = total + core_swap(total)
    for ring in ("x", "z", "y"):
        total = total + exchange(total, ring, (1, 1))
        total = total + exchange(total, ring, (2, 2) if ring == "y" else (3, 3))
    half = lax.dynamic_slice_in_dim(total[:8], yl * (D // 2), D // 2, 1)
    t_ln1_g, t_ln1_b, t_bu, t_bv, t_ln2_g, t_ln2_b, t_bout, t_convb = [half[i] for i in range(8)]
    t_bin = lax.dynamic_slice_in_dim(total[8:12], yl * 2, 2, 0).reshape(-1)
    return (
        mixed_out[None],
        compressed_next[None],
        recon_loss[None],
        d_tokens[None],
        t_ln1_g,
        t_ln1_b,
        g_q,
        g_kv,
        g_r,
        t_bu,
        t_bv,
        g_o,
        t_ln2_g,
        t_ln2_b,
        g_in,
        t_bin,
        g_out,
        t_bout,
        g_conv,
        t_convb,
    )


def solution(mesh):
    fine = Mesh(mesh.devices.reshape(2, 4, 4, 2, 2), AXES)
    stream = P(AXES, None, None)
    vec, mat = P("yl"), P("yl", None)
    weights = (vec, vec, mat, mat, mat, vec, vec, mat, vec, vec, mat, vec, mat, vec, mat, vec)
    return jax.shard_map(
        per_device,
        mesh=fine,
        in_specs=(stream,) * 4 + weights,
        out_specs=(stream, stream, P(AXES), stream) + weights,
        check_vma=False,
    )
```

```python
import jax
import jax.numpy as jnp
from jax import lax
from jax.experimental import pallas as pl
from jax.experimental.pallas import tpu as pltpu
from jax.sharding import Mesh, PartitionSpec as P

H = 8
HD = 128
D = 1024
T = 192
KEYS = 576
PAD = 640
FF = 4096
FACTOR = HD ** (-0.5)
f32 = jnp.float32
bf16 = jnp.bfloat16
AXES = ("yh", "x", "z", "c", "yl")
RING = {"x": ("x", "c"), "z": ("z", "c"), "y": ("yh", "c", "yl")}


def sinusoid(key_count, model_dim):
    distance = (key_count - 1 - jnp.arange(key_count)).astype(f32)
    inverse = 1.0 / 10000.0 ** (jnp.arange(0, model_dim, 2).astype(f32) / model_dim)
    angles = distance[:, None] * inverse[None, :]
    return jnp.concatenate([jnp.sin(angles), jnp.cos(angles)], axis=-1)


def dot(a, b):
    return jnp.dot(a, b, preferred_element_type=f32)


def dot_t(a, b):
    return lax.dot_general(a, b, (((1,), (1,)), ((), ())), preferred_element_type=f32)


def t_dot(a, b):
    return lax.dot_general(a, b, (((0,), (0,)), ((), ())), preferred_element_type=f32)


class Line:
    def __init__(self):
        self.held = []

    def hold(self, *values):
        self.held += values

    def later(self, value):
        return lax.optimization_barrier((value, *self.held))[0] if self.held else value

    def ran(self, value):
        self.held = [value]


line = Line()


def call(kernel, out, grid, in_specs, out_specs, scalars, args, scratch=()):
    result = run_kernel(
        kernel, out, grid, in_specs, out_specs, line.later(scalars), args, scratch
    )
    line.ran(jax.tree.leaves(result)[0])
    return result


def run_kernel(kernel, out, grid, in_specs, out_specs, scalars, args, scratch):
    return pl.pallas_call(
        kernel,
        out_shape=out,
        grid_spec=pltpu.PrefetchScalarGridSpec(
            num_scalar_prefetch=1,
            grid=grid,
            in_specs=in_specs,
            out_specs=out_specs,
            scratch_shapes=list(scratch),
        ),
        compiler_params=pltpu.CompilerParams(vmem_limit_bytes=56 << 20),
    )(scalars, *args)


def whole(a):
    zeros = (0,) * a.ndim
    return pl.BlockSpec(a.shape, lambda *_: zeros)


def shape(dims, dtype):
    return jax.ShapeDtypeStruct(dims, dtype)


def at(offset):
    return pl.multiple_of(offset, 128)


def center_scale(v):
    mid = v - jnp.mean(v, axis=-1, keepdims=True)
    r = lax.rsqrt(jnp.mean(mid * mid, axis=-1, keepdims=True) + 1e-5)
    return mid * r, r


def norm_back(xhat, r, g, dn):
    gd = dn * g
    return r * (
        gd
        - jnp.mean(gd, axis=-1, keepdims=True)
        - xhat * jnp.mean(gd * xhat, axis=-1, keepdims=True)
    )


def softmax(s):
    e = jnp.exp(s - jnp.max(s, axis=-1, keepdims=True))
    return e / jnp.sum(e, axis=-1, keepdims=True)


def first_norm(compressed, memory, tokens, g, b, offsets):
    def kernel(s, comp, mem, tok, g, b, out, out_rel, old):
        gain, bias = g[...], b[...]

        def part(ref, base):
            for i in range(0, T, 32):
                xhat, r = center_scale(ref[i : i + 32, :].astype(f32))
                out[base + i : base + i + 32, :] = (xhat * gain + bias).astype(bf16)

        part(comp, 0)
        part(mem, T)
        part(tok, 2 * T)
        start = 0
        for i, width in enumerate((D // 2, D // 4, D // 4)):
            out_rel[:, start : start + width] = out[:, pl.ds(at(s[i]), width)]
            start += width
        row = lax.broadcasted_iota(jnp.int32, (T // 3, T), 0)
        col = lax.broadcasted_iota(jnp.int32, (T // 3, T), 1)
        low = mem[...].astype(bf16)
        for tap in range(3):
            take = jnp.where(col == 3 * row + tap, 1.0, 0.0).astype(bf16)
            old[:, tap * D : (tap + 1) * D] = dot(take, low).astype(bf16)

    args = (compressed, memory, tokens, g, b)
    out = (shape((KEYS, D), bf16), shape((KEYS, D), bf16), shape((T // 3, 3 * D), bf16))
    return call(
        kernel, out, (1,), [whole(a) for a in args], [whole(o) for o in out], offsets, args
    )


PAIR = 2
STEPS = H // PAIR


def head(rows, row_block=0, first=0):
    return pl.BlockSpec((rows, PAIR * HD), lambda h, s: (row_block, first // PAIR + h))


def vec_head():
    return pl.BlockSpec((1, PAIR * HD), lambda h, s: (0, h))


def each_head(body):
    for i in range(PAIR):
        body(i, slice(i * HD, (i + 1) * HD))


def attend(queries, key_value, relative, bias_u, bias_v, none):
    def kernel(_, q, k, v, rel, bu, bv, probs, out):
        pad = jnp.zeros((PAD - KEYS, HD), bf16)
        row = lax.broadcasted_iota(jnp.int32, (T, PAD), 0)
        col = lax.broadcasted_iota(jnp.int32, (T, PAD), 1)
        seen = col <= row + (KEYS - T)

        def body(i, cut):
            content = ((q[:, cut] + bu[:, cut]) * FACTOR).astype(bf16)
            located = ((q[:, cut] + bv[:, cut]) * FACTOR).astype(bf16)
            raw = dot_t(located, jnp.concatenate([rel[:, cut], pad], axis=0))
            raw = pltpu.roll(raw, PAD - T + 1, 1, stride=1, stride_axis=0)
            s = dot_t(content, jnp.concatenate([k[:, cut], pad], axis=0)) + raw
            p = softmax(jnp.where(seen, s, -1e30))
            probs[i] = p
            low = p.astype(bf16)
            out[:, cut] = dot(low, jnp.concatenate([v[:, cut], pad], axis=0)).astype(bf16)

        each_head(body)

    return call(
        kernel,
        (shape((H, T, PAD), f32), shape((T, D), bf16)),
        (STEPS,),
        [head(T), head(KEYS), head(KEYS, 0, H), head(KEYS), vec_head(), vec_head()],
        [pl.BlockSpec((PAIR, T, PAD), lambda h, s: (h, 0, 0)), head(T)],
        none,
        (queries, key_value, key_value, relative, bias_u, bias_v),
    )


def attend_back(queries, key_value, relative, bias_u, bias_v, probs, d_attended, none):
    def kernel(_, q, k, v, rel, bu, bv, probs, d_att, d_kv, d_rel, d_q, d_bu, d_bv):
        pad = jnp.zeros((PAD - KEYS, HD), bf16)
        row = lax.broadcasted_iota(jnp.int32, (T, T), 0)
        col = lax.broadcasted_iota(jnp.int32, (T, T), 1)
        flip = jnp.where(row + col == T - 1, 1.0, 0.0).astype(bf16)

        def body(i, cut):
            content = ((q[:, cut] + bu[:, cut]) * FACTOR).astype(bf16)
            located = ((q[:, cut] + bv[:, cut]) * FACTOR).astype(bf16)
            p, da = probs[i], d_att[:, cut]
            d_p = dot_t(da, jnp.concatenate([v[:, cut], pad], axis=0))
            d_kv[1, :, cut] = t_dot(p.astype(bf16), da)[:KEYS].astype(bf16)
            d_s = (p * (d_p - jnp.sum(p * d_p, axis=-1, keepdims=True))).astype(bf16)
            d_c = dot(d_s, jnp.concatenate([k[:, cut], pad], axis=0)) * FACTOR
            d_kv[0, :, cut] = t_dot(d_s, content)[:KEYS].astype(bf16)
            d_raw = pltpu.roll(dot(flip, d_s), 0, 1, stride=1, stride_axis=0)
            d_raw = dot(flip, d_raw.astype(bf16)).astype(bf16)
            d_l = dot(d_raw, jnp.concatenate([rel[:, cut], pad], axis=0)) * FACTOR
            d_rel[:, cut] = t_dot(d_raw, located)[:KEYS].astype(bf16)
            d_q[:, cut] = (d_c + d_l).astype(bf16)
            d_bu[:, cut] = jnp.sum(d_c, axis=0, keepdims=True)
            d_bv[:, cut] = jnp.sum(d_l, axis=0, keepdims=True)

        each_head(body)

    return call(
        kernel,
        (
            shape((2, KEYS, D), bf16),
            shape((KEYS, D), bf16),
            shape((T, D), bf16),
            shape((1, D), f32),
            shape((1, D), f32),
        ),
        (STEPS,),
        [
            head(T),
            head(KEYS),
            head(KEYS, 0, H),
            head(KEYS),
            vec_head(),
            vec_head(),
            pl.BlockSpec((PAIR, T, PAD), lambda h, s: (h, 0, 0)),
            head(T),
        ],
        [
            pl.BlockSpec((2, KEYS, PAIR * HD), lambda h, s: (0, 0, h)),
            head(KEYS),
            head(T),
            vec_head(),
            vec_head(),
        ],
        none,
        (queries, key_value, key_value, relative, bias_u, bias_v, probs, d_attended),
    )


def out_and_norm(attended, pieces, offsets, tokens, g, b):
    def kernel(s, att, w0, w1, w2, tok, g, b, res, n2):
        total = tok[...].astype(f32)
        for i, w in enumerate((w0, w1, w2)):
            total = total + dot(att[:, pl.ds(at(s[i]), w.shape[0])], w[...])
        res[...] = total
        xhat, r = center_scale(total)
        n2[...] = (xhat * g[...] + b[...]).astype(bf16)

    args = (attended, *pieces, tokens, g, b)
    out = (shape((T, D), f32), shape((T, D), bf16))
    return call(
        kernel, out, (1,), [whole(a) for a in args], [whole(o) for o in out], offsets, args
    )


STEP = 512
HALF = FF // 2 // STEP


def feed_forward(n2, residual, cotangent, w_in, w_out, spread, b_in, b_out, scalars):
    n_in = w_in.shape[0] // 32
    n_out = w_out.shape[0] // 32
    skip = FF // D * n_in
    per = STEP // n_out
    K_NORM = 0.7978845608028654

    def natural(j, s):
        return lax.rem(j + s[0] * HALF, 2 * HALF)

    def kernel(s, n2, res, cot, wi0, wi1, wo0, wo1, bi, bo, hid, dpre, mixed, dn2, dbi, acc):
        j = pl.program_id(0)
        n = natural(j, s)
        mine = at(s[0] * (D // 2))
        theirs = at((1 - s[0]) * (D // 2))

        @pl.when(j == 0)
        def _():
            acc[...] = jnp.zeros_like(acc)
            dn2[...] = jnp.zeros_like(dn2)

        win0 = wi0[...]
        win1 = wi1[...].reshape(D // 2, STEP)
        pre = (
            dot(n2[:, pl.ds(mine, D // 2)], win0)
            + dot(n2[:, pl.ds(theirs, D // 2)], win1)
            + bi[pl.ds(n, 1), :]
        )
        cube = K_NORM * (pre + 0.044715 * (pre * pre * pre))
        t = jnp.tanh(cube)
        hidden = (0.5 * pre * (1.0 + t)).astype(bf16)
        slope = 0.5 * (1.0 + t) + (0.5 * K_NORM) * pre * (1.0 - t * t) * (
            1.0 + (3 * 0.044715) * (pre * pre)
        )
        hid[...] = hidden

        def rest(wo):
            d_pre = (dot_t(cot[...], wo) * slope).astype(bf16)
            dpre[...] = d_pre
            dbi[pl.ds(n, 1), :] = jnp.sum(d_pre.astype(f32), axis=0, keepdims=True)
            acc[...] += dot(hidden, wo)
            dn2[:, pl.ds(mine, D // 2)] += dot_t(d_pre, win0)
            dn2[:, pl.ds(theirs, D // 2)] += dot_t(d_pre, win1)

        @pl.when(j < HALF)
        def _():
            rest(wo0[...])

        @pl.when(j >= HALF)
        def _():
            rest(wo1[...].reshape(STEP, D))

        @pl.when(j == 2 * HALF - 1)
        def _():
            mixed[...] = (res[...] + acc[...] + bo[...]).astype(bf16)

    sub = D // STEP

    def in_other(j, s):
        n = natural(j, s)
        return (0, n // sub, lax.rem(n, sub))

    out = (
        shape((T, FF), bf16),
        shape((T, FF), bf16),
        shape((T, D), bf16),
        shape((T, D), f32),
        shape((2 * HALF, STEP), f32),
    )
    by_unit = pl.BlockSpec((T, STEP), lambda j, s: (0, natural(j, s)))
    return call(
        kernel,
        out,
        (2 * HALF,),
        [
            whole(n2),
            whole(residual),
            whole(cotangent),
            pl.BlockSpec((D // 2, STEP), lambda j, s: (0, natural(j, s))),
            pl.BlockSpec((32, n_in, STEP), in_other),
            pl.BlockSpec((STEP, D), lambda j, s: (jnp.minimum(j, HALF - 1), 0)),
            pl.BlockSpec(
                (per, n_out, D), lambda j, s: (jnp.maximum(j - HALF, 0), skip // n_out, 0)
            ),
            whole(b_in),
            whole(b_out),
        ],
        [by_unit, by_unit, whole(out[2]), whole(out[3]), whole(out[4])],
        scalars,
        (n2, residual, cotangent, w_in, spread, w_out, spread, b_in, b_out),
        [pltpu.VMEM((T, D), f32)],
    )


def second_norm_back(cotangent, d_n2, residual, g, pieces, offsets):
    def kernel(s, cot, dn, res, g, w0, w1, w2, d_res, d_br, d_att, dg, db, dbo):
        xhat, r = center_scale(res[...])
        dn, wide = dn[...], cot[...].astype(f32)
        dg[...] = jnp.sum(dn * xhat, axis=0, keepdims=True)
        db[...] = jnp.sum(dn, axis=0, keepdims=True)
        dbo[...] = jnp.sum(wide, axis=0, keepdims=True)
        total = wide + norm_back(xhat, r, g[...], dn)
        d_res[...] = total
        low = total.astype(bf16)
        d_br[...] = low
        for i, w in enumerate((w0, w1, w2)):
            d_att[:, pl.ds(at(s[i]), w.shape[0])] = dot_t(low, w[...]).astype(bf16)

    args = (cotangent, d_n2, residual, g, *pieces)
    out = (
        shape((T, D), f32),
        shape((T, D), bf16),
        shape((T, D), bf16),
        shape((1, D), f32),
        shape((1, D), f32),
        shape((1, D), f32),
    )
    return call(
        kernel, out, (1,), [whole(a) for a in args], [whole(o) for o in out], offsets, args
    )


def first_norm_back(d_kv, d_q, kv_pieces, q_pieces, compressed, memory, tokens, g, d_res, offsets):
    steps = 8
    wide, slim = 2 * D // steps, D // steps

    def kernel(s, dkv, dq, k0, k1, k2, q0, q1, q2, comp, mem, tok, g, dres, dtok, dg, db, acc):
        j = pl.program_id(0)

        @pl.when(j == 0)
        def _():
            acc[...] = jnp.zeros_like(acc)

        for i, (kw, qw) in enumerate(((k0, q0), (k1, q1), (k2, q2))):
            columns = pl.ds(at(s[i]), kw.shape[0])
            acc[:, columns] += dot_t(dkv[0], kw[...])
            acc[2 * T :, columns] += dot_t(dq[...], qw[...])

        @pl.when(j == steps - 1)
        def _():
            gain = g[...]
            sum_g = jnp.zeros((1, D), f32)
            sum_b = jnp.zeros((1, D), f32)
            for block, ref in enumerate((comp, mem, tok)):
                for i in range(0, T, 32):
                    xhat, r = center_scale(ref[i : i + 32, :].astype(f32))
                    dn = acc[block * T + i : block * T + i + 32, :]
                    sum_g += jnp.sum(dn * xhat, axis=0, keepdims=True)
                    sum_b += jnp.sum(dn, axis=0, keepdims=True)
                    if block == 2:
                        dtok[i : i + 32, :] = dres[i : i + 32, :] + norm_back(xhat, r, gain, dn)
            dg[...] = sum_g
            db[...] = sum_b

    rest = (compressed, memory, tokens, g, d_res)
    out = (shape((T, D), f32), shape((1, D), f32), shape((1, D), f32))
    return call(
        kernel,
        out,
        (steps,),
        [
            pl.BlockSpec((1, KEYS, wide), lambda j, s: (j // (steps // 2), 0, lax.rem(j, steps // 2))),
            pl.BlockSpec((T, slim), lambda j, s: (0, j)),
        ]
        + [pl.BlockSpec((w.shape[0], wide), lambda j, s: (0, j)) for w in kv_pieces]
        + [pl.BlockSpec((w.shape[0], slim), lambda j, s: (0, j)) for w in q_pieces]
        + [whole(a) for a in rest],
        [whole(o) for o in out],
        offsets,
        (d_kv, d_q, *kv_pieces, *q_pieces, *rest),
        [pltpu.VMEM((KEYS, D), f32)],
    )


def compress(oldest, pieces, offsets, bias, g, b):
    block = 256
    rows = T // 3

    def kernel(s, x, w0, w1, w2, bias, g, b, compact, normed, natural):
        j = pl.program_id(0)
        total = bias[:, pl.ds(at(j * block), block)]
        for i, w in enumerate((w0, w1, w2)):
            total = total + dot(x[:, pl.ds(at(s[i]), w.shape[0])], w[...])
        compact[:, pl.ds(at(j * block), block)] = total

        @pl.when(j == D // block - 1)
        def _():
            xhat, r = center_scale(compact[...])
            natural[...] = (xhat * g[...] + b[...]).astype(bf16)
            start = 0
            for i, width in enumerate((D // 2, D // 4, D // 4)):
                normed[:, start : start + width] = natural[:, pl.ds(at(s[3 + i]), width)]
                start += width

    rest = (bias, g, b)
    out = (shape((rows, D), f32), shape((rows, D), bf16))
    return call(
        kernel,
        out,
        (D // block,),
        [whole(oldest)]
        + [pl.BlockSpec((w.shape[0], block), lambda j, s: (0, j)) for w in pieces]
        + [whole(a) for a in rest],
        [whole(o) for o in out],
        offsets,
        (oldest, *pieces, *rest),
        [pltpu.VMEM((rows, D), bf16)],
    )


def reconstruct(queries, key_value, comp_pair, none):
    rows = T // 3

    def kernel(_, q, k, v, ck, cv, loss, dck, dcv):
        @pl.when(pl.program_id(0) == 0)
        def _():
            loss[...] = jnp.zeros_like(loss)

        def body(i, cut):
            asking = (q[:, cut] * FACTOR).astype(bf16)
            cvh = cv[:, cut]
            p = softmax(dot_t(asking, k[:, cut])).astype(bf16)
            gp = softmax(dot_t(asking, ck[:, cut]))
            low = gp.astype(bf16)
            miss = dot(p, v[:, cut]) - dot(low, cvh)
            loss[...] += jnp.sum(miss * miss, axis=0, keepdims=True)
            d_guess = ((-2.0 / (T * D)) * miss).astype(bf16)
            d_gp = dot_t(d_guess, cvh)
            dcv[:, cut] = t_dot(low, d_guess).astype(bf16)
            d_gs = (gp * (d_gp - jnp.sum(gp * d_gp, axis=-1, keepdims=True))).astype(bf16)
            dck[:, cut] = t_dot(d_gs, asking).astype(bf16)

        each_head(body)

    return call(
        kernel,
        (shape((1, HD), f32), shape((rows, D), bf16), shape((rows, D), bf16)),
        (STEPS,),
        [head(T), head(T, 1), head(T, 1, H), head(rows), head(rows, 0, H)],
        [pl.BlockSpec((1, HD), lambda h, s: (0, 0)), head(rows), head(rows)],
        none,
        (queries, key_value, key_value, comp_pair, comp_pair),
    )


def compress_back(dck, dcv, pieces, offsets, compact, g):
    rows = T // 3

    def kernel(s, dck, dcv, w0, w1, w2, compact, g, d_compact, d_bias, dn):
        for i, w in enumerate((w0, w1, w2)):
            dn[:, pl.ds(at(s[i]), w.shape[0])] = dot_t(dck[...], w[:, :D]) + dot_t(
                dcv[...], w[:, D:]
            )
        xhat, r = center_scale(compact[...])
        low = norm_back(xhat, r, g[...], dn[...]).astype(bf16)
        d_compact[...] = low
        d_bias[...] = jnp.sum(low.astype(f32), axis=0, keepdims=True)

    args = (dck, dcv, *pieces, compact, g)
    out = (shape((rows, D), bf16), shape((1, D), f32))
    return call(
        kernel,
        out,
        (1,),
        [whole(a) for a in args],
        [whole(o) for o in out],
        offsets,
        args,
        [pltpu.VMEM((rows, D), f32)],
    )


def weight_grads(groups, scalars):
    in_specs, args, outs, out_specs, layout = [], [], [], [], []
    for ring, jobs in groups:
        first = 1 if ring == "x" else 5
        block = jobs[0][0][0].shape[1] // 8
        widths = []
        for xs, row_block, rows, dys, ready in jobs:
            width = dys[0].shape[1] // (1 if ready else 2)
            widths.append(width)
            for x in xs:
                for y in range(2):
                    in_specs.append(
                        pl.BlockSpec(
                            (rows, block),
                            lambda q, s, r=row_block, f=first, y=y: (r, y * 4 + s[f + q]),
                        )
                    )
                    args.append(x)
            for dy in dys:
                in_specs.append(
                    pl.BlockSpec((rows, width), lambda q, s, r=ready: (0, 0 if r else s[0]))
                )
                args.append(dy)
        dims = (1, 2, block, sum(widths))
        outs += [shape((2, *dims[1:]), bf16)] * 2
        out_specs += [
            pl.BlockSpec(dims, lambda q, s: (jnp.minimum(q, 1), 0, 0, 0)),
            pl.BlockSpec(dims, lambda q, s: (jnp.maximum(q - 2, 0), 0, 0, 0)),
        ]
        layout.append(widths)

    def kernel(s, *refs):
        q = pl.program_id(0)
        place = 0
        results = refs[len(in_specs) :]
        for i, widths in enumerate(layout):
            start = 0
            for width in widths:
                a0, a1, b0, b1, da, db = refs[place : place + 6]
                place += 6
                for y, (xa, xb) in enumerate(((a0, b0), (a1, b1))):
                    value = (t_dot(xa[...], da[...]) + t_dot(xb[...], db[...])).astype(bf16)
                    columns = slice(start, start + width)

                    @pl.when(q < 2)
                    def _(i=i, y=y, columns=columns, value=value):
                        results[2 * i][0, y, :, columns] = value

                    @pl.when(q >= 2)
                    def _(i=i, y=y, columns=columns, value=value):
                        results[2 * i + 1][0, y, :, columns] = value

                start += width

    flat = call(kernel, tuple(outs), (4,), in_specs, out_specs, scalars, args)
    return [(flat[2 * i], flat[2 * i + 1]) for i in range(len(groups))]


def widen(gathered, start, rows, columns, swapped, none):
    u = rows // 16
    sub = u // 32
    chunks = columns // 2 // STEP
    order = [x * 4 + z for z in range(4) for x in range(4)] if swapped else list(range(16))

    def kernel(_, *refs):
        out = refs[-1]
        for k, src in enumerate(refs[:-1]):
            for to, frm in enumerate(order):
                out[to, :, k * STEP : (k + 1) * STEP] = src[frm].astype(f32)

    return call(
        kernel,
        shape((16, u, columns), f32),
        (sub, 2),
        [
            pl.BlockSpec((16, 32, STEP), lambda i, c, s, k=k: (c, start // 32 + k * sub + i, 0))
            for k in range(chunks)
        ],
        pl.BlockSpec((16, 32, STEP * chunks), lambda i, c, s: (0, i, c)),
        none,
        (gathered,) * chunks,
    ).reshape(rows, columns)


def core_swap(v):
    return lax.ppermute(v, "c", [(0, 1), (1, 0)])


def pair_swap(v):
    return lax.ppermute(v, "yl", [(0, 1), (1, 0)])


def exchange(v, ring, masks):
    def flat(i, c):
        return (i // 2 * 2 + c) * 2 + i % 2 if ring == "y" else 2 * i + c

    pairs = [(flat(i, c), flat(i ^ masks[c], c)) for i in range(4) for c in range(2)]
    return lax.ppermute(v, RING[ring], pairs)


def pick(v, index, axis):
    return lax.dynamic_index_in_dim(v, index, axis, keepdims=False)


def quarters(place, core):
    first = jnp.where(core == 0, 1, 3)
    second = jnp.where(core == 0, 3, 1)
    return place, place ^ first, place ^ 2, place ^ second


class Flow:
    def __init__(self, ring, pair, place, core):
        self.rings = (ring, "z" if ring == "x" else "x")
        self.place, self.core = place, core
        send, self.keep = pair
        self.got = exchange(send, ring, (1, 3))

    def onward(self, ring):
        got = line.later(self.got)
        self.near = got[0]
        value = (self.keep[1].astype(f32) + got[1].astype(f32)).astype(bf16)
        self.last = exchange(value, ring, (3, 1))
        line.hold(value)

    def settle(self):
        last = line.later(self.last)
        return self.keep[0].astype(f32) + self.near.astype(f32) + last.astype(f32)

    def second(self):
        self.onward(self.rings[0])

    def third(self):
        v = self.settle()
        y, rows, columns = v.shape
        v = v.reshape(y, 4, rows // 4, columns)
        ring = self.rings[1]
        own, first, far, second = quarters(self.place[ring], self.core)
        send = jnp.stack([pick(v, first, 1), pick(v, far, 1)]).astype(bf16)
        self.keep = (pick(v, own, 1), pick(v, second, 1))
        self.got = exchange(send, ring, (1, 3))
        line.hold(send, *self.keep)

    def fourth(self):
        self.onward(self.rings[1])

    def rows(self):
        v = self.settle()
        y, u, columns = v.shape
        v = v.reshape(y, u, columns // STEP, STEP).transpose(0, 2, 1, 3)
        return v.reshape(y, -1, STEP)


class Finish:
    def __init__(self, parts, yl):
        v = jnp.concatenate(parts, axis=1)
        self.mine = pick(v, yl, 0)
        send = pick(v, 1 - yl, 0).astype(bf16)
        self.got = exchange(send, "y", (1, 3))
        line.hold(send, self.mine)

    def second(self):
        got = line.later(self.got)
        self.mine = (self.mine + got.astype(f32)).astype(bf16)
        self.far = lax.ppermute(self.mine, "yh", [(0, 1), (1, 0)])
        line.hold(self.mine)

    def done(self):
        far = line.later(self.far)
        return (self.mine.astype(f32) + far.astype(f32)).astype(bf16)


def per_device(
    tokens,
    memory,
    compressed,
    cotangent,
    ln1_g,
    ln1_b,
    w_q,
    w_kv,
    w_r,
    bias_u,
    bias_v,
    w_o,
    ln2_g,
    ln2_b,
    w_in,
    b_in,
    w_out,
    b_out,
    conv_w,
    conv_b,
):
    line.held = []
    tokens, memory, compressed, cotangent = tokens[0], memory[0], compressed[0], cotangent[0]
    yl, core = lax.axis_index("yl"), lax.axis_index("c")
    place = {"x": lax.axis_index("x"), "z": lax.axis_index("z")}
    none = jnp.zeros((1,), jnp.int32)
    ints = lambda *v: jnp.stack([jnp.asarray(i, jnp.int32) for i in v])

    def thirds(rows):
        half = rows // 2
        other = (1 - yl) * half
        return ints(yl * half, other + core * (half // 2), other + (1 - core) * (half // 2))

    flat = jnp.concatenate(
        [ln1_g, ln1_b, bias_u, bias_v, ln2_g, ln2_b, b_out, conv_b, b_in]
    ).reshape(-1, STEP)
    flat_other = pair_swap(flat)
    low = jnp.where(yl == 0, flat, flat_other).astype(f32)
    high = jnp.where(yl == 0, flat_other, flat).astype(f32)
    full = jnp.concatenate([low[:8], high[:8]], axis=1)
    ln1_g, ln1_b, bias_u, bias_v, ln2_g, ln2_b, b_out, conv_b = [full[i : i + 1] for i in range(8)]
    b_in = jnp.concatenate([low[8:], high[8:]], axis=0)

    def over_y(w):
        n = w.shape[0] // 2
        return exchange(lax.dynamic_slice_in_dim(w, core * n, n, 0), "y", (1, 3))

    spot = (place["x"] * 4 + place["z"]) * 2 + core
    n_in, n_out = w_in.shape[0] // 32, w_out.shape[0] // 32
    piece_in = lax.dynamic_slice_in_dim(w_in, spot * n_in, n_in, 0)
    piece_out = lax.dynamic_slice_in_dim(w_out, spot * n_out, n_out, 0)
    piece = pair_swap(
        jnp.concatenate(
            [piece_in[:, i * D : (i + 1) * D] for i in range(FF // D)] + [piece_out], axis=0
        )
    )
    spread = lax.all_gather(piece, ("x", "z", "c"), axis=0)
    kv_got, q_got, r_got, o_got = over_y(w_kv), over_y(w_q), over_y(w_r), over_y(w_o)
    conv_got = over_y(conv_w)
    thirds_d = thirds(D)
    thirds_c = jnp.concatenate([thirds(3 * D), thirds_d])

    def both(v):
        return (v, core_swap(v))

    both_cot = both(cotangent)
    normed, normed_rel, oldest = first_norm(
        compressed, memory, tokens, ln1_g, ln1_b, thirds_d
    )
    both_normed = both(normed)
    both_oldest = both(oldest)
    sinus_table = sinusoid(KEYS, D).astype(bf16)
    sinus_rel = jnp.concatenate(
        [
            lax.dynamic_slice_in_dim(sinus_table, thirds_d[i], width, 1)
            for i, width in enumerate((D // 2, D // 4, D // 4))
        ],
        axis=1,
    )

    def joined(w, got):
        return jnp.concatenate([w, got, core_swap(got)], axis=0)

    kv_whole = joined(w_kv, kv_got)
    key_value = dot(line.later(normed_rel), kv_whole).astype(bf16)
    line.hold(key_value)
    queries = dot(line.later(normed_rel[2 * T :]), joined(w_q, q_got))
    line.hold(queries)
    relative = dot(line.later(sinus_rel), joined(w_r, r_got)).astype(bf16)
    line.hold(relative)
    kv_pieces = (w_kv, kv_got, core_swap(kv_got))
    q_pieces = (w_q, q_got, core_swap(q_got))
    o_pieces = (w_o, o_got, core_swap(o_got))
    conv_pieces = (conv_w, conv_got, core_swap(conv_got))
    probs, attended = attend(queries, key_value, relative, bias_u, bias_v, none)
    residual, normed2 = out_and_norm(attended, o_pieces, thirds_d, tokens, ln2_g, ln2_b)
    both_n2, both_att = both(normed2), both(attended)

    compact, comp_normed = compress(oldest, conv_pieces, thirds_c, conv_b, ln1_g, ln1_b)
    comp_pair = dot(comp_normed, kv_whole).astype(bf16)
    loss, d_ck, d_cv = reconstruct(queries, key_value, comp_pair, none)
    recon_loss = jnp.sum(loss) / (T * D)
    compressed_next = jnp.concatenate([compressed[T // 3 :], compact], axis=0)
    d_compact, d_conv_b = compress_back(d_ck, d_cv, kv_pieces, thirds_d, compact, ln1_g)
    both_compact = both(d_compact)

    cuts = []
    for ring in ("x", "z"):
        own, first, far, second = quarters(place[ring], core)
        cuts += [first, far, own, second]
    cuts = ints(core, *cuts)

    def flows(groups):
        pairs = weight_grads(groups, cuts)
        return [Flow(ring, pair, place, core) for (ring, _), pair in zip(groups, pairs)]

    hidden, d_pre, mixed_out, d_normed2, d_b_in = feed_forward(
        normed2, residual, cotangent, w_in, w_out, spread, b_in, b_out, ints(yl)
    )
    both_hidden, both_pre = both(hidden), both(d_pre)
    (conv_flow,) = flows([("x", [(both_oldest, 0, T // 3, both_compact, False)])])
    d_residual, d_branch, d_attended, d_ln2_g, d_ln2_b, d_b_out = second_norm_back(
        cotangent, d_normed2, residual, ln2_g, o_pieces, thirds_d
    )
    both_branch = both(d_branch)
    out_flow, in_flow = flows(
        [
            ("x", [(both_hidden, 0, T, both_cot, False)]),
            ("z", [(both_n2, 0, T, both_pre, False)]),
        ]
    )
    d_kv, d_relative, d_queries, d_bias_u, d_bias_v = attend_back(
        queries, key_value, relative, bias_u, bias_v, probs, d_attended, none
    )
    both_kv = (pick(d_kv, core, 0), core_swap(pick(d_kv, 1 - core, 0)))
    both_q, both_rel = both(d_queries), both(d_relative)
    conv_flow.second()
    d_tokens, d_ln1_g, d_ln1_b = first_norm_back(
        d_kv, d_queries, kv_pieces, q_pieces, compressed, memory, tokens, ln1_g, d_residual,
        thirds_d,
    )
    out_flow.second()
    in_flow.second()
    conv_flow.third()
    x_flow, z_flow = flows(
        [
            (
                "x",
                [(both_normed, 0, KEYS, both_kv, True), (both_att, 0, T, both_branch, False)],
            ),
            (
                "z",
                [
                    (both_normed, 2, T, both_q, False),
                    ((sinus_table, sinus_table), 0, KEYS, both_rel, False),
                ],
            ),
        ]
    )
    conv_flow.fourth()
    out_flow.third()
    in_flow.third()
    x_flow.second()
    z_flow.second()
    out_flow.fourth()
    in_flow.fourth()
    early = Finish([out_flow.rows(), in_flow.rows(), conv_flow.rows()], yl)
    x_flow.third()
    z_flow.third()
    early.second()
    x_flow.fourth()
    z_flow.fourth()
    early_sums = lax.all_gather(early.done(), ("c", "x", "z"), axis=0)

    total = jnp.concatenate(
        [d_ln1_g, d_ln1_b, d_bias_u, d_bias_v, d_ln2_g, d_ln2_b, d_b_out, d_conv_b]
        + [d_b_in.reshape(4, D)]
    )
    total = jnp.concatenate(
        [total[:8].reshape(8, 2, STEP).transpose(1, 0, 2), total[8:].reshape(2, 4, STEP)], axis=1
    )
    late = Finish([x_flow.rows(), z_flow.rows(), total, jnp.zeros((2, 4, STEP), f32)], yl)
    late.second()
    late_sums = lax.all_gather(late.done(), ("c", "x", "z"), axis=0)

    g_in = widen(early_sums, 128, D // 2, FF, True, none)
    g_out = widen(early_sums, 0, FF // 2, D, False, none)
    g_conv = widen(early_sums, 256, 3 * D // 2, D, False, none)
    g_kv = widen(late_sums, 0, D // 2, 2 * D, False, none)
    g_o = widen(late_sums, 64, D // 2, D, False, none)
    g_q = widen(late_sums, 96, D // 2, D, True, none)
    g_r = widen(late_sums, 128, D // 2, D, True, none)
    half = jnp.sum(late_sums[:, 160:172].astype(f32), axis=0)
    t_ln1_g, t_ln1_b, t_bu, t_bv, t_ln2_g, t_ln2_b, t_bout, t_convb = [half[i] for i in range(8)]
    t_bin = half[8:].reshape(-1)
    return (
        mixed_out[None],
        compressed_next[None],
        recon_loss[None],
        d_tokens[None],
        t_ln1_g,
        t_ln1_b,
        g_q,
        g_kv,
        g_r,
        t_bu,
        t_bv,
        g_o,
        t_ln2_g,
        t_ln2_b,
        g_in,
        t_bin,
        g_out,
        t_bout,
        g_conv,
        t_convb,
    )


def solution(mesh):
    fine = Mesh(mesh.devices.reshape(2, 4, 4, 2, 2), AXES)
    stream = P(AXES, None, None)
    vec, mat = P("yl"), P("yl", None)
    weights = (vec, vec, mat, mat, mat, vec, vec, mat, vec, vec, mat, vec, mat, vec, mat, vec)
    return jax.shard_map(
        per_device,
        mesh=fine,
        in_specs=(stream,) * 4 + weights,
        out_specs=(stream, stream, P(AXES), stream) + weights,
        check_vma=False,
    )
```

```python
import jax
import jax.numpy as jnp
from jax import lax
from jax.experimental import pallas as pl
from jax.experimental.pallas import tpu as pltpu
from jax.sharding import Mesh, PartitionSpec as P

H = 8
HD = 128
D = 1024
T = 192
KEYS = 576
PAD = 640
FF = 4096
FACTOR = HD ** (-0.5)
f32 = jnp.float32
bf16 = jnp.bfloat16
AXES = ("yh", "x", "z", "c", "yl")
RING = {"x": ("x", "c"), "z": ("z", "c"), "y": ("yh", "c", "yl")}


def sinusoid(key_count, model_dim):
    distance = (key_count - 1 - jnp.arange(key_count)).astype(f32)
    inverse = 1.0 / 10000.0 ** (jnp.arange(0, model_dim, 2).astype(f32) / model_dim)
    angles = distance[:, None] * inverse[None, :]
    return jnp.concatenate([jnp.sin(angles), jnp.cos(angles)], axis=-1)


def dot(a, b):
    return jnp.dot(a, b, preferred_element_type=f32)


def dot_t(a, b):
    return lax.dot_general(a, b, (((1,), (1,)), ((), ())), preferred_element_type=f32)


def t_dot(a, b):
    return lax.dot_general(a, b, (((0,), (0,)), ((), ())), preferred_element_type=f32)


class Line:
    def __init__(self):
        self.held = []

    def hold(self, *values):
        self.held += values

    def later(self, value):
        return lax.optimization_barrier((value, *self.held))[0] if self.held else value

    def ran(self, value):
        self.held = [value]


line = Line()


def call(kernel, out, grid, in_specs, out_specs, scalars, args, scratch=()):
    result = run_kernel(
        kernel, out, grid, in_specs, out_specs, line.later(scalars), args, scratch
    )
    line.ran(jax.tree.leaves(result)[0])
    return result


def run_kernel(kernel, out, grid, in_specs, out_specs, scalars, args, scratch):
    return pl.pallas_call(
        kernel,
        out_shape=out,
        grid_spec=pltpu.PrefetchScalarGridSpec(
            num_scalar_prefetch=1,
            grid=grid,
            in_specs=in_specs,
            out_specs=out_specs,
            scratch_shapes=list(scratch),
        ),
        compiler_params=pltpu.CompilerParams(vmem_limit_bytes=56 << 20),
    )(scalars, *args)


def whole(a):
    zeros = (0,) * a.ndim
    return pl.BlockSpec(a.shape, lambda *_: zeros)


def shape(dims, dtype):
    return jax.ShapeDtypeStruct(dims, dtype)


def at(offset):
    return pl.multiple_of(offset, 128)


def center_scale(v):
    mid = v - jnp.mean(v, axis=-1, keepdims=True)
    r = lax.rsqrt(jnp.mean(mid * mid, axis=-1, keepdims=True) + 1e-5)
    return mid * r, r


def norm_back(xhat, r, g, dn):
    gd = dn * g
    return r * (
        gd
        - jnp.mean(gd, axis=-1, keepdims=True)
        - xhat * jnp.mean(gd * xhat, axis=-1, keepdims=True)
    )


def softmax(s):
    e = jnp.exp(s - jnp.max(s, axis=-1, keepdims=True))
    return e / jnp.sum(e, axis=-1, keepdims=True)


(LN1_G, LN1_B, BIAS_U, BIAS_V, LN2_G, LN2_B, B_OUT, CONV_B) = range(8)


def row(ref, i):
    return ref[i : i + 1, :]


def unpack(mine, theirs, scalars):
    half = D // 2

    def kernel(s, mine, theirs, vectors, b_in):
        a, b = mine[...].astype(f32), theirs[...].astype(f32)
        low = jnp.where(s[0] == 0, a, b)
        high = jnp.where(s[0] == 0, b, a)
        vectors[:, :half] = low[:8]
        vectors[:, half:] = high[:8]
        for i in range(FF // D):
            part, k = (low, i) if i < 2 else (high, i - 2)
            b_in[i : i + 1, :half] = part[8 + 2 * k : 9 + 2 * k]
            b_in[i : i + 1, half:] = part[9 + 2 * k : 10 + 2 * k]

    args = (mine, theirs)
    out = (shape((8, D), f32), shape((FF // D, D), f32))
    return call(
        kernel, out, (1,), [whole(a) for a in args], [whole(o) for o in out], scalars, args
    )


def relative_columns(x, s, widths):
    parts = [x[:, pl.ds(at(s[i]), width)] for i, width in enumerate(widths)]
    return jnp.concatenate(parts, axis=1)


def natural_columns(out, x, s, widths):
    start = 0
    for i, width in enumerate(widths):
        out[:, pl.ds(at(s[i]), width)] = x[:, start : start + width]
        start += width


THIRDS = (D // 2, D // 4, D // 4)


def first_norm(compressed, memory, tokens, vectors, offsets):
    def kernel(s, comp, mem, tok, vec, out, out_rel, old):
        gain, bias = row(vec, LN1_G), row(vec, LN1_B)

        def part(ref, base):
            for i in range(0, T, 32):
                xhat, r = center_scale(ref[i : i + 32, :].astype(f32))
                out[base + i : base + i + 32, :] = (xhat * gain + bias).astype(bf16)

        part(comp, 0)
        part(mem, T)
        part(tok, 2 * T)
        out_rel[...] = relative_columns(out, s, THIRDS)
        line_of = lax.broadcasted_iota(jnp.int32, (T // 3, T), 0)
        col = lax.broadcasted_iota(jnp.int32, (T // 3, T), 1)
        low = mem[...].astype(bf16)
        for tap in range(3):
            take = jnp.where(col == 3 * line_of + tap, 1.0, 0.0).astype(bf16)
            old[:, tap * D : (tap + 1) * D] = dot(take, low).astype(bf16)

    args = (compressed, memory, tokens, vectors)
    out = (shape((KEYS, D), bf16), shape((KEYS, D), bf16), shape((T // 3, 3 * D), bf16))
    return call(
        kernel, out, (1,), [whole(a) for a in args], [whole(o) for o in out], offsets, args
    )


PAIR = 2
STEPS = H // PAIR


def head(rows, row_block=0, first=0):
    return pl.BlockSpec((rows, PAIR * HD), lambda h, s: (row_block, first // PAIR + h))


def vec_head(rows=1):
    return pl.BlockSpec((rows, PAIR * HD), lambda h, s: (0, h))


def each_head(body):
    for i in range(PAIR):
        body(i, slice(i * HD, (i + 1) * HD))


def attend(queries, key_value, relative, vectors, none):
    def kernel(_, q, k, v, rel, vec, probs, out):
        pad = jnp.zeros((PAD - KEYS, HD), bf16)
        row = lax.broadcasted_iota(jnp.int32, (T, PAD), 0)
        col = lax.broadcasted_iota(jnp.int32, (T, PAD), 1)
        seen = col <= row + (KEYS - T)

        def body(i, cut):
            content = ((q[:, cut] + vec[BIAS_U : BIAS_U + 1, cut]) * FACTOR).astype(bf16)
            located = ((q[:, cut] + vec[BIAS_V : BIAS_V + 1, cut]) * FACTOR).astype(bf16)
            raw = dot_t(located, jnp.concatenate([rel[:, cut], pad], axis=0))
            raw = pltpu.roll(raw, PAD - T + 1, 1, stride=1, stride_axis=0)
            s = dot_t(content, jnp.concatenate([k[:, cut], pad], axis=0)) + raw
            p = softmax(jnp.where(seen, s, -1e30))
            probs[i] = p
            low = p.astype(bf16)
            out[:, cut] = dot(low, jnp.concatenate([v[:, cut], pad], axis=0)).astype(bf16)

        each_head(body)

    return call(
        kernel,
        (shape((H, T, PAD), f32), shape((T, D), bf16)),
        (STEPS,),
        [head(T), head(KEYS), head(KEYS, 0, H), head(KEYS), vec_head(8)],
        [pl.BlockSpec((PAIR, T, PAD), lambda h, s: (h, 0, 0)), head(T)],
        none,
        (queries, key_value, key_value, relative, vectors),
    )


def attend_back(queries, key_value, relative, vectors, probs, d_attended, none):
    def kernel(_, q, k, v, rel, vec, probs, d_att, d_kv, d_rel, d_q, d_bu, d_bv):
        pad = jnp.zeros((PAD - KEYS, HD), bf16)
        row = lax.broadcasted_iota(jnp.int32, (T, T), 0)
        col = lax.broadcasted_iota(jnp.int32, (T, T), 1)
        flip = jnp.where(row + col == T - 1, 1.0, 0.0).astype(bf16)

        def body(i, cut):
            content = ((q[:, cut] + vec[BIAS_U : BIAS_U + 1, cut]) * FACTOR).astype(bf16)
            located = ((q[:, cut] + vec[BIAS_V : BIAS_V + 1, cut]) * FACTOR).astype(bf16)
            p, da = probs[i], d_att[:, cut]
            d_p = dot_t(da, jnp.concatenate([v[:, cut], pad], axis=0))
            d_kv[1, :, cut] = t_dot(p.astype(bf16), da)[:KEYS].astype(bf16)
            d_s = (p * (d_p - jnp.sum(p * d_p, axis=-1, keepdims=True))).astype(bf16)
            d_c = dot(d_s, jnp.concatenate([k[:, cut], pad], axis=0)) * FACTOR
            d_kv[0, :, cut] = t_dot(d_s, content)[:KEYS].astype(bf16)
            d_raw = pltpu.roll(dot(flip, d_s), 0, 1, stride=1, stride_axis=0)
            d_raw = dot(flip, d_raw.astype(bf16)).astype(bf16)
            d_l = dot(d_raw, jnp.concatenate([rel[:, cut], pad], axis=0)) * FACTOR
            d_rel[:, cut] = t_dot(d_raw, located)[:KEYS].astype(bf16)
            d_q[:, cut] = (d_c + d_l).astype(bf16)
            d_bu[:, cut] = jnp.sum(d_c, axis=0, keepdims=True)
            d_bv[:, cut] = jnp.sum(d_l, axis=0, keepdims=True)

        each_head(body)

    return call(
        kernel,
        (
            shape((2, KEYS, D), bf16),
            shape((KEYS, D), bf16),
            shape((T, D), bf16),
            shape((1, D), f32),
            shape((1, D), f32),
        ),
        (STEPS,),
        [
            head(T),
            head(KEYS),
            head(KEYS, 0, H),
            head(KEYS),
            vec_head(8),
            pl.BlockSpec((PAIR, T, PAD), lambda h, s: (h, 0, 0)),
            head(T),
        ],
        [
            pl.BlockSpec((2, KEYS, PAIR * HD), lambda h, s: (0, 0, h)),
            head(KEYS),
            head(T),
            vec_head(),
            vec_head(),
        ],
        none,
        (queries, key_value, key_value, relative, vectors, probs, d_attended),
    )


def out_and_norm(attended, w_o, tokens, vectors, offsets):
    def kernel(s, att, w, tok, vec, res, n2, n2_rel):
        total = tok[...].astype(f32) + dot(relative_columns(att, s, THIRDS), w[...])
        res[...] = total
        xhat, r = center_scale(total)
        n2[...] = (xhat * row(vec, LN2_G) + row(vec, LN2_B)).astype(bf16)
        other = at(D // 2 - s[0])
        n2_rel[:, : D // 2] = n2[:, pl.ds(at(s[0]), D // 2)]
        n2_rel[:, D // 2 :] = n2[:, pl.ds(other, D // 2)]

    args = (attended, w_o, tokens, vectors)
    out = (shape((T, D), f32), shape((T, D), bf16), shape((T, D), bf16))
    return call(
        kernel, out, (1,), [whole(a) for a in args], [whole(o) for o in out], offsets, args
    )


STEP = 512
UNITS = 1024
HALF = FF // 2 // UNITS


def feed_forward(n2_rel, residual, cotangent, w_in, w_out, spread, b_in, vectors, scalars):
    n_in = w_in.shape[0] // 32
    n_out = w_out.shape[0] // 32
    skip = FF // D * n_in
    per = UNITS // n_out
    K_NORM = 0.7978845608028654

    def natural(j, s):
        return lax.rem(j + s[0] * HALF, 2 * HALF)

    def kernel(s, n2, res, cot, wi0, wi1, wo0, wo1, bi, vec, hid, dpre, mixed, dn2, dbi, acc, back):
        j = pl.program_id(0)
        n = natural(j, s)
        win = jnp.concatenate([wi0[...], wi1[...].reshape(D // 2, UNITS)], axis=0)
        pre = dot(n2[...], win) + bi[pl.ds(n, 1), :]
        t = jnp.tanh(K_NORM * (pre + 0.044715 * (pre * pre * pre)))
        hidden = (0.5 * pre * (1.0 + t)).astype(bf16)
        slope = 0.5 * (1.0 + t) + (0.5 * K_NORM) * pre * (1.0 - t * t) * (
            1.0 + (3 * 0.044715) * (pre * pre)
        )
        hid[...] = hidden

        def rest(wo, start):
            d_pre = (dot_t(cot[...], wo) * slope).astype(bf16)
            dpre[...] = d_pre
            dbi[pl.ds(n, 1), :] = jnp.sum(d_pre.astype(f32), axis=0, keepdims=True)
            if start:
                acc[...] = dot(hidden, wo)
                back[...] = dot_t(d_pre, win)
            else:
                acc[...] += dot(hidden, wo)
                back[...] += dot_t(d_pre, win)

        @pl.when(j == 0)
        def _():
            rest(wo0[...], True)

        @pl.when((j > 0) & (j < HALF))
        def _():
            rest(wo0[...], False)

        @pl.when(j >= HALF)
        def _():
            rest(wo1[...].reshape(UNITS, D), False)

        @pl.when(j == 2 * HALF - 1)
        def _():
            mixed[...] = (res[...] + acc[...] + row(vec, B_OUT)).astype(bf16)
            dn2[:, pl.ds(at(s[0] * (D // 2)), D // 2)] = back[:, : D // 2]
            dn2[:, pl.ds(at((1 - s[0]) * (D // 2)), D // 2)] = back[:, D // 2 :]

    out = (
        shape((T, FF), bf16),
        shape((T, FF), bf16),
        shape((T, D), bf16),
        shape((T, D), f32),
        shape((2 * HALF, UNITS), f32),
    )
    by_unit = pl.BlockSpec((T, UNITS), lambda j, s: (0, natural(j, s)))
    return call(
        kernel,
        out,
        (2 * HALF,),
        [
            whole(n2_rel),
            whole(residual),
            whole(cotangent),
            pl.BlockSpec((D // 2, UNITS), lambda j, s: (0, natural(j, s))),
            pl.BlockSpec((32, n_in, UNITS), lambda j, s: (0, natural(j, s), 0)),
            pl.BlockSpec((UNITS, D), lambda j, s: (jnp.minimum(j, HALF - 1), 0)),
            pl.BlockSpec(
                (per, n_out, D), lambda j, s: (jnp.maximum(j - HALF, 0), skip // n_out, 0)
            ),
            whole(b_in),
            whole(vectors),
        ],
        [by_unit, by_unit, whole(out[2]), whole(out[3]), whole(out[4])],
        scalars,
        (n2_rel, residual, cotangent, w_in, spread, w_out, spread, b_in, vectors),
        [pltpu.VMEM((T, D), f32), pltpu.VMEM((T, D), f32)],
    )


def second_norm_back(cotangent, d_n2, residual, vectors, w_o, offsets):
    def kernel(s, cot, dn, res, vec, w, d_res, d_br, d_att, dg, db, dbo):
        xhat, r = center_scale(res[...])
        dn, wide = dn[...], cot[...].astype(f32)
        dg[...] = jnp.sum(dn * xhat, axis=0, keepdims=True)
        db[...] = jnp.sum(dn, axis=0, keepdims=True)
        dbo[...] = jnp.sum(wide, axis=0, keepdims=True)
        total = wide + norm_back(xhat, r, row(vec, LN2_G), dn)
        d_res[...] = total
        low = total.astype(bf16)
        d_br[...] = low
        natural_columns(d_att, dot_t(low, w[...]).astype(bf16), s, THIRDS)

    args = (cotangent, d_n2, residual, vectors, w_o)
    out = (
        shape((T, D), f32),
        shape((T, D), bf16),
        shape((T, D), bf16),
        shape((1, D), f32),
        shape((1, D), f32),
        shape((1, D), f32),
    )
    return call(
        kernel, out, (1,), [whole(a) for a in args], [whole(o) for o in out], offsets, args
    )


def first_norm_back(d_kv, d_q, w_kv, w_q, compressed, memory, tokens, vectors, d_res, offsets):
    steps = 4
    wide, slim = 2 * D // steps, D // steps

    def kernel(s, dkv, dq, kw, qw, comp, mem, tok, vec, dres, dtok, dg, db, acc, nat):
        j = pl.program_id(0)

        @pl.when(j == 0)
        def _():
            acc[...] = dot_t(dkv[0], kw[...])

        @pl.when(j > 0)
        def _():
            acc[...] += dot_t(dkv[0], kw[...])

        acc[2 * T :, :] += dot_t(dq[...], qw[...])

        @pl.when(j == steps - 1)
        def _():
            natural_columns(nat, acc, s, THIRDS)
            gain = row(vec, LN1_G)
            sum_g = jnp.zeros((1, D), f32)
            sum_b = jnp.zeros((1, D), f32)
            for block, ref in enumerate((comp, mem, tok)):
                for i in range(0, T, 32):
                    xhat, r = center_scale(ref[i : i + 32, :].astype(f32))
                    dn = nat[block * T + i : block * T + i + 32, :]
                    sum_g += jnp.sum(dn * xhat, axis=0, keepdims=True)
                    sum_b += jnp.sum(dn, axis=0, keepdims=True)
                    if block == 2:
                        dtok[i : i + 32, :] = dres[i : i + 32, :] + norm_back(xhat, r, gain, dn)
            dg[...] = sum_g
            db[...] = sum_b

    rest = (compressed, memory, tokens, vectors, d_res)
    out = (shape((T, D), f32), shape((1, D), f32), shape((1, D), f32))
    return call(
        kernel,
        out,
        (steps,),
        [
            pl.BlockSpec((1, KEYS, wide), lambda j, s: (j // (steps // 2), 0, lax.rem(j, steps // 2))),
            pl.BlockSpec((T, slim), lambda j, s: (0, j)),
            pl.BlockSpec((D, wide), lambda j, s: (0, j)),
            pl.BlockSpec((D, slim), lambda j, s: (0, j)),
        ]
        + [whole(a) for a in rest],
        [whole(o) for o in out],
        offsets,
        (d_kv, d_q, w_kv, w_q, *rest),
        [pltpu.VMEM((KEYS, D), f32), pltpu.VMEM((KEYS, D), f32)],
    )


def compress(oldest, pieces, vectors, offsets):
    block = 256
    rows = T // 3

    def kernel(s, x, w0, w1, w2, vec, compact, normed, x_rel, natural):
        j = pl.program_id(0)

        @pl.when(j == 0)
        def _():
            x_rel[...] = relative_columns(x, s, (3 * D // 2, 3 * D // 4, 3 * D // 4))

        w = jnp.concatenate([w0[...], w1[...], w2[...]], axis=0)
        here = pl.ds(at(j * block), block)
        compact[:, here] = dot(x_rel[...], w) + vec[CONV_B : CONV_B + 1, here]

        @pl.when(j == D // block - 1)
        def _():
            xhat, r = center_scale(compact[...])
            natural[...] = (xhat * row(vec, LN1_G) + row(vec, LN1_B)).astype(bf16)
            start = 0
            for i, width in enumerate(THIRDS):
                normed[:, start : start + width] = natural[:, pl.ds(at(s[3 + i]), width)]
                start += width

    out = (shape((rows, D), f32), shape((rows, D), bf16))
    return call(
        kernel,
        out,
        (D // block,),
        [whole(oldest)]
        + [pl.BlockSpec((w.shape[0], block), lambda j, s: (0, j)) for w in pieces]
        + [whole(vectors)],
        [whole(o) for o in out],
        offsets,
        (oldest, *pieces, vectors),
        [pltpu.VMEM((rows, 3 * D), bf16), pltpu.VMEM((rows, D), bf16)],
    )


def reconstruct(queries, key_value, comp_pair, none):
    rows = T // 3

    def kernel(_, q, k, v, ck, cv, loss, dck, dcv):
        @pl.when(pl.program_id(0) == 0)
        def _():
            loss[...] = jnp.zeros_like(loss)

        def body(i, cut):
            asking = (q[:, cut] * FACTOR).astype(bf16)
            cvh = cv[:, cut]
            p = softmax(dot_t(asking, k[:, cut])).astype(bf16)
            gp = softmax(dot_t(asking, ck[:, cut]))
            low = gp.astype(bf16)
            miss = dot(p, v[:, cut]) - dot(low, cvh)
            loss[...] += jnp.sum(miss * miss, axis=0, keepdims=True)
            d_guess = ((-2.0 / (T * D)) * miss).astype(bf16)
            d_gp = dot_t(d_guess, cvh)
            dcv[:, cut] = t_dot(low, d_guess).astype(bf16)
            d_gs = (gp * (d_gp - jnp.sum(gp * d_gp, axis=-1, keepdims=True))).astype(bf16)
            dck[:, cut] = t_dot(d_gs, asking).astype(bf16)

        each_head(body)

    return call(
        kernel,
        (shape((1, HD), f32), shape((rows, D), bf16), shape((rows, D), bf16)),
        (STEPS,),
        [head(T), head(T, 1), head(T, 1, H), head(rows), head(rows, 0, H)],
        [pl.BlockSpec((1, HD), lambda h, s: (0, 0)), head(rows), head(rows)],
        none,
        (queries, key_value, key_value, comp_pair, comp_pair),
    )


def compress_back(dck, dcv, w_kv, compact, vectors, offsets):
    rows = T // 3

    def kernel(s, dck, dcv, w, compact, vec, d_compact, d_bias, dn):
        back = dot_t(jnp.concatenate([dck[...], dcv[...]], axis=1), w[...])
        natural_columns(dn, back, s, THIRDS)
        xhat, r = center_scale(compact[...])
        low = norm_back(xhat, r, row(vec, LN1_G), dn[...]).astype(bf16)
        d_compact[...] = low
        d_bias[...] = jnp.sum(low.astype(f32), axis=0, keepdims=True)

    args = (dck, dcv, w_kv, compact, vectors)
    out = (shape((rows, D), bf16), shape((1, D), f32))
    return call(
        kernel,
        out,
        (1,),
        [whole(a) for a in args],
        [whole(o) for o in out],
        offsets,
        args,
        [pltpu.VMEM((rows, D), f32)],
    )


def weight_grads(groups, scalars):
    in_specs, args, outs, out_specs, layout = [], [], [], [], []
    for ring, jobs in groups:
        first = 1 if ring == "x" else 5
        block = jobs[0][0][0].shape[1] // 8
        widths = []
        for xs, row_block, rows, dys, ready in jobs:
            width = dys[0].shape[1] // (1 if ready else 2)
            widths.append(width)
            for x in xs:
                for y in range(2):
                    in_specs.append(
                        pl.BlockSpec(
                            (rows, block),
                            lambda q, s, r=row_block, f=first, y=y: (r, y * 4 + s[f + q]),
                        )
                    )
                    args.append(x)
            for dy in dys:
                in_specs.append(
                    pl.BlockSpec((rows, width), lambda q, s, r=ready: (0, 0 if r else s[0]))
                )
                args.append(dy)
        dims = (1, 2, block, sum(widths))
        outs += [shape((2, *dims[1:]), bf16)] * 2
        out_specs += [
            pl.BlockSpec(dims, lambda q, s: (jnp.minimum(q, 1), 0, 0, 0)),
            pl.BlockSpec(dims, lambda q, s: (jnp.maximum(q - 2, 0), 0, 0, 0)),
        ]
        layout.append(widths)

    def kernel(s, *refs):
        q = pl.program_id(0)
        place = 0
        results = refs[len(in_specs) :]
        for i, widths in enumerate(layout):
            send, keep = results[2 * i : 2 * i + 2]
            block = send.shape[2]
            start = 0
            for width in widths:
                a0, a1, b0, b1, da, db = (r[...] for r in refs[place : place + 6])
                place += 6
                x = jnp.concatenate(
                    [jnp.concatenate([a0, a1], axis=1), jnp.concatenate([b0, b1], axis=1)], axis=0
                )
                value = t_dot(x, jnp.concatenate([da, db], axis=0)).astype(bf16)
                value = value.reshape(2, block, width)
                cut = slice(start, start + width)
                send[0, :, :, cut] = jnp.where(q < 2, value, send[0, :, :, cut])
                keep[0, :, :, cut] = value
                start += width

    flat = call(kernel, tuple(outs), (4,), in_specs, out_specs, scalars, args)
    return [(flat[2 * i], flat[2 * i + 1]) for i in range(len(groups))]


def widen(gathered, start, rows, columns, swapped, none):
    u = rows // 16
    sub = u // 32
    chunks = columns // 2 // STEP
    order = [x * 4 + z for z in range(4) for x in range(4)] if swapped else list(range(16))

    def kernel(_, *refs):
        out = refs[-1]
        for k, src in enumerate(refs[:-1]):
            for to, frm in enumerate(order):
                out[to, :, k * STEP : (k + 1) * STEP] = src[frm].astype(f32)

    return call(
        kernel,
        shape((16, u, columns), f32),
        (sub, 2),
        [
            pl.BlockSpec((16, 32, STEP), lambda i, c, s, k=k: (c, start // 32 + k * sub + i, 0))
            for k in range(chunks)
        ],
        pl.BlockSpec((16, 32, STEP * chunks), lambda i, c, s: (0, i, c)),
        none,
        (gathered,) * chunks,
    ).reshape(rows, columns)


def widen_near(own, twin, start, columns, swapped, scalars):
    chunks = columns // 2 // STEP
    u = D // 32

    def kernel(s, own, twin, out):
        def fill(src, base):
            for a in range(4):
                for b in range(4):
                    first, second = s[base + a], s[base + 4 + b]
                    place = second * 4 + first if swapped else first * 4 + second
                    for k in range(chunks):
                        rows = slice(start + k * u, start + (k + 1) * u)
                        value = src[a, b, rows, :].astype(f32)
                        out[pl.ds(place, 1), :, k * STEP : (k + 1) * STEP] = value[None]

        @pl.when(pl.program_id(0) == 0)
        def _():
            fill(own, 1)

        @pl.when(pl.program_id(0) == 1)
        def _():
            fill(twin, 9)

    return call(
        kernel,
        shape((16, u, columns), f32),
        (2,),
        [whole(own), whole(twin)],
        pl.BlockSpec((16, u, chunks * STEP), lambda h, s: (0, 0, lax.rem(h + s[0], 2))),
        scalars,
        (own, twin),
    ).reshape(D // 2, columns)


def core_swap(v):
    return lax.ppermute(v, "c", [(0, 1), (1, 0)])


def pair_swap(v):
    return lax.ppermute(v, "yl", [(0, 1), (1, 0)])


def exchange(v, ring, masks):
    def flat(i, c):
        return (i // 2 * 2 + c) * 2 + i % 2 if ring == "y" else 2 * i + c

    pairs = [(flat(i, c), flat(i ^ masks[c], c)) for i in range(4) for c in range(2)]
    return lax.ppermute(v, RING[ring], pairs)


def pick(v, index, axis):
    return lax.dynamic_index_in_dim(v, index, axis, keepdims=False)


def quarters(place, core):
    first = jnp.where(core == 0, 1, 3)
    second = jnp.where(core == 0, 3, 1)
    return place, place ^ first, place ^ 2, place ^ second


class Flow:
    def __init__(self, ring, pair, place, core):
        self.rings = (ring, "z" if ring == "x" else "x")
        self.place, self.core = place, core
        send, self.keep = pair
        self.got = exchange(send, ring, (1, 3))

    def onward(self, ring):
        got = line.later(self.got)
        self.near = got[0]
        value = (self.keep[1].astype(f32) + got[1].astype(f32)).astype(bf16)
        self.last = exchange(value, ring, (3, 1))
        line.hold(value)

    def settle(self):
        last = line.later(self.last)
        return self.keep[0].astype(f32) + self.near.astype(f32) + last.astype(f32)

    def second(self):
        self.onward(self.rings[0])

    def third(self):
        v = self.settle()
        y, rows, columns = v.shape
        v = v.reshape(y, 4, rows // 4, columns)
        ring = self.rings[1]
        own, first, far, second = quarters(self.place[ring], self.core)
        send = jnp.stack([pick(v, first, 1), pick(v, far, 1)]).astype(bf16)
        self.keep = (pick(v, own, 1), pick(v, second, 1))
        self.got = exchange(send, ring, (1, 3))
        line.hold(send, *self.keep)

    def fourth(self):
        self.onward(self.rings[1])

    def rows(self):
        v = self.settle()
        y, u, columns = v.shape
        v = v.reshape(y, u, columns // STEP, STEP).transpose(0, 2, 1, 3)
        return v.reshape(y, -1, STEP)


class Spread:
    def __init__(self, v, rings):
        self.rings = rings
        self.v = v
        self.got = exchange(v, rings[0], (1, 3))
        line.hold(v)

    def second(self, ring=None):
        pair = jnp.stack([self.v, line.later(self.got)])
        self.v = pair
        self.got = exchange(pair, ring or self.rings[0], (3, 1))
        line.hold(pair)

    def third(self):
        four = jnp.concatenate([self.v, line.later(self.got)])
        self.v = four
        self.got = exchange(four, self.rings[1], (1, 3))
        line.hold(four)

    def fourth(self):
        self.second(self.rings[1])

    def done(self):
        all_ = jnp.concatenate([self.v, line.later(self.got)])
        return all_, core_swap(all_)


class Finish:
    def __init__(self, parts, yl):
        v = jnp.concatenate(parts, axis=1)
        self.mine = pick(v, yl, 0)
        send = pick(v, 1 - yl, 0).astype(bf16)
        self.got = exchange(send, "y", (1, 3))
        line.hold(send, self.mine)

    def second(self):
        got = line.later(self.got)
        self.mine = (self.mine + got.astype(f32)).astype(bf16)
        self.far = lax.ppermute(self.mine, "yh", [(0, 1), (1, 0)])
        line.hold(self.mine)

    def done(self):
        far = line.later(self.far)
        return (self.mine.astype(f32) + far.astype(f32)).astype(bf16)


def per_device(
    tokens,
    memory,
    compressed,
    cotangent,
    ln1_g,
    ln1_b,
    w_q,
    w_kv,
    w_r,
    bias_u,
    bias_v,
    w_o,
    ln2_g,
    ln2_b,
    w_in,
    b_in,
    w_out,
    b_out,
    conv_w,
    conv_b,
):
    line.held = []
    tokens, memory, compressed, cotangent = tokens[0], memory[0], compressed[0], cotangent[0]
    yl, core = lax.axis_index("yl"), lax.axis_index("c")
    place = {"x": lax.axis_index("x"), "z": lax.axis_index("z")}
    none = jnp.zeros((1,), jnp.int32)
    ints = lambda *v: jnp.stack([jnp.asarray(i, jnp.int32) for i in v])

    def thirds(rows):
        half = rows // 2
        other = (1 - yl) * half
        return [yl * half, other + core * (half // 2), other + (1 - core) * (half // 2)]

    def both(v):
        return (v, core_swap(v))

    spot = (place["x"] * 4 + place["z"]) * 2 + core
    n_in, n_out = w_in.shape[0] // 32, w_out.shape[0] // 32
    piece_in = lax.dynamic_slice_in_dim(w_in, spot * n_in, n_in, 0)
    piece_out = lax.dynamic_slice_in_dim(w_out, spot * n_out, n_out, 0)
    piece = jnp.concatenate(
        [piece_in[:, i * D : (i + 1) * D] for i in range(FF // D)] + [piece_out], axis=0
    )
    piece_got = pair_swap(piece)
    line.hold(piece)

    flat = jnp.concatenate(
        [
            line.later(ln1_g), ln1_b, bias_u, bias_v, ln2_g, ln2_b, b_out, conv_b, b_in
        ]
    ).reshape(-1, STEP)
    flat_got = pair_swap(flat)
    line.hold(flat)

    def over_y(w):
        n = w.shape[0] // 2
        part = lax.dynamic_slice_in_dim(line.later(w), core * n, n, 0)
        line.hold(part)
        return exchange(part, "y", (1, 3))

    def joined(w, got, twin):
        return jnp.concatenate([w, got, twin], axis=0)

    kv_got = over_y(w_kv)
    n = w_q.shape[0] // 2
    small = jnp.stack([lax.dynamic_slice_in_dim(line.later(w), core * n, n, 0) for w in (w_q, w_r, w_o)])
    small_got = exchange(small, "y", (1, 3))
    line.hold(small)
    conv_got = over_y(conv_w)
    spread = lax.all_gather(piece_got, ("x", "z", "c"), axis=0)

    thirds_d, thirds_c = ints(*thirds(D)), ints(*thirds(3 * D), *thirds(D))
    sinus_table = sinusoid(KEYS, D).astype(bf16)
    sinus_rel = jnp.concatenate(
        [
            lax.dynamic_slice_in_dim(sinus_table, thirds_d[i], width, 1)
            for i, width in enumerate(THIRDS)
        ],
        axis=1,
    )
    line.hold(sinus_rel)
    vectors, b_in = unpack(flat, flat_got, ints(yl))

    normed, normed_rel, oldest = first_norm(compressed, memory, tokens, vectors, thirds_d)
    both_normed, both_oldest, both_cot = both(normed), both(oldest), both(cotangent)
    kv_got = line.later(kv_got)
    kv_whole = joined(w_kv, kv_got, core_swap(kv_got))
    key_value = dot(normed_rel, kv_whole).astype(bf16)
    line.hold(key_value)
    small_got = line.later(small_got)
    small_twin = core_swap(small_got)
    q_whole, r_whole, o_whole = [
        joined(w, small_got[i], small_twin[i]) for i, w in enumerate((w_q, w_r, w_o))
    ]
    queries = dot(normed_rel[2 * T :], q_whole)
    relative = dot(sinus_rel, r_whole).astype(bf16)
    line.hold(queries, relative)
    probs, attended = attend(queries, key_value, relative, vectors, none)
    residual, normed2, normed2_rel = out_and_norm(attended, o_whole, tokens, vectors, thirds_d)
    both_n2, both_att = both(normed2), both(attended)

    conv_got = line.later(conv_got)
    compact, comp_normed = compress(
        oldest, (conv_w, conv_got, core_swap(conv_got)), vectors, thirds_c
    )
    comp_pair = dot(comp_normed, kv_whole).astype(bf16)
    loss, d_ck, d_cv = reconstruct(queries, key_value, comp_pair, none)
    recon_loss = jnp.sum(loss) / (T * D)
    compressed_next = jnp.concatenate([compressed[T // 3 :], compact], axis=0)
    d_compact, d_conv_b = compress_back(d_ck, d_cv, kv_whole, compact, vectors, thirds_d)
    both_compact = both(d_compact)

    cuts, rels, twins = [], [], []
    for ring in ("x", "z"):
        own, first, far, second = quarters(place[ring], core)
        cuts += [first, far, own, second]
        rels.append([own, first, second, far])
        twins.append([own, second, first, far])
    cuts = ints(core, *cuts)

    def flows(groups):
        pairs = weight_grads(groups, cuts)
        return [Flow(ring, pair, place, core) for (ring, _), pair in zip(groups, pairs)]

    hidden, d_pre, mixed_out, d_normed2, d_b_in = feed_forward(
        normed2_rel, residual, cotangent, w_in, w_out, spread, b_in, vectors, ints(yl)
    )
    both_hidden, both_pre = both(hidden), both(d_pre)
    (conv_flow,) = flows([("x", [(both_oldest, 0, T // 3, both_compact, False)])])
    d_residual, d_branch, d_attended, d_ln2_g, d_ln2_b, d_b_out = second_norm_back(
        cotangent, d_normed2, residual, vectors, o_whole, thirds_d
    )
    both_branch = both(d_branch)
    out_flow, in_flow = flows(
        [
            ("x", [(both_hidden, 0, T, both_cot, False)]),
            ("z", [(both_n2, 0, T, both_pre, False), (both_att, 0, T, both_branch, False)]),
        ]
    )
    d_kv, d_relative, d_queries, d_bias_u, d_bias_v = attend_back(
        queries, key_value, relative, vectors, probs, d_attended, none
    )
    give_kv = pick(d_kv, 1 - core, 0)
    both_kv = (pick(d_kv, core, 0), core_swap(give_kv))
    both_q, both_rel = both(d_queries), both(d_relative)
    line.hold(give_kv)
    conv_flow.second()
    d_tokens, d_ln1_g, d_ln1_b = first_norm_back(
        d_kv, d_queries, kv_whole, q_whole, compressed, memory, tokens, vectors, d_residual,
        thirds_d,
    )
    conv_flow.third()
    x_flow, z_flow = flows(
        [
            ("x", [(both_normed, 0, KEYS, both_kv, True)]),
            (
                "z",
                [
                    (both_normed, 2, T, both_q, False),
                    ((sinus_table, sinus_table), 0, KEYS, both_rel, False),
                ],
            ),
        ]
    )
    out_flow.second()
    in_flow.second()
    conv_flow.fourth()
    x_flow.second()
    z_flow.second()
    out_flow.third()
    in_flow.third()
    x_flow.third()
    z_flow.third()
    out_flow.fourth()
    in_flow.fourth()
    early = Finish([out_flow.rows(), in_flow.rows(), conv_flow.rows()], yl)
    x_flow.fourth()
    z_flow.fourth()
    early.second()

    total = jnp.concatenate(
        [d_ln1_g, d_ln1_b, d_bias_u, d_bias_v, d_ln2_g, d_ln2_b, d_b_out, d_conv_b]
        + [d_b_in]
    )
    total = jnp.concatenate(
        [total[:8].reshape(8, 2, STEP).transpose(1, 0, 2), total[8:].reshape(2, 4, STEP)], axis=1
    )
    late = Finish([x_flow.rows(), z_flow.rows(), total, jnp.zeros((2, 4, STEP), f32)], yl)
    early_done = early.done()
    line.hold(early_done)
    early_sums = lax.all_gather(early_done, ("c", "x", "z"), axis=0)
    late.second()
    late_done = late.done()
    kv_spread = Spread(late_done[:64], ("z", "x"))
    qr_spread = Spread(late_done[64:], ("x", "z"))
    kv_spread.second()
    qr_spread.second()
    kv_spread.third()
    qr_spread.third()
    kv_spread.fourth()
    qr_spread.fourth()
    (kv_own, kv_twin), (qr_own, qr_twin) = kv_spread.done(), qr_spread.done()
    x_places, z_places = rels
    x_twin, z_twin = twins
    along = ints(core, *x_places, *z_places, *x_twin, *z_twin)
    across = ints(core, *z_places, *x_places, *z_twin, *x_twin)
    g_kv = widen_near(kv_own, kv_twin, 0, 2 * D, False, along)
    g_q = widen_near(qr_own, qr_twin, 0, D, False, across)
    g_r = widen_near(qr_own, qr_twin, 32, D, False, across)
    g_out = widen(early_sums, 0, FF // 2, D, False, none)
    g_in = widen(early_sums, 128, D // 2, FF, True, none)
    g_o = widen(early_sums, 256, D // 2, D, True, none)
    g_conv = widen(early_sums, 288, 3 * D // 2, D, False, none)

    def four(v):
        return (v[0] + v[1]) + (v[2] + v[3])

    half = four(four(qr_own[:, :, 64:76].astype(f32))) + four(
        four(qr_twin[:, :, 64:76].astype(f32))
    )
    t_ln1_g, t_ln1_b, t_bu, t_bv, t_ln2_g, t_ln2_b, t_bout, t_convb = [half[i] for i in range(8)]
    t_bin = half[8:].reshape(-1)
    return (
        mixed_out[None],
        compressed_next[None],
        recon_loss[None],
        d_tokens[None],
        t_ln1_g,
        t_ln1_b,
        g_q,
        g_kv,
        g_r,
        t_bu,
        t_bv,
        g_o,
        t_ln2_g,
        t_ln2_b,
        g_in,
        t_bin,
        g_out,
        t_bout,
        g_conv,
        t_convb,
    )


def solution(mesh):
    fine = Mesh(mesh.devices.reshape(2, 4, 4, 2, 2), AXES)
    stream = P(AXES, None, None)
    vec, mat = P("yl"), P("yl", None)
    weights = (vec, vec, mat, mat, mat, vec, vec, mat, vec, vec, mat, vec, mat, vec, mat, vec)
    return jax.shard_map(
        per_device,
        mesh=fine,
        in_specs=(stream,) * 4 + weights,
        out_specs=(stream, stream, P(AXES), stream) + weights,
        check_vma=False,
    )
```

```python
import jax
import jax.numpy as jnp
from jax import lax
from jax.experimental import pallas as pl
from jax.experimental.pallas import tpu as pltpu
from jax.sharding import Mesh, PartitionSpec as P

H = 8
HD = 128
D = 1024
T = 192
KEYS = 576
PAD = 640
FF = 4096
FACTOR = HD ** (-0.5)
f32 = jnp.float32
bf16 = jnp.bfloat16
AXES = ("yh", "x", "z", "c", "yl")
RING = {"x": ("x", "c"), "z": ("z", "c"), "y": ("yh", "c", "yl")}


def sinusoid(key_count, model_dim):
    distance = (key_count - 1 - jnp.arange(key_count)).astype(f32)
    inverse = 1.0 / 10000.0 ** (jnp.arange(0, model_dim, 2).astype(f32) / model_dim)
    angles = distance[:, None] * inverse[None, :]
    return jnp.concatenate([jnp.sin(angles), jnp.cos(angles)], axis=-1)


def dot(a, b):
    return jnp.dot(a, b, preferred_element_type=f32)


def dot_t(a, b):
    return lax.dot_general(a, b, (((1,), (1,)), ((), ())), preferred_element_type=f32)


def t_dot(a, b):
    return lax.dot_general(a, b, (((0,), (0,)), ((), ())), preferred_element_type=f32)


class Line:
    def __init__(self):
        self.held = []

    def hold(self, *values):
        self.held += values

    def later(self, value):
        return lax.optimization_barrier((value, *self.held))[0] if self.held else value

    def ran(self, value):
        self.held = [value]


line = Line()


def call(kernel, out, grid, in_specs, out_specs, scalars, args, scratch=()):
    result = run_kernel(
        kernel, out, grid, in_specs, out_specs, line.later(scalars), args, scratch
    )
    line.ran(jax.tree.leaves(result)[0])
    return result


def run_kernel(kernel, out, grid, in_specs, out_specs, scalars, args, scratch):
    return pl.pallas_call(
        kernel,
        out_shape=out,
        grid_spec=pltpu.PrefetchScalarGridSpec(
            num_scalar_prefetch=1,
            grid=grid,
            in_specs=in_specs,
            out_specs=out_specs,
            scratch_shapes=list(scratch),
        ),
        compiler_params=pltpu.CompilerParams(vmem_limit_bytes=56 << 20),
    )(scalars, *args)


def whole(a):
    zeros = (0,) * a.ndim
    return pl.BlockSpec(a.shape, lambda *_: zeros)


def shape(dims, dtype):
    return jax.ShapeDtypeStruct(dims, dtype)


def at(offset):
    return pl.multiple_of(offset, 128)


def center_scale(v):
    mid = v - jnp.mean(v, axis=-1, keepdims=True)
    r = lax.rsqrt(jnp.mean(mid * mid, axis=-1, keepdims=True) + 1e-5)
    return mid * r, r


def norm_back(xhat, r, g, dn):
    gd = dn * g
    return r * (
        gd
        - jnp.mean(gd, axis=-1, keepdims=True)
        - xhat * jnp.mean(gd * xhat, axis=-1, keepdims=True)
    )


def softmax(s):
    e = jnp.exp(s - jnp.max(s, axis=-1, keepdims=True))
    return e / jnp.sum(e, axis=-1, keepdims=True)


(LN1_G, LN1_B, BIAS_U, BIAS_V, LN2_G, LN2_B, B_OUT, CONV_B) = range(8)


def row(ref, i):
    return ref[i : i + 1, :]


def pack(vectors, w_in, w_out, conv_w, scalars):
    n_in, n_out, n_conv = (w.shape[0] // 32 for w in (w_in, w_out, conv_w))
    chunks = FF // D
    rows = n_out + n_in * chunks + n_conv

    def kernel(_, *refs):
        wi, wo, wc, flat, piece = refs[-5:]
        for i, ref in enumerate(refs[:8]):
            flat[i : i + 1, :] = ref[...].astype(f32).reshape(1, STEP)
        b_in = refs[8][...].astype(f32).reshape(chunks, STEP)
        flat[8 : 8 + chunks, :] = b_in
        flat[8 + chunks :, :] = jnp.zeros((16 - 8 - chunks, STEP), f32)
        piece[:n_out, :] = wo[...]
        for i in range(chunks):
            piece[n_out + i * n_in : n_out + (i + 1) * n_in, :] = wi[:, i * D : (i + 1) * D]
        piece[n_out + n_in * chunks :, :] = wc[...]

    out = (shape((16, STEP), f32), shape((rows, D), bf16))
    return call(
        kernel,
        out,
        (1,),
        [whole(v) for v in vectors]
        + [
            pl.BlockSpec((w.shape[0] // 32, w.shape[1]), lambda j, s: (s[0], 0))
            for w in (w_in, w_out, conv_w)
        ],
        [whole(o) for o in out],
        scalars,
        (*vectors, w_in, w_out, conv_w),
    )


def pack_rows(w_kv, w_q, w_r, w_o, scalars):
    n = w_q.shape[0] // 2

    def kernel(_, kv, q, r, o, kv_out, out):
        kv_out[...] = kv[...]
        for i, ref in enumerate((q, r, o)):
            out[i] = ref[...]

    out = (shape((n, 2 * D), bf16), shape((3, n, D), bf16))
    return call(
        kernel,
        out,
        (1,),
        [
            pl.BlockSpec((n, w.shape[1]), lambda j, s: (s[0], 0))
            for w in (w_kv, w_q, w_r, w_o)
        ],
        [whole(o) for o in out],
        scalars,
        (w_kv, w_q, w_r, w_o),
    )


def unpack(mine, theirs, scalars):
    half = D // 2

    def kernel(s, mine, theirs, vectors, b_in):
        a, b = mine[...], theirs[...]
        low = jnp.where(s[0] == 0, a, b)
        high = jnp.where(s[0] == 0, b, a)
        vectors[:, :half] = low[:8]
        vectors[:, half:] = high[:8]
        for i in range(FF // D):
            part, k = (low, i) if i < 2 else (high, i - 2)
            b_in[i : i + 1, :half] = part[8 + 2 * k : 9 + 2 * k]
            b_in[i : i + 1, half:] = part[9 + 2 * k : 10 + 2 * k]

    args = (mine, theirs)
    out = (shape((8, D), f32), shape((FF // D, D), f32))
    return call(
        kernel, out, (1,), [whole(a) for a in args], [whole(o) for o in out], scalars, args
    )


def relative_columns(x, s, widths):
    parts = [x[:, pl.ds(at(s[i]), width)] for i, width in enumerate(widths)]
    return jnp.concatenate(parts, axis=1)


def natural_columns(out, x, s, widths):
    start = 0
    for i, width in enumerate(widths):
        out[:, pl.ds(at(s[i]), width)] = x[:, start : start + width]
        start += width


THIRDS = (D // 2, D // 4, D // 4)


def first_norm(compressed, memory, tokens, vectors, offsets):
    def kernel(s, comp, mem, tok, vec, out, out_rel, old):
        gain, bias = row(vec, LN1_G), row(vec, LN1_B)

        def part(ref, base):
            for i in range(0, T, 32):
                xhat, r = center_scale(ref[i : i + 32, :].astype(f32))
                out[base + i : base + i + 32, :] = (xhat * gain + bias).astype(bf16)

        part(comp, 0)
        part(mem, T)
        part(tok, 2 * T)
        out_rel[...] = relative_columns(out, s, THIRDS)
        line_of = lax.broadcasted_iota(jnp.int32, (T // 3, T), 0)
        col = lax.broadcasted_iota(jnp.int32, (T // 3, T), 1)
        low = mem[...].astype(bf16)
        for tap in range(3):
            take = jnp.where(col == 3 * line_of + tap, 1.0, 0.0).astype(bf16)
            old[:, tap * D : (tap + 1) * D] = dot(take, low).astype(bf16)

    args = (compressed, memory, tokens, vectors)
    out = (shape((KEYS, D), bf16), shape((KEYS, D), bf16), shape((T // 3, 3 * D), bf16))
    return call(
        kernel, out, (1,), [whole(a) for a in args], [whole(o) for o in out], offsets, args
    )


PAIR = 2
STEPS = H // PAIR


def head(rows, row_block=0, first=0):
    return pl.BlockSpec((rows, PAIR * HD), lambda h, s: (row_block, first // PAIR + h))


def vec_head(rows=1):
    return pl.BlockSpec((rows, PAIR * HD), lambda h, s: (0, h))


def each_head(body):
    for i in range(PAIR):
        body(i, slice(i * HD, (i + 1) * HD))


def attend(queries, key_value, relative, vectors, none):
    def kernel(_, q, k, v, rel, vec, probs, out):
        pad = jnp.zeros((PAD - KEYS, HD), bf16)
        row = lax.broadcasted_iota(jnp.int32, (T, PAD), 0)
        col = lax.broadcasted_iota(jnp.int32, (T, PAD), 1)
        seen = col <= row + (KEYS - T)

        def body(i, cut):
            content = ((q[:, cut] + vec[BIAS_U : BIAS_U + 1, cut]) * FACTOR).astype(bf16)
            located = ((q[:, cut] + vec[BIAS_V : BIAS_V + 1, cut]) * FACTOR).astype(bf16)
            raw = dot_t(located, jnp.concatenate([rel[:, cut], pad], axis=0))
            raw = pltpu.roll(raw, PAD - T + 1, 1, stride=1, stride_axis=0)
            s = dot_t(content, jnp.concatenate([k[:, cut], pad], axis=0)) + raw
            p = softmax(jnp.where(seen, s, -1e30))
            probs[i] = p
            low = p.astype(bf16)
            out[:, cut] = dot(low, jnp.concatenate([v[:, cut], pad], axis=0)).astype(bf16)

        each_head(body)

    return call(
        kernel,
        (shape((H, T, PAD), f32), shape((T, D), bf16)),
        (STEPS,),
        [head(T), head(KEYS), head(KEYS, 0, H), head(KEYS), vec_head(8)],
        [pl.BlockSpec((PAIR, T, PAD), lambda h, s: (h, 0, 0)), head(T)],
        none,
        (queries, key_value, key_value, relative, vectors),
    )


def attend_back(queries, key_value, relative, vectors, probs, d_attended, scalars):
    def kernel(s, q, k, v, rel, vec, probs, d_att, d_kv, mine, give, d_rel, d_q, d_bu, d_bv):
        pad = jnp.zeros((PAD - KEYS, HD), bf16)
        row = lax.broadcasted_iota(jnp.int32, (T, T), 0)
        col = lax.broadcasted_iota(jnp.int32, (T, T), 1)
        flip = jnp.where(row + col == T - 1, 1.0, 0.0).astype(bf16)

        def body(i, cut):
            content = ((q[:, cut] + vec[BIAS_U : BIAS_U + 1, cut]) * FACTOR).astype(bf16)
            located = ((q[:, cut] + vec[BIAS_V : BIAS_V + 1, cut]) * FACTOR).astype(bf16)
            p, da = probs[i], d_att[:, cut]
            d_p = dot_t(da, jnp.concatenate([v[:, cut], pad], axis=0))
            d_v = t_dot(p.astype(bf16), da)[:KEYS].astype(bf16)
            d_s = (p * (d_p - jnp.sum(p * d_p, axis=-1, keepdims=True))).astype(bf16)
            d_c = dot(d_s, jnp.concatenate([k[:, cut], pad], axis=0)) * FACTOR
            d_k = t_dot(d_s, content)[:KEYS].astype(bf16)
            d_kv[0, :, cut] = d_k
            d_kv[1, :, cut] = d_v
            mine[:, cut] = jnp.where(s[0] == 0, d_k, d_v)
            give[:, cut] = jnp.where(s[0] == 0, d_v, d_k)
            d_raw = pltpu.roll(dot(flip, d_s), 0, 1, stride=1, stride_axis=0)
            d_raw = dot(flip, d_raw.astype(bf16)).astype(bf16)
            d_l = dot(d_raw, jnp.concatenate([rel[:, cut], pad], axis=0)) * FACTOR
            d_rel[:, cut] = t_dot(d_raw, located)[:KEYS].astype(bf16)
            d_q[:, cut] = (d_c + d_l).astype(bf16)
            d_bu[:, cut] = jnp.sum(d_c, axis=0, keepdims=True)
            d_bv[:, cut] = jnp.sum(d_l, axis=0, keepdims=True)

        each_head(body)

    return call(
        kernel,
        (
            shape((2, KEYS, D), bf16),
            shape((KEYS, D), bf16),
            shape((KEYS, D), bf16),
            shape((KEYS, D), bf16),
            shape((T, D), bf16),
            shape((1, D), f32),
            shape((1, D), f32),
        ),
        (STEPS,),
        [
            head(T),
            head(KEYS),
            head(KEYS, 0, H),
            head(KEYS),
            vec_head(8),
            pl.BlockSpec((PAIR, T, PAD), lambda h, s: (h, 0, 0)),
            head(T),
        ],
        [
            pl.BlockSpec((2, KEYS, PAIR * HD), lambda h, s: (0, 0, h)),
            head(KEYS),
            head(KEYS),
            head(KEYS),
            head(T),
            vec_head(),
            vec_head(),
        ],
        scalars,
        (queries, key_value, key_value, relative, vectors, probs, d_attended),
    )


def out_and_norm(attended, w_o, tokens, vectors, offsets):
    def kernel(s, att, w, tok, vec, res, n2, n2_rel):
        total = tok[...].astype(f32) + dot(relative_columns(att, s, THIRDS), w[...])
        res[...] = total
        xhat, r = center_scale(total)
        n2[...] = (xhat * row(vec, LN2_G) + row(vec, LN2_B)).astype(bf16)
        other = at(D // 2 - s[0])
        n2_rel[:, : D // 2] = n2[:, pl.ds(at(s[0]), D // 2)]
        n2_rel[:, D // 2 :] = n2[:, pl.ds(other, D // 2)]

    args = (attended, w_o, tokens, vectors)
    out = (shape((T, D), f32), shape((T, D), bf16), shape((T, D), bf16))
    return call(
        kernel, out, (1,), [whole(a) for a in args], [whole(o) for o in out], offsets, args
    )


STEP = 512
UNITS = 1024
HALF = FF // 2 // UNITS


def feed_forward(n2_rel, residual, cotangent, w_in, w_out, spread, b_in, vectors, scalars):
    n_in = w_in.shape[0] // 32
    n_out = w_out.shape[0] // 32
    skip = n_out // n_in
    per = UNITS // n_out
    K_NORM = 0.7978845608028654

    def natural(j, s):
        return lax.rem(j + s[0] * HALF, 2 * HALF)

    def kernel(s, n2, res, cot, wi0, wi1, wo0, wo1, bi, vec, hid, dpre, mixed, dn2, dbi, acc, back):
        j = pl.program_id(0)
        n = natural(j, s)
        win = jnp.concatenate([wi0[...], wi1[...].reshape(D // 2, UNITS)], axis=0)
        pre = dot(n2[...], win) + bi[pl.ds(n, 1), :]
        t = jnp.tanh(K_NORM * (pre + 0.044715 * (pre * pre * pre)))
        hidden = (0.5 * pre * (1.0 + t)).astype(bf16)
        slope = 0.5 * (1.0 + t) + (0.5 * K_NORM) * pre * (1.0 - t * t) * (
            1.0 + (3 * 0.044715) * (pre * pre)
        )
        hid[...] = hidden

        def rest(wo, start):
            d_pre = (dot_t(cot[...], wo) * slope).astype(bf16)
            dpre[...] = d_pre
            dbi[pl.ds(n, 1), :] = jnp.sum(d_pre.astype(f32), axis=0, keepdims=True)
            if start:
                acc[...] = dot(hidden, wo)
                back[...] = dot_t(d_pre, win)
            else:
                acc[...] += dot(hidden, wo)
                back[...] += dot_t(d_pre, win)

        @pl.when(j == 0)
        def _():
            rest(wo0[...], True)

        @pl.when((j > 0) & (j < HALF))
        def _():
            rest(wo0[...], False)

        @pl.when(j >= HALF)
        def _():
            rest(wo1[...].reshape(UNITS, D), False)

        @pl.when(j == 2 * HALF - 1)
        def _():
            mixed[...] = (res[...] + acc[...] + row(vec, B_OUT)).astype(bf16)
            dn2[:, pl.ds(at(s[0] * (D // 2)), D // 2)] = back[:, : D // 2]
            dn2[:, pl.ds(at((1 - s[0]) * (D // 2)), D // 2)] = back[:, D // 2 :]

    out = (
        shape((T, FF), bf16),
        shape((T, FF), bf16),
        shape((T, D), bf16),
        shape((T, D), f32),
        shape((2 * HALF, UNITS), f32),
    )
    by_unit = pl.BlockSpec((T, UNITS), lambda j, s: (0, natural(j, s)))
    return call(
        kernel,
        out,
        (2 * HALF,),
        [
            whole(n2_rel),
            whole(residual),
            whole(cotangent),
            pl.BlockSpec((D // 2, UNITS), lambda j, s: (0, natural(j, s))),
            pl.BlockSpec((32, n_in, UNITS), lambda j, s: (0, skip + natural(j, s), 0)),
            pl.BlockSpec((UNITS, D), lambda j, s: (jnp.minimum(j, HALF - 1), 0)),
            pl.BlockSpec(
                (per, n_out, D), lambda j, s: (jnp.maximum(j - HALF, 0), 0, 0)
            ),
            whole(b_in),
            whole(vectors),
        ],
        [by_unit, by_unit, whole(out[2]), whole(out[3]), whole(out[4])],
        scalars,
        (n2_rel, residual, cotangent, w_in, spread, w_out, spread, b_in, vectors),
        [pltpu.VMEM((T, D), f32), pltpu.VMEM((T, D), f32)],
    )


def second_norm_back(cotangent, d_n2, residual, vectors, w_o, offsets):
    def kernel(s, cot, dn, res, vec, w, d_res, d_br, d_att, dg, db, dbo):
        xhat, r = center_scale(res[...])
        dn, wide = dn[...], cot[...].astype(f32)
        dg[...] = jnp.sum(dn * xhat, axis=0, keepdims=True)
        db[...] = jnp.sum(dn, axis=0, keepdims=True)
        dbo[...] = jnp.sum(wide, axis=0, keepdims=True)
        total = wide + norm_back(xhat, r, row(vec, LN2_G), dn)
        d_res[...] = total
        low = total.astype(bf16)
        d_br[...] = low
        natural_columns(d_att, dot_t(low, w[...]).astype(bf16), s, THIRDS)

    args = (cotangent, d_n2, residual, vectors, w_o)
    out = (
        shape((T, D), f32),
        shape((T, D), bf16),
        shape((T, D), bf16),
        shape((1, D), f32),
        shape((1, D), f32),
        shape((1, D), f32),
    )
    return call(
        kernel, out, (1,), [whole(a) for a in args], [whole(o) for o in out], offsets, args
    )


def first_norm_back(d_kv, d_q, w_kv, w_q, compressed, memory, tokens, vectors, d_res, offsets):
    steps = 4
    wide, slim = 2 * D // steps, D // steps

    def kernel(s, dkv, dq, kw, qw, comp, mem, tok, vec, dres, dtok, dg, db, acc, nat):
        j = pl.program_id(0)

        @pl.when(j == 0)
        def _():
            acc[...] = dot_t(dkv[0], kw[...])

        @pl.when(j > 0)
        def _():
            acc[...] += dot_t(dkv[0], kw[...])

        acc[2 * T :, :] += dot_t(dq[...], qw[...])

        @pl.when(j == steps - 1)
        def _():
            natural_columns(nat, acc, s, THIRDS)
            gain = row(vec, LN1_G)
            sum_g = jnp.zeros((1, D), f32)
            sum_b = jnp.zeros((1, D), f32)
            for block, ref in enumerate((comp, mem, tok)):
                for i in range(0, T, 32):
                    xhat, r = center_scale(ref[i : i + 32, :].astype(f32))
                    dn = nat[block * T + i : block * T + i + 32, :]
                    sum_g += jnp.sum(dn * xhat, axis=0, keepdims=True)
                    sum_b += jnp.sum(dn, axis=0, keepdims=True)
                    if block == 2:
                        dtok[i : i + 32, :] = dres[i : i + 32, :] + norm_back(xhat, r, gain, dn)
            dg[...] = sum_g
            db[...] = sum_b

    rest = (compressed, memory, tokens, vectors, d_res)
    out = (shape((T, D), f32), shape((1, D), f32), shape((1, D), f32))
    return call(
        kernel,
        out,
        (steps,),
        [
            pl.BlockSpec((1, KEYS, wide), lambda j, s: (j // (steps // 2), 0, lax.rem(j, steps // 2))),
            pl.BlockSpec((T, slim), lambda j, s: (0, j)),
            pl.BlockSpec((D, wide), lambda j, s: (0, j)),
            pl.BlockSpec((D, slim), lambda j, s: (0, j)),
        ]
        + [whole(a) for a in rest],
        [whole(o) for o in out],
        offsets,
        (d_kv, d_q, w_kv, w_q, *rest),
        [pltpu.VMEM((KEYS, D), f32), pltpu.VMEM((KEYS, D), f32)],
    )


def compress(oldest, conv_w, spread, vectors, offsets):
    block = 256
    rows = T // 3
    n = conv_w.shape[0] // 32
    skip = (spread.shape[1] - n) // 16

    def kernel(s, x, own, w0, w1, w2, vec, compact, normed, x_rel, natural):
        j = pl.program_id(0)

        @pl.when(j == 0)
        def _():
            x_rel[...] = relative_columns(x, s, (3 * D // 2, 3 * D // 2))

        other = jnp.concatenate([w0[...], w1[...], w2[...]], axis=1).reshape(32 * n, block)
        w = jnp.concatenate([own[...], other], axis=0)
        here = pl.ds(at(j * block), block)
        compact[:, here] = dot(x_rel[...], w) + vec[CONV_B : CONV_B + 1, here]

        @pl.when(j == D // block - 1)
        def _():
            xhat, r = center_scale(compact[...])
            natural[...] = (xhat * row(vec, LN1_G) + row(vec, LN1_B)).astype(bf16)
            start = 0
            for i, width in enumerate(THIRDS):
                normed[:, start : start + width] = natural[:, pl.ds(at(s[2 + i]), width)]
                start += width

    out = (shape((rows, D), f32), shape((rows, D), bf16))
    return call(
        kernel,
        out,
        (D // block,),
        [whole(oldest), pl.BlockSpec((conv_w.shape[0], block), lambda j, s: (0, j))]
        + [
            pl.BlockSpec((32, 16, block), lambda j, s, i=i: (0, skip + i, j))
            for i in range(n // 16)
        ]
        + [whole(vectors)],
        [whole(o) for o in out],
        offsets,
        (oldest, conv_w) + (spread,) * (n // 16) + (vectors,),
        [pltpu.VMEM((rows, 3 * D), bf16), pltpu.VMEM((rows, D), bf16)],
    )


def reconstruct(queries, key_value, comp_pair, none):
    rows = T // 3

    def kernel(_, q, k, v, ck, cv, loss, dck, dcv):
        @pl.when(pl.program_id(0) == 0)
        def _():
            loss[...] = jnp.zeros_like(loss)

        def body(i, cut):
            asking = (q[:, cut] * FACTOR).astype(bf16)
            cvh = cv[:, cut]
            p = softmax(dot_t(asking, k[:, cut])).astype(bf16)
            gp = softmax(dot_t(asking, ck[:, cut]))
            low = gp.astype(bf16)
            miss = dot(p, v[:, cut]) - dot(low, cvh)
            loss[...] += jnp.sum(miss * miss, axis=0, keepdims=True)
            d_guess = ((-2.0 / (T * D)) * miss).astype(bf16)
            d_gp = dot_t(d_guess, cvh)
            dcv[:, cut] = t_dot(low, d_guess).astype(bf16)
            d_gs = (gp * (d_gp - jnp.sum(gp * d_gp, axis=-1, keepdims=True))).astype(bf16)
            dck[:, cut] = t_dot(d_gs, asking).astype(bf16)

        each_head(body)

    return call(
        kernel,
        (shape((1, HD), f32), shape((rows, D), bf16), shape((rows, D), bf16)),
        (STEPS,),
        [head(T), head(T, 1), head(T, 1, H), head(rows), head(rows, 0, H)],
        [pl.BlockSpec((1, HD), lambda h, s: (0, 0)), head(rows), head(rows)],
        none,
        (queries, key_value, key_value, comp_pair, comp_pair),
    )


def compress_back(dck, dcv, w_kv, compact, vectors, offsets):
    rows = T // 3

    def kernel(s, dck, dcv, w, compact, vec, d_compact, d_bias, dn):
        back = dot_t(jnp.concatenate([dck[...], dcv[...]], axis=1), w[...])
        natural_columns(dn, back, s, THIRDS)
        xhat, r = center_scale(compact[...])
        low = norm_back(xhat, r, row(vec, LN1_G), dn[...]).astype(bf16)
        d_compact[...] = low
        d_bias[...] = jnp.sum(low.astype(f32), axis=0, keepdims=True)

    args = (dck, dcv, w_kv, compact, vectors)
    out = (shape((rows, D), bf16), shape((1, D), f32))
    return call(
        kernel,
        out,
        (1,),
        [whole(a) for a in args],
        [whole(o) for o in out],
        offsets,
        args,
        [pltpu.VMEM((rows, D), f32)],
    )


def weight_grads(groups, scalars):
    in_specs, args, outs, out_specs, layout = [], [], [], [], []
    for ring, jobs in groups:
        first = 1 if ring == "x" else 5
        block = jobs[0][0][0].shape[1] // 8
        widths = []
        for xs, row_block, rows, dys, ready in jobs:
            width = dys[0].shape[1] // (1 if ready else 2)
            widths.append(width)
            for x in xs:
                for y in range(2):
                    in_specs.append(
                        pl.BlockSpec(
                            (rows, block),
                            lambda q, s, r=row_block, f=first, y=y: (r, y * 4 + s[f + q]),
                        )
                    )
                    args.append(x)
            for dy in dys:
                in_specs.append(
                    pl.BlockSpec((rows, width), lambda q, s, r=ready: (0, 0 if r else s[0]))
                )
                args.append(dy)
        dims = (1, 2, block, sum(widths))
        outs += [shape((2, *dims[1:]), bf16)] * 2
        out_specs += [
            pl.BlockSpec(dims, lambda q, s: (jnp.minimum(q, 1), 0, 0, 0)),
            pl.BlockSpec(dims, lambda q, s: (jnp.maximum(q - 2, 0), 0, 0, 0)),
        ]
        layout.append(widths)

    def kernel(s, *refs):
        q = pl.program_id(0)
        place = 0
        results = refs[len(in_specs) :]
        for i, widths in enumerate(layout):
            send, keep = results[2 * i : 2 * i + 2]
            block = send.shape[2]
            start = 0
            for width in widths:
                a0, a1, b0, b1, da, db = (r[...] for r in refs[place : place + 6])
                place += 6
                x = jnp.concatenate(
                    [jnp.concatenate([a0, a1], axis=1), jnp.concatenate([b0, b1], axis=1)], axis=0
                )
                value = t_dot(x, jnp.concatenate([da, db], axis=0)).astype(bf16)
                value = value.reshape(2, block, width)
                cut = slice(start, start + width)
                send[0, :, :, cut] = jnp.where(q < 2, value, send[0, :, :, cut])
                keep[0, :, :, cut] = value
                start += width

    flat = call(kernel, tuple(outs), (4,), in_specs, out_specs, scalars, args)
    return [(flat[2 * i], flat[2 * i + 1]) for i in range(len(groups))]


def widen(gathered, start, rows, columns, swapped, none):
    u = rows // 16
    sub = u // 32
    chunks = columns // 2 // STEP
    order = [x * 4 + z for z in range(4) for x in range(4)] if swapped else list(range(16))

    def kernel(_, *refs):
        out = refs[-1]
        for k, src in enumerate(refs[:-1]):
            for to, frm in enumerate(order):
                out[to, :, k * STEP : (k + 1) * STEP] = src[frm].astype(f32)

    return call(
        kernel,
        shape((16, u, columns), f32),
        (sub, 2),
        [
            pl.BlockSpec((16, 32, STEP), lambda i, c, s, k=k: (c, start // 32 + k * sub + i, 0))
            for k in range(chunks)
        ],
        pl.BlockSpec((16, 32, STEP * chunks), lambda i, c, s: (0, i, c)),
        none,
        (gathered,) * chunks,
    ).reshape(rows, columns)


def widen_near(own, twin, start, columns, swapped, scalars):
    chunks = columns // 2 // STEP
    u = D // 32

    def kernel(s, own, twin, out):
        def fill(src, base):
            for a in range(4):
                for b in range(4):
                    first, second = s[base + a], s[base + 4 + b]
                    place = second * 4 + first if swapped else first * 4 + second
                    for k in range(chunks):
                        rows = slice(start + k * u, start + (k + 1) * u)
                        value = src[a, b, rows, :].astype(f32)
                        out[pl.ds(place, 1), :, k * STEP : (k + 1) * STEP] = value[None]

        @pl.when(pl.program_id(0) == 0)
        def _():
            fill(own, 1)

        @pl.when(pl.program_id(0) == 1)
        def _():
            fill(twin, 9)

    return call(
        kernel,
        shape((16, u, columns), f32),
        (2,),
        [whole(own), whole(twin)],
        pl.BlockSpec((16, u, chunks * STEP), lambda h, s: (0, 0, lax.rem(h + s[0], 2))),
        scalars,
        (own, twin),
    ).reshape(D // 2, columns)


def core_swap(v):
    return lax.ppermute(v, "c", [(0, 1), (1, 0)])


def pair_swap(v):
    return lax.ppermute(v, "yl", [(0, 1), (1, 0)])


def exchange(v, ring, masks):
    def flat(i, c):
        return (i // 2 * 2 + c) * 2 + i % 2 if ring == "y" else 2 * i + c

    pairs = [(flat(i, c), flat(i ^ masks[c], c)) for i in range(4) for c in range(2)]
    return lax.ppermute(v, RING[ring], pairs)


def pick(v, index, axis):
    return lax.dynamic_index_in_dim(v, index, axis, keepdims=False)


def quarters(place, core):
    first = jnp.where(core == 0, 1, 3)
    second = jnp.where(core == 0, 3, 1)
    return place, place ^ first, place ^ 2, place ^ second


class Flow:
    def __init__(self, ring, pair, place, core):
        self.rings = (ring, "z" if ring == "x" else "x")
        self.place, self.core = place, core
        send, self.keep = pair
        self.got = exchange(send, ring, (1, 3))

    def onward(self, ring):
        got = line.later(self.got)
        self.near = got[0]
        value = (self.keep[1].astype(f32) + got[1].astype(f32)).astype(bf16)
        self.last = exchange(value, ring, (3, 1))
        line.hold(value)

    def settle(self):
        last = line.later(self.last)
        return self.keep[0].astype(f32) + self.near.astype(f32) + last.astype(f32)

    def second(self):
        self.onward(self.rings[0])

    def third(self):
        v = self.settle()
        y, rows, columns = v.shape
        v = v.reshape(y, 4, rows // 4, columns)
        ring = self.rings[1]
        own, first, far, second = quarters(self.place[ring], self.core)
        send = jnp.stack([pick(v, first, 1), pick(v, far, 1)]).astype(bf16)
        self.keep = (pick(v, own, 1), pick(v, second, 1))
        self.got = exchange(send, ring, (1, 3))
        line.hold(send, *self.keep)

    def fourth(self):
        self.onward(self.rings[1])

    def rows(self):
        v = self.settle()
        y, u, columns = v.shape
        v = v.reshape(y, u, columns // STEP, STEP).transpose(0, 2, 1, 3)
        return v.reshape(y, -1, STEP)


class Spread:
    def __init__(self, v, rings):
        self.rings = rings
        self.v = v
        self.got = exchange(v, rings[0], (1, 3))
        line.hold(v)

    def second(self, ring=None):
        pair = jnp.stack([self.v, line.later(self.got)])
        self.v = pair
        self.got = exchange(pair, ring or self.rings[0], (3, 1))
        line.hold(pair)

    def third(self):
        four = jnp.concatenate([self.v, line.later(self.got)])
        self.v = four
        self.got = exchange(four, self.rings[1], (1, 3))
        line.hold(four)

    def fourth(self):
        self.second(self.rings[1])

    def done(self):
        all_ = jnp.concatenate([self.v, line.later(self.got)])
        return all_, core_swap(all_)


class Finish:
    def __init__(self, parts, yl):
        v = jnp.concatenate(parts, axis=1)
        self.mine = pick(v, yl, 0)
        send = pick(v, 1 - yl, 0).astype(bf16)
        self.got = exchange(send, "y", (1, 3))
        line.hold(send, self.mine)

    def second(self):
        got = line.later(self.got)
        self.mine = (self.mine + got.astype(f32)).astype(bf16)
        self.far = lax.ppermute(self.mine, "yh", [(0, 1), (1, 0)])
        line.hold(self.mine)

    def done(self):
        far = line.later(self.far)
        return (self.mine.astype(f32) + far.astype(f32)).astype(bf16)


def per_device(
    tokens,
    memory,
    compressed,
    cotangent,
    ln1_g,
    ln1_b,
    w_q,
    w_kv,
    w_r,
    bias_u,
    bias_v,
    w_o,
    ln2_g,
    ln2_b,
    w_in,
    b_in,
    w_out,
    b_out,
    conv_w,
    conv_b,
):
    line.held = []
    tokens, memory, compressed, cotangent = tokens[0], memory[0], compressed[0], cotangent[0]
    yl, core = lax.axis_index("yl"), lax.axis_index("c")
    place = {"x": lax.axis_index("x"), "z": lax.axis_index("z")}
    none = jnp.zeros((1,), jnp.int32)
    ints = lambda *v: jnp.stack([jnp.asarray(i, jnp.int32) for i in v])

    def thirds(rows):
        half = rows // 2
        other = (1 - yl) * half
        return [yl * half, other + core * (half // 2), other + (1 - core) * (half // 2)]

    def both(v):
        return (v, core_swap(v))

    spot = (place["x"] * 4 + place["z"]) * 2 + core
    flat, piece = pack(
        (ln1_g, ln1_b, bias_u, bias_v, ln2_g, ln2_b, b_out, conv_b, b_in),
        w_in,
        w_out,
        conv_w,
        ints(spot),
    )
    piece_got = exchange(piece, "y", (1, 3))
    flat_got = exchange(flat, "y", (1, 3))

    kv_part, small = pack_rows(w_kv, w_q, w_r, w_o, ints(core))
    kv_got = exchange(kv_part, "y", (1, 3))
    small_got = exchange(small, "y", (1, 3))

    def joined(w, got, twin):
        return jnp.concatenate([w, got, twin], axis=0)

    spread = lax.all_gather(piece_got, ("x", "z", "c"), axis=0)
    thirds_d = ints(*thirds(D))
    thirds_c = ints(yl * (3 * D // 2), (1 - yl) * (3 * D // 2), *thirds(D))
    sinus_table = sinusoid(KEYS, D).astype(bf16)
    sinus_rel = jnp.concatenate(
        [
            lax.dynamic_slice_in_dim(sinus_table, thirds_d[i], width, 1)
            for i, width in enumerate(THIRDS)
        ],
        axis=1,
    )
    line.hold(sinus_rel)
    vectors, b_in = unpack(flat, flat_got, ints(yl))

    normed, normed_rel, oldest = first_norm(compressed, memory, tokens, vectors, thirds_d)
    both_normed, both_oldest, both_cot = both(normed), both(oldest), both(cotangent)
    kv_got = line.later(kv_got)
    kv_whole = joined(w_kv, kv_got, core_swap(kv_got))
    key_value = dot(normed_rel, kv_whole).astype(bf16)
    line.hold(key_value)
    small_got = line.later(small_got)
    small_twin = core_swap(small_got)
    q_whole, r_whole, o_whole = [
        joined(w, small_got[i], small_twin[i]) for i, w in enumerate((w_q, w_r, w_o))
    ]
    queries = dot(normed_rel[2 * T :], q_whole)
    relative = dot(sinus_rel, r_whole).astype(bf16)
    line.hold(queries, relative)
    probs, attended = attend(queries, key_value, relative, vectors, none)
    residual, normed2, normed2_rel = out_and_norm(attended, o_whole, tokens, vectors, thirds_d)
    both_n2, both_att = both(normed2), both(attended)

    cuts, rels, twins = [], [], []
    for ring in ("x", "z"):
        own, first, far, second = quarters(place[ring], core)
        cuts += [first, far, own, second]
        rels.append([own, first, second, far])
        twins.append([own, second, first, far])
    cuts = ints(core, *cuts)

    def flows(groups):
        pairs = weight_grads(groups, cuts)
        return [Flow(ring, pair, place, core) for (ring, _), pair in zip(groups, pairs)]

    hidden, d_pre, mixed_out, d_normed2, d_b_in = feed_forward(
        normed2_rel, residual, cotangent, w_in, w_out, spread, b_in, vectors, ints(yl)
    )
    both_hidden, both_pre = both(hidden), both(d_pre)
    d_residual, d_branch, d_attended, d_ln2_g, d_ln2_b, d_b_out = second_norm_back(
        cotangent, d_normed2, residual, vectors, o_whole, thirds_d
    )
    both_branch = both(d_branch)
    out_flow, in_flow = flows(
        [
            ("x", [(both_hidden, 0, T, both_cot, False)]),
            ("z", [(both_n2, 0, T, both_pre, False), (both_att, 0, T, both_branch, False)]),
        ]
    )

    compact, comp_normed = compress(oldest, conv_w, spread, vectors, thirds_c)
    comp_pair = dot(comp_normed, kv_whole).astype(bf16)
    loss, d_ck, d_cv = reconstruct(queries, key_value, comp_pair, none)
    recon_loss = jnp.sum(loss) / (T * D)
    compressed_next = jnp.concatenate([compressed[T // 3 :], compact], axis=0)
    d_compact, d_conv_b = compress_back(d_ck, d_cv, kv_whole, compact, vectors, thirds_d)
    both_compact = both(d_compact)
    out_flow.second()
    in_flow.second()
    d_kv, my_kv, give_kv, d_relative, d_queries, d_bias_u, d_bias_v = attend_back(
        queries, key_value, relative, vectors, probs, d_attended, ints(core)
    )
    both_kv = (my_kv, core_swap(give_kv))
    both_q, both_rel = both(d_queries), both(d_relative)
    (conv_flow,) = flows([("x", [(both_oldest, 0, T // 3, both_compact, False)])])
    out_flow.third()
    in_flow.third()
    d_tokens, d_ln1_g, d_ln1_b = first_norm_back(
        d_kv, d_queries, kv_whole, q_whole, compressed, memory, tokens, vectors, d_residual,
        thirds_d,
    )
    out_flow.fourth()
    in_flow.fourth()
    x_flow, z_flow = flows(
        [
            ("x", [(both_normed, 0, KEYS, both_kv, True)]),
            (
                "z",
                [
                    (both_normed, 2, T, both_q, False),
                    ((sinus_table, sinus_table), 0, KEYS, both_rel, False),
                ],
            ),
        ]
    )
    conv_flow.second()
    conv_flow.third()
    x_flow.second()
    z_flow.second()
    conv_flow.fourth()
    x_flow.third()
    z_flow.third()
    early = Finish([out_flow.rows(), in_flow.rows(), conv_flow.rows()], yl)
    x_flow.fourth()
    z_flow.fourth()
    early.second()

    total = jnp.concatenate(
        [d_ln1_g, d_ln1_b, d_bias_u, d_bias_v, d_ln2_g, d_ln2_b, d_b_out, d_conv_b]
        + [d_b_in]
    )
    total = jnp.concatenate(
        [total[:8].reshape(8, 2, STEP).transpose(1, 0, 2), total[8:].reshape(2, 4, STEP)], axis=1
    )
    late = Finish([x_flow.rows(), z_flow.rows(), total, jnp.zeros((2, 4, STEP), f32)], yl)
    early_done = early.done()
    line.hold(early_done)
    early_sums = lax.all_gather(early_done, ("c", "x", "z"), axis=0)
    late.second()
    late_done = late.done()
    kv_spread = Spread(late_done[:64], ("z", "x"))
    qr_spread = Spread(late_done[64:], ("x", "z"))
    kv_spread.second()
    qr_spread.second()
    kv_spread.third()
    qr_spread.third()
    kv_spread.fourth()
    qr_spread.fourth()
    (kv_own, kv_twin), (qr_own, qr_twin) = kv_spread.done(), qr_spread.done()
    x_places, z_places = rels
    x_twin, z_twin = twins
    along = ints(core, *x_places, *z_places, *x_twin, *z_twin)
    across = ints(core, *z_places, *x_places, *z_twin, *x_twin)
    g_kv = widen_near(kv_own, kv_twin, 0, 2 * D, False, along)
    g_q = widen_near(qr_own, qr_twin, 0, D, False, across)
    g_r = widen_near(qr_own, qr_twin, 32, D, False, across)
    g_out = widen(early_sums, 0, FF // 2, D, False, none)
    g_in = widen(early_sums, 128, D // 2, FF, True, none)
    g_o = widen(early_sums, 256, D // 2, D, True, none)
    g_conv = widen(early_sums, 288, 3 * D // 2, D, False, none)

    def four(v):
        return (v[0] + v[1]) + (v[2] + v[3])

    half = four(four(qr_own[:, :, 64:76].astype(f32))) + four(
        four(qr_twin[:, :, 64:76].astype(f32))
    )
    t_ln1_g, t_ln1_b, t_bu, t_bv, t_ln2_g, t_ln2_b, t_bout, t_convb = [half[i] for i in range(8)]
    t_bin = half[8:].reshape(-1)
    return (
        mixed_out[None],
        compressed_next[None],
        recon_loss[None],
        d_tokens[None],
        t_ln1_g,
        t_ln1_b,
        g_q,
        g_kv,
        g_r,
        t_bu,
        t_bv,
        g_o,
        t_ln2_g,
        t_ln2_b,
        g_in,
        t_bin,
        g_out,
        t_bout,
        g_conv,
        t_convb,
    )


def solution(mesh):
    fine = Mesh(mesh.devices.reshape(2, 4, 4, 2, 2), AXES)
    stream = P(AXES, None, None)
    vec, mat = P("yl"), P("yl", None)
    weights = (vec, vec, mat, mat, mat, vec, vec, mat, vec, vec, mat, vec, mat, vec, mat, vec)
    return jax.shard_map(
        per_device,
        mesh=fine,
        in_specs=(stream,) * 4 + weights,
        out_specs=(stream, stream, P(AXES), stream) + weights,
        check_vma=False,
    )
```

```python
import jax
import jax.numpy as jnp
from jax import lax
from jax.experimental import pallas as pl
from jax.experimental.pallas import tpu as pltpu
from jax.sharding import Mesh, PartitionSpec as P

H = 8
HD = 128
D = 1024
T = 192
KEYS = 576
PAD = 640
FF = 4096
FACTOR = HD ** (-0.5)
f32 = jnp.float32
bf16 = jnp.bfloat16
AXES = ("yh", "x", "z", "c", "yl")
RING = {"x": ("x", "c"), "z": ("z", "c"), "y": ("yh", "c", "yl")}


def sinusoid(key_count, model_dim):
    distance = (key_count - 1 - jnp.arange(key_count)).astype(f32)
    inverse = 1.0 / 10000.0 ** (jnp.arange(0, model_dim, 2).astype(f32) / model_dim)
    angles = distance[:, None] * inverse[None, :]
    return jnp.concatenate([jnp.sin(angles), jnp.cos(angles)], axis=-1)


def dot(a, b):
    return jnp.dot(a, b, preferred_element_type=f32)


def dot_t(a, b):
    return lax.dot_general(a, b, (((1,), (1,)), ((), ())), preferred_element_type=f32)


def t_dot(a, b):
    return lax.dot_general(a, b, (((0,), (0,)), ((), ())), preferred_element_type=f32)


class Line:
    def __init__(self):
        self.held = []

    def hold(self, *values):
        self.held += values

    def later(self, value):
        return lax.optimization_barrier((value, *self.held))[0] if self.held else value


line = Line()


def call(kernel, out, grid, in_specs, out_specs, scalars, args, scratch=()):
    held, n = line.held, len(args)

    def body(s, *refs):
        kernel(s, *refs[:n], *refs[n + len(held) :])

    result = pl.pallas_call(
        body,
        out_shape=out,
        grid_spec=pltpu.PrefetchScalarGridSpec(
            num_scalar_prefetch=1,
            grid=grid,
            in_specs=list(in_specs) + [pl.BlockSpec(memory_space=pl.ANY)] * len(held),
            out_specs=out_specs,
            scratch_shapes=list(scratch),
        ),
        compiler_params=pltpu.CompilerParams(vmem_limit_bytes=56 << 20),
    )(scalars, *args, *held)
    line.held = [jax.tree.leaves(result)[0]]
    return result


def whole(a):
    zeros = (0,) * a.ndim
    return pl.BlockSpec(a.shape, lambda *_: zeros)


def shape(dims, dtype):
    return jax.ShapeDtypeStruct(dims, dtype)


def at(offset):
    return pl.multiple_of(offset, 128)


def center_scale(v):
    mid = v - jnp.mean(v, axis=-1, keepdims=True)
    r = lax.rsqrt(jnp.mean(mid * mid, axis=-1, keepdims=True) + 1e-5)
    return mid * r, r


def norm_back(xhat, r, g, dn):
    gd = dn * g
    return r * (
        gd
        - jnp.mean(gd, axis=-1, keepdims=True)
        - xhat * jnp.mean(gd * xhat, axis=-1, keepdims=True)
    )


def softmax(s):
    e = jnp.exp(s - jnp.max(s, axis=-1, keepdims=True))
    return e / jnp.sum(e, axis=-1, keepdims=True)


(LN1_G, LN1_B, BIAS_U, BIAS_V, LN2_G, LN2_B, B_OUT, CONV_B) = range(8)


def row(ref, i):
    return ref[i : i + 1, :]


def pack(vectors, w_in, w_out, conv_w, scalars):
    n_in, n_out, n_conv = (w.shape[0] // 32 for w in (w_in, w_out, conv_w))
    chunks = FF // D
    rows = n_out + n_in * chunks + n_conv
    half = D // 2

    def kernel(_, *refs):
        wi, wo, wc, piece, flat = refs[-5:]
        flat[...] = jnp.zeros_like(flat)
        for i, ref in enumerate(refs[:8]):
            flat[i : i + 1, :half] = ref[...].astype(f32).reshape(1, half)
        flat[8 : 8 + FF // 2 // D, :] = refs[8][...].astype(f32).reshape(FF // 2 // D, D)
        piece[:n_out, :] = wo[...]
        for i in range(chunks):
            piece[n_out + i * n_in : n_out + (i + 1) * n_in, :] = wi[:, i * D : (i + 1) * D]
        piece[n_out + n_in * chunks : rows, :] = wc[...]
        piece[rows:, :] = flat[...].astype(bf16)

    out = shape((rows + 16, D), bf16)
    return call(
        kernel,
        out,
        (1,),
        [whole(v) for v in vectors]
        + [
            pl.BlockSpec((w.shape[0] // 32, w.shape[1]), lambda j, s: (s[0], 0))
            for w in (w_in, w_out, conv_w)
        ],
        whole(out),
        scalars,
        (*vectors, w_in, w_out, conv_w),
        [pltpu.VMEM((16, D), f32)],
    )


def pack_rows(w_kv, w_q, w_r, w_o, scalars):
    n = w_q.shape[0] // 2

    def kernel(_, kv, q, r, o, kv_out, out):
        kv_out[...] = kv[...]
        for i, ref in enumerate((q, r, o)):
            out[i] = ref[...]

    out = (shape((n, 2 * D), bf16), shape((3, n, D), bf16))
    return call(
        kernel,
        out,
        (1,),
        [
            pl.BlockSpec((n, w.shape[1]), lambda j, s: (s[0], 0))
            for w in (w_kv, w_q, w_r, w_o)
        ],
        [whole(o) for o in out],
        scalars,
        (w_kv, w_q, w_r, w_o),
    )


def unpack(mine, theirs, scalars):
    half = D // 2
    at_row = mine.shape[0] // 16 - 1
    tail = pl.BlockSpec((16, D), lambda j, s: (at_row, 0))

    def kernel(s, mine, theirs, vectors, b_in):
        a, b = mine[...].astype(f32), theirs[...].astype(f32)
        low = jnp.where(s[0] == 0, a, b)
        high = jnp.where(s[0] == 0, b, a)
        vectors[:, :half] = low[:8, :half]
        vectors[:, half:] = high[:8, :half]
        rows = FF // 2 // D
        b_in[:rows] = low[8 : 8 + rows]
        b_in[rows:] = high[8 : 8 + rows]

    out = (shape((8, D), f32), shape((FF // D, D), f32))
    return call(
        kernel, out, (1,), [tail, tail], [whole(o) for o in out], scalars, (mine, theirs)
    )


def relative_columns(x, s, widths):
    parts = [x[:, pl.ds(at(s[i]), width)] for i, width in enumerate(widths)]
    return jnp.concatenate(parts, axis=1)


def natural_columns(out, x, s, widths):
    start = 0
    for i, width in enumerate(widths):
        out[:, pl.ds(at(s[i]), width)] = x[:, start : start + width]
        start += width


THIRDS = (D // 2, D // 4, D // 4)


def first_norm(compressed, memory, tokens, vectors, offsets):
    def kernel(s, comp, mem, tok, vec, out, out_rel, old):
        gain, bias = row(vec, LN1_G), row(vec, LN1_B)

        def part(ref, base):
            for i in range(0, T, 32):
                xhat, r = center_scale(ref[i : i + 32, :].astype(f32))
                out[base + i : base + i + 32, :] = (xhat * gain + bias).astype(bf16)

        part(comp, 0)
        part(mem, T)
        part(tok, 2 * T)
        out_rel[...] = relative_columns(out, s, THIRDS)
        line_of = lax.broadcasted_iota(jnp.int32, (T // 3, T), 0)
        col = lax.broadcasted_iota(jnp.int32, (T // 3, T), 1)
        low = mem[...].astype(bf16)
        for tap in range(3):
            take = jnp.where(col == 3 * line_of + tap, 1.0, 0.0).astype(bf16)
            old[:, tap * D : (tap + 1) * D] = dot(take, low).astype(bf16)

    args = (compressed, memory, tokens, vectors)
    out = (shape((KEYS, D), bf16), shape((KEYS, D), bf16), shape((T // 3, 3 * D), bf16))
    return call(
        kernel, out, (1,), [whole(a) for a in args], [whole(o) for o in out], offsets, args
    )


PAIR = 2
STEPS = H // PAIR


def head(rows, row_block=0, first=0):
    return pl.BlockSpec((rows, PAIR * HD), lambda h, s: (row_block, first // PAIR + h))


def vec_head(rows=1):
    return pl.BlockSpec((rows, PAIR * HD), lambda h, s: (0, h))


def each_head(body):
    for i in range(PAIR):
        body(i, slice(i * HD, (i + 1) * HD))


def attend(queries, key_value, relative, vectors, none):
    def kernel(_, q, k, v, rel, vec, probs, out):
        pad = jnp.zeros((PAD - KEYS, HD), bf16)
        row = lax.broadcasted_iota(jnp.int32, (T, PAD), 0)
        col = lax.broadcasted_iota(jnp.int32, (T, PAD), 1)
        seen = col <= row + (KEYS - T)

        def body(i, cut):
            content = ((q[:, cut] + vec[BIAS_U : BIAS_U + 1, cut]) * FACTOR).astype(bf16)
            located = ((q[:, cut] + vec[BIAS_V : BIAS_V + 1, cut]) * FACTOR).astype(bf16)
            raw = dot_t(located, jnp.concatenate([rel[:, cut], pad], axis=0))
            raw = pltpu.roll(raw, PAD - T + 1, 1, stride=1, stride_axis=0)
            s = dot_t(content, jnp.concatenate([k[:, cut], pad], axis=0)) + raw
            p = softmax(jnp.where(seen, s, -1e30))
            probs[i] = p
            low = p.astype(bf16)
            out[:, cut] = dot(low, jnp.concatenate([v[:, cut], pad], axis=0)).astype(bf16)

        each_head(body)

    return call(
        kernel,
        (shape((H, T, PAD), f32), shape((T, D), bf16)),
        (STEPS,),
        [head(T), head(KEYS), head(KEYS, 0, H), head(KEYS), vec_head(8)],
        [pl.BlockSpec((PAIR, T, PAD), lambda h, s: (h, 0, 0)), head(T)],
        none,
        (queries, key_value, key_value, relative, vectors),
    )


def attend_back(queries, key_value, relative, vectors, probs, d_attended, scalars):
    def kernel(s, q, k, v, rel, vec, probs, d_att, d_kv, mine, give, d_rel, d_q, d_bu, d_bv):
        pad = jnp.zeros((PAD - KEYS, HD), bf16)
        row = lax.broadcasted_iota(jnp.int32, (T, T), 0)
        col = lax.broadcasted_iota(jnp.int32, (T, T), 1)
        flip = jnp.where(row + col == T - 1, 1.0, 0.0).astype(bf16)

        def body(i, cut):
            content = ((q[:, cut] + vec[BIAS_U : BIAS_U + 1, cut]) * FACTOR).astype(bf16)
            located = ((q[:, cut] + vec[BIAS_V : BIAS_V + 1, cut]) * FACTOR).astype(bf16)
            p, da = probs[i], d_att[:, cut]
            d_p = dot_t(da, jnp.concatenate([v[:, cut], pad], axis=0))
            d_v = t_dot(p.astype(bf16), da)[:KEYS].astype(bf16)
            d_s = (p * (d_p - jnp.sum(p * d_p, axis=-1, keepdims=True))).astype(bf16)
            d_c = dot(d_s, jnp.concatenate([k[:, cut], pad], axis=0)) * FACTOR
            d_k = t_dot(d_s, content)[:KEYS].astype(bf16)
            d_kv[0, :, cut] = d_k
            d_kv[1, :, cut] = d_v
            mine[:, cut] = jnp.where(s[0] == 0, d_k, d_v)
            give[:, cut] = jnp.where(s[0] == 0, d_v, d_k)
            d_raw = pltpu.roll(dot(flip, d_s), 0, 1, stride=1, stride_axis=0)
            d_raw = dot(flip, d_raw.astype(bf16)).astype(bf16)
            d_l = dot(d_raw, jnp.concatenate([rel[:, cut], pad], axis=0)) * FACTOR
            d_rel[:, cut] = t_dot(d_raw, located)[:KEYS].astype(bf16)
            d_q[:, cut] = (d_c + d_l).astype(bf16)
            d_bu[:, cut] = jnp.sum(d_c, axis=0, keepdims=True)
            d_bv[:, cut] = jnp.sum(d_l, axis=0, keepdims=True)

        each_head(body)

    return call(
        kernel,
        (
            shape((2, KEYS, D), bf16),
            shape((KEYS, D), bf16),
            shape((KEYS, D), bf16),
            shape((KEYS, D), bf16),
            shape((T, D), bf16),
            shape((1, D), f32),
            shape((1, D), f32),
        ),
        (STEPS,),
        [
            head(T),
            head(KEYS),
            head(KEYS, 0, H),
            head(KEYS),
            vec_head(8),
            pl.BlockSpec((PAIR, T, PAD), lambda h, s: (h, 0, 0)),
            head(T),
        ],
        [
            pl.BlockSpec((2, KEYS, PAIR * HD), lambda h, s: (0, 0, h)),
            head(KEYS),
            head(KEYS),
            head(KEYS),
            head(T),
            vec_head(),
            vec_head(),
        ],
        scalars,
        (queries, key_value, key_value, relative, vectors, probs, d_attended),
    )


def out_and_norm(attended, w_o, tokens, vectors, offsets):
    def kernel(s, att, w, tok, vec, res, n2, n2_rel):
        total = tok[...].astype(f32) + dot(relative_columns(att, s, THIRDS), w[...])
        res[...] = total
        xhat, r = center_scale(total)
        n2[...] = (xhat * row(vec, LN2_G) + row(vec, LN2_B)).astype(bf16)
        other = at(D // 2 - s[0])
        n2_rel[:, : D // 2] = n2[:, pl.ds(at(s[0]), D // 2)]
        n2_rel[:, D // 2 :] = n2[:, pl.ds(other, D // 2)]

    args = (attended, w_o, tokens, vectors)
    out = (shape((T, D), f32), shape((T, D), bf16), shape((T, D), bf16))
    return call(
        kernel, out, (1,), [whole(a) for a in args], [whole(o) for o in out], offsets, args
    )


STEP = 512
UNITS = 1024
HALF = FF // 2 // UNITS


def feed_forward(n2_rel, residual, cotangent, w_in, w_out, spread, b_in, vectors, scalars):
    n_in = w_in.shape[0] // 32
    n_out = w_out.shape[0] // 32
    skip = n_out // n_in
    per = UNITS // n_out
    K_NORM = 0.7978845608028654

    def natural(j, s):
        return lax.rem(j + s[0] * HALF, 2 * HALF)

    def kernel(s, n2, res, cot, wi0, wi1, wo0, wo1, bi, vec, hid, dpre, mixed, dn2, dbi, acc, back):
        j = pl.program_id(0)
        n = natural(j, s)
        win = jnp.concatenate([wi0[...], wi1[...].reshape(D // 2, UNITS)], axis=0)
        pre = dot(n2[...], win) + bi[pl.ds(n, 1), :]
        t = jnp.tanh(K_NORM * (pre + 0.044715 * (pre * pre * pre)))
        hidden = (0.5 * pre * (1.0 + t)).astype(bf16)
        slope = 0.5 * (1.0 + t) + (0.5 * K_NORM) * pre * (1.0 - t * t) * (
            1.0 + (3 * 0.044715) * (pre * pre)
        )
        hid[...] = hidden

        def rest(wo, start):
            d_pre = (dot_t(cot[...], wo) * slope).astype(bf16)
            dpre[...] = d_pre
            dbi[pl.ds(n, 1), :] = jnp.sum(d_pre.astype(f32), axis=0, keepdims=True)
            if start:
                acc[...] = dot(hidden, wo)
                back[...] = dot_t(d_pre, win)
            else:
                acc[...] += dot(hidden, wo)
                back[...] += dot_t(d_pre, win)

        @pl.when(j == 0)
        def _():
            rest(wo0[...], True)

        @pl.when((j > 0) & (j < HALF))
        def _():
            rest(wo0[...], False)

        @pl.when(j >= HALF)
        def _():
            rest(wo1[...].reshape(UNITS, D), False)

        @pl.when(j == 2 * HALF - 1)
        def _():
            mixed[...] = (res[...] + acc[...] + row(vec, B_OUT)).astype(bf16)
            dn2[:, pl.ds(at(s[0] * (D // 2)), D // 2)] = back[:, : D // 2]
            dn2[:, pl.ds(at((1 - s[0]) * (D // 2)), D // 2)] = back[:, D // 2 :]

    out = (
        shape((T, FF), bf16),
        shape((T, FF), bf16),
        shape((T, D), bf16),
        shape((T, D), f32),
        shape((2 * HALF, UNITS), f32),
    )
    by_unit = pl.BlockSpec((T, UNITS), lambda j, s: (0, natural(j, s)))
    return call(
        kernel,
        out,
        (2 * HALF,),
        [
            whole(n2_rel),
            whole(residual),
            whole(cotangent),
            pl.BlockSpec((D // 2, UNITS), lambda j, s: (0, natural(j, s))),
            pl.BlockSpec((32, n_in, UNITS), lambda j, s: (0, skip + natural(j, s), 0)),
            pl.BlockSpec((UNITS, D), lambda j, s: (jnp.minimum(j, HALF - 1), 0)),
            pl.BlockSpec(
                (per, n_out, D), lambda j, s: (jnp.maximum(j - HALF, 0), 0, 0)
            ),
            whole(b_in),
            whole(vectors),
        ],
        [by_unit, by_unit, whole(out[2]), whole(out[3]), whole(out[4])],
        scalars,
        (n2_rel, residual, cotangent, w_in, spread, w_out, spread, b_in, vectors),
        [pltpu.VMEM((T, D), f32), pltpu.VMEM((T, D), f32)],
    )


def second_norm_back(cotangent, d_n2, residual, vectors, w_o, offsets):
    def kernel(s, cot, dn, res, vec, w, d_res, d_br, d_att, dg, db, dbo):
        xhat, r = center_scale(res[...])
        dn, wide = dn[...], cot[...].astype(f32)
        dg[...] = jnp.sum(dn * xhat, axis=0, keepdims=True)
        db[...] = jnp.sum(dn, axis=0, keepdims=True)
        dbo[...] = jnp.sum(wide, axis=0, keepdims=True)
        total = wide + norm_back(xhat, r, row(vec, LN2_G), dn)
        d_res[...] = total
        low = total.astype(bf16)
        d_br[...] = low
        natural_columns(d_att, dot_t(low, w[...]).astype(bf16), s, THIRDS)

    args = (cotangent, d_n2, residual, vectors, w_o)
    out = (
        shape((T, D), f32),
        shape((T, D), bf16),
        shape((T, D), bf16),
        shape((1, D), f32),
        shape((1, D), f32),
        shape((1, D), f32),
    )
    return call(
        kernel, out, (1,), [whole(a) for a in args], [whole(o) for o in out], offsets, args
    )


def first_norm_back(d_kv, d_q, w_kv, w_q, compressed, memory, tokens, vectors, d_res, offsets):
    steps = 4
    wide, slim = 2 * D // steps, D // steps

    def kernel(s, dkv, dq, kw, qw, comp, mem, tok, vec, dres, dtok, dg, db, acc, nat):
        j = pl.program_id(0)

        @pl.when(j == 0)
        def _():
            acc[...] = dot_t(dkv[0], kw[...])

        @pl.when(j > 0)
        def _():
            acc[...] += dot_t(dkv[0], kw[...])

        acc[2 * T :, :] += dot_t(dq[...], qw[...])

        @pl.when(j == steps - 1)
        def _():
            natural_columns(nat, acc, s, THIRDS)
            gain = row(vec, LN1_G)
            sum_g = jnp.zeros((1, D), f32)
            sum_b = jnp.zeros((1, D), f32)
            for block, ref in enumerate((comp, mem, tok)):
                for i in range(0, T, 32):
                    xhat, r = center_scale(ref[i : i + 32, :].astype(f32))
                    dn = nat[block * T + i : block * T + i + 32, :]
                    sum_g += jnp.sum(dn * xhat, axis=0, keepdims=True)
                    sum_b += jnp.sum(dn, axis=0, keepdims=True)
                    if block == 2:
                        dtok[i : i + 32, :] = dres[i : i + 32, :] + norm_back(xhat, r, gain, dn)
            dg[...] = sum_g
            db[...] = sum_b

    rest = (compressed, memory, tokens, vectors, d_res)
    out = (shape((T, D), f32), shape((1, D), f32), shape((1, D), f32))
    return call(
        kernel,
        out,
        (steps,),
        [
            pl.BlockSpec((1, KEYS, wide), lambda j, s: (j // (steps // 2), 0, lax.rem(j, steps // 2))),
            pl.BlockSpec((T, slim), lambda j, s: (0, j)),
            pl.BlockSpec((D, wide), lambda j, s: (0, j)),
            pl.BlockSpec((D, slim), lambda j, s: (0, j)),
        ]
        + [whole(a) for a in rest],
        [whole(o) for o in out],
        offsets,
        (d_kv, d_q, w_kv, w_q, *rest),
        [pltpu.VMEM((KEYS, D), f32), pltpu.VMEM((KEYS, D), f32)],
    )


def compress(oldest, conv_w, spread, vectors, offsets):
    block = 256
    rows = T // 3
    n = conv_w.shape[0] // 32
    skip = (spread.shape[1] - n) // 16

    def kernel(s, x, own, w0, w1, w2, vec, compact, normed, x_rel, natural):
        j = pl.program_id(0)

        @pl.when(j == 0)
        def _():
            x_rel[...] = relative_columns(x, s, (3 * D // 2, 3 * D // 2))

        other = jnp.concatenate([w0[...], w1[...], w2[...]], axis=1).reshape(32 * n, block)
        w = jnp.concatenate([own[...], other], axis=0)
        here = pl.ds(at(j * block), block)
        compact[:, here] = dot(x_rel[...], w) + vec[CONV_B : CONV_B + 1, here]

        @pl.when(j == D // block - 1)
        def _():
            xhat, r = center_scale(compact[...])
            natural[...] = (xhat * row(vec, LN1_G) + row(vec, LN1_B)).astype(bf16)
            start = 0
            for i, width in enumerate(THIRDS):
                normed[:, start : start + width] = natural[:, pl.ds(at(s[2 + i]), width)]
                start += width

    out = (shape((rows, D), f32), shape((rows, D), bf16))
    return call(
        kernel,
        out,
        (D // block,),
        [whole(oldest), pl.BlockSpec((conv_w.shape[0], block), lambda j, s: (0, j))]
        + [
            pl.BlockSpec((32, 16, block), lambda j, s, i=i: (0, skip + i, j))
            for i in range(n // 16)
        ]
        + [whole(vectors)],
        [whole(o) for o in out],
        offsets,
        (oldest, conv_w) + (spread,) * (n // 16) + (vectors,),
        [pltpu.VMEM((rows, 3 * D), bf16), pltpu.VMEM((rows, D), bf16)],
    )


def reconstruct(queries, key_value, comp_pair, none):
    rows = T // 3

    def kernel(_, q, k, v, ck, cv, loss, dck, dcv):
        @pl.when(pl.program_id(0) == 0)
        def _():
            loss[...] = jnp.zeros_like(loss)

        def body(i, cut):
            asking = (q[:, cut] * FACTOR).astype(bf16)
            cvh = cv[:, cut]
            p = softmax(dot_t(asking, k[:, cut])).astype(bf16)
            gp = softmax(dot_t(asking, ck[:, cut]))
            low = gp.astype(bf16)
            miss = dot(p, v[:, cut]) - dot(low, cvh)
            loss[...] += jnp.sum(miss * miss, axis=0, keepdims=True)
            d_guess = ((-2.0 / (T * D)) * miss).astype(bf16)
            d_gp = dot_t(d_guess, cvh)
            dcv[:, cut] = t_dot(low, d_guess).astype(bf16)
            d_gs = (gp * (d_gp - jnp.sum(gp * d_gp, axis=-1, keepdims=True))).astype(bf16)
            dck[:, cut] = t_dot(d_gs, asking).astype(bf16)

        each_head(body)

    return call(
        kernel,
        (shape((1, HD), f32), shape((rows, D), bf16), shape((rows, D), bf16)),
        (STEPS,),
        [head(T), head(T, 1), head(T, 1, H), head(rows), head(rows, 0, H)],
        [pl.BlockSpec((1, HD), lambda h, s: (0, 0)), head(rows), head(rows)],
        none,
        (queries, key_value, key_value, comp_pair, comp_pair),
    )


def compress_back(dck, dcv, w_kv, compact, vectors, offsets):
    rows = T // 3

    def kernel(s, dck, dcv, w, compact, vec, d_compact, d_bias, dn):
        back = dot_t(jnp.concatenate([dck[...], dcv[...]], axis=1), w[...])
        natural_columns(dn, back, s, THIRDS)
        xhat, r = center_scale(compact[...])
        low = norm_back(xhat, r, row(vec, LN1_G), dn[...]).astype(bf16)
        d_compact[...] = low
        d_bias[...] = jnp.sum(low.astype(f32), axis=0, keepdims=True)

    args = (dck, dcv, w_kv, compact, vectors)
    out = (shape((rows, D), bf16), shape((1, D), f32))
    return call(
        kernel,
        out,
        (1,),
        [whole(a) for a in args],
        [whole(o) for o in out],
        offsets,
        args,
        [pltpu.VMEM((rows, D), f32)],
    )


def weight_grads(groups, scalars):
    in_specs, args, outs, out_specs, layout = [], [], [], [], []
    for ring, jobs in groups:
        first = 1 if ring == "x" else 5
        block = jobs[0][0][0].shape[1] // 8
        widths = []
        for xs, row_block, rows, dys, ready in jobs:
            width = dys[0].shape[1] // (1 if ready else 2)
            widths.append(width)
            for x in xs:
                for y in range(2):
                    in_specs.append(
                        pl.BlockSpec(
                            (rows, block),
                            lambda q, s, r=row_block, f=first, y=y: (r, y * 4 + s[f + q]),
                        )
                    )
                    args.append(x)
            for dy in dys:
                in_specs.append(
                    pl.BlockSpec((rows, width), lambda q, s, r=ready: (0, 0 if r else s[0]))
                )
                args.append(dy)
        dims = (1, 2, block, sum(widths))
        outs += [shape((2, *dims[1:]), bf16)] * 2
        out_specs += [
            pl.BlockSpec(dims, lambda q, s: (jnp.minimum(q, 1), 0, 0, 0)),
            pl.BlockSpec(dims, lambda q, s: (jnp.maximum(q - 2, 0), 0, 0, 0)),
        ]
        layout.append(widths)

    def kernel(s, *refs):
        q = pl.program_id(0)
        place = 0
        results = refs[len(in_specs) :]
        for i, widths in enumerate(layout):
            send, keep = results[2 * i : 2 * i + 2]
            block = send.shape[2]
            start = 0
            for width in widths:
                a0, a1, b0, b1, da, db = (r[...] for r in refs[place : place + 6])
                place += 6
                x = jnp.concatenate(
                    [jnp.concatenate([a0, a1], axis=1), jnp.concatenate([b0, b1], axis=1)], axis=0
                )
                value = t_dot(x, jnp.concatenate([da, db], axis=0)).astype(bf16)
                value = value.reshape(2, block, width)
                cut = slice(start, start + width)
                send[0, :, :, cut] = jnp.where(q < 2, value, send[0, :, :, cut])
                keep[0, :, :, cut] = value
                start += width

    flat = call(kernel, tuple(outs), (4,), in_specs, out_specs, scalars, args)
    return [(flat[2 * i], flat[2 * i + 1]) for i in range(len(groups))]


def widen(gathered, start, rows, columns, swapped, none):
    u = rows // 16
    sub = u // 32
    chunks = columns // 2 // STEP
    order = [x * 4 + z for z in range(4) for x in range(4)] if swapped else list(range(16))

    def kernel(_, *refs):
        out = refs[-1]
        for k, src in enumerate(refs[:-1]):
            for to, frm in enumerate(order):
                out[to, :, k * STEP : (k + 1) * STEP] = src[frm].astype(f32)

    return call(
        kernel,
        shape((16, u, columns), f32),
        (sub, 2),
        [
            pl.BlockSpec((16, 32, STEP), lambda i, c, s, k=k: (c, start // 32 + k * sub + i, 0))
            for k in range(chunks)
        ],
        pl.BlockSpec((16, 32, STEP * chunks), lambda i, c, s: (0, i, c)),
        none,
        (gathered,) * chunks,
    ).reshape(rows, columns)


def widen_near(own, twin, start, rows, columns, swapped, scalars):
    chunks = columns // 2 // STEP
    u = rows // 16

    def kernel(s, own, twin, out):
        def fill(src, base):
            for a in range(4):
                for b in range(4):
                    first, second = s[base + a], s[base + 4 + b]
                    place = second * 4 + first if swapped else first * 4 + second
                    for k in range(chunks):
                        value = src[a, b, start + k * u : start + (k + 1) * u, :].astype(f32)
                        out[pl.ds(place, 1), :, k * STEP : (k + 1) * STEP] = value[None]

        @pl.when(pl.program_id(0) == 0)
        def _():
            fill(own, 1)

        @pl.when(pl.program_id(0) == 1)
        def _():
            fill(twin, 9)

    return call(
        kernel,
        shape((16, u, columns), f32),
        (2,),
        [whole(own), whole(twin)],
        pl.BlockSpec((16, u, chunks * STEP), lambda h, s: (0, 0, lax.rem(h + s[0], 2))),
        scalars,
        (own, twin),
    ).reshape(rows, columns)


def core_swap(v):
    return lax.ppermute(v, "c", [(0, 1), (1, 0)])


def pair_swap(v):
    return lax.ppermute(v, "yl", [(0, 1), (1, 0)])


def exchange(v, ring, masks):
    def flat(i, c):
        return (i // 2 * 2 + c) * 2 + i % 2 if ring == "y" else 2 * i + c

    pairs = [(flat(i, c), flat(i ^ masks[c], c)) for i in range(4) for c in range(2)]
    return lax.ppermute(v, RING[ring], pairs)


def pick(v, index, axis):
    return lax.dynamic_index_in_dim(v, index, axis, keepdims=False)


def quarters(place, core):
    first = jnp.where(core == 0, 1, 3)
    second = jnp.where(core == 0, 3, 1)
    return place, place ^ first, place ^ 2, place ^ second


class Flow:
    def __init__(self, ring, pair):
        self.ring, self.other = ring, "z" if ring == "x" else "x"
        send, self.keep = pair
        self.got = exchange(send, ring, (1, 3))


def onward(flows, none):
    def kernel(_, *refs):
        n = len(flows)
        for i in range(n):
            keep, got = refs[2 * i : 2 * i + 2]
            refs[2 * n + i][0] = (keep[0, 0].astype(f32) + got[0, 0].astype(f32)).astype(bf16)

    dims = [f.keep.shape[2:] for f in flows]
    sums = call(
        kernel,
        tuple(shape((2, *d), bf16) for d in dims),
        (2,),
        [pl.BlockSpec((1, 1, *d), lambda y, s: (1, y, 0, 0)) for d in dims for _ in range(2)],
        [pl.BlockSpec((1, *d), lambda y, s: (y, 0, 0)) for d in dims],
        none,
        [a for f in flows for a in (f.keep, f.got)],
    )
    for f, v in zip(flows, sums):
        f.last = exchange(v, f.ring, (3, 1))


def turn(flows, cuts):
    in_specs, outs, out_specs, args = [], [], [], []
    for f in flows:
        first = 1 if f.other == "x" else 5
        rows, columns = f.keep.shape[2] // 4, f.keep.shape[3]
        in_specs += [
            pl.BlockSpec((1, 2, rows, columns), lambda q, s, i=first: (0, 0, s[i + q], 0))
        ] * 2 + [pl.BlockSpec((2, rows, columns), lambda q, s, i=first: (0, s[i + q], 0))]
        args += [f.keep, f.got, f.last]
        dims = (1, 2, rows, columns)
        outs += [shape((2, *dims[1:]), bf16), shape((2, *dims[1:]), f32)]
        out_specs += [
            pl.BlockSpec(dims, lambda q, s: (jnp.minimum(q, 1), 0, 0, 0)),
            pl.BlockSpec(dims, lambda q, s: (jnp.maximum(q - 2, 0), 0, 0, 0)),
        ]

    def kernel(_, *refs):
        n = len(flows)
        q = pl.program_id(0)
        for i in range(n):
            keep, got, last = refs[3 * i : 3 * i + 3]
            send, kept = refs[3 * n + 2 * i : 3 * n + 2 * i + 2]
            value = keep[0].astype(f32) + got[0].astype(f32) + last[...].astype(f32)
            send[0] = jnp.where(q < 2, value.astype(bf16), send[0])
            kept[0] = value

    out = call(kernel, tuple(outs), (4,), in_specs, out_specs, cuts, args)
    for i, f in enumerate(flows):
        f.ring = f.other
        f.keep = out[2 * i + 1]
        f.got = exchange(out[2 * i], f.ring, (1, 3))


class Finish:
    def __init__(self, flows, extra, scalars):
        sizes = [(f.keep.shape[2], f.keep.shape[3] // STEP) for f in flows]
        rows = sum(u * n for u, n in sizes) + sum(e.shape[1] for e in extra)

        def kernel(s, *refs):
            send, mine = refs[-2:]
            zero = s[0] == 0
            start = 0
            for i, (u, n) in enumerate(sizes):
                keep, got, last = refs[3 * i : 3 * i + 3]
                v = [
                    keep[0, y].astype(f32) + got[0, y].astype(f32) + last[y].astype(f32)
                    for y in range(2)
                ]
                near = jnp.where(zero, v[0], v[1])
                away = jnp.where(zero, v[1], v[0]).astype(bf16)
                for k in range(n):
                    cut = slice(k * STEP, (k + 1) * STEP)
                    mine[start : start + u, :] = near[:, cut]
                    send[start : start + u, :] = away[:, cut]
                    start += u
            for ref in refs[3 * len(sizes) : -2]:
                u = ref.shape[1]
                mine[start : start + u, :] = jnp.where(zero, ref[0], ref[1])
                send[start : start + u, :] = jnp.where(zero, ref[1], ref[0]).astype(bf16)
                start += u

        in_specs, args = [], []
        for f in flows:
            dims = (1, *f.keep.shape[1:])
            in_specs += [pl.BlockSpec(dims, lambda j, s: (0, 0, 0, 0))] * 2 + [whole(f.last)]
            args += [f.keep, f.got, f.last]
        out = (shape((rows, STEP), bf16), shape((rows, STEP), f32))
        send, self.mine = call(
            kernel,
            out,
            (1,),
            in_specs + [whole(e) for e in extra],
            [whole(o) for o in out],
            scalars,
            args + list(extra),
        )
        self.got = exchange(send, "y", (1, 3))

    def second(self):
        self.mine = (self.mine + self.got.astype(f32)).astype(bf16)
        self.far = lax.ppermute(self.mine, "yh", [(0, 1), (1, 0)])
        line.hold(self.mine)

    def done(self):
        return (self.mine.astype(f32) + self.far.astype(f32)).astype(bf16)


class Spread:
    def __init__(self, v, rings):
        self.rings = rings
        self.v = v
        self.got = exchange(v, rings[0], (1, 3))
        line.hold(v)

    def second(self, ring=None):
        pair = jnp.stack([self.v, self.got])
        self.v = pair
        self.got = exchange(pair, ring or self.rings[0], (3, 1))
        line.hold(pair)

    def third(self):
        four = jnp.concatenate([self.v, self.got])
        self.v = four
        self.got = exchange(four, self.rings[1], (1, 3))
        line.hold(four)

    def fourth(self):
        self.second(self.rings[1])

    def done(self):
        all_ = jnp.concatenate([self.v, self.got])
        return all_, core_swap(all_)


def per_device(
    tokens,
    memory,
    compressed,
    cotangent,
    ln1_g,
    ln1_b,
    w_q,
    w_kv,
    w_r,
    bias_u,
    bias_v,
    w_o,
    ln2_g,
    ln2_b,
    w_in,
    b_in,
    w_out,
    b_out,
    conv_w,
    conv_b,
):
    line.held = []
    tokens, memory, compressed, cotangent = tokens[0], memory[0], compressed[0], cotangent[0]
    yl, core = lax.axis_index("yl"), lax.axis_index("c")
    place = {"x": lax.axis_index("x"), "z": lax.axis_index("z")}
    none = jnp.zeros((1,), jnp.int32)
    ints = lambda *v: jnp.stack([jnp.asarray(i, jnp.int32) for i in v])

    def thirds(rows):
        half = rows // 2
        other = (1 - yl) * half
        return [yl * half, other + core * (half // 2), other + (1 - core) * (half // 2)]

    def both(v):
        return (v, core_swap(v))

    spot = (place["x"] * 4 + place["z"]) * 2 + core
    piece = pack(
        (ln1_g, ln1_b, bias_u, bias_v, ln2_g, ln2_b, b_out, conv_b, b_in),
        w_in,
        w_out,
        conv_w,
        ints(spot),
    )
    piece_got = exchange(piece, "y", (1, 3))

    kv_part, small = pack_rows(w_kv, w_q, w_r, w_o, ints(core))
    kv_got = exchange(kv_part, "y", (1, 3))
    small_got = exchange(small, "y", (1, 3))

    def joined(w, got, twin):
        return jnp.concatenate([w, got, twin], axis=0)

    spread = lax.all_gather(piece_got[:-16], ("x", "z", "c"), axis=0)
    thirds_d = ints(*thirds(D))
    thirds_c = ints(yl * (3 * D // 2), (1 - yl) * (3 * D // 2), *thirds(D))
    sinus_table = sinusoid(KEYS, D).astype(bf16)
    sinus_rel = jnp.concatenate(
        [
            lax.dynamic_slice_in_dim(sinus_table, thirds_d[i], width, 1)
            for i, width in enumerate(THIRDS)
        ],
        axis=1,
    )
    line.hold(sinus_rel)
    vectors, b_in = unpack(piece, piece_got, ints(yl))

    normed, normed_rel, oldest = first_norm(compressed, memory, tokens, vectors, thirds_d)
    both_normed, both_oldest, both_cot = both(normed), both(oldest), both(cotangent)
    kv_whole = joined(w_kv, kv_got, core_swap(kv_got))
    key_value = dot(normed_rel, kv_whole).astype(bf16)
    line.hold(key_value)
    small_twin = core_swap(small_got)
    q_whole, r_whole, o_whole = [
        joined(w, small_got[i], small_twin[i]) for i, w in enumerate((w_q, w_r, w_o))
    ]
    queries = dot(normed_rel[2 * T :], q_whole)
    relative = dot(sinus_rel, r_whole).astype(bf16)
    line.hold(queries, relative)
    probs, attended = attend(queries, key_value, relative, vectors, none)
    residual, normed2, normed2_rel = out_and_norm(attended, o_whole, tokens, vectors, thirds_d)
    both_n2, both_att = both(normed2), both(attended)

    cuts, rels, twins = [], [], []
    for ring in ("x", "z"):
        own, first, far, second = quarters(place[ring], core)
        cuts += [first, far, own, second]
        rels.append([own, first, second, far])
        twins.append([own, second, first, far])
    cuts = ints(core, *cuts)

    def flows(groups):
        pairs = weight_grads(groups, cuts)
        return [Flow(ring, pair) for (ring, _), pair in zip(groups, pairs)]

    hidden, d_pre, mixed_out, d_normed2, d_b_in = feed_forward(
        normed2_rel, residual, cotangent, w_in, w_out, spread, b_in, vectors, ints(yl)
    )
    both_hidden, both_pre = both(hidden), both(d_pre)
    d_residual, d_branch, d_attended, d_ln2_g, d_ln2_b, d_b_out = second_norm_back(
        cotangent, d_normed2, residual, vectors, o_whole, thirds_d
    )
    both_branch = both(d_branch)
    large = flows(
        [
            ("x", [(both_hidden, 0, T, both_cot, False)]),
            ("z", [(both_n2, 0, T, both_pre, False), (both_att, 0, T, both_branch, False)]),
        ]
    )
    d_kv, my_kv, give_kv, d_relative, d_queries, d_bias_u, d_bias_v = attend_back(
        queries, key_value, relative, vectors, probs, d_attended, ints(core)
    )
    both_kv = (my_kv, core_swap(give_kv))
    both_q, both_rel = both(d_queries), both(d_relative)

    compact, comp_normed = compress(oldest, conv_w, spread, vectors, thirds_c)
    comp_pair = dot(comp_normed, kv_whole).astype(bf16)
    compressed_next = jnp.concatenate([compressed[T // 3 :], compact], axis=0)
    near = flows(
        [
            ("x", [(both_normed, 0, KEYS, both_kv, True)]),
            (
                "z",
                [
                    (both_normed, 2, T, both_q, False),
                    ((sinus_table, sinus_table), 0, KEYS, both_rel, False),
                ],
            ),
        ]
    )
    onward(large, none)
    loss, d_ck, d_cv = reconstruct(queries, key_value, comp_pair, none)
    recon_loss = jnp.sum(loss) / (T * D)
    d_compact, d_conv_b = compress_back(d_ck, d_cv, kv_whole, compact, vectors, thirds_d)
    both_compact = both(d_compact)
    turn(large, cuts)
    onward(near, none)
    conv = flows([("x", [(both_oldest, 0, T // 3, both_compact, False)])])
    d_tokens, d_ln1_g, d_ln1_b = first_norm_back(
        d_kv, d_queries, kv_whole, q_whole, compressed, memory, tokens, vectors, d_residual,
        thirds_d,
    )
    onward(large, none)
    turn(near, cuts)
    early = Finish(large, [], ints(yl))
    onward(conv, none)
    onward(near, none)
    early.second()
    turn(conv, cuts)
    early_done = early.done()
    line.hold(early_done)
    early_sums = lax.all_gather(early_done, ("c", "x", "z"), axis=0)
    onward(conv, none)

    total = jnp.concatenate(
        [d_ln1_g, d_ln1_b, d_bias_u, d_bias_v, d_ln2_g, d_ln2_b, d_b_out, d_conv_b]
        + [d_b_in]
    )
    total = jnp.concatenate(
        [
            total[:8].reshape(8, 2, STEP).transpose(1, 0, 2),
            total[8:].reshape(2, 4, STEP),
            jnp.zeros((2, 4, STEP), f32),
        ],
        axis=1,
    )
    late = Finish([*near, *conv], [total], ints(yl))
    late.second()
    late_done = late.done()
    one = Spread(late_done[:128], ("z", "x"))
    two = Spread(late_done[128:], ("x", "z"))
    one.second()
    two.second()
    one.third()
    two.third()
    one.fourth()
    two.fourth()
    (one_own, one_twin), (two_own, two_twin) = one.done(), two.done()
    x_places, z_places = rels
    x_twin, z_twin = twins
    along = ints(core, *x_places, *z_places, *x_twin, *z_twin)
    across = ints(core, *z_places, *x_places, *z_twin, *x_twin)
    g_kv = widen_near(one_own, one_twin, 0, D // 2, 2 * D, False, along)
    g_q = widen_near(one_own, one_twin, 64, D // 2, D, True, along)
    g_r = widen_near(one_own, one_twin, 96, D // 2, D, True, along)
    g_conv = widen_near(two_own, two_twin, 0, 3 * D // 2, D, True, across)
    g_out = widen(early_sums, 0, FF // 2, D, False, none)
    g_in = widen(early_sums, 128, D // 2, FF, True, none)
    g_o = widen(early_sums, 256, D // 2, D, True, none)

    def four(v):
        return (v[0] + v[1]) + (v[2] + v[3])

    half = four(four(two_own[:, :, 96:108].astype(f32))) + four(
        four(two_twin[:, :, 96:108].astype(f32))
    )
    t_ln1_g, t_ln1_b, t_bu, t_bv, t_ln2_g, t_ln2_b, t_bout, t_convb = [half[i] for i in range(8)]
    t_bin = half[8:].reshape(-1)
    return (
        mixed_out[None],
        compressed_next[None],
        recon_loss[None],
        d_tokens[None],
        t_ln1_g,
        t_ln1_b,
        g_q,
        g_kv,
        g_r,
        t_bu,
        t_bv,
        g_o,
        t_ln2_g,
        t_ln2_b,
        g_in,
        t_bin,
        g_out,
        t_bout,
        g_conv,
        t_convb,
    )


def solution(mesh):
    fine = Mesh(mesh.devices.reshape(2, 4, 4, 2, 2), AXES)
    stream = P(AXES, None, None)
    vec, mat = P("yl"), P("yl", None)
    weights = (vec, vec, mat, mat, mat, vec, vec, mat, vec, vec, mat, vec, mat, vec, mat, vec)
    return jax.shard_map(
        per_device,
        mesh=fine,
        in_specs=(stream,) * 4 + weights,
        out_specs=(stream, stream, P(AXES), stream) + weights,
        check_vma=False,
    )
```

```python
import jax
import jax.numpy as jnp
from jax import lax
from jax.experimental import pallas as pl
from jax.experimental.pallas import tpu as pltpu
from jax.sharding import Mesh, PartitionSpec as P

H = 8
HD = 128
D = 1024
T = 192
KEYS = 576
PAD = 640
FF = 4096
FACTOR = HD ** (-0.5)
f32 = jnp.float32
bf16 = jnp.bfloat16
AXES = ("yh", "x", "z", "c", "yl")
RING = {"x": ("x", "c"), "z": ("z", "c"), "y": ("yh", "c", "yl")}


def sinusoid(key_count, model_dim):
    distance = (key_count - 1 - jnp.arange(key_count)).astype(f32)
    inverse = 1.0 / 10000.0 ** (jnp.arange(0, model_dim, 2).astype(f32) / model_dim)
    angles = distance[:, None] * inverse[None, :]
    return jnp.concatenate([jnp.sin(angles), jnp.cos(angles)], axis=-1)


def dot(a, b):
    return jnp.dot(a, b, preferred_element_type=f32)


def dot_t(a, b):
    return lax.dot_general(a, b, (((1,), (1,)), ((), ())), preferred_element_type=f32)


def t_dot(a, b):
    return lax.dot_general(a, b, (((0,), (0,)), ((), ())), preferred_element_type=f32)


class Line:
    def __init__(self):
        self.held, self.due = [], {}

    def hold(self, *values):
        self.held += values

    def expect(self, gap, *values):
        self.due.setdefault(gap, []).extend(values)

    def ran(self, result):
        self.held = [result, *self.due.get(1, [])]
        self.due = {gap - 1: values for gap, values in self.due.items() if gap > 1}

    def later(self, value):
        return lax.optimization_barrier((value, *self.held))[0] if self.held else value


line = Line()


def call(kernel, out, grid, in_specs, out_specs, scalars, args, scratch=()):
    held, n = line.held, len(args)

    def body(s, *refs):
        kernel(s, *refs[:n], *refs[n + len(held) :])

    result = pl.pallas_call(
        body,
        out_shape=out,
        grid_spec=pltpu.PrefetchScalarGridSpec(
            num_scalar_prefetch=1,
            grid=grid,
            in_specs=list(in_specs) + [pl.BlockSpec(memory_space=pl.ANY)] * len(held),
            out_specs=out_specs,
            scratch_shapes=list(scratch),
        ),
        compiler_params=pltpu.CompilerParams(vmem_limit_bytes=56 << 20),
        cost_estimate=pl.CostEstimate(flops=1, bytes_accessed=1, transcendentals=0),
    )(scalars, *args, *held)
    line.ran(jax.tree.leaves(result)[0])
    return result


def gate(value, *after):
    anywhere = pl.BlockSpec(memory_space=pl.ANY)
    return pl.pallas_call(
        lambda *refs: None,
        out_shape=jax.ShapeDtypeStruct(value.shape, value.dtype),
        in_specs=[anywhere] * (1 + len(after)),
        out_specs=anywhere,
        input_output_aliases={0: 0},
    )(value, *after)


def whole(a):
    zeros = (0,) * a.ndim
    return pl.BlockSpec(a.shape, lambda *_: zeros)


def shape(dims, dtype):
    return jax.ShapeDtypeStruct(dims, dtype)


def at(offset):
    return pl.multiple_of(offset, 128)


def center_scale(v):
    mid = v - jnp.mean(v, axis=-1, keepdims=True)
    r = lax.rsqrt(jnp.mean(mid * mid, axis=-1, keepdims=True) + 1e-5)
    return mid * r, r


def norm_back(xhat, r, g, dn):
    gd = dn * g
    return r * (
        gd
        - jnp.mean(gd, axis=-1, keepdims=True)
        - xhat * jnp.mean(gd * xhat, axis=-1, keepdims=True)
    )


def softmax(s):
    e = jnp.exp(s - jnp.max(s, axis=-1, keepdims=True))
    return e / jnp.sum(e, axis=-1, keepdims=True)


(LN1_G, LN1_B, BIAS_U, BIAS_V, LN2_G, LN2_B, B_OUT, CONV_B) = range(8)


def row(ref, i):
    return ref[i : i + 1, :]


def pack(vectors, w_in, w_out, conv_w, scalars):
    n_in, n_out, n_conv = (w.shape[0] // 32 for w in (w_in, w_out, conv_w))
    chunks = FF // D
    rows = n_out + n_in * chunks + n_conv
    half = D // 2

    def kernel(_, *refs):
        wi, wo, wc, piece, flat = refs[-5:]
        flat[...] = jnp.zeros_like(flat)
        for i, ref in enumerate(refs[:8]):
            flat[i : i + 1, :half] = ref[...].astype(f32).reshape(1, half)
        flat[8 : 8 + FF // 2 // D, :] = refs[8][...].astype(f32).reshape(FF // 2 // D, D)
        piece[:n_out, :] = wo[...]
        for i in range(chunks):
            piece[n_out + i * n_in : n_out + (i + 1) * n_in, :] = wi[:, i * D : (i + 1) * D]
        piece[n_out + n_in * chunks : rows, :] = wc[...]
        piece[rows:, :] = flat[...].astype(bf16)

    out = shape((rows + 16, D), bf16)
    return call(
        kernel,
        out,
        (1,),
        [whole(v) for v in vectors]
        + [
            pl.BlockSpec((w.shape[0] // 32, w.shape[1]), lambda j, s: (s[0], 0))
            for w in (w_in, w_out, conv_w)
        ],
        whole(out),
        scalars,
        (*vectors, w_in, w_out, conv_w),
        [pltpu.VMEM((16, D), f32)],
    )


def pack_rows(w_kv, w_q, w_r, w_o, scalars):
    n = w_q.shape[0] // 2

    def kernel(_, kv, q, r, o, kv_out, out):
        kv_out[...] = kv[...]
        for i, ref in enumerate((q, r, o)):
            out[i] = ref[...]

    out = (shape((n, 2 * D), bf16), shape((3, n, D), bf16))
    return call(
        kernel,
        out,
        (1,),
        [
            pl.BlockSpec((n, w.shape[1]), lambda j, s: (s[0], 0))
            for w in (w_kv, w_q, w_r, w_o)
        ],
        [whole(o) for o in out],
        scalars,
        (w_kv, w_q, w_r, w_o),
    )


def unpack(mine, theirs, scalars):
    half = D // 2
    at_row = mine.shape[0] // 16 - 1
    tail = pl.BlockSpec((16, D), lambda j, s: (at_row, 0))

    def kernel(s, mine, theirs, vectors, b_in):
        a, b = mine[...].astype(f32), theirs[...].astype(f32)
        low = jnp.where(s[0] == 0, a, b)
        high = jnp.where(s[0] == 0, b, a)
        vectors[:, :half] = low[:8, :half]
        vectors[:, half:] = high[:8, :half]
        rows = FF // 2 // D
        b_in[:rows] = low[8 : 8 + rows]
        b_in[rows:] = high[8 : 8 + rows]

    out = (shape((8, D), f32), shape((FF // D, D), f32))
    return call(
        kernel, out, (1,), [tail, tail], [whole(o) for o in out], scalars, (mine, theirs)
    )


def relative_columns(x, s, widths):
    parts = [x[:, pl.ds(at(s[i]), width)] for i, width in enumerate(widths)]
    return jnp.concatenate(parts, axis=1)


def natural_columns(out, x, s, widths):
    start = 0
    for i, width in enumerate(widths):
        out[:, pl.ds(at(s[i]), width)] = x[:, start : start + width]
        start += width


THIRDS = (D // 2, D // 4, D // 4)


def first_norm(compressed, memory, tokens, vectors, offsets):
    def kernel(s, comp, mem, tok, vec, out, out_rel, old):
        gain, bias = row(vec, LN1_G), row(vec, LN1_B)

        def part(ref, base):
            for i in range(0, T, 32):
                xhat, r = center_scale(ref[i : i + 32, :].astype(f32))
                out[base + i : base + i + 32, :] = (xhat * gain + bias).astype(bf16)

        part(comp, 0)
        part(mem, T)
        part(tok, 2 * T)
        out_rel[...] = relative_columns(out, s, THIRDS)
        line_of = lax.broadcasted_iota(jnp.int32, (T // 3, T), 0)
        col = lax.broadcasted_iota(jnp.int32, (T // 3, T), 1)
        low = mem[...].astype(bf16)
        for tap in range(3):
            take = jnp.where(col == 3 * line_of + tap, 1.0, 0.0).astype(bf16)
            old[:, tap * D : (tap + 1) * D] = dot(take, low).astype(bf16)

    args = (compressed, memory, tokens, vectors)
    out = (shape((KEYS, D), bf16), shape((KEYS, D), bf16), shape((T // 3, 3 * D), bf16))
    return call(
        kernel, out, (1,), [whole(a) for a in args], [whole(o) for o in out], offsets, args
    )


PAIR = 2
STEPS = H // PAIR


def head(rows, row_block=0, first=0):
    return pl.BlockSpec((rows, PAIR * HD), lambda h, s: (row_block, first // PAIR + h))


def vec_head(rows=1):
    return pl.BlockSpec((rows, PAIR * HD), lambda h, s: (0, h))


def each_head(body):
    for i in range(PAIR):
        body(i, slice(i * HD, (i + 1) * HD))


def attend(queries, key_value, relative, vectors, none):
    def kernel(_, q, k, v, rel, vec, probs, out):
        pad = jnp.zeros((PAD - KEYS, HD), bf16)
        row = lax.broadcasted_iota(jnp.int32, (T, PAD), 0)
        col = lax.broadcasted_iota(jnp.int32, (T, PAD), 1)
        seen = col <= row + (KEYS - T)

        def body(i, cut):
            content = ((q[:, cut] + vec[BIAS_U : BIAS_U + 1, cut]) * FACTOR).astype(bf16)
            located = ((q[:, cut] + vec[BIAS_V : BIAS_V + 1, cut]) * FACTOR).astype(bf16)
            raw = dot_t(located, jnp.concatenate([rel[:, cut], pad], axis=0))
            raw = pltpu.roll(raw, PAD - T + 1, 1, stride=1, stride_axis=0)
            s = dot_t(content, jnp.concatenate([k[:, cut], pad], axis=0)) + raw
            p = softmax(jnp.where(seen, s, -1e30))
            probs[i] = p
            low = p.astype(bf16)
            out[:, cut] = dot(low, jnp.concatenate([v[:, cut], pad], axis=0)).astype(bf16)

        each_head(body)

    return call(
        kernel,
        (shape((H, T, PAD), f32), shape((T, D), bf16)),
        (STEPS,),
        [head(T), head(KEYS), head(KEYS, 0, H), head(KEYS), vec_head(8)],
        [pl.BlockSpec((PAIR, T, PAD), lambda h, s: (h, 0, 0)), head(T)],
        none,
        (queries, key_value, key_value, relative, vectors),
    )


def attend_back(queries, key_value, relative, vectors, probs, d_attended, scalars):
    def kernel(s, q, k, v, rel, vec, probs, d_att, d_kv, mine, give, d_rel, d_q, d_bu, d_bv):
        pad = jnp.zeros((PAD - KEYS, HD), bf16)
        row = lax.broadcasted_iota(jnp.int32, (T, T), 0)
        col = lax.broadcasted_iota(jnp.int32, (T, T), 1)
        flip = jnp.where(row + col == T - 1, 1.0, 0.0).astype(bf16)

        def body(i, cut):
            content = ((q[:, cut] + vec[BIAS_U : BIAS_U + 1, cut]) * FACTOR).astype(bf16)
            located = ((q[:, cut] + vec[BIAS_V : BIAS_V + 1, cut]) * FACTOR).astype(bf16)
            p, da = probs[i], d_att[:, cut]
            d_p = dot_t(da, jnp.concatenate([v[:, cut], pad], axis=0))
            d_v = t_dot(p.astype(bf16), da)[:KEYS].astype(bf16)
            d_s = (p * (d_p - jnp.sum(p * d_p, axis=-1, keepdims=True))).astype(bf16)
            d_c = dot(d_s, jnp.concatenate([k[:, cut], pad], axis=0)) * FACTOR
            d_k = t_dot(d_s, content)[:KEYS].astype(bf16)
            d_kv[0, :, cut] = d_k
            d_kv[1, :, cut] = d_v
            mine[:, cut] = jnp.where(s[0] == 0, d_k, d_v)
            give[:, cut] = jnp.where(s[0] == 0, d_v, d_k)
            d_raw = pltpu.roll(dot(flip, d_s), 0, 1, stride=1, stride_axis=0)
            d_raw = dot(flip, d_raw.astype(bf16)).astype(bf16)
            d_l = dot(d_raw, jnp.concatenate([rel[:, cut], pad], axis=0)) * FACTOR
            d_rel[:, cut] = t_dot(d_raw, located)[:KEYS].astype(bf16)
            d_q[:, cut] = (d_c + d_l).astype(bf16)
            d_bu[:, cut] = jnp.sum(d_c, axis=0, keepdims=True)
            d_bv[:, cut] = jnp.sum(d_l, axis=0, keepdims=True)

        each_head(body)

    return call(
        kernel,
        (
            shape((2, KEYS, D), bf16),
            shape((KEYS, D), bf16),
            shape((KEYS, D), bf16),
            shape((KEYS, D), bf16),
            shape((T, D), bf16),
            shape((1, D), f32),
            shape((1, D), f32),
        ),
        (STEPS,),
        [
            head(T),
            head(KEYS),
            head(KEYS, 0, H),
            head(KEYS),
            vec_head(8),
            pl.BlockSpec((PAIR, T, PAD), lambda h, s: (h, 0, 0)),
            head(T),
        ],
        [
            pl.BlockSpec((2, KEYS, PAIR * HD), lambda h, s: (0, 0, h)),
            head(KEYS),
            head(KEYS),
            head(KEYS),
            head(T),
            vec_head(),
            vec_head(),
        ],
        scalars,
        (queries, key_value, key_value, relative, vectors, probs, d_attended),
    )


def out_and_norm(attended, w_o, tokens, vectors, offsets):
    def kernel(s, att, w, tok, vec, res, n2, n2_rel):
        total = tok[...].astype(f32) + dot(relative_columns(att, s, THIRDS), w[...])
        res[...] = total
        xhat, r = center_scale(total)
        n2[...] = (xhat * row(vec, LN2_G) + row(vec, LN2_B)).astype(bf16)
        other = at(D // 2 - s[0])
        n2_rel[:, : D // 2] = n2[:, pl.ds(at(s[0]), D // 2)]
        n2_rel[:, D // 2 :] = n2[:, pl.ds(other, D // 2)]

    args = (attended, w_o, tokens, vectors)
    out = (shape((T, D), f32), shape((T, D), bf16), shape((T, D), bf16))
    return call(
        kernel, out, (1,), [whole(a) for a in args], [whole(o) for o in out], offsets, args
    )


STEP = 512
UNITS = 1024
HALF = FF // 2 // UNITS


def feed_forward(n2_rel, residual, cotangent, w_in, w_out, spread, b_in, vectors, scalars):
    n_in = w_in.shape[0] // 32
    n_out = w_out.shape[0] // 32
    skip = n_out // n_in
    per = UNITS // n_out
    K_NORM = 0.7978845608028654

    def natural(j, s):
        return lax.rem(j + s[0] * HALF, 2 * HALF)

    def kernel(s, n2, res, cot, wi0, wi1, wo0, wo1, bi, vec, hid, dpre, mixed, dn2, dbi, acc, back):
        j = pl.program_id(0)
        n = natural(j, s)
        win = jnp.concatenate([wi0[...], wi1[...].reshape(D // 2, UNITS)], axis=0)
        pre = dot(n2[...], win) + bi[pl.ds(n, 1), :]
        t = jnp.tanh(K_NORM * (pre + 0.044715 * (pre * pre * pre)))
        hidden = (0.5 * pre * (1.0 + t)).astype(bf16)
        slope = 0.5 * (1.0 + t) + (0.5 * K_NORM) * pre * (1.0 - t * t) * (
            1.0 + (3 * 0.044715) * (pre * pre)
        )
        hid[...] = hidden

        def rest(wo, start):
            d_pre = (dot_t(cot[...], wo) * slope).astype(bf16)
            dpre[...] = d_pre
            dbi[pl.ds(n, 1), :] = jnp.sum(d_pre.astype(f32), axis=0, keepdims=True)
            if start:
                acc[...] = dot(hidden, wo)
                back[...] = dot_t(d_pre, win)
            else:
                acc[...] += dot(hidden, wo)
                back[...] += dot_t(d_pre, win)

        @pl.when(j == 0)
        def _():
            rest(wo0[...], True)

        @pl.when((j > 0) & (j < HALF))
        def _():
            rest(wo0[...], False)

        @pl.when(j >= HALF)
        def _():
            rest(wo1[...].reshape(UNITS, D), False)

        @pl.when(j == 2 * HALF - 1)
        def _():
            mixed[...] = (res[...] + acc[...] + row(vec, B_OUT)).astype(bf16)
            dn2[:, pl.ds(at(s[0] * (D // 2)), D // 2)] = back[:, : D // 2]
            dn2[:, pl.ds(at((1 - s[0]) * (D // 2)), D // 2)] = back[:, D // 2 :]

    out = (
        shape((T, FF), bf16),
        shape((T, FF), bf16),
        shape((T, D), bf16),
        shape((T, D), f32),
        shape((2 * HALF, UNITS), f32),
    )
    by_unit = pl.BlockSpec((T, UNITS), lambda j, s: (0, natural(j, s)))
    return call(
        kernel,
        out,
        (2 * HALF,),
        [
            whole(n2_rel),
            whole(residual),
            whole(cotangent),
            pl.BlockSpec((D // 2, UNITS), lambda j, s: (0, natural(j, s))),
            pl.BlockSpec((32, n_in, UNITS), lambda j, s: (0, skip + natural(j, s), 0)),
            pl.BlockSpec((UNITS, D), lambda j, s: (jnp.minimum(j, HALF - 1), 0)),
            pl.BlockSpec(
                (per, n_out, D), lambda j, s: (jnp.maximum(j - HALF, 0), 0, 0)
            ),
            whole(b_in),
            whole(vectors),
        ],
        [by_unit, by_unit, whole(out[2]), whole(out[3]), whole(out[4])],
        scalars,
        (n2_rel, residual, cotangent, w_in, spread, w_out, spread, b_in, vectors),
        [pltpu.VMEM((T, D), f32), pltpu.VMEM((T, D), f32)],
    )


def second_norm_back(cotangent, d_n2, residual, vectors, w_o, offsets):
    def kernel(s, cot, dn, res, vec, w, d_res, d_br, d_att, dg, db, dbo):
        xhat, r = center_scale(res[...])
        dn, wide = dn[...], cot[...].astype(f32)
        dg[...] = jnp.sum(dn * xhat, axis=0, keepdims=True)
        db[...] = jnp.sum(dn, axis=0, keepdims=True)
        dbo[...] = jnp.sum(wide, axis=0, keepdims=True)
        total = wide + norm_back(xhat, r, row(vec, LN2_G), dn)
        d_res[...] = total
        low = total.astype(bf16)
        d_br[...] = low
        natural_columns(d_att, dot_t(low, w[...]).astype(bf16), s, THIRDS)

    args = (cotangent, d_n2, residual, vectors, w_o)
    out = (
        shape((T, D), f32),
        shape((T, D), bf16),
        shape((T, D), bf16),
        shape((1, D), f32),
        shape((1, D), f32),
        shape((1, D), f32),
    )
    return call(
        kernel, out, (1,), [whole(a) for a in args], [whole(o) for o in out], offsets, args
    )


def first_norm_back(d_kv, d_q, w_kv, w_q, compressed, memory, tokens, vectors, d_res, offsets):
    steps = 4
    wide, slim = 2 * D // steps, D // steps

    def kernel(s, dkv, dq, kw, qw, comp, mem, tok, vec, dres, dtok, dg, db, acc, nat):
        j = pl.program_id(0)

        @pl.when(j == 0)
        def _():
            acc[...] = dot_t(dkv[0], kw[...])

        @pl.when(j > 0)
        def _():
            acc[...] += dot_t(dkv[0], kw[...])

        acc[2 * T :, :] += dot_t(dq[...], qw[...])

        @pl.when(j == steps - 1)
        def _():
            natural_columns(nat, acc, s, THIRDS)
            gain = row(vec, LN1_G)
            sum_g = jnp.zeros((1, D), f32)
            sum_b = jnp.zeros((1, D), f32)
            for block, ref in enumerate((comp, mem, tok)):
                for i in range(0, T, 32):
                    xhat, r = center_scale(ref[i : i + 32, :].astype(f32))
                    dn = nat[block * T + i : block * T + i + 32, :]
                    sum_g += jnp.sum(dn * xhat, axis=0, keepdims=True)
                    sum_b += jnp.sum(dn, axis=0, keepdims=True)
                    if block == 2:
                        dtok[i : i + 32, :] = dres[i : i + 32, :] + norm_back(xhat, r, gain, dn)
            dg[...] = sum_g
            db[...] = sum_b

    rest = (compressed, memory, tokens, vectors, d_res)
    out = (shape((T, D), f32), shape((1, D), f32), shape((1, D), f32))
    return call(
        kernel,
        out,
        (steps,),
        [
            pl.BlockSpec((1, KEYS, wide), lambda j, s: (j // (steps // 2), 0, lax.rem(j, steps // 2))),
            pl.BlockSpec((T, slim), lambda j, s: (0, j)),
            pl.BlockSpec((D, wide), lambda j, s: (0, j)),
            pl.BlockSpec((D, slim), lambda j, s: (0, j)),
        ]
        + [whole(a) for a in rest],
        [whole(o) for o in out],
        offsets,
        (d_kv, d_q, w_kv, w_q, *rest),
        [pltpu.VMEM((KEYS, D), f32), pltpu.VMEM((KEYS, D), f32)],
    )


def compress(oldest, conv_w, spread, vectors, offsets):
    block = 256
    rows = T // 3
    n = conv_w.shape[0] // 32
    skip = (spread.shape[1] - n) // 16

    def kernel(s, x, own, w0, w1, w2, vec, compact, normed, x_rel, natural):
        j = pl.program_id(0)

        @pl.when(j == 0)
        def _():
            x_rel[...] = relative_columns(x, s, (3 * D // 2, 3 * D // 2))

        other = jnp.concatenate([w0[...], w1[...], w2[...]], axis=1).reshape(32 * n, block)
        w = jnp.concatenate([own[...], other], axis=0)
        here = pl.ds(at(j * block), block)
        compact[:, here] = dot(x_rel[...], w) + vec[CONV_B : CONV_B + 1, here]

        @pl.when(j == D // block - 1)
        def _():
            xhat, r = center_scale(compact[...])
            natural[...] = (xhat * row(vec, LN1_G) + row(vec, LN1_B)).astype(bf16)
            start = 0
            for i, width in enumerate(THIRDS):
                normed[:, start : start + width] = natural[:, pl.ds(at(s[2 + i]), width)]
                start += width

    out = (shape((rows, D), f32), shape((rows, D), bf16))
    return call(
        kernel,
        out,
        (D // block,),
        [whole(oldest), pl.BlockSpec((conv_w.shape[0], block), lambda j, s: (0, j))]
        + [
            pl.BlockSpec((32, 16, block), lambda j, s, i=i: (0, skip + i, j))
            for i in range(n // 16)
        ]
        + [whole(vectors)],
        [whole(o) for o in out],
        offsets,
        (oldest, conv_w) + (spread,) * (n // 16) + (vectors,),
        [pltpu.VMEM((rows, 3 * D), bf16), pltpu.VMEM((rows, D), bf16)],
    )


def reconstruct(queries, key_value, comp_pair, none):
    rows = T // 3

    def kernel(_, q, k, v, ck, cv, loss, dck, dcv):
        @pl.when(pl.program_id(0) == 0)
        def _():
            loss[...] = jnp.zeros_like(loss)

        def body(i, cut):
            asking = (q[:, cut] * FACTOR).astype(bf16)
            cvh = cv[:, cut]
            p = softmax(dot_t(asking, k[:, cut])).astype(bf16)
            gp = softmax(dot_t(asking, ck[:, cut]))
            low = gp.astype(bf16)
            miss = dot(p, v[:, cut]) - dot(low, cvh)
            loss[...] += jnp.sum(miss * miss, axis=0, keepdims=True)
            d_guess = ((-2.0 / (T * D)) * miss).astype(bf16)
            d_gp = dot_t(d_guess, cvh)
            dcv[:, cut] = t_dot(low, d_guess).astype(bf16)
            d_gs = (gp * (d_gp - jnp.sum(gp * d_gp, axis=-1, keepdims=True))).astype(bf16)
            dck[:, cut] = t_dot(d_gs, asking).astype(bf16)

        each_head(body)

    return call(
        kernel,
        (shape((1, HD), f32), shape((rows, D), bf16), shape((rows, D), bf16)),
        (STEPS,),
        [head(T), head(T, 1), head(T, 1, H), head(rows), head(rows, 0, H)],
        [pl.BlockSpec((1, HD), lambda h, s: (0, 0)), head(rows), head(rows)],
        none,
        (queries, key_value, key_value, comp_pair, comp_pair),
    )


def compress_back(dck, dcv, w_kv, compact, vectors, offsets):
    rows = T // 3

    def kernel(s, dck, dcv, w, compact, vec, d_compact, d_bias, dn):
        back = dot_t(jnp.concatenate([dck[...], dcv[...]], axis=1), w[...])
        natural_columns(dn, back, s, THIRDS)
        xhat, r = center_scale(compact[...])
        low = norm_back(xhat, r, row(vec, LN1_G), dn[...]).astype(bf16)
        d_compact[...] = low
        d_bias[...] = jnp.sum(low.astype(f32), axis=0, keepdims=True)

    args = (dck, dcv, w_kv, compact, vectors)
    out = (shape((rows, D), bf16), shape((1, D), f32))
    return call(
        kernel,
        out,
        (1,),
        [whole(a) for a in args],
        [whole(o) for o in out],
        offsets,
        args,
        [pltpu.VMEM((rows, D), f32)],
    )


def weight_grads(groups, scalars):
    in_specs, args, outs, out_specs, layout = [], [], [], [], []
    for ring, jobs in groups:
        first = 1 if ring == "x" else 5
        block = jobs[0][0][0].shape[1] // 8
        widths = []
        for xs, row_block, rows, dys, ready in jobs:
            width = dys[0].shape[1] // (1 if ready else 2)
            widths.append(width)
            for x in xs:
                for y in range(2):
                    in_specs.append(
                        pl.BlockSpec(
                            (rows, block),
                            lambda q, s, r=row_block, f=first, y=y: (r, y * 4 + s[f + q]),
                        )
                    )
                    args.append(x)
            for dy in dys:
                in_specs.append(
                    pl.BlockSpec((rows, width), lambda q, s, r=ready: (0, 0 if r else s[0]))
                )
                args.append(dy)
        dims = (1, 2, block, sum(widths))
        outs += [shape((2, *dims[1:]), bf16)] * 2
        out_specs += [
            pl.BlockSpec(dims, lambda q, s: (jnp.minimum(q, 1), 0, 0, 0)),
            pl.BlockSpec(dims, lambda q, s: (jnp.maximum(q - 2, 0), 0, 0, 0)),
        ]
        layout.append(widths)

    def kernel(s, *refs):
        q = pl.program_id(0)
        place = 0
        results = refs[len(in_specs) :]
        for i, widths in enumerate(layout):
            send, keep = results[2 * i : 2 * i + 2]
            block = send.shape[2]
            start = 0
            for width in widths:
                a0, a1, b0, b1, da, db = (r[...] for r in refs[place : place + 6])
                place += 6
                x = jnp.concatenate(
                    [jnp.concatenate([a0, a1], axis=1), jnp.concatenate([b0, b1], axis=1)], axis=0
                )
                value = t_dot(x, jnp.concatenate([da, db], axis=0)).astype(bf16)
                value = value.reshape(2, block, width)
                cut = slice(start, start + width)
                send[0, :, :, cut] = jnp.where(q < 2, value, send[0, :, :, cut])
                keep[0, :, :, cut] = value
                start += width

    flat = call(kernel, tuple(outs), (4,), in_specs, out_specs, scalars, args)
    return [(flat[2 * i], flat[2 * i + 1]) for i in range(len(groups))]


def widen(gathered, start, rows, columns, swapped, none):
    u = rows // 16
    sub = u // 32
    chunks = columns // 2 // STEP
    order = [x * 4 + z for z in range(4) for x in range(4)] if swapped else list(range(16))

    def kernel(_, *refs):
        out = refs[-1]
        for k, src in enumerate(refs[:-1]):
            for to, frm in enumerate(order):
                out[to, :, k * STEP : (k + 1) * STEP] = src[frm].astype(f32)

    return call(
        kernel,
        shape((16, u, columns), f32),
        (sub, 2),
        [
            pl.BlockSpec((16, 32, STEP), lambda i, c, s, k=k: (c, start // 32 + k * sub + i, 0))
            for k in range(chunks)
        ],
        pl.BlockSpec((16, 32, STEP * chunks), lambda i, c, s: (0, i, c)),
        none,
        (gathered,) * chunks,
    ).reshape(rows, columns)


def core_swap(v):
    return lax.ppermute(v, "c", [(0, 1), (1, 0)])


def pair_swap(v):
    return lax.ppermute(v, "yl", [(0, 1), (1, 0)])


def exchange(v, ring, masks):
    def flat(i, c):
        return (i // 2 * 2 + c) * 2 + i % 2 if ring == "y" else 2 * i + c

    pairs = [(flat(i, c), flat(i ^ masks[c], c)) for i in range(4) for c in range(2)]
    return lax.ppermute(v, RING[ring], pairs)


def pick(v, index, axis):
    return lax.dynamic_index_in_dim(v, index, axis, keepdims=False)


def quarters(place, core):
    first = jnp.where(core == 0, 1, 3)
    second = jnp.where(core == 0, 3, 1)
    return place, place ^ first, place ^ 2, place ^ second


class Flow:
    def __init__(self, ring, pair):
        self.ring, self.other = ring, "z" if ring == "x" else "x"
        send, self.keep = pair
        self.got = exchange(send, ring, (1, 3))


def onward(flows, none):
    def kernel(_, *refs):
        n = len(flows)
        for i in range(n):
            keep, got = refs[2 * i : 2 * i + 2]
            refs[2 * n + i][0] = (keep[0, 0].astype(f32) + got[0, 0].astype(f32)).astype(bf16)

    dims = [f.keep.shape[2:] for f in flows]
    sums = call(
        kernel,
        tuple(shape((2, *d), bf16) for d in dims),
        (2,),
        [pl.BlockSpec((1, 1, *d), lambda y, s: (1, y, 0, 0)) for d in dims for _ in range(2)],
        [pl.BlockSpec((1, *d), lambda y, s: (y, 0, 0)) for d in dims],
        none,
        [a for f in flows for a in (f.keep, f.got)],
    )
    for f, v in zip(flows, sums):
        f.last = exchange(v, f.ring, (3, 1))


def turn(flows, cuts):
    in_specs, outs, out_specs, args = [], [], [], []
    for f in flows:
        first = 1 if f.other == "x" else 5
        rows, columns = f.keep.shape[2] // 4, f.keep.shape[3]
        in_specs += [
            pl.BlockSpec((1, 2, rows, columns), lambda q, s, i=first: (0, 0, s[i + q], 0))
        ] * 2 + [pl.BlockSpec((2, rows, columns), lambda q, s, i=first: (0, s[i + q], 0))]
        args += [f.keep, f.got, f.last]
        dims = (1, 2, rows, columns)
        outs += [shape((2, *dims[1:]), bf16), shape((2, *dims[1:]), f32)]
        out_specs += [
            pl.BlockSpec(dims, lambda q, s: (jnp.minimum(q, 1), 0, 0, 0)),
            pl.BlockSpec(dims, lambda q, s: (jnp.maximum(q - 2, 0), 0, 0, 0)),
        ]

    def kernel(_, *refs):
        n = len(flows)
        q = pl.program_id(0)
        for i in range(n):
            keep, got, last = refs[3 * i : 3 * i + 3]
            send, kept = refs[3 * n + 2 * i : 3 * n + 2 * i + 2]
            value = keep[0].astype(f32) + got[0].astype(f32) + last[...].astype(f32)
            send[0] = jnp.where(q < 2, value.astype(bf16), send[0])
            kept[0] = value

    out = call(kernel, tuple(outs), (4,), in_specs, out_specs, cuts, args)
    for i, f in enumerate(flows):
        f.ring = f.other
        f.keep = out[2 * i + 1]
        f.got = exchange(out[2 * i], f.ring, (1, 3))


def add(a, b, none):
    def kernel(_, a, b, out):
        out[...] = (a[...].astype(f32) + b[...].astype(f32)).astype(bf16)

    out = shape(a.shape, bf16)
    return call(kernel, out, (1,), [whole(a), whole(b)], whole(out), none, (a, b))


class Finish:
    def __init__(self, flows, extra, scalars):
        sizes = [(f.keep.shape[2], f.keep.shape[3] // STEP) for f in flows]
        rows = sum(u * n for u, n in sizes) + sum(e.shape[1] for e in extra)

        def kernel(s, *refs):
            send, mine = refs[-2:]
            zero = s[0] == 0
            start = 0
            for i, (u, n) in enumerate(sizes):
                keep, got, last = refs[3 * i : 3 * i + 3]
                v = [
                    keep[0, y].astype(f32) + got[0, y].astype(f32) + last[y].astype(f32)
                    for y in range(2)
                ]
                near = jnp.where(zero, v[0], v[1])
                away = jnp.where(zero, v[1], v[0]).astype(bf16)
                for k in range(n):
                    cut = slice(k * STEP, (k + 1) * STEP)
                    mine[start : start + u, :] = near[:, cut]
                    send[start : start + u, :] = away[:, cut]
                    start += u
            for ref in refs[3 * len(sizes) : -2]:
                u = ref.shape[1]
                mine[start : start + u, :] = jnp.where(zero, ref[0], ref[1])
                send[start : start + u, :] = jnp.where(zero, ref[1], ref[0]).astype(bf16)
                start += u

        in_specs, args = [], []
        for f in flows:
            dims = (1, *f.keep.shape[1:])
            in_specs += [pl.BlockSpec(dims, lambda j, s: (0, 0, 0, 0))] * 2 + [whole(f.last)]
            args += [f.keep, f.got, f.last]
        out = (shape((rows, STEP), bf16), shape((rows, STEP), f32))
        send, self.mine = call(
            kernel,
            out,
            (1,),
            in_specs + [whole(e) for e in extra],
            [whole(o) for o in out],
            scalars,
            args + list(extra),
        )
        self.got = exchange(send, "y", (1, 3))

    def second(self, none):
        self.mine = add(self.mine, self.got, none)
        self.far = lax.ppermute(self.mine, "yh", [(0, 1), (1, 0)])

    def gather(self, none):
        return lax.all_gather(add(self.mine, self.far, none), ("c", "x", "z"), axis=0)


def per_device(
    tokens,
    memory,
    compressed,
    cotangent,
    ln1_g,
    ln1_b,
    w_q,
    w_kv,
    w_r,
    bias_u,
    bias_v,
    w_o,
    ln2_g,
    ln2_b,
    w_in,
    b_in,
    w_out,
    b_out,
    conv_w,
    conv_b,
):
    line.held, line.due = [], {}
    tokens, memory, compressed, cotangent = tokens[0], memory[0], compressed[0], cotangent[0]
    yl, core = lax.axis_index("yl"), lax.axis_index("c")
    place = {"x": lax.axis_index("x"), "z": lax.axis_index("z")}
    none = jnp.zeros((1,), jnp.int32)
    ints = lambda *v: jnp.stack([jnp.asarray(i, jnp.int32) for i in v])

    def thirds(rows):
        half = rows // 2
        other = (1 - yl) * half
        return [yl * half, other + core * (half // 2), other + (1 - core) * (half // 2)]

    def both(v):
        return (v, core_swap(v))

    spot = (place["x"] * 4 + place["z"]) * 2 + core
    piece = pack(
        (ln1_g, ln1_b, bias_u, bias_v, ln2_g, ln2_b, b_out, conv_b, b_in),
        w_in,
        w_out,
        conv_w,
        ints(spot),
    )
    piece_got = exchange(piece, "y", (1, 3))

    kv_part, small = pack_rows(w_kv, w_q, w_r, w_o, ints(core))
    kv_got = exchange(kv_part, "y", (1, 3))
    small_got = exchange(small, "y", (1, 3))

    def joined(w, got, twin):
        return jnp.concatenate([w, got, twin], axis=0)

    spread = lax.all_gather(piece_got[:-16], ("x", "z", "c"), axis=0)
    thirds_d = ints(*thirds(D))
    thirds_c = ints(yl * (3 * D // 2), (1 - yl) * (3 * D // 2), *thirds(D))
    sinus_table = sinusoid(KEYS, D).astype(bf16)
    sinus_rel = jnp.concatenate(
        [
            lax.dynamic_slice_in_dim(sinus_table, thirds_d[i], width, 1)
            for i, width in enumerate(THIRDS)
        ],
        axis=1,
    )
    line.hold(sinus_rel)
    vectors, b_in = unpack(piece, piece_got, ints(yl))

    normed, normed_rel, oldest = first_norm(compressed, memory, tokens, vectors, thirds_d)
    both_normed, both_oldest, both_cot = both(normed), both(oldest), both(cotangent)
    kv_got = gate(kv_got, normed)
    kv_whole = joined(w_kv, kv_got, core_swap(kv_got))
    key_value = dot(normed_rel, kv_whole).astype(bf16)
    line.hold(key_value)
    small_got = gate(small_got, key_value)
    small_twin = core_swap(small_got)
    q_whole, r_whole, o_whole = [
        joined(w, small_got[i], small_twin[i]) for i, w in enumerate((w_q, w_r, w_o))
    ]
    queries = dot(normed_rel[2 * T :], q_whole)
    relative = dot(sinus_rel, r_whole).astype(bf16)
    line.hold(queries, relative)
    probs, attended = attend(queries, key_value, relative, vectors, none)
    residual, normed2, normed2_rel = out_and_norm(attended, o_whole, tokens, vectors, thirds_d)
    both_n2, both_att = both(normed2), both(attended)

    cuts, rels, twins = [], [], []
    for ring in ("x", "z"):
        own, first, far, second = quarters(place[ring], core)
        cuts += [first, far, own, second]
        rels.append([own, first, second, far])
        twins.append([own, second, first, far])
    cuts = ints(core, *cuts)

    def flows(groups):
        pairs = weight_grads(groups, cuts)
        return [Flow(ring, pair) for (ring, _), pair in zip(groups, pairs)]

    hidden, d_pre, mixed_out, d_normed2, d_b_in = feed_forward(
        normed2_rel, residual, cotangent, w_in, w_out, spread, b_in, vectors, ints(yl)
    )
    both_hidden, both_pre = both(hidden), both(d_pre)
    d_residual, d_branch, d_attended, d_ln2_g, d_ln2_b, d_b_out = second_norm_back(
        cotangent, d_normed2, residual, vectors, o_whole, thirds_d
    )
    both_branch = both(d_branch)
    large = flows(
        [
            ("x", [(both_hidden, 0, T, both_cot, False)]),
            ("z", [(both_n2, 0, T, both_pre, False), (both_att, 0, T, both_branch, False)]),
        ]
    )
    d_kv, my_kv, give_kv, d_relative, d_queries, d_bias_u, d_bias_v = attend_back(
        queries, key_value, relative, vectors, probs, d_attended, ints(core)
    )
    both_kv = (my_kv, core_swap(give_kv))
    both_q, both_rel = both(d_queries), both(d_relative)

    compact, comp_normed = compress(oldest, conv_w, spread, vectors, thirds_c)
    comp_pair = dot(comp_normed, kv_whole).astype(bf16)
    compressed_next = jnp.concatenate([compressed[T // 3 :], compact], axis=0)
    near = flows(
        [
            ("x", [(both_normed, 0, KEYS, both_kv, True)]),
            (
                "z",
                [
                    (both_normed, 2, T, both_q, False),
                    ((sinus_table, sinus_table), 0, KEYS, both_rel, False),
                ],
            ),
        ]
    )
    loss, d_ck, d_cv = reconstruct(queries, key_value, comp_pair, none)
    recon_loss = jnp.sum(loss) / (T * D)
    onward(large, none)
    d_compact, d_conv_b = compress_back(d_ck, d_cv, kv_whole, compact, vectors, thirds_d)
    both_compact = both(d_compact)
    onward(near, none)
    conv = flows([("x", [(both_oldest, 0, T // 3, both_compact, False)])])
    turn(large, cuts)
    turn(near, cuts)
    line.expect(1, *[f.got for f in near])
    d_tokens, d_ln1_g, d_ln1_b = first_norm_back(
        d_kv, d_queries, kv_whole, q_whole, compressed, memory, tokens, vectors, d_residual,
        thirds_d,
    )
    onward(large, none)
    onward(conv, none)
    onward(near, none)
    line.expect(2, *[f.last for f in near])
    early = Finish(large, [], ints(yl))
    turn(conv, cuts)
    early.second(none)
    onward(conv, none)
    early_sums = early.gather(none)

    total = jnp.concatenate(
        [d_ln1_g, d_ln1_b, d_bias_u, d_bias_v, d_ln2_g, d_ln2_b, d_b_out, d_conv_b]
        + [d_b_in]
    )
    total = jnp.concatenate(
        [
            total[:8].reshape(8, 2, STEP).transpose(1, 0, 2),
            total[8:].reshape(2, 4, STEP),
            jnp.zeros((2, 4, STEP), f32),
        ],
        axis=1,
    )
    late = Finish([*near, *conv], [total], ints(yl))
    late.second(none)
    late_sums = late.gather(none)

    g_in = widen(early_sums, 128, D // 2, FF, True, none)
    g_out = widen(early_sums, 0, FF // 2, D, False, none)
    g_o = widen(early_sums, 256, D // 2, D, True, none)
    g_conv = widen(late_sums, 128, 3 * D // 2, D, False, none)
    g_kv = widen(late_sums, 0, D // 2, 2 * D, False, none)
    g_q = widen(late_sums, 64, D // 2, D, True, none)
    g_r = widen(late_sums, 96, D // 2, D, True, none)
    half = jnp.sum(late_sums[:, 224:236].astype(f32), axis=0)
    t_ln1_g, t_ln1_b, t_bu, t_bv, t_ln2_g, t_ln2_b, t_bout, t_convb = [half[i] for i in range(8)]
    t_bin = half[8:].reshape(-1)
    return (
        mixed_out[None],
        compressed_next[None],
        recon_loss[None],
        d_tokens[None],
        t_ln1_g,
        t_ln1_b,
        g_q,
        g_kv,
        g_r,
        t_bu,
        t_bv,
        g_o,
        t_ln2_g,
        t_ln2_b,
        g_in,
        t_bin,
        g_out,
        t_bout,
        g_conv,
        t_convb,
    )


def solution(mesh):
    fine = Mesh(mesh.devices.reshape(2, 4, 4, 2, 2), AXES)
    stream = P(AXES, None, None)
    vec, mat = P("yl"), P("yl", None)
    weights = (vec, vec, mat, mat, mat, vec, vec, mat, vec, vec, mat, vec, mat, vec, mat, vec)
    return jax.shard_map(
        per_device,
        mesh=fine,
        in_specs=(stream,) * 4 + weights,
        out_specs=(stream, stream, P(AXES), stream) + weights,
        check_vma=False,
    )
```

```python
import jax
import jax.numpy as jnp
from jax import lax
from jax.experimental import pallas as pl
from jax.experimental.pallas import tpu as pltpu
from jax.sharding import Mesh, PartitionSpec as P

H = 8
HD = 128
D = 1024
T = 192
KEYS = 576
PAD = 640
FF = 4096
FACTOR = HD ** (-0.5)
f32 = jnp.float32
bf16 = jnp.bfloat16
AXES = ("yh", "x", "z", "c", "yl")
RING = {"x": ("x", "c"), "z": ("z", "c"), "y": ("yh", "c", "yl")}


def sinusoid(key_count, model_dim):
    distance = (key_count - 1 - jnp.arange(key_count)).astype(f32)
    inverse = 1.0 / 10000.0 ** (jnp.arange(0, model_dim, 2).astype(f32) / model_dim)
    angles = distance[:, None] * inverse[None, :]
    return jnp.concatenate([jnp.sin(angles), jnp.cos(angles)], axis=-1)


def dot(a, b):
    return jnp.dot(a, b, preferred_element_type=f32)


def dot_t(a, b):
    return lax.dot_general(a, b, (((1,), (1,)), ((), ())), preferred_element_type=f32)


def t_dot(a, b):
    return lax.dot_general(a, b, (((0,), (0,)), ((), ())), preferred_element_type=f32)


class Line:
    def __init__(self):
        self.held, self.due = [], {}

    def hold(self, *values):
        self.held += values

    def expect(self, gap, *values):
        self.due.setdefault(gap, []).extend(values)

    def ran(self, result):
        self.held = [result, *self.due.get(1, [])]
        self.due = {gap - 1: values for gap, values in self.due.items() if gap > 1}

    def later(self, value):
        return lax.optimization_barrier((value, *self.held))[0] if self.held else value


line = Line()


def call(kernel, out, grid, in_specs, out_specs, scalars, args, scratch=()):
    held, n = line.held, len(args)

    def body(s, *refs):
        kernel(s, *refs[:n], *refs[n + len(held) :])

    result = pl.pallas_call(
        body,
        out_shape=out,
        grid_spec=pltpu.PrefetchScalarGridSpec(
            num_scalar_prefetch=1,
            grid=grid,
            in_specs=list(in_specs) + [pl.BlockSpec(memory_space=pl.ANY)] * len(held),
            out_specs=out_specs,
            scratch_shapes=list(scratch),
        ),
        compiler_params=pltpu.CompilerParams(vmem_limit_bytes=56 << 20),
        cost_estimate=pl.CostEstimate(flops=1, bytes_accessed=1, transcendentals=0),
    )(scalars, *args, *held)
    line.ran(jax.tree.leaves(result)[0])
    return result


def gate(values, *after):
    n = len(values)
    anywhere = pl.BlockSpec(memory_space=pl.ANY)
    return pl.pallas_call(
        lambda *refs: None,
        out_shape=[jax.ShapeDtypeStruct(v.shape, v.dtype) for v in values],
        in_specs=[anywhere] * (n + len(after)),
        out_specs=[anywhere] * n,
        input_output_aliases={i: i for i in range(n)},
    )(*values, *after)


def whole(a):
    zeros = (0,) * a.ndim
    return pl.BlockSpec(a.shape, lambda *_: zeros)


def shape(dims, dtype):
    return jax.ShapeDtypeStruct(dims, dtype)


def at(offset):
    return pl.multiple_of(offset, 128)


def center_scale(v):
    mid = v - jnp.mean(v, axis=-1, keepdims=True)
    r = lax.rsqrt(jnp.mean(mid * mid, axis=-1, keepdims=True) + 1e-5)
    return mid * r, r


def norm_back(xhat, r, g, dn):
    gd = dn * g
    return r * (
        gd
        - jnp.mean(gd, axis=-1, keepdims=True)
        - xhat * jnp.mean(gd * xhat, axis=-1, keepdims=True)
    )


def softmax(s):
    e = jnp.exp(s - jnp.max(s, axis=-1, keepdims=True))
    return e / jnp.sum(e, axis=-1, keepdims=True)


(LN1_G, LN1_B, BIAS_U, BIAS_V, LN2_G, LN2_B, B_OUT, CONV_B) = range(8)


def row(ref, i):
    return ref[i : i + 1, :]


def pack(vectors, w_in, w_out, scalars):
    n_in, n_out = (w.shape[0] // 32 for w in (w_in, w_out))
    chunks = FF // D
    rows = n_out + n_in * chunks
    half = D // 2

    def kernel(_, *refs):
        wi, wo, piece, flat = refs[-4:]
        flat[...] = jnp.zeros_like(flat)
        for i, ref in enumerate(refs[:8]):
            flat[i : i + 1, :half] = ref[...].astype(f32).reshape(1, half)
        flat[8 : 8 + FF // 2 // D, :] = refs[8][...].astype(f32).reshape(FF // 2 // D, D)
        piece[:n_out, :] = wo[...]
        for i in range(chunks):
            piece[n_out + i * n_in : n_out + (i + 1) * n_in, :] = wi[:, i * D : (i + 1) * D]
        piece[rows:, :] = flat[...].astype(bf16)

    out = shape((rows + 16, D), bf16)
    return call(
        kernel,
        out,
        (1,),
        [whole(v) for v in vectors]
        + [
            pl.BlockSpec((w.shape[0] // 32, w.shape[1]), lambda j, s: (s[0], 0))
            for w in (w_in, w_out)
        ],
        whole(out),
        scalars,
        (*vectors, w_in, w_out),
        [pltpu.VMEM((16, D), f32)],
    )


def pack_rows(w_kv, w_q, w_r, w_o, conv_w, scalars):
    n, n_conv = w_q.shape[0] // 2, conv_w.shape[0] // 2

    def kernel(_, kv, q, r, o, conv, kv_out, out, conv_out):
        kv_out[...] = kv[...]
        for i, ref in enumerate((q, r, o)):
            out[i] = ref[...]
        conv_out[...] = conv[...]

    args = (w_kv, w_q, w_r, w_o, conv_w)
    out = (shape((n, 2 * D), bf16), shape((3, n, D), bf16), shape((n_conv, D), bf16))
    return call(
        kernel,
        out,
        (1,),
        [pl.BlockSpec((w.shape[0] // 2, w.shape[1]), lambda j, s: (s[0], 0)) for w in args],
        [whole(o) for o in out],
        scalars,
        args,
    )


def unpack(mine, theirs, scalars):
    half = D // 2
    at_row = mine.shape[0] // 16 - 1
    tail = pl.BlockSpec((16, D), lambda j, s: (at_row, 0))

    def kernel(s, mine, theirs, vectors, b_in):
        a, b = mine[...].astype(f32), theirs[...].astype(f32)
        low = jnp.where(s[0] == 0, a, b)
        high = jnp.where(s[0] == 0, b, a)
        vectors[:, :half] = low[:8, :half]
        vectors[:, half:] = high[:8, :half]
        rows = FF // 2 // D
        b_in[:rows] = low[8 : 8 + rows]
        b_in[rows:] = high[8 : 8 + rows]

    out = (shape((8, D), f32), shape((FF // D, D), f32))
    return call(
        kernel, out, (1,), [tail, tail], [whole(o) for o in out], scalars, (mine, theirs)
    )


def relative_columns(x, s, widths):
    parts = [x[:, pl.ds(at(s[i]), width)] for i, width in enumerate(widths)]
    return jnp.concatenate(parts, axis=1)


def natural_columns(out, x, s, widths):
    start = 0
    for i, width in enumerate(widths):
        out[:, pl.ds(at(s[i]), width)] = x[:, start : start + width]
        start += width


THIRDS = (D // 2, D // 4, D // 4)


def first_norm(compressed, memory, tokens, vectors, offsets):
    def kernel(s, comp, mem, tok, vec, out, out_rel, old):
        gain, bias = row(vec, LN1_G), row(vec, LN1_B)

        def part(ref, base):
            for i in range(0, T, 32):
                xhat, r = center_scale(ref[i : i + 32, :].astype(f32))
                out[base + i : base + i + 32, :] = (xhat * gain + bias).astype(bf16)

        part(comp, 0)
        part(mem, T)
        part(tok, 2 * T)
        out_rel[...] = relative_columns(out, s, THIRDS)
        line_of = lax.broadcasted_iota(jnp.int32, (T // 3, T), 0)
        col = lax.broadcasted_iota(jnp.int32, (T // 3, T), 1)
        low = mem[...].astype(bf16)
        for tap in range(3):
            take = jnp.where(col == 3 * line_of + tap, 1.0, 0.0).astype(bf16)
            old[:, tap * D : (tap + 1) * D] = dot(take, low).astype(bf16)

    args = (compressed, memory, tokens, vectors)
    out = (shape((KEYS, D), bf16), shape((KEYS, D), bf16), shape((T // 3, 3 * D), bf16))
    return call(
        kernel, out, (1,), [whole(a) for a in args], [whole(o) for o in out], offsets, args
    )


def head(n, rows, row_block=0, first=0):
    return pl.BlockSpec((rows, n * HD), lambda h, s: (row_block, first // n + h))


def columns_of(n):
    return [slice(i * HD, (i + 1) * HD) for i in range(n)]


def attend(queries, key_value, relative, vectors, none):
    n = 2

    def kernel(_, q, k, v, rel, vec, probs, out):
        pad = jnp.zeros((PAD - KEYS, HD), bf16)
        i = lax.broadcasted_iota(jnp.int32, (T, PAD), 0)
        j = lax.broadcasted_iota(jnp.int32, (T, PAD), 1)
        seen = j <= i + (KEYS - T)
        cuts = columns_of(n)
        content = [((q[:, c] + vec[BIAS_U : BIAS_U + 1, c]) * FACTOR).astype(bf16) for c in cuts]
        located = [((q[:, c] + vec[BIAS_V : BIAS_V + 1, c]) * FACTOR).astype(bf16) for c in cuts]
        raw = [
            dot_t(x, jnp.concatenate([rel[:, c], pad], axis=0)) for x, c in zip(located, cuts)
        ]
        near = [dot_t(x, jnp.concatenate([k[:, c], pad], axis=0)) for x, c in zip(content, cuts)]
        raw = [pltpu.roll(x, PAD - T + 1, 1, stride=1, stride_axis=0) for x in raw]
        p = [softmax(jnp.where(seen, a + b, -1e30)) for a, b in zip(near, raw)]
        for h, c in enumerate(cuts):
            probs[h] = p[h]
            value = jnp.concatenate([v[:, c], pad], axis=0)
            out[:, c] = dot(p[h].astype(bf16), value).astype(bf16)

    return call(
        kernel,
        (shape((H, T, PAD), f32), shape((T, D), bf16)),
        (H // n,),
        [head(n, T), head(n, KEYS), head(n, KEYS, 0, H), head(n, KEYS), head(n, 8)],
        [pl.BlockSpec((n, T, PAD), lambda h, s: (h, 0, 0)), head(n, T)],
        none,
        (queries, key_value, key_value, relative, vectors),
    )


def attend_back(queries, key_value, relative, vectors, probs, d_attended, scalars):
    n = 2

    def kernel(s, q, k, v, rel, vec, probs, d_att, d_kv, mine, give, d_rel, d_q, d_bu, d_bv):
        pad = jnp.zeros((PAD - KEYS, HD), bf16)
        i = lax.broadcasted_iota(jnp.int32, (T, T), 0)
        j = lax.broadcasted_iota(jnp.int32, (T, T), 1)
        flip = jnp.where(i + j == T - 1, 1.0, 0.0).astype(bf16)
        cuts = columns_of(n)
        content = [((q[:, c] + vec[BIAS_U : BIAS_U + 1, c]) * FACTOR).astype(bf16) for c in cuts]
        located = [((q[:, c] + vec[BIAS_V : BIAS_V + 1, c]) * FACTOR).astype(bf16) for c in cuts]
        da = [d_att[:, c] for c in cuts]
        d_p = [dot_t(x, jnp.concatenate([v[:, c], pad], axis=0)) for x, c in zip(da, cuts)]
        d_v = [t_dot(probs[h].astype(bf16), x)[:KEYS].astype(bf16) for h, x in enumerate(da)]
        d_s = []
        for h, x in enumerate(d_p):
            p = probs[h]
            d_s.append((p * (x - jnp.sum(p * x, axis=-1, keepdims=True))).astype(bf16))
        d_raw = [dot(flip, x) for x in d_s]
        d_c = [
            dot(x, jnp.concatenate([k[:, c], pad], axis=0)) * FACTOR for x, c in zip(d_s, cuts)
        ]
        d_k = [t_dot(x, y)[:KEYS].astype(bf16) for x, y in zip(d_s, content)]
        d_raw = [pltpu.roll(x, 0, 1, stride=1, stride_axis=0).astype(bf16) for x in d_raw]
        d_raw = [dot(flip, x).astype(bf16) for x in d_raw]
        d_l = [
            dot(x, jnp.concatenate([rel[:, c], pad], axis=0)) * FACTOR for x, c in zip(d_raw, cuts)
        ]
        for h, c in enumerate(cuts):
            d_rel[:, c] = t_dot(d_raw[h], located[h])[:KEYS].astype(bf16)
            d_kv[0, :, c] = d_k[h]
            d_kv[1, :, c] = d_v[h]
            mine[:, c] = jnp.where(s[0] == 0, d_k[h], d_v[h])
            give[:, c] = jnp.where(s[0] == 0, d_v[h], d_k[h])
            d_q[:, c] = (d_c[h] + d_l[h]).astype(bf16)
            d_bu[:, c] = jnp.sum(d_c[h], axis=0, keepdims=True)
            d_bv[:, c] = jnp.sum(d_l[h], axis=0, keepdims=True)

    return call(
        kernel,
        (shape((2, KEYS, D), bf16),)
        + (shape((KEYS, D), bf16),) * 3
        + (shape((T, D), bf16), shape((1, D), f32), shape((1, D), f32)),
        (H // n,),
        [
            head(n, T),
            head(n, KEYS),
            head(n, KEYS, 0, H),
            head(n, KEYS),
            head(n, 8),
            pl.BlockSpec((n, T, PAD), lambda h, s: (h, 0, 0)),
            head(n, T),
        ],
        [
            pl.BlockSpec((2, KEYS, n * HD), lambda h, s: (0, 0, h)),
            head(n, KEYS),
            head(n, KEYS),
            head(n, KEYS),
            head(n, T),
            head(n, 1),
            head(n, 1),
        ],
        scalars,
        (queries, key_value, key_value, relative, vectors, probs, d_attended),
    )


def out_and_norm(attended, w_o, tokens, vectors, offsets):
    def kernel(s, att, w, tok, vec, res, n2, n2_rel):
        total = tok[...].astype(f32) + dot(relative_columns(att, s, THIRDS), w[...])
        res[...] = total
        xhat, r = center_scale(total)
        n2[...] = (xhat * row(vec, LN2_G) + row(vec, LN2_B)).astype(bf16)
        other = at(D // 2 - s[0])
        n2_rel[:, : D // 2] = n2[:, pl.ds(at(s[0]), D // 2)]
        n2_rel[:, D // 2 :] = n2[:, pl.ds(other, D // 2)]

    args = (attended, w_o, tokens, vectors)
    out = (shape((T, D), f32), shape((T, D), bf16), shape((T, D), bf16))
    return call(
        kernel, out, (1,), [whole(a) for a in args], [whole(o) for o in out], offsets, args
    )


STEP = 512
UNITS = 1024
HALF = FF // 2 // UNITS


def feed_forward(n2_rel, residual, cotangent, w_in, w_out, spread, b_in, vectors, scalars):
    n_in = w_in.shape[0] // 32
    n_out = w_out.shape[0] // 32
    skip = n_out // n_in
    per = UNITS // n_out
    K_NORM = 0.7978845608028654

    def natural(j, s):
        return lax.rem(j + s[0] * HALF, 2 * HALF)

    def kernel(s, n2, res, cot, wi0, wi1, wo0, wo1, bi, vec, hid, dpre, mixed, dn2, dbi, acc, back):
        j = pl.program_id(0)
        n = natural(j, s)

        @pl.when(j == 0)
        def _():
            acc[...] = jnp.zeros_like(acc)
            back[...] = jnp.zeros_like(back)

        wo = jnp.where(j < HALF, wo0[...], wo1[...].reshape(UNITS, D))
        win = jnp.concatenate([wi0[...], wi1[...].reshape(D // 2, UNITS)], axis=0)
        pre = dot(n2[...], win) + bi[pl.ds(n, 1), :]
        d_hidden = dot_t(cot[...], wo)
        square = pre * pre
        t = jnp.tanh(K_NORM * pre * (1.0 + 0.044715 * square))
        gate_ = 0.5 * (1.0 + t)
        hidden = (pre * gate_).astype(bf16)
        slope = gate_ + (0.5 * K_NORM) * pre * (1.0 - t * t) * (1.0 + (3 * 0.044715) * square)
        d_pre = (d_hidden * slope).astype(bf16)
        hid[...] = hidden
        dpre[...] = d_pre
        dbi[pl.ds(n, 1), :] = jnp.sum(d_pre.astype(f32), axis=0, keepdims=True)
        acc[...] += dot(hidden, wo)
        back[...] += dot_t(d_pre, win)

        @pl.when(j == 2 * HALF - 1)
        def _():
            mixed[...] = (res[...] + acc[...] + row(vec, B_OUT)).astype(bf16)
            dn2[:, pl.ds(at(s[0] * (D // 2)), D // 2)] = back[:, : D // 2]
            dn2[:, pl.ds(at((1 - s[0]) * (D // 2)), D // 2)] = back[:, D // 2 :]

    out = (
        shape((T, FF), bf16),
        shape((T, FF), bf16),
        shape((T, D), bf16),
        shape((T, D), f32),
        shape((2 * HALF, UNITS), f32),
    )
    by_unit = pl.BlockSpec((T, UNITS), lambda j, s: (0, natural(j, s)))
    return call(
        kernel,
        out,
        (2 * HALF,),
        [
            whole(n2_rel),
            whole(residual),
            whole(cotangent),
            pl.BlockSpec((D // 2, UNITS), lambda j, s: (0, natural(j, s))),
            pl.BlockSpec((32, n_in, UNITS), lambda j, s: (0, skip + natural(j, s), 0)),
            pl.BlockSpec((UNITS, D), lambda j, s: (jnp.minimum(j, HALF - 1), 0)),
            pl.BlockSpec(
                (per, n_out, D), lambda j, s: (jnp.maximum(j - HALF, 0), 0, 0)
            ),
            whole(b_in),
            whole(vectors),
        ],
        [by_unit, by_unit, whole(out[2]), whole(out[3]), whole(out[4])],
        scalars,
        (n2_rel, residual, cotangent, w_in, spread, w_out, spread, b_in, vectors),
        [pltpu.VMEM((T, D), f32), pltpu.VMEM((T, D), f32)],
    )


def second_norm_back(cotangent, d_n2, residual, vectors, w_o, offsets):
    def kernel(s, cot, dn, res, vec, w, d_res, d_br, d_att, dg, db, dbo):
        xhat, r = center_scale(res[...])
        dn, wide = dn[...], cot[...].astype(f32)
        dg[...] = jnp.sum(dn * xhat, axis=0, keepdims=True)
        db[...] = jnp.sum(dn, axis=0, keepdims=True)
        dbo[...] = jnp.sum(wide, axis=0, keepdims=True)
        total = wide + norm_back(xhat, r, row(vec, LN2_G), dn)
        d_res[...] = total
        low = total.astype(bf16)
        d_br[...] = low
        natural_columns(d_att, dot_t(low, w[...]).astype(bf16), s, THIRDS)

    args = (cotangent, d_n2, residual, vectors, w_o)
    out = (
        shape((T, D), f32),
        shape((T, D), bf16),
        shape((T, D), bf16),
        shape((1, D), f32),
        shape((1, D), f32),
        shape((1, D), f32),
    )
    return call(
        kernel, out, (1,), [whole(a) for a in args], [whole(o) for o in out], offsets, args
    )


def first_norm_back(d_kv, d_q, w_kv, w_q, compressed, memory, tokens, vectors, d_res, offsets):
    steps = 4
    wide, slim = 2 * D // steps, D // steps

    def kernel(s, dkv, dq, kw, qw, comp, mem, tok, vec, dres, dtok, dg, db, acc, nat, xh, rs):
        j = pl.program_id(0)

        def product(start):
            value = dot_t(dkv[0], kw[...])
            if start:
                acc[...] = value
            else:
                acc[...] += value
            acc[2 * T :, :] += dot_t(dq[...], qw[...])

        for block, ref in enumerate((comp, mem, tok)):

            @pl.when(j == block)
            def _(block=block, ref=ref):
                product(block == 0)
                for i in range(0, T, 32):
                    xhat, r = center_scale(ref[i : i + 32, :].astype(f32))
                    xh[block * T + i : block * T + i + 32, :] = xhat
                    if block == 2:
                        rs[i : i + 32, :] = jnp.broadcast_to(r, (32, HD))

        @pl.when(j == steps - 1)
        def _():
            product(False)
            natural_columns(nat, acc, s, THIRDS)
            gain = row(vec, LN1_G)
            sum_g = jnp.zeros((8, D), f32)
            sum_b = jnp.zeros((8, D), f32)
            for i in range(0, KEYS, 32):
                dn, xhat = nat[i : i + 32, :], xh[i : i + 32, :]
                both = dn * xhat
                sum_g += (both[:8] + both[8:16]) + (both[16:24] + both[24:])
                sum_b += (dn[:8] + dn[8:16]) + (dn[16:24] + dn[24:])
                if i >= 2 * T:
                    k = i - 2 * T
                    r = rs[k : k + 32, :1]
                    dtok[k : k + 32, :] = dres[k : k + 32, :] + norm_back(xhat, r, gain, dn)
            dg[...] = jnp.sum(sum_g, axis=0, keepdims=True)
            db[...] = jnp.sum(sum_b, axis=0, keepdims=True)

    rest = (compressed, memory, tokens, vectors, d_res)
    out = (shape((T, D), f32), shape((1, D), f32), shape((1, D), f32))
    return call(
        kernel,
        out,
        (steps,),
        [
            pl.BlockSpec((1, KEYS, wide), lambda j, s: (j // (steps // 2), 0, lax.rem(j, steps // 2))),
            pl.BlockSpec((T, slim), lambda j, s: (0, j)),
            pl.BlockSpec((D, wide), lambda j, s: (0, j)),
            pl.BlockSpec((D, slim), lambda j, s: (0, j)),
        ]
        + [whole(a) for a in rest],
        [whole(o) for o in out],
        offsets,
        (d_kv, d_q, w_kv, w_q, *rest),
        [pltpu.VMEM((KEYS, D), f32)] * 3 + [pltpu.VMEM((T, HD), f32)],
    )


def compress(oldest, pieces, vectors, offsets):
    block = 256
    rows = T // 3

    def kernel(s, x, w0, w1, w2, vec, compact, normed, x_rel, natural):
        j = pl.program_id(0)

        @pl.when(j == 0)
        def _():
            x_rel[...] = relative_columns(x, s, (3 * D // 2, 3 * D // 4, 3 * D // 4))

        w = jnp.concatenate([w0[...], w1[...], w2[...]], axis=0)
        here = pl.ds(at(j * block), block)
        compact[:, here] = dot(x_rel[...], w) + vec[CONV_B : CONV_B + 1, here]

        @pl.when(j == D // block - 1)
        def _():
            xhat, r = center_scale(compact[...])
            natural[...] = (xhat * row(vec, LN1_G) + row(vec, LN1_B)).astype(bf16)
            start = 0
            for i, width in enumerate(THIRDS):
                normed[:, start : start + width] = natural[:, pl.ds(at(s[3 + i]), width)]
                start += width

    out = (shape((rows, D), f32), shape((rows, D), bf16))
    return call(
        kernel,
        out,
        (D // block,),
        [whole(oldest)]
        + [pl.BlockSpec((w.shape[0], block), lambda j, s: (0, j)) for w in pieces]
        + [whole(vectors)],
        [whole(o) for o in out],
        offsets,
        (oldest, *pieces, vectors),
        [pltpu.VMEM((rows, 3 * D), bf16), pltpu.VMEM((rows, D), bf16)],
    )


def reconstruct(queries, key_value, comp_pair, none):
    rows = T // 3
    n = 4

    def kernel(_, q, k, v, ck, cv, loss, dck, dcv):
        cuts = columns_of(n)
        asking = [(q[:, c] * FACTOR).astype(bf16) for c in cuts]
        far = [dot_t(x, k[:, c]) for x, c in zip(asking, cuts)]
        near = [dot_t(x, ck[:, c]) for x, c in zip(asking, cuts)]
        p = [softmax(x).astype(bf16) for x in far]
        gp = [softmax(x) for x in near]
        low = [x.astype(bf16) for x in gp]
        miss = [dot(p[h], v[:, c]) - dot(low[h], cv[:, c]) for h, c in enumerate(cuts)]
        total = sum(jnp.sum(x * x, axis=0, keepdims=True) for x in miss)
        d_guess = [((-2.0 / (T * D)) * x).astype(bf16) for x in miss]
        d_gp = [dot_t(x, cv[:, c]) for x, c in zip(d_guess, cuts)]
        d_gs = [
            (x * (y - jnp.sum(x * y, axis=-1, keepdims=True))).astype(bf16)
            for x, y in zip(gp, d_gp)
        ]
        for h, c in enumerate(cuts):
            dcv[:, c] = t_dot(low[h], d_guess[h]).astype(bf16)
            dck[:, c] = t_dot(d_gs[h], asking[h]).astype(bf16)

        @pl.when(pl.program_id(0) == 0)
        def _():
            loss[...] = total

        @pl.when(pl.program_id(0) > 0)
        def _():
            loss[...] += total

    return call(
        kernel,
        (shape((1, HD), f32), shape((rows, D), bf16), shape((rows, D), bf16)),
        (H // n,),
        [head(n, T), head(n, T, 1), head(n, T, 1, H), head(n, rows), head(n, rows, 0, H)],
        [pl.BlockSpec((1, HD), lambda h, s: (0, 0)), head(n, rows), head(n, rows)],
        none,
        (queries, key_value, key_value, comp_pair, comp_pair),
    )


def compress_back(dck, dcv, w_kv, compact, vectors, offsets):
    rows = T // 3

    def kernel(s, dck, dcv, w, compact, vec, d_compact, d_bias, dn):
        back = dot_t(jnp.concatenate([dck[...], dcv[...]], axis=1), w[...])
        natural_columns(dn, back, s, THIRDS)
        xhat, r = center_scale(compact[...])
        low = norm_back(xhat, r, row(vec, LN1_G), dn[...]).astype(bf16)
        d_compact[...] = low
        d_bias[...] = jnp.sum(low.astype(f32), axis=0, keepdims=True)

    args = (dck, dcv, w_kv, compact, vectors)
    out = (shape((rows, D), bf16), shape((1, D), f32))
    return call(
        kernel,
        out,
        (1,),
        [whole(a) for a in args],
        [whole(o) for o in out],
        offsets,
        args,
        [pltpu.VMEM((rows, D), f32)],
    )


def weight_grads(groups, scalars):
    in_specs, args, outs, out_specs, layout, scratch = [], [], [], [], [], []
    for ring, jobs in groups:
        first = 1 if ring == "x" else 5
        block = jobs[0][0][0].shape[1] // 8
        plan = []
        for xs, row_block, rows, dys, ready in jobs:
            width = dys[0].shape[1] // (1 if ready else 2)
            plan.append((width, rows, len(xs)))
            for x in xs:
                for y in range(2):
                    in_specs.append(
                        pl.BlockSpec(
                            (rows, block),
                            lambda q, s, r=row_block, f=first, y=y: (r, y * 4 + s[f + q]),
                        )
                    )
                    args.append(x)
            for dy in dys:
                in_specs.append(
                    pl.BlockSpec((rows, width), lambda q, s, r=ready: (0, 0 if r else s[0]))
                )
                args.append(dy)
            scratch.append(pltpu.VMEM((rows * len(xs), width), bf16))
        dims = (1, 2, block, sum(p[0] for p in plan))
        outs += [shape((2, *dims[1:]), bf16)] * 2
        out_specs += [
            pl.BlockSpec(dims, lambda q, s: (jnp.minimum(q, 1), 0, 0, 0)),
            pl.BlockSpec(dims, lambda q, s: (jnp.maximum(q - 2, 0), 0, 0, 0)),
        ]
        layout.append(plan)
    n_in, n_out = len(in_specs), len(outs)

    def kernel(s, *refs):
        ins, results, joined = refs[:n_in], refs[n_in : n_in + n_out], refs[n_in + n_out :]
        q = pl.program_id(0)

        @pl.when(q == 0)
        def _():
            place, k = 0, 0
            for plan in layout:
                for _, rows, n in plan:
                    da, db = ins[place + 2 * n], ins[place + 2 * n + 1]
                    if n == 2:
                        joined[k][:rows, :] = da[...]
                        joined[k][rows:, :] = db[...]
                    else:
                        joined[k][...] = (da[...].astype(f32) + db[...].astype(f32)).astype(bf16)
                    place += 2 * n + 2
                    k += 1

        place, k = 0, 0
        for i, plan in enumerate(layout):
            send, keep = results[2 * i : 2 * i + 2]
            block = send.shape[2]
            start = 0
            for width, rows, n in plan:
                x = jnp.concatenate([r[...] for r in ins[place : place + 2]], axis=1)
                if n == 2:
                    other = jnp.concatenate([r[...] for r in ins[place + 2 : place + 4]], axis=1)
                    x = jnp.concatenate([x, other], axis=0)
                value = t_dot(x, joined[k][...]).astype(bf16).reshape(2, block, width)
                cut = slice(start, start + width)
                send[0, :, :, cut] = jnp.where(q < 2, value, send[0, :, :, cut])
                keep[0, :, :, cut] = value
                start += width
                place += 2 * n + 2
                k += 1

    flat = call(kernel, tuple(outs), (4,), in_specs, out_specs, scalars, args, scratch)
    return [(flat[2 * i], flat[2 * i + 1]) for i in range(len(groups))]


def widen(gathered, start, rows, columns, swapped, none):
    u = rows // 16
    sub = u // 32
    chunks = columns // 2 // STEP
    order = [x * 4 + z for z in range(4) for x in range(4)] if swapped else list(range(16))

    def kernel(_, *refs):
        out = refs[-1]
        for k, src in enumerate(refs[:-1]):
            for to, frm in enumerate(order):
                out[to, :, k * STEP : (k + 1) * STEP] = src[frm].astype(f32)

    return call(
        kernel,
        shape((16, u, columns), f32),
        (sub, 2),
        [
            pl.BlockSpec((16, 32, STEP), lambda i, c, s, k=k: (c, start // 32 + k * sub + i, 0))
            for k in range(chunks)
        ],
        pl.BlockSpec((16, 32, STEP * chunks), lambda i, c, s: (0, i, c)),
        none,
        (gathered,) * chunks,
    ).reshape(rows, columns)


def core_swap(v):
    return lax.ppermute(v, "c", [(0, 1), (1, 0)])


def pair_swap(v):
    return lax.ppermute(v, "yl", [(0, 1), (1, 0)])


def exchange(v, ring, masks):
    def flat(i, c):
        return (i // 2 * 2 + c) * 2 + i % 2 if ring == "y" else 2 * i + c

    pairs = [(flat(i, c), flat(i ^ masks[c], c)) for i in range(4) for c in range(2)]
    return lax.ppermute(v, RING[ring], pairs)


def pick(v, index, axis):
    return lax.dynamic_index_in_dim(v, index, axis, keepdims=False)


def quarters(place, core):
    first = jnp.where(core == 0, 1, 3)
    second = jnp.where(core == 0, 3, 1)
    return place, place ^ first, place ^ 2, place ^ second


class Flow:
    def __init__(self, ring, pair):
        self.ring, self.other = ring, "z" if ring == "x" else "x"
        send, self.keep = pair
        self.got = exchange(send, ring, (1, 3))
        self.before = None

    def kept(self, which):
        if self.before is None:
            dims = (1, *self.keep.shape[1:])
            return [pl.BlockSpec(dims, lambda j, s: (which, 0, 0, 0))], [self.keep]
        return self.before(2 + which)


def onward(flows, cuts):
    in_specs, args, counts = [], [], []
    for f in flows:
        specs, arrays = f.kept(1)
        dims = (1, *f.got.shape[1:])
        in_specs += specs + [pl.BlockSpec(dims, lambda j, s: (1, 0, 0, 0))]
        args += arrays + [f.got]
        counts.append(len(arrays) + 1)
    out = tuple(shape(f.got.shape[1:], bf16) for f in flows)

    def kernel(_, *refs):
        k = 0
        for i, n in enumerate(counts):
            total = sum(value_of(r) for r in refs[k : k + n])
            refs[len(args) + i][...] = total.astype(bf16)
            k += n

    sums = call(kernel, out, (1,), in_specs, [whole(o) for o in out], cuts, args)
    for f, v in zip(flows, sums):
        f.last = exchange(v, f.ring, (3, 1))


def value_of(ref):
    return (ref[0] if len(ref.shape) == 4 else ref[...]).astype(f32)


def turn(flows, cuts):
    in_specs, outs, out_specs, args = [], [], [], []

    def parts(f, index):
        first = 1 if f.other == "x" else 5
        rows, columns = f.keep.shape[2] // 4, f.keep.shape[3]
        arrays = [f.keep, f.got, f.last]

        def spec(pick):
            four = pl.BlockSpec((1, 2, rows, columns), lambda j, s: (0, 0, s[first + pick(j)], 0))
            three = pl.BlockSpec((2, rows, columns), lambda j, s: (0, s[first + pick(j)], 0))
            return [four, four, three]

        return spec(index), arrays

    for f in flows:
        specs, arrays = parts(f, lambda j: j)
        in_specs += specs
        args += arrays
        dims = (1, 2, f.keep.shape[2] // 4, f.keep.shape[3])
        outs.append(shape((2, *dims[1:]), bf16))
        out_specs.append(pl.BlockSpec(dims, lambda j, s: (j, 0, 0, 0)))

    def kernel(_, *refs):
        for i in range(len(flows)):
            total = sum(value_of(r) for r in refs[3 * i : 3 * i + 3])
            refs[len(args) + i][0] = total.astype(bf16)

    sends = call(kernel, tuple(outs), (2,), in_specs, out_specs, cuts, args)
    for f, send in zip(flows, sends):
        whole_parts = parts(f, lambda j: 2)[1]
        f.before = lambda which, f=f, arrays=whole_parts, made=[
            parts(f, lambda j: 2)[0],
            parts(f, lambda j: 3)[0],
        ]: (made[which - 2], arrays)
        f.ring = f.other
        f.got = exchange(send, f.ring, (1, 3))


def add(a, b, none):
    def kernel(_, a, b, out):
        out[...] = (a[...].astype(f32) + b[...].astype(f32)).astype(bf16)

    out = shape(a.shape, bf16)
    return call(kernel, out, (1,), [whole(a), whole(b)], whole(out), none, (a, b))


class Finish:
    def __init__(self, flows, extra, cuts):
        in_specs, args, sizes = [], [], []
        for f in flows:
            specs, arrays = f.kept(0)
            dims = (1, *f.got.shape[1:])
            in_specs += specs + [pl.BlockSpec(dims, lambda j, s: (0, 0, 0, 0)), whole(f.last)]
            args += arrays + [f.got, f.last]
            sizes.append((len(arrays) + 2, f.got.shape[2], f.got.shape[3] // STEP))
        in_specs += [whole(e) for e in extra]
        args += extra
        rows = sum(u * n for _, u, n in sizes) + sum(e.shape[1] for e in extra)

        def kernel(s, *refs):
            send, mine = refs[-2:]
            zero = s[9] == 0
            start, k = 0, 0
            for count, u, n in sizes:
                v = sum(value_of(r) for r in refs[k : k + count])
                near = jnp.where(zero, v[0], v[1])
                away = jnp.where(zero, v[1], v[0]).astype(bf16)
                for i in range(n):
                    cut = slice(i * STEP, (i + 1) * STEP)
                    mine[start : start + u, :] = near[:, cut]
                    send[start : start + u, :] = away[:, cut]
                    start += u
                k += count
            for ref in refs[k:-2]:
                u = ref.shape[1]
                mine[start : start + u, :] = jnp.where(zero, ref[0], ref[1])
                send[start : start + u, :] = jnp.where(zero, ref[1], ref[0]).astype(bf16)
                start += u

        out = (shape((rows, STEP), bf16), shape((rows, STEP), f32))
        send, self.mine = call(
            kernel, out, (1,), in_specs, [whole(o) for o in out], cuts, args
        )
        self.got = exchange(send, "y", (1, 3))

    def second(self, none):
        self.mine = add(self.mine, self.got, none)
        self.far = lax.ppermute(self.mine, "yh", [(0, 1), (1, 0)])

    def gather(self, none):
        return lax.all_gather(add(self.mine, self.far, none), ("c", "x", "z"), axis=0)


def per_device(
    tokens,
    memory,
    compressed,
    cotangent,
    ln1_g,
    ln1_b,
    w_q,
    w_kv,
    w_r,
    bias_u,
    bias_v,
    w_o,
    ln2_g,
    ln2_b,
    w_in,
    b_in,
    w_out,
    b_out,
    conv_w,
    conv_b,
):
    line.held, line.due = [], {}
    tokens, memory, compressed, cotangent = tokens[0], memory[0], compressed[0], cotangent[0]
    yl, core = lax.axis_index("yl"), lax.axis_index("c")
    place = {"x": lax.axis_index("x"), "z": lax.axis_index("z")}
    none = jnp.zeros((1,), jnp.int32)
    ints = lambda *v: jnp.stack([jnp.asarray(i, jnp.int32) for i in v])

    def thirds(rows):
        half = rows // 2
        other = (1 - yl) * half
        return [yl * half, other + core * (half // 2), other + (1 - core) * (half // 2)]

    def both(v):
        return (v, core_swap(v))

    spot = (place["x"] * 4 + place["z"]) * 2 + core
    piece = pack(
        (ln1_g, ln1_b, bias_u, bias_v, ln2_g, ln2_b, b_out, conv_b, b_in),
        w_in,
        w_out,
        ints(spot),
    )
    piece_got = exchange(piece, "y", (1, 3))

    kv_part, small, conv_part = pack_rows(w_kv, w_q, w_r, w_o, conv_w, ints(core))
    kv_got = exchange(kv_part, "y", (1, 3))
    small_got = exchange(small, "y", (1, 3))
    conv_got = exchange(conv_part, "y", (1, 3))

    def joined(w, got, twin):
        return jnp.concatenate([w, got, twin], axis=0)

    spread = lax.all_gather(piece_got[:-16], ("x", "z", "c"), axis=0)
    thirds_d = ints(*thirds(D))
    thirds_c = ints(*thirds(3 * D), *thirds(D))
    sinus_table = sinusoid(KEYS, D).astype(bf16)
    sinus_rel = jnp.concatenate(
        [
            lax.dynamic_slice_in_dim(sinus_table, thirds_d[i], width, 1)
            for i, width in enumerate(THIRDS)
        ],
        axis=1,
    )
    line.hold(sinus_rel)
    vectors, b_in = unpack(piece, piece_got, ints(yl))

    normed, normed_rel, oldest = first_norm(compressed, memory, tokens, vectors, thirds_d)
    both_normed, both_oldest, both_cot = both(normed), both(oldest), both(cotangent)
    kv_got, small_got = gate((kv_got, small_got), normed)
    kv_whole = joined(w_kv, kv_got, core_swap(kv_got))
    key_value = dot(normed_rel, kv_whole).astype(bf16)
    line.hold(key_value)
    small_twin = core_swap(small_got)
    q_whole, r_whole, o_whole = [
        joined(w, small_got[i], small_twin[i]) for i, w in enumerate((w_q, w_r, w_o))
    ]
    queries = dot(normed_rel[2 * T :], q_whole)
    relative = dot(sinus_rel, r_whole).astype(bf16)
    line.hold(queries, relative)
    probs, attended = attend(queries, key_value, relative, vectors, none)
    residual, normed2, normed2_rel = out_and_norm(attended, o_whole, tokens, vectors, thirds_d)
    both_n2, both_att = both(normed2), both(attended)

    cuts, rels, twins = [], [], []
    for ring in ("x", "z"):
        own, first, far, second = quarters(place[ring], core)
        cuts += [first, far, own, second]
        rels.append([own, first, second, far])
        twins.append([own, second, first, far])
    cuts = ints(core, *cuts, yl)

    def flows(groups):
        pairs = weight_grads(groups, cuts)
        return [Flow(ring, pair) for (ring, _), pair in zip(groups, pairs)]

    hidden, d_pre, mixed_out, d_normed2, d_b_in = feed_forward(
        normed2_rel, residual, cotangent, w_in, w_out, spread, b_in, vectors, ints(yl)
    )
    both_hidden, both_pre = both(hidden), both(d_pre)
    (conv_got,) = gate((conv_got,), hidden)
    conv_pieces = (conv_w, conv_got, core_swap(conv_got))
    d_residual, d_branch, d_attended, d_ln2_g, d_ln2_b, d_b_out = second_norm_back(
        cotangent, d_normed2, residual, vectors, o_whole, thirds_d
    )
    both_branch = both(d_branch)
    large = flows(
        [
            ("x", [(both_hidden, 0, T, both_cot, False)]),
            ("z", [(both_n2, 0, T, both_pre, False), (both_att, 0, T, both_branch, False)]),
        ]
    )
    d_kv, my_kv, give_kv, d_relative, d_queries, d_bias_u, d_bias_v = attend_back(
        queries, key_value, relative, vectors, probs, d_attended, ints(core)
    )
    both_kv = (my_kv, core_swap(give_kv))
    both_q, both_rel = both(d_queries), both(d_relative)

    compact, comp_normed = compress(oldest, conv_pieces, vectors, thirds_c)
    comp_pair = dot(comp_normed, kv_whole).astype(bf16)
    compressed_next = jnp.concatenate([compressed[T // 3 :], compact], axis=0)
    near = flows(
        [
            ("x", [(both_normed, 0, KEYS, both_kv, True)]),
            (
                "z",
                [
                    (both_normed, 2, T, both_q, False),
                    ((sinus_table,), 0, KEYS, both_rel, False),
                ],
            ),
        ]
    )
    loss, d_ck, d_cv = reconstruct(queries, key_value, comp_pair, none)
    recon_loss = jnp.sum(loss) / (T * D)
    onward(large, cuts)
    d_compact, d_conv_b = compress_back(d_ck, d_cv, kv_whole, compact, vectors, thirds_d)
    both_compact = both(d_compact)
    onward(near, cuts)
    conv = flows([("x", [(both_oldest, 0, T // 3, both_compact, False)])])
    turn(large, cuts)
    d_tokens, d_ln1_g, d_ln1_b = first_norm_back(
        d_kv, d_queries, kv_whole, q_whole, compressed, memory, tokens, vectors, d_residual,
        thirds_d,
    )
    turn(near, cuts)
    line.expect(1, *[f.got for f in near])
    onward(large, cuts)
    onward(conv, cuts)
    onward(near, cuts)
    early = Finish(large, [], cuts)
    turn(conv, cuts)
    early.second(none)
    onward(conv, cuts)
    early_sums = early.gather(none)
    total = jnp.concatenate(
        [d_ln1_g, d_ln1_b, d_bias_u, d_bias_v, d_ln2_g, d_ln2_b, d_b_out, d_conv_b]
        + [d_b_in]
    )
    total = jnp.concatenate(
        [
            total[:8].reshape(8, 2, STEP).transpose(1, 0, 2),
            total[8:].reshape(2, 4, STEP),
            jnp.zeros((2, 4, STEP), f32),
        ],
        axis=1,
    )
    late = Finish([*near, *conv], [total], cuts)
    late.second(none)
    late_sums = late.gather(none)

    g_in = widen(early_sums, 128, D // 2, FF, True, none)
    g_out = widen(early_sums, 0, FF // 2, D, False, none)
    g_o = widen(early_sums, 256, D // 2, D, True, none)
    g_conv = widen(late_sums, 128, 3 * D // 2, D, False, none)
    g_kv = widen(late_sums, 0, D // 2, 2 * D, False, none)
    g_q = widen(late_sums, 64, D // 2, D, True, none)
    g_r = widen(late_sums, 96, D // 2, D, True, none)
    half = jnp.sum(late_sums[:, 224:236].astype(f32), axis=0)
    t_ln1_g, t_ln1_b, t_bu, t_bv, t_ln2_g, t_ln2_b, t_bout, t_convb = [half[i] for i in range(8)]
    t_bin = half[8:].reshape(-1)
    return (
        mixed_out[None],
        compressed_next[None],
        recon_loss[None],
        d_tokens[None],
        t_ln1_g,
        t_ln1_b,
        g_q,
        g_kv,
        g_r,
        t_bu,
        t_bv,
        g_o,
        t_ln2_g,
        t_ln2_b,
        g_in,
        t_bin,
        g_out,
        t_bout,
        g_conv,
        t_convb,
    )


def solution(mesh):
    fine = Mesh(mesh.devices.reshape(2, 4, 4, 2, 2), AXES)
    stream = P(AXES, None, None)
    vec, mat = P("yl"), P("yl", None)
    weights = (vec, vec, mat, mat, mat, vec, vec, mat, vec, vec, mat, vec, mat, vec, mat, vec)
    return jax.shard_map(
        per_device,
        mesh=fine,
        in_specs=(stream,) * 4 + weights,
        out_specs=(stream, stream, P(AXES), stream) + weights,
        check_vma=False,
    )
```

```python
import jax
import jax.numpy as jnp
from jax import lax
from jax.experimental import pallas as pl
from jax.experimental.pallas import tpu as pltpu
from jax.sharding import Mesh, PartitionSpec as P

H = 8
HD = 128
D = 1024
T = 192
KEYS = 576
PAD = 640
FF = 4096
FACTOR = HD ** (-0.5)
f32 = jnp.float32
bf16 = jnp.bfloat16
AXES = ("yh", "x", "z", "c", "yl")
RING = {"x": ("x", "c"), "z": ("z", "c"), "y": ("yh", "c", "yl")}


def sinusoid(key_count, model_dim):
    distance = (key_count - 1 - jnp.arange(key_count)).astype(f32)
    inverse = 1.0 / 10000.0 ** (jnp.arange(0, model_dim, 2).astype(f32) / model_dim)
    angles = distance[:, None] * inverse[None, :]
    return jnp.concatenate([jnp.sin(angles), jnp.cos(angles)], axis=-1)


def dot(a, b):
    return jnp.dot(a, b, preferred_element_type=f32)


def dot_t(a, b):
    return lax.dot_general(a, b, (((1,), (1,)), ((), ())), preferred_element_type=f32)


def t_dot(a, b):
    return lax.dot_general(a, b, (((0,), (0,)), ((), ())), preferred_element_type=f32)


class Line:
    def __init__(self):
        self.held, self.due = [], {}

    def hold(self, *values):
        self.held += values

    def expect(self, gap, *values):
        self.due.setdefault(gap, []).extend(values)

    def ran(self, result):
        self.held = [result, *self.due.get(1, [])]
        self.due = {gap - 1: values for gap, values in self.due.items() if gap > 1}

    def later(self, value):
        return lax.optimization_barrier((value, *self.held))[0] if self.held else value


line = Line()


def call(kernel, out, grid, in_specs, out_specs, scalars, args, scratch=()):
    held, n = line.held, len(args)

    def body(s, *refs):
        kernel(s, *refs[:n], *refs[n + len(held) :])

    result = pl.pallas_call(
        body,
        out_shape=out,
        grid_spec=pltpu.PrefetchScalarGridSpec(
            num_scalar_prefetch=1,
            grid=grid,
            in_specs=list(in_specs) + [pl.BlockSpec(memory_space=pl.ANY)] * len(held),
            out_specs=out_specs,
            scratch_shapes=list(scratch),
        ),
        compiler_params=pltpu.CompilerParams(vmem_limit_bytes=56 << 20),
    )(scalars, *args, *held)
    line.ran(jax.tree.leaves(result)[0])
    return result


def gate(values, *after):
    n = len(values)
    anywhere = pl.BlockSpec(memory_space=pl.ANY)
    return pl.pallas_call(
        lambda *refs: None,
        out_shape=[jax.ShapeDtypeStruct(v.shape, v.dtype) for v in values],
        in_specs=[anywhere] * (n + len(after)),
        out_specs=[anywhere] * n,
        input_output_aliases={i: i for i in range(n)},
    )(*values, *after)


def whole(a):
    zeros = (0,) * a.ndim
    return pl.BlockSpec(a.shape, lambda *_: zeros)


def shape(dims, dtype):
    return jax.ShapeDtypeStruct(dims, dtype)


def at(offset):
    return pl.multiple_of(offset, 128)


def center_scale(v):
    mid = v - jnp.mean(v, axis=-1, keepdims=True)
    r = lax.rsqrt(jnp.mean(mid * mid, axis=-1, keepdims=True) + 1e-5)
    return mid * r, r


def norm_back(xhat, r, g, dn):
    gd = dn * g
    return r * (
        gd
        - jnp.mean(gd, axis=-1, keepdims=True)
        - xhat * jnp.mean(gd * xhat, axis=-1, keepdims=True)
    )


def softmax(s):
    e = jnp.exp(s - jnp.max(s, axis=-1, keepdims=True))
    return e / jnp.sum(e, axis=-1, keepdims=True)


(LN1_G, LN1_B, BIAS_U, BIAS_V, LN2_G, LN2_B, B_OUT, CONV_B) = range(8)


def row(ref, i):
    return ref[i : i + 1, :]


def pack(vectors, w_in, w_out, scalars):
    n_in, n_out = (w.shape[0] // 32 for w in (w_in, w_out))
    chunks = FF // D
    rows = n_out + n_in * chunks
    half = D // 2

    def kernel(_, *refs):
        wi, wo, piece, flat = refs[-4:]
        flat[...] = jnp.zeros_like(flat)
        for i, ref in enumerate(refs[:8]):
            flat[i : i + 1, :half] = ref[...].astype(f32).reshape(1, half)
        flat[8 : 8 + FF // 2 // D, :] = refs[8][...].astype(f32).reshape(FF // 2 // D, D)
        piece[:n_out, :] = wo[...]
        for i in range(chunks):
            piece[n_out + i * n_in : n_out + (i + 1) * n_in, :] = wi[:, i * D : (i + 1) * D]
        piece[rows:, :] = flat[...].astype(bf16)

    out = shape((rows + 16, D), bf16)
    return call(
        kernel,
        out,
        (1,),
        [whole(v) for v in vectors]
        + [
            pl.BlockSpec((w.shape[0] // 32, w.shape[1]), lambda j, s: (s[0], 0))
            for w in (w_in, w_out)
        ],
        whole(out),
        scalars,
        (*vectors, w_in, w_out),
        [pltpu.VMEM((16, D), f32)],
    )


def pack_rows(w_kv, w_q, w_r, w_o, conv_w, scalars):
    n, n_conv = w_q.shape[0] // 2, conv_w.shape[0] // 2

    def kernel(_, kv, q, r, o, conv, kv_out, out, conv_out):
        kv_out[...] = kv[...]
        for i, ref in enumerate((q, r, o)):
            out[i] = ref[...]
        conv_out[...] = conv[...]

    args = (w_kv, w_q, w_r, w_o, conv_w)
    out = (shape((n, 2 * D), bf16), shape((3, n, D), bf16), shape((n_conv, D), bf16))
    return call(
        kernel,
        out,
        (1,),
        [pl.BlockSpec((w.shape[0] // 2, w.shape[1]), lambda j, s: (s[0], 0)) for w in args],
        [whole(o) for o in out],
        scalars,
        args,
    )


def unpack(mine, theirs, scalars):
    half = D // 2
    at_row = mine.shape[0] // 16 - 1
    tail = pl.BlockSpec((16, D), lambda j, s: (at_row, 0))

    def kernel(s, mine, theirs, vectors, b_in):
        a, b = mine[...].astype(f32), theirs[...].astype(f32)
        low = jnp.where(s[0] == 0, a, b)
        high = jnp.where(s[0] == 0, b, a)
        vectors[:, :half] = low[:8, :half]
        vectors[:, half:] = high[:8, :half]
        rows = FF // 2 // D
        b_in[:rows] = low[8 : 8 + rows]
        b_in[rows:] = high[8 : 8 + rows]

    out = (shape((8, D), f32), shape((FF // D, D), f32))
    return call(
        kernel, out, (1,), [tail, tail], [whole(o) for o in out], scalars, (mine, theirs)
    )


def relative_columns(x, s, widths):
    parts = [x[:, pl.ds(at(s[i]), width)] for i, width in enumerate(widths)]
    return jnp.concatenate(parts, axis=1)


def natural_columns(out, x, s, widths):
    start = 0
    for i, width in enumerate(widths):
        out[:, pl.ds(at(s[i]), width)] = x[:, start : start + width]
        start += width


THIRDS = (D // 2, D // 4, D // 4)


def first_norm(compressed, memory, tokens, vectors, offsets):
    def kernel(s, comp, mem, tok, vec, out, out_rel, old):
        gain, bias = row(vec, LN1_G), row(vec, LN1_B)

        def part(ref, base):
            for i in range(0, T, 32):
                xhat, r = center_scale(ref[i : i + 32, :].astype(f32))
                out[base + i : base + i + 32, :] = (xhat * gain + bias).astype(bf16)

        part(comp, 0)
        part(mem, T)
        part(tok, 2 * T)
        out_rel[...] = relative_columns(out, s, THIRDS)
        line_of = lax.broadcasted_iota(jnp.int32, (T // 3, T), 0)
        col = lax.broadcasted_iota(jnp.int32, (T // 3, T), 1)
        low = mem[...].astype(bf16)
        for tap in range(3):
            take = jnp.where(col == 3 * line_of + tap, 1.0, 0.0).astype(bf16)
            old[:, tap * D : (tap + 1) * D] = dot(take, low).astype(bf16)

    args = (compressed, memory, tokens, vectors)
    out = (shape((KEYS, D), bf16), shape((KEYS, D), bf16), shape((T // 3, 3 * D), bf16))
    return call(
        kernel, out, (1,), [whole(a) for a in args], [whole(o) for o in out], offsets, args
    )


def head(n, rows, row_block=0, first=0):
    return pl.BlockSpec((rows, n * HD), lambda h, s: (row_block, first // n + h))


def columns_of(n):
    return [slice(i * HD, (i + 1) * HD) for i in range(n)]


def attend(queries, key_value, relative, vectors, none):
    n = 2

    def kernel(_, q, k, v, rel, vec, probs, out):
        pad = jnp.zeros((PAD - KEYS, HD), bf16)
        i = lax.broadcasted_iota(jnp.int32, (T, PAD), 0)
        j = lax.broadcasted_iota(jnp.int32, (T, PAD), 1)
        seen = j <= i + (KEYS - T)
        cuts = columns_of(n)
        content = [((q[:, c] + vec[BIAS_U : BIAS_U + 1, c]) * FACTOR).astype(bf16) for c in cuts]
        located = [((q[:, c] + vec[BIAS_V : BIAS_V + 1, c]) * FACTOR).astype(bf16) for c in cuts]
        raw = [
            dot_t(x, jnp.concatenate([rel[:, c], pad], axis=0)) for x, c in zip(located, cuts)
        ]
        near = [dot_t(x, jnp.concatenate([k[:, c], pad], axis=0)) for x, c in zip(content, cuts)]
        raw = [pltpu.roll(x, PAD - T + 1, 1, stride=1, stride_axis=0) for x in raw]
        p = [softmax(jnp.where(seen, a + b, -1e30)) for a, b in zip(near, raw)]
        for h, c in enumerate(cuts):
            probs[h] = p[h]
            value = jnp.concatenate([v[:, c], pad], axis=0)
            out[:, c] = dot(p[h].astype(bf16), value).astype(bf16)

    return call(
        kernel,
        (shape((H, T, PAD), f32), shape((T, D), bf16)),
        (H // n,),
        [head(n, T), head(n, KEYS), head(n, KEYS, 0, H), head(n, KEYS), head(n, 8)],
        [pl.BlockSpec((n, T, PAD), lambda h, s: (h, 0, 0)), head(n, T)],
        none,
        (queries, key_value, key_value, relative, vectors),
    )


def attend_back(queries, key_value, relative, vectors, probs, d_attended, scalars):
    n = 2

    def kernel(s, q, k, v, rel, vec, probs, d_att, d_kv, mine, give, d_rel, d_q, d_bu, d_bv):
        pad = jnp.zeros((PAD - KEYS, HD), bf16)
        i = lax.broadcasted_iota(jnp.int32, (T, T), 0)
        j = lax.broadcasted_iota(jnp.int32, (T, T), 1)
        flip = jnp.where(i + j == T - 1, 1.0, 0.0).astype(bf16)
        cuts = columns_of(n)
        content = [((q[:, c] + vec[BIAS_U : BIAS_U + 1, c]) * FACTOR).astype(bf16) for c in cuts]
        located = [((q[:, c] + vec[BIAS_V : BIAS_V + 1, c]) * FACTOR).astype(bf16) for c in cuts]
        da = [d_att[:, c] for c in cuts]
        d_p = [dot_t(x, jnp.concatenate([v[:, c], pad], axis=0)) for x, c in zip(da, cuts)]
        d_v = [t_dot(probs[h].astype(bf16), x)[:KEYS].astype(bf16) for h, x in enumerate(da)]
        d_s = []
        for h, x in enumerate(d_p):
            p = probs[h]
            d_s.append((p * (x - jnp.sum(p * x, axis=-1, keepdims=True))).astype(bf16))
        d_raw = [dot(flip, x) for x in d_s]
        d_c = [
            dot(x, jnp.concatenate([k[:, c], pad], axis=0)) * FACTOR for x, c in zip(d_s, cuts)
        ]
        d_k = [t_dot(x, y)[:KEYS].astype(bf16) for x, y in zip(d_s, content)]
        d_raw = [pltpu.roll(x, 0, 1, stride=1, stride_axis=0).astype(bf16) for x in d_raw]
        d_raw = [dot(flip, x).astype(bf16) for x in d_raw]
        d_l = [
            dot(x, jnp.concatenate([rel[:, c], pad], axis=0)) * FACTOR for x, c in zip(d_raw, cuts)
        ]
        for h, c in enumerate(cuts):
            d_rel[:, c] = t_dot(d_raw[h], located[h])[:KEYS].astype(bf16)
            d_kv[0, :, c] = d_k[h]
            d_kv[1, :, c] = d_v[h]
            mine[:, c] = jnp.where(s[0] == 0, d_k[h], d_v[h])
            give[:, c] = jnp.where(s[0] == 0, d_v[h], d_k[h])
            d_q[:, c] = (d_c[h] + d_l[h]).astype(bf16)
            d_bu[:, c] = jnp.sum(d_c[h], axis=0, keepdims=True)
            d_bv[:, c] = jnp.sum(d_l[h], axis=0, keepdims=True)

    return call(
        kernel,
        (shape((2, KEYS, D), bf16),)
        + (shape((KEYS, D), bf16),) * 3
        + (shape((T, D), bf16), shape((1, D), f32), shape((1, D), f32)),
        (H // n,),
        [
            head(n, T),
            head(n, KEYS),
            head(n, KEYS, 0, H),
            head(n, KEYS),
            head(n, 8),
            pl.BlockSpec((n, T, PAD), lambda h, s: (h, 0, 0)),
            head(n, T),
        ],
        [
            pl.BlockSpec((2, KEYS, n * HD), lambda h, s: (0, 0, h)),
            head(n, KEYS),
            head(n, KEYS),
            head(n, KEYS),
            head(n, T),
            head(n, 1),
            head(n, 1),
        ],
        scalars,
        (queries, key_value, key_value, relative, vectors, probs, d_attended),
    )


def out_and_norm(attended, w_o, tokens, vectors, offsets):
    def kernel(s, att, w, tok, vec, res, n2, n2_rel):
        total = tok[...].astype(f32) + dot(relative_columns(att, s, THIRDS), w[...])
        res[...] = total
        xhat, r = center_scale(total)
        n2[...] = (xhat * row(vec, LN2_G) + row(vec, LN2_B)).astype(bf16)
        other = at(D // 2 - s[0])
        n2_rel[:, : D // 2] = n2[:, pl.ds(at(s[0]), D // 2)]
        n2_rel[:, D // 2 :] = n2[:, pl.ds(other, D // 2)]

    args = (attended, w_o, tokens, vectors)
    out = (shape((T, D), f32), shape((T, D), bf16), shape((T, D), bf16))
    return call(
        kernel, out, (1,), [whole(a) for a in args], [whole(o) for o in out], offsets, args
    )


STEP = 512
UNITS = 1024
HALF = FF // 2 // UNITS


def feed_forward(n2_rel, residual, cotangent, w_in, w_out, spread, b_in, vectors, scalars):
    n_in = w_in.shape[0] // 32
    n_out = w_out.shape[0] // 32
    skip = n_out // n_in
    per = UNITS // n_out
    K_NORM = 0.7978845608028654

    def natural(j, s):
        return lax.rem(j + s[0] * HALF, 2 * HALF)

    def kernel(s, n2, res, cot, wi0, wi1, wo0, wo1, bi, vec, hid, dpre, mixed, dn2, dbi, acc, back):
        j = pl.program_id(0)
        n = natural(j, s)

        @pl.when(j == 0)
        def _():
            acc[...] = jnp.zeros_like(acc)
            back[...] = jnp.zeros_like(back)

        wo = jnp.where(j < HALF, wo0[...], wo1[...].reshape(UNITS, D))
        win = jnp.concatenate([wi0[...], wi1[...].reshape(D // 2, UNITS)], axis=0)
        pre = dot(n2[...], win) + bi[pl.ds(n, 1), :]
        d_hidden = dot_t(cot[...], wo)
        square = pre * pre
        t = jnp.tanh(K_NORM * pre * (1.0 + 0.044715 * square))
        gate_ = 0.5 * (1.0 + t)
        hidden = (pre * gate_).astype(bf16)
        slope = gate_ + (0.5 * K_NORM) * pre * (1.0 - t * t) * (1.0 + (3 * 0.044715) * square)
        d_pre = (d_hidden * slope).astype(bf16)
        hid[...] = hidden
        dpre[...] = d_pre
        dbi[pl.ds(n, 1), :] = jnp.sum(d_pre.astype(f32), axis=0, keepdims=True)
        acc[...] += dot(hidden, wo)
        back[...] += dot_t(d_pre, win)

        @pl.when(j == 2 * HALF - 1)
        def _():
            mixed[...] = (res[...] + acc[...] + row(vec, B_OUT)).astype(bf16)
            dn2[:, pl.ds(at(s[0] * (D // 2)), D // 2)] = back[:, : D // 2]
            dn2[:, pl.ds(at((1 - s[0]) * (D // 2)), D // 2)] = back[:, D // 2 :]

    out = (
        shape((T, FF), bf16),
        shape((T, FF), bf16),
        shape((T, D), bf16),
        shape((T, D), f32),
        shape((2 * HALF, UNITS), f32),
    )
    by_unit = pl.BlockSpec((T, UNITS), lambda j, s: (0, natural(j, s)))
    return call(
        kernel,
        out,
        (2 * HALF,),
        [
            whole(n2_rel),
            whole(residual),
            whole(cotangent),
            pl.BlockSpec((D // 2, UNITS), lambda j, s: (0, natural(j, s))),
            pl.BlockSpec((32, n_in, UNITS), lambda j, s: (0, skip + natural(j, s), 0)),
            pl.BlockSpec((UNITS, D), lambda j, s: (jnp.minimum(j, HALF - 1), 0)),
            pl.BlockSpec(
                (per, n_out, D), lambda j, s: (jnp.maximum(j - HALF, 0), 0, 0)
            ),
            whole(b_in),
            whole(vectors),
        ],
        [by_unit, by_unit, whole(out[2]), whole(out[3]), whole(out[4])],
        scalars,
        (n2_rel, residual, cotangent, w_in, spread, w_out, spread, b_in, vectors),
        [pltpu.VMEM((T, D), f32), pltpu.VMEM((T, D), f32)],
    )


def second_norm_back(cotangent, d_n2, residual, vectors, w_o, offsets):
    def kernel(s, cot, dn, res, vec, w, d_res, d_br, d_att, dg, db, dbo):
        xhat, r = center_scale(res[...])
        dn, wide = dn[...], cot[...].astype(f32)
        dg[...] = jnp.sum(dn * xhat, axis=0, keepdims=True)
        db[...] = jnp.sum(dn, axis=0, keepdims=True)
        dbo[...] = jnp.sum(wide, axis=0, keepdims=True)
        total = wide + norm_back(xhat, r, row(vec, LN2_G), dn)
        d_res[...] = total
        low = total.astype(bf16)
        d_br[...] = low
        natural_columns(d_att, dot_t(low, w[...]).astype(bf16), s, THIRDS)

    args = (cotangent, d_n2, residual, vectors, w_o)
    out = (
        shape((T, D), f32),
        shape((T, D), bf16),
        shape((T, D), bf16),
        shape((1, D), f32),
        shape((1, D), f32),
        shape((1, D), f32),
    )
    return call(
        kernel, out, (1,), [whole(a) for a in args], [whole(o) for o in out], offsets, args
    )


def first_norm_back(d_kv, d_q, w_kv, w_q, compressed, memory, tokens, vectors, d_res, offsets):
    steps = 4
    wide, slim = 2 * D // steps, D // steps

    def kernel(s, dkv, dq, kw, qw, comp, mem, tok, vec, dres, dtok, dg, db, acc, nat, xh, rs):
        j = pl.program_id(0)

        def product(start):
            value = dot_t(dkv[0], kw[...])
            if start:
                acc[...] = value
            else:
                acc[...] += value
            acc[2 * T :, :] += dot_t(dq[...], qw[...])

        for block, ref in enumerate((comp, mem, tok)):

            @pl.when(j == block)
            def _(block=block, ref=ref):
                product(block == 0)
                for i in range(0, T, 32):
                    xhat, r = center_scale(ref[i : i + 32, :].astype(f32))
                    xh[block * T + i : block * T + i + 32, :] = xhat
                    if block == 2:
                        rs[i : i + 32, :] = jnp.broadcast_to(r, (32, HD))

        @pl.when(j == steps - 1)
        def _():
            product(False)
            natural_columns(nat, acc, s, THIRDS)
            gain = row(vec, LN1_G)
            sum_g = jnp.zeros((8, D), f32)
            sum_b = jnp.zeros((8, D), f32)
            for i in range(0, KEYS, 32):
                dn, xhat = nat[i : i + 32, :], xh[i : i + 32, :]
                both = dn * xhat
                sum_g += (both[:8] + both[8:16]) + (both[16:24] + both[24:])
                sum_b += (dn[:8] + dn[8:16]) + (dn[16:24] + dn[24:])
                if i >= 2 * T:
                    k = i - 2 * T
                    r = rs[k : k + 32, :1]
                    dtok[k : k + 32, :] = dres[k : k + 32, :] + norm_back(xhat, r, gain, dn)
            dg[...] = jnp.sum(sum_g, axis=0, keepdims=True)
            db[...] = jnp.sum(sum_b, axis=0, keepdims=True)

    rest = (compressed, memory, tokens, vectors, d_res)
    out = (shape((T, D), f32), shape((1, D), f32), shape((1, D), f32))
    return call(
        kernel,
        out,
        (steps,),
        [
            pl.BlockSpec((1, KEYS, wide), lambda j, s: (j // (steps // 2), 0, lax.rem(j, steps // 2))),
            pl.BlockSpec((T, slim), lambda j, s: (0, j)),
            pl.BlockSpec((D, wide), lambda j, s: (0, j)),
            pl.BlockSpec((D, slim), lambda j, s: (0, j)),
        ]
        + [whole(a) for a in rest],
        [whole(o) for o in out],
        offsets,
        (d_kv, d_q, w_kv, w_q, *rest),
        [pltpu.VMEM((KEYS, D), f32)] * 3 + [pltpu.VMEM((T, HD), f32)],
    )


def compress(oldest, pieces, vectors, offsets):
    block = 256
    rows = T // 3

    def kernel(s, x, w0, w1, w2, vec, compact, normed, x_rel, natural):
        j = pl.program_id(0)

        @pl.when(j == 0)
        def _():
            x_rel[...] = relative_columns(x, s, (3 * D // 2, 3 * D // 4, 3 * D // 4))

        w = jnp.concatenate([w0[...], w1[...], w2[...]], axis=0)
        here = pl.ds(at(j * block), block)
        compact[:, here] = dot(x_rel[...], w) + vec[CONV_B : CONV_B + 1, here]

        @pl.when(j == D // block - 1)
        def _():
            xhat, r = center_scale(compact[...])
            natural[...] = (xhat * row(vec, LN1_G) + row(vec, LN1_B)).astype(bf16)
            start = 0
            for i, width in enumerate(THIRDS):
                normed[:, start : start + width] = natural[:, pl.ds(at(s[3 + i]), width)]
                start += width

    out = (shape((rows, D), f32), shape((rows, D), bf16))
    return call(
        kernel,
        out,
        (D // block,),
        [whole(oldest)]
        + [pl.BlockSpec((w.shape[0], block), lambda j, s: (0, j)) for w in pieces]
        + [whole(vectors)],
        [whole(o) for o in out],
        offsets,
        (oldest, *pieces, vectors),
        [pltpu.VMEM((rows, 3 * D), bf16), pltpu.VMEM((rows, D), bf16)],
    )


def reconstruct(queries, key_value, comp_pair, none):
    rows = T // 3
    n = 4

    def kernel(_, q, k, v, ck, cv, loss, dck, dcv):
        cuts = columns_of(n)
        asking = [(q[:, c] * FACTOR).astype(bf16) for c in cuts]
        far = [dot_t(x, k[:, c]) for x, c in zip(asking, cuts)]
        near = [dot_t(x, ck[:, c]) for x, c in zip(asking, cuts)]
        p = [softmax(x).astype(bf16) for x in far]
        gp = [softmax(x) for x in near]
        low = [x.astype(bf16) for x in gp]
        miss = [dot(p[h], v[:, c]) - dot(low[h], cv[:, c]) for h, c in enumerate(cuts)]
        total = sum(jnp.sum(x * x, axis=0, keepdims=True) for x in miss)
        d_guess = [((-2.0 / (T * D)) * x).astype(bf16) for x in miss]
        d_gp = [dot_t(x, cv[:, c]) for x, c in zip(d_guess, cuts)]
        d_gs = [
            (x * (y - jnp.sum(x * y, axis=-1, keepdims=True))).astype(bf16)
            for x, y in zip(gp, d_gp)
        ]
        for h, c in enumerate(cuts):
            dcv[:, c] = t_dot(low[h], d_guess[h]).astype(bf16)
            dck[:, c] = t_dot(d_gs[h], asking[h]).astype(bf16)

        @pl.when(pl.program_id(0) == 0)
        def _():
            loss[...] = total

        @pl.when(pl.program_id(0) > 0)
        def _():
            loss[...] += total

    return call(
        kernel,
        (shape((1, HD), f32), shape((rows, D), bf16), shape((rows, D), bf16)),
        (H // n,),
        [head(n, T), head(n, T, 1), head(n, T, 1, H), head(n, rows), head(n, rows, 0, H)],
        [pl.BlockSpec((1, HD), lambda h, s: (0, 0)), head(n, rows), head(n, rows)],
        none,
        (queries, key_value, key_value, comp_pair, comp_pair),
    )


def compress_back(dck, dcv, w_kv, compact, vectors, offsets):
    rows = T // 3

    def kernel(s, dck, dcv, w, compact, vec, d_compact, d_bias, dn):
        back = dot_t(jnp.concatenate([dck[...], dcv[...]], axis=1), w[...])
        natural_columns(dn, back, s, THIRDS)
        xhat, r = center_scale(compact[...])
        low = norm_back(xhat, r, row(vec, LN1_G), dn[...]).astype(bf16)
        d_compact[...] = low
        d_bias[...] = jnp.sum(low.astype(f32), axis=0, keepdims=True)

    args = (dck, dcv, w_kv, compact, vectors)
    out = (shape((rows, D), bf16), shape((1, D), f32))
    return call(
        kernel,
        out,
        (1,),
        [whole(a) for a in args],
        [whole(o) for o in out],
        offsets,
        args,
        [pltpu.VMEM((rows, D), f32)],
    )


def weight_grads(groups, scalars):
    in_specs, args, outs, out_specs, layout, scratch = [], [], [], [], [], []
    for ring, jobs in groups:
        first = 1 if ring == "x" else 5
        block = jobs[0][0][0].shape[1] // 8
        plan = []
        for xs, row_block, rows, dys, ready in jobs:
            width = dys[0].shape[1] // (1 if ready else 2)
            plan.append((width, rows, len(xs)))
            for x in xs:
                for y in range(2):
                    in_specs.append(
                        pl.BlockSpec(
                            (rows, block),
                            lambda q, s, r=row_block, f=first, y=y: (r, y * 4 + s[f + q]),
                        )
                    )
                    args.append(x)
            for dy in dys:
                in_specs.append(
                    pl.BlockSpec((rows, width), lambda q, s, r=ready: (0, 0 if r else s[0]))
                )
                args.append(dy)
            scratch.append(pltpu.VMEM((rows * len(xs), width), bf16))
        dims = (1, 2, block, sum(p[0] for p in plan))
        outs += [shape((2, *dims[1:]), bf16)] * 2
        out_specs += [
            pl.BlockSpec(dims, lambda q, s: (jnp.minimum(q, 1), 0, 0, 0)),
            pl.BlockSpec(dims, lambda q, s: (jnp.maximum(q - 2, 0), 0, 0, 0)),
        ]
        layout.append(plan)
    n_in, n_out = len(in_specs), len(outs)

    def kernel(s, *refs):
        ins, results, joined = refs[:n_in], refs[n_in : n_in + n_out], refs[n_in + n_out :]
        q = pl.program_id(0)

        @pl.when(q == 0)
        def _():
            place, k = 0, 0
            for plan in layout:
                for _, rows, n in plan:
                    da, db = ins[place + 2 * n], ins[place + 2 * n + 1]
                    if n == 2:
                        joined[k][:rows, :] = da[...]
                        joined[k][rows:, :] = db[...]
                    else:
                        joined[k][...] = (da[...].astype(f32) + db[...].astype(f32)).astype(bf16)
                    place += 2 * n + 2
                    k += 1

        place, k = 0, 0
        for i, plan in enumerate(layout):
            send, keep = results[2 * i : 2 * i + 2]
            block = send.shape[2]
            start = 0
            for width, rows, n in plan:
                x = jnp.concatenate([r[...] for r in ins[place : place + 2]], axis=1)
                if n == 2:
                    other = jnp.concatenate([r[...] for r in ins[place + 2 : place + 4]], axis=1)
                    x = jnp.concatenate([x, other], axis=0)
                value = t_dot(x, joined[k][...]).astype(bf16).reshape(2, block, width)
                cut = slice(start, start + width)
                send[0, :, :, cut] = jnp.where(q < 2, value, send[0, :, :, cut])
                keep[0, :, :, cut] = value
                start += width
                place += 2 * n + 2
                k += 1

    flat = call(kernel, tuple(outs), (4,), in_specs, out_specs, scalars, args, scratch)
    return [(flat[2 * i], flat[2 * i + 1]) for i in range(len(groups))]


def widen(gathered, plan, none):
    outs, specs, layout = [], [], []
    start = 0
    for rows, columns, ring in plan:
        u, chunks = rows // 16, columns // 2 // STEP
        outs.append(shape((4, 4, u, columns), f32))
        if ring == "x":
            specs.append(
                pl.BlockSpec((1, 4, u, chunks * STEP), lambda c, x, s: (x, 0, 0, c))
            )
        else:
            specs.append(
                pl.BlockSpec((4, 1, u, chunks * STEP), lambda c, x, s: (0, x, 0, c))
            )
        layout.append((start, u, chunks, ring))
        start += u * chunks

    def kernel(_, src, *results):
        for out, (start, u, chunks, ring) in zip(results, layout):
            for k in range(chunks):
                cut = slice(k * STEP, (k + 1) * STEP)
                for z in range(4):
                    value = src[z, start + k * u : start + (k + 1) * u, :].astype(f32)
                    if ring == "x":
                        out[0, z, :, cut] = value
                    else:
                        out[z, 0, :, cut] = value

    results = call(
        kernel,
        tuple(outs),
        (2, 4),
        [pl.BlockSpec((4, gathered.shape[1], STEP), lambda c, x, s: (c * 4 + x, 0, 0))],
        specs,
        none,
        (gathered,),
    )
    return [r.reshape(rows, columns) for r, (rows, columns, _) in zip(results, plan)]


def core_swap(v):
    return lax.ppermute(v, "c", [(0, 1), (1, 0)])


def pair_swap(v):
    return lax.ppermute(v, "yl", [(0, 1), (1, 0)])


def exchange(v, ring, masks):
    def flat(i, c):
        return (i // 2 * 2 + c) * 2 + i % 2 if ring == "y" else 2 * i + c

    pairs = [(flat(i, c), flat(i ^ masks[c], c)) for i in range(4) for c in range(2)]
    return lax.ppermute(v, RING[ring], pairs)


def pick(v, index, axis):
    return lax.dynamic_index_in_dim(v, index, axis, keepdims=False)


def quarters(place, core):
    first = jnp.where(core == 0, 1, 3)
    second = jnp.where(core == 0, 3, 1)
    return place, place ^ first, place ^ 2, place ^ second


class Flow:
    def __init__(self, ring, pair):
        self.ring, self.other = ring, "z" if ring == "x" else "x"
        send, self.keep = pair
        self.got = exchange(send, ring, (1, 3))
        self.before = None

    def kept(self, which):
        if self.before is None:
            dims = (1, 1, *self.keep.shape[2:])
            return [pl.BlockSpec(dims, lambda y, s: (which, y, 0, 0))], [self.keep]
        return self.before(2 + which)


def onward(flows, cuts):
    in_specs, args, counts = [], [], []
    for f in flows:
        specs, arrays = f.kept(1)
        dims = (1, 1, *f.got.shape[2:])
        in_specs += specs + [pl.BlockSpec(dims, lambda y, s: (1, y, 0, 0))]
        args += arrays + [f.got]
        counts.append(len(arrays) + 1)
    out = tuple(shape(f.got.shape[1:], bf16) for f in flows)

    def kernel(_, *refs):
        k = 0
        for i, n in enumerate(counts):
            total = sum(value_of(r) for r in refs[k : k + n])
            refs[len(args) + i][...] = total.astype(bf16)
            k += n

    sums = call(
        kernel,
        out,
        (2,),
        in_specs,
        [pl.BlockSpec((1, *o.shape[1:]), lambda y, s: (y, 0, 0)) for o in out],
        cuts,
        args,
    )
    for f, v in zip(flows, sums):
        f.last = exchange(v, f.ring, (3, 1))


def value_of(ref):
    return (ref[0] if len(ref.shape) == 4 else ref[...]).astype(f32)


def turn(flows, cuts):
    in_specs, outs, out_specs, args = [], [], [], []

    for f in flows:
        first = 1 if f.other == "x" else 5
        rows, columns = f.keep.shape[2] // 4, f.keep.shape[3]
        four = pl.BlockSpec((1, 2, rows, columns), lambda j, s, i=first: (0, 0, s[i + j], 0))
        three = pl.BlockSpec((2, rows, columns), lambda j, s, i=first: (0, s[i + j], 0))
        in_specs += [four, four, three]
        args += [f.keep, f.got, f.last]
        dims = (1, 2, rows, columns)
        outs.append(shape((2, *dims[1:]), bf16))
        out_specs.append(pl.BlockSpec(dims, lambda j, s: (j, 0, 0, 0)))

    def kernel(_, *refs):
        for i in range(len(flows)):
            total = sum(value_of(r) for r in refs[3 * i : 3 * i + 3])
            refs[len(args) + i][0] = total.astype(bf16)

    sends = call(kernel, tuple(outs), (2,), in_specs, out_specs, cuts, args)
    for f, send in zip(flows, sends):
        f.before = halves_of(f)
        f.ring = f.other
        f.got = exchange(send, f.ring, (1, 3))


def halves_of(f):
    arrays = [f.keep, f.got, f.last]
    first = 1 if f.other == "x" else 5
    rows, columns = f.keep.shape[2] // 4, f.keep.shape[3]

    def quarter(which):
        four = pl.BlockSpec((1, 1, rows, columns), lambda y, s: (0, y, s[first + which], 0))
        three = pl.BlockSpec((1, rows, columns), lambda y, s: (y, s[first + which], 0))
        return [four, four, three], arrays

    return quarter


def add(a, b, none):
    def kernel(_, a, b, out):
        out[...] = (a[...].astype(f32) + b[...].astype(f32)).astype(bf16)

    out = shape(a.shape, bf16)
    return call(kernel, out, (1,), [whole(a), whole(b)], whole(out), none, (a, b))


class Finish:
    def __init__(self, flows, extra, cuts):
        in_specs, args, sizes = [], [], []
        def half(spec):
            return pl.BlockSpec(
                spec.block_shape, lambda j, s: spec.index_map(lax.rem(j + s[9], 2), s)
            )

        for f in flows:
            specs, arrays = f.kept(0)
            dims = (1, 1, *f.got.shape[2:])
            specs = specs + [
                pl.BlockSpec(dims, lambda y, s: (0, y, 0, 0)),
                pl.BlockSpec((1, *f.last.shape[1:]), lambda y, s: (y, 0, 0)),
            ]
            in_specs += [half(spec) for spec in specs]
            args += arrays + [f.got, f.last]
            sizes.append((len(arrays) + 2, f.got.shape[2], f.got.shape[3] // STEP))
        for e in extra:
            in_specs.append(half(pl.BlockSpec((1, *e.shape[1:]), lambda y, s: (y, 0, 0))))
        args += extra
        rows = sum(u * n for _, u, n in sizes) + sum(e.shape[1] for e in extra)

        def kernel(_, *refs):
            send, mine = refs[-2:]
            j = pl.program_id(0)

            def put(here, value):
                @pl.when(j == 0)
                def _():
                    mine[here, :] = value

                @pl.when(j == 1)
                def _():
                    send[here, :] = value.astype(bf16)

            start, k = 0, 0
            for count, u, n in sizes:
                v = sum(value_of(r) for r in refs[k : k + count])[0]
                for i in range(n):
                    put(slice(start, start + u), v[:, i * STEP : (i + 1) * STEP])
                    start += u
                k += count
            for ref in refs[k:-2]:
                put(slice(start, start + ref.shape[1]), ref[0])
                start += ref.shape[1]

        out = (shape((rows, STEP), bf16), shape((rows, STEP), f32))
        send, self.mine = call(
            kernel, out, (2,), in_specs, [whole(o) for o in out], cuts, args
        )
        self.got = exchange(send, "y", (1, 3))

    def second(self, none):
        self.mine = add(self.mine, self.got, none)
        self.far = lax.ppermute(self.mine, "yh", [(0, 1), (1, 0)])

    def gather(self, none):
        return lax.all_gather(add(self.mine, self.far, none), ("c", "x", "z"), axis=0)


def per_device(
    tokens,
    memory,
    compressed,
    cotangent,
    ln1_g,
    ln1_b,
    w_q,
    w_kv,
    w_r,
    bias_u,
    bias_v,
    w_o,
    ln2_g,
    ln2_b,
    w_in,
    b_in,
    w_out,
    b_out,
    conv_w,
    conv_b,
):
    line.held, line.due = [], {}
    tokens, memory, compressed, cotangent = tokens[0], memory[0], compressed[0], cotangent[0]
    yl, core = lax.axis_index("yl"), lax.axis_index("c")
    place = {"x": lax.axis_index("x"), "z": lax.axis_index("z")}
    none = jnp.zeros((1,), jnp.int32)
    ints = lambda *v: jnp.stack([jnp.asarray(i, jnp.int32) for i in v])

    def thirds(rows):
        half = rows // 2
        other = (1 - yl) * half
        return [yl * half, other + core * (half // 2), other + (1 - core) * (half // 2)]

    def both(v):
        return (v, core_swap(v))

    spot = (place["x"] * 4 + place["z"]) * 2 + core
    piece = pack(
        (ln1_g, ln1_b, bias_u, bias_v, ln2_g, ln2_b, b_out, conv_b, b_in),
        w_in,
        w_out,
        ints(spot),
    )
    piece_got = exchange(piece, "y", (1, 3))

    kv_part, small, conv_part = pack_rows(w_kv, w_q, w_r, w_o, conv_w, ints(core))
    kv_got = exchange(kv_part, "y", (1, 3))
    small_got = exchange(small, "y", (1, 3))
    conv_got = exchange(conv_part, "y", (1, 3))

    def joined(w, got, twin):
        return jnp.concatenate([w, got, twin], axis=0)

    spread = lax.all_gather(piece_got[:-16], ("x", "z", "c"), axis=0)
    thirds_d = ints(*thirds(D))
    thirds_c = ints(*thirds(3 * D), *thirds(D))
    sinus_table = sinusoid(KEYS, D).astype(bf16)
    sinus_rel = jnp.concatenate(
        [
            lax.dynamic_slice_in_dim(sinus_table, thirds_d[i], width, 1)
            for i, width in enumerate(THIRDS)
        ],
        axis=1,
    )
    line.hold(sinus_rel)
    vectors, b_in = unpack(piece, piece_got, ints(yl))

    normed, normed_rel, oldest = first_norm(compressed, memory, tokens, vectors, thirds_d)
    both_normed, both_oldest, both_cot = both(normed), both(oldest), both(cotangent)
    half = D // 2
    kv_own = dot(normed_rel[:, :half], w_kv)
    q_own = dot(normed_rel[2 * T :, :half], w_q)
    r_own = dot(sinus_rel[:, :half], w_r)
    kv_got, small_got = gate((kv_got, small_got), normed, kv_own, q_own, r_own)
    kv_twin, small_twin = core_swap(kv_got), core_swap(small_got)
    kv_whole = joined(w_kv, kv_got, kv_twin)
    q_whole, r_whole, o_whole = [
        joined(w, small_got[i], small_twin[i]) for i, w in enumerate((w_q, w_r, w_o))
    ]
    key_value = (kv_own + dot(normed_rel[:, half:], kv_whole[half:])).astype(bf16)
    queries = q_own + dot(normed_rel[2 * T :, half:], q_whole[half:])
    relative = (r_own + dot(sinus_rel[:, half:], r_whole[half:])).astype(bf16)
    line.hold(queries, relative)
    probs, attended = attend(queries, key_value, relative, vectors, none)
    line.hold(both_normed[1], both_oldest[1], both_cot[1])
    residual, normed2, normed2_rel = out_and_norm(attended, o_whole, tokens, vectors, thirds_d)
    both_n2, both_att = both(normed2), both(attended)

    cuts, rels, twins = [], [], []
    for ring in ("x", "z"):
        own, first, far, second = quarters(place[ring], core)
        cuts += [first, far, own, second]
        rels.append([own, first, second, far])
        twins.append([own, second, first, far])
    cuts = ints(core, *cuts, yl)

    def flows(groups):
        pairs = weight_grads(groups, cuts)
        return [Flow(ring, pair) for (ring, _), pair in zip(groups, pairs)]

    hidden, d_pre, mixed_out, d_normed2, d_b_in = feed_forward(
        normed2_rel, residual, cotangent, w_in, w_out, spread, b_in, vectors, ints(yl)
    )
    both_hidden, both_pre = both(hidden), both(d_pre)
    (conv_got,) = gate((conv_got,), hidden)
    conv_pieces = (conv_w, conv_got, core_swap(conv_got))
    d_residual, d_branch, d_attended, d_ln2_g, d_ln2_b, d_b_out = second_norm_back(
        cotangent, d_normed2, residual, vectors, o_whole, thirds_d
    )
    both_branch = both(d_branch)
    large = flows(
        [
            ("x", [(both_hidden, 0, T, both_cot, False)]),
            ("z", [(both_n2, 0, T, both_pre, False), (both_att, 0, T, both_branch, False)]),
        ]
    )
    d_kv, my_kv, give_kv, d_relative, d_queries, d_bias_u, d_bias_v = attend_back(
        queries, key_value, relative, vectors, probs, d_attended, ints(core)
    )
    both_kv = (my_kv, core_swap(give_kv))
    both_q, both_rel = both(d_queries), both(d_relative)

    compact, comp_normed = compress(oldest, conv_pieces, vectors, thirds_c)
    comp_pair = dot(comp_normed, kv_whole).astype(bf16)
    compressed_next = jnp.concatenate([compressed[T // 3 :], compact], axis=0)
    loss, d_ck, d_cv = reconstruct(queries, key_value, comp_pair, none)
    recon_loss = jnp.sum(loss) / (T * D)
    d_compact, d_conv_b = compress_back(d_ck, d_cv, kv_whole, compact, vectors, thirds_d)
    both_compact = both(d_compact)
    onward(large, cuts)
    small = flows(
        [
            ("x", [(both_normed, 0, KEYS, both_kv, True)]),
            (
                "z",
                [
                    (both_normed, 2, T, both_q, False),
                    ((sinus_table,), 0, KEYS, both_rel, False),
                ],
            ),
            ("x", [(both_oldest, 0, T // 3, both_compact, False)]),
        ]
    )
    turn(large, cuts)
    d_tokens, d_ln1_g, d_ln1_b = first_norm_back(
        d_kv, d_queries, kv_whole, q_whole, compressed, memory, tokens, vectors, d_residual,
        thirds_d,
    )
    onward(large, cuts)
    onward(small, cuts)
    early = Finish(large, [], cuts)
    turn(small, cuts)
    early.second(none)
    onward(small, cuts)
    early_sums = early.gather(none)

    total = jnp.concatenate(
        [d_ln1_g, d_ln1_b, d_bias_u, d_bias_v, d_ln2_g, d_ln2_b, d_b_out, d_conv_b]
        + [d_b_in]
    )
    total = jnp.concatenate(
        [
            total[:8].reshape(8, 2, STEP).transpose(1, 0, 2),
            total[8:].reshape(2, 4, STEP),
            jnp.zeros((2, 4, STEP), f32),
        ],
        axis=1,
    )
    late = Finish(small, [total], cuts)
    late.second(none)
    line.hold(early_sums)
    late_sums = late.gather(none)

    g_out, g_in, g_o = widen(
        early_sums, [(FF // 2, D, "x"), (D // 2, FF, "z"), (D // 2, D, "z")], none
    )
    g_kv, g_q, g_r, g_conv = widen(
        late_sums,
        [(D // 2, 2 * D, "x"), (D // 2, D, "z"), (D // 2, D, "z"), (3 * D // 2, D, "x")],
        none,
    )
    half = jnp.sum(late_sums[:, 224:236].astype(f32), axis=0)
    t_ln1_g, t_ln1_b, t_bu, t_bv, t_ln2_g, t_ln2_b, t_bout, t_convb = [half[i] for i in range(8)]
    t_bin = half[8:].reshape(-1)
    return (
        mixed_out[None],
        compressed_next[None],
        recon_loss[None],
        d_tokens[None],
        t_ln1_g,
        t_ln1_b,
        g_q,
        g_kv,
        g_r,
        t_bu,
        t_bv,
        g_o,
        t_ln2_g,
        t_ln2_b,
        g_in,
        t_bin,
        g_out,
        t_bout,
        g_conv,
        t_convb,
    )


def solution(mesh):
    fine = Mesh(mesh.devices.reshape(2, 4, 4, 2, 2), AXES)
    stream = P(AXES, None, None)
    vec, mat = P("yl"), P("yl", None)
    weights = (vec, vec, mat, mat, mat, vec, vec, mat, vec, vec, mat, vec, mat, vec, mat, vec)
    return jax.shard_map(
        per_device,
        mesh=fine,
        in_specs=(stream,) * 4 + weights,
        out_specs=(stream, stream, P(AXES), stream) + weights,
        check_vma=False,
    )
```

```python
import jax
import jax.numpy as jnp
from jax import lax
from jax.experimental import pallas as pl
from jax.experimental.pallas import tpu as pltpu
from jax.sharding import Mesh, PartitionSpec as P

H = 8
HD = 128
D = 1024
T = 192
KEYS = 576
PAD = 640
FF = 4096
FACTOR = HD ** (-0.5)
f32 = jnp.float32
bf16 = jnp.bfloat16
AXES = ("yh", "x", "z", "c", "yl")
RING = {"x": ("x", "c"), "z": ("z", "c"), "y": ("yh", "c", "yl")}


def sinusoid(key_count, model_dim):
    distance = (key_count - 1 - jnp.arange(key_count)).astype(f32)
    inverse = 1.0 / 10000.0 ** (jnp.arange(0, model_dim, 2).astype(f32) / model_dim)
    angles = distance[:, None] * inverse[None, :]
    return jnp.concatenate([jnp.sin(angles), jnp.cos(angles)], axis=-1)


def dot(a, b):
    return jnp.dot(a, b, preferred_element_type=f32)


def dot_t(a, b):
    return lax.dot_general(a, b, (((1,), (1,)), ((), ())), preferred_element_type=f32)


def t_dot(a, b):
    return lax.dot_general(a, b, (((0,), (0,)), ((), ())), preferred_element_type=f32)


class Line:
    def __init__(self):
        self.held, self.due = [], {}

    def hold(self, *values):
        self.held += values

    def expect(self, gap, *values):
        self.due.setdefault(gap, []).extend(values)

    def ran(self, result):
        self.held = [result, *self.due.get(1, [])]
        self.due = {gap - 1: values for gap, values in self.due.items() if gap > 1}

    def later(self, value):
        return lax.optimization_barrier((value, *self.held))[0] if self.held else value


line = Line()


def call(kernel, out, grid, in_specs, out_specs, scalars, args, scratch=()):
    held, n = line.held, len(args)

    def body(s, *refs):
        kernel(s, *refs[:n], *refs[n + len(held) :])

    result = pl.pallas_call(
        body,
        out_shape=out,
        grid_spec=pltpu.PrefetchScalarGridSpec(
            num_scalar_prefetch=1,
            grid=grid,
            in_specs=list(in_specs) + [pl.BlockSpec(memory_space=pl.ANY)] * len(held),
            out_specs=out_specs,
            scratch_shapes=list(scratch),
        ),
        compiler_params=pltpu.CompilerParams(vmem_limit_bytes=56 << 20),
    )(scalars, *args, *held)
    line.ran(jax.tree.leaves(result)[0])
    return result


def gate(values, *after):
    n = len(values)
    anywhere = pl.BlockSpec(memory_space=pl.ANY)
    return pl.pallas_call(
        lambda *refs: None,
        out_shape=[jax.ShapeDtypeStruct(v.shape, v.dtype) for v in values],
        in_specs=[anywhere] * (n + len(after)),
        out_specs=[anywhere] * n,
        input_output_aliases={i: i for i in range(n)},
    )(*values, *after)


def whole(a):
    zeros = (0,) * a.ndim
    return pl.BlockSpec(a.shape, lambda *_: zeros)


def shape(dims, dtype):
    return jax.ShapeDtypeStruct(dims, dtype)


def at(offset):
    return pl.multiple_of(offset, 128)


def center_scale(v):
    mid = v - jnp.mean(v, axis=-1, keepdims=True)
    r = lax.rsqrt(jnp.mean(mid * mid, axis=-1, keepdims=True) + 1e-5)
    return mid * r, r


def norm_back(xhat, r, g, dn):
    gd = dn * g
    return r * (
        gd
        - jnp.mean(gd, axis=-1, keepdims=True)
        - xhat * jnp.mean(gd * xhat, axis=-1, keepdims=True)
    )


def softmax(s):
    e = jnp.exp(s - jnp.max(s, axis=-1, keepdims=True))
    return e / jnp.sum(e, axis=-1, keepdims=True)


(LN1_G, LN1_B, BIAS_U, BIAS_V, LN2_G, LN2_B, B_OUT, CONV_B) = range(8)


def row(ref, i):
    return ref[i : i + 1, :]


def pack(vectors, w_in, w_out, scalars):
    n_in, n_out = (w.shape[0] // 32 for w in (w_in, w_out))
    chunks = FF // D
    rows = n_out + n_in * chunks
    half = D // 2

    def kernel(_, *refs):
        wi, wo, piece, flat = refs[-4:]
        flat[...] = jnp.zeros_like(flat)
        for i, ref in enumerate(refs[:8]):
            flat[i : i + 1, :half] = ref[...].astype(f32).reshape(1, half)
        flat[8 : 8 + FF // 2 // D, :] = refs[8][...].astype(f32).reshape(FF // 2 // D, D)
        piece[:n_out, :] = wo[...]
        for i in range(chunks):
            piece[n_out + i * n_in : n_out + (i + 1) * n_in, :] = wi[:, i * D : (i + 1) * D]
        piece[rows:, :] = flat[...].astype(bf16)

    out = shape((rows + 16, D), bf16)
    return call(
        kernel,
        out,
        (1,),
        [whole(v) for v in vectors]
        + [
            pl.BlockSpec((w.shape[0] // 32, w.shape[1]), lambda j, s: (s[0], 0))
            for w in (w_in, w_out)
        ],
        whole(out),
        scalars,
        (*vectors, w_in, w_out),
        [pltpu.VMEM((16, D), f32)],
    )


def pack_rows(w_kv, w_q, w_r, w_o, conv_w, scalars):
    n, n_conv = w_q.shape[0] // 2, conv_w.shape[0] // 2

    def kernel(_, kv, q, r, o, conv, kv_out, out, conv_out):
        kv_out[...] = kv[...]
        for i, ref in enumerate((q, r, o)):
            out[i] = ref[...]
        conv_out[...] = conv[...]

    args = (w_kv, w_q, w_r, w_o, conv_w)
    out = (shape((n, 2 * D), bf16), shape((3, n, D), bf16), shape((n_conv, D), bf16))
    return call(
        kernel,
        out,
        (1,),
        [pl.BlockSpec((w.shape[0] // 2, w.shape[1]), lambda j, s: (s[0], 0)) for w in args],
        [whole(o) for o in out],
        scalars,
        args,
    )


def unpack(mine, theirs, scalars):
    half = D // 2
    at_row = mine.shape[0] // 16 - 1
    tail = pl.BlockSpec((16, D), lambda j, s: (at_row, 0))

    def kernel(s, mine, theirs, vectors, b_in):
        a, b = mine[...].astype(f32), theirs[...].astype(f32)
        low = jnp.where(s[0] == 0, a, b)
        high = jnp.where(s[0] == 0, b, a)
        vectors[:, :half] = low[:8, :half]
        vectors[:, half:] = high[:8, :half]
        rows = FF // 2 // D
        b_in[:rows] = low[8 : 8 + rows]
        b_in[rows:] = high[8 : 8 + rows]

    out = (shape((8, D), f32), shape((FF // D, D), f32))
    return call(
        kernel, out, (1,), [tail, tail], [whole(o) for o in out], scalars, (mine, theirs)
    )


def relative_columns(x, s, widths):
    parts = [x[:, pl.ds(at(s[i]), width)] for i, width in enumerate(widths)]
    return jnp.concatenate(parts, axis=1)


def natural_columns(out, x, s, widths):
    start = 0
    for i, width in enumerate(widths):
        out[:, pl.ds(at(s[i]), width)] = x[:, start : start + width]
        start += width


THIRDS = (D // 2, D // 4, D // 4)


def first_norm(compressed, memory, tokens, vectors, offsets):
    def kernel(s, comp, mem, tok, vec, out, out_rel, old, old_quarters):
        gain, bias = row(vec, LN1_G), row(vec, LN1_B)

        def part(ref, base):
            for i in range(0, T, 32):
                xhat, r = center_scale(ref[i : i + 32, :].astype(f32))
                out[base + i : base + i + 32, :] = (xhat * gain + bias).astype(bf16)

        part(comp, 0)
        part(mem, T)
        part(tok, 2 * T)
        out_rel[...] = relative_columns(out, s, THIRDS)
        line_of = lax.broadcasted_iota(jnp.int32, (T // 3, T), 0)
        col = lax.broadcasted_iota(jnp.int32, (T // 3, T), 1)
        low = mem[...].astype(bf16)
        for tap in range(3):
            take = jnp.where(col == 3 * line_of + tap, 1.0, 0.0).astype(bf16)
            old[:, tap * D : (tap + 1) * D] = dot(take, low).astype(bf16)
        width = 3 * D // 8
        for q in range(4):
            for y in range(2):
                begin = y * 3 * D // 2 + q * width
                old_quarters[q, :, y * width : (y + 1) * width] = old[:, begin : begin + width]

    args = (compressed, memory, tokens, vectors)
    out = (
        shape((KEYS, D), bf16),
        shape((KEYS, D), bf16),
        shape((T // 3, 3 * D), bf16),
        shape((4, T // 3, 3 * D // 4), bf16),
    )
    return call(
        kernel, out, (1,), [whole(a) for a in args], [whole(o) for o in out], offsets, args
    )


def head(n, rows, row_block=0, first=0):
    return pl.BlockSpec((rows, n * HD), lambda h, s: (row_block, first // n + h))


def columns_of(n):
    return [slice(i * HD, (i + 1) * HD) for i in range(n)]


def attend(queries, key_value, relative, vectors, none):
    n = 2

    def kernel(_, q, k, v, rel, vec, probs, out):
        pad = jnp.zeros((PAD - KEYS, HD), bf16)
        i = lax.broadcasted_iota(jnp.int32, (T, PAD), 0)
        j = lax.broadcasted_iota(jnp.int32, (T, PAD), 1)
        seen = j <= i + (KEYS - T)
        cuts = columns_of(n)
        content = [((q[:, c] + vec[BIAS_U : BIAS_U + 1, c]) * FACTOR).astype(bf16) for c in cuts]
        located = [((q[:, c] + vec[BIAS_V : BIAS_V + 1, c]) * FACTOR).astype(bf16) for c in cuts]
        raw = [
            dot_t(x, jnp.concatenate([rel[:, c], pad], axis=0)) for x, c in zip(located, cuts)
        ]
        near = [dot_t(x, jnp.concatenate([k[:, c], pad], axis=0)) for x, c in zip(content, cuts)]
        raw = [pltpu.roll(x, PAD - T + 1, 1, stride=1, stride_axis=0) for x in raw]
        p = [softmax(jnp.where(seen, a + b, -1e30)) for a, b in zip(near, raw)]
        for h, c in enumerate(cuts):
            probs[h] = p[h]
            value = jnp.concatenate([v[:, c], pad], axis=0)
            out[:, c] = dot(p[h].astype(bf16), value).astype(bf16)

    return call(
        kernel,
        (shape((H, T, PAD), f32), shape((T, D), bf16)),
        (H // n,),
        [head(n, T), head(n, KEYS), head(n, KEYS, 0, H), head(n, KEYS), head(n, 8)],
        [pl.BlockSpec((n, T, PAD), lambda h, s: (h, 0, 0)), head(n, T)],
        none,
        (queries, key_value, key_value, relative, vectors),
    )


def attend_back(queries, key_value, relative, vectors, probs, d_attended, scalars):
    n = 2

    def kernel(s, q, k, v, rel, vec, probs, d_att, d_kv, mine, give, d_rel, d_q, d_bu, d_bv):
        pad = jnp.zeros((PAD - KEYS, HD), bf16)
        i = lax.broadcasted_iota(jnp.int32, (T, T), 0)
        j = lax.broadcasted_iota(jnp.int32, (T, T), 1)
        flip = jnp.where(i + j == T - 1, 1.0, 0.0).astype(bf16)
        cuts = columns_of(n)
        content = [((q[:, c] + vec[BIAS_U : BIAS_U + 1, c]) * FACTOR).astype(bf16) for c in cuts]
        located = [((q[:, c] + vec[BIAS_V : BIAS_V + 1, c]) * FACTOR).astype(bf16) for c in cuts]
        da = [d_att[:, c] for c in cuts]
        d_p = [dot_t(x, jnp.concatenate([v[:, c], pad], axis=0)) for x, c in zip(da, cuts)]
        d_v = [t_dot(probs[h].astype(bf16), x)[:KEYS].astype(bf16) for h, x in enumerate(da)]
        d_s = []
        for h, x in enumerate(d_p):
            p = probs[h]
            d_s.append((p * (x - jnp.sum(p * x, axis=-1, keepdims=True))).astype(bf16))
        d_raw = [dot(flip, x) for x in d_s]
        d_c = [
            dot(x, jnp.concatenate([k[:, c], pad], axis=0)) * FACTOR for x, c in zip(d_s, cuts)
        ]
        d_k = [t_dot(x, y)[:KEYS].astype(bf16) for x, y in zip(d_s, content)]
        d_raw = [pltpu.roll(x, 0, 1, stride=1, stride_axis=0).astype(bf16) for x in d_raw]
        d_raw = [dot(flip, x).astype(bf16) for x in d_raw]
        d_l = [
            dot(x, jnp.concatenate([rel[:, c], pad], axis=0)) * FACTOR for x, c in zip(d_raw, cuts)
        ]
        for h, c in enumerate(cuts):
            d_rel[:, c] = t_dot(d_raw[h], located[h])[:KEYS].astype(bf16)
            d_kv[0, :, c] = d_k[h]
            d_kv[1, :, c] = d_v[h]
            mine[:, c] = jnp.where(s[0] == 0, d_k[h], d_v[h])
            give[:, c] = jnp.where(s[0] == 0, d_v[h], d_k[h])
            d_q[:, c] = (d_c[h] + d_l[h]).astype(bf16)
            d_bu[:, c] = jnp.sum(d_c[h], axis=0, keepdims=True)
            d_bv[:, c] = jnp.sum(d_l[h], axis=0, keepdims=True)

    return call(
        kernel,
        (shape((2, KEYS, D), bf16),)
        + (shape((KEYS, D), bf16),) * 3
        + (shape((T, D), bf16), shape((1, D), f32), shape((1, D), f32)),
        (H // n,),
        [
            head(n, T),
            head(n, KEYS),
            head(n, KEYS, 0, H),
            head(n, KEYS),
            head(n, 8),
            pl.BlockSpec((n, T, PAD), lambda h, s: (h, 0, 0)),
            head(n, T),
        ],
        [
            pl.BlockSpec((2, KEYS, n * HD), lambda h, s: (0, 0, h)),
            head(n, KEYS),
            head(n, KEYS),
            head(n, KEYS),
            head(n, T),
            head(n, 1),
            head(n, 1),
        ],
        scalars,
        (queries, key_value, key_value, relative, vectors, probs, d_attended),
    )


def out_and_norm(attended, w_o, tokens, vectors, offsets):
    def kernel(s, att, w, tok, vec, res, n2, n2_rel):
        total = tok[...].astype(f32) + dot(relative_columns(att, s, THIRDS), w[...])
        res[...] = total
        xhat, r = center_scale(total)
        n2[...] = (xhat * row(vec, LN2_G) + row(vec, LN2_B)).astype(bf16)
        other = at(D // 2 - s[0])
        n2_rel[:, : D // 2] = n2[:, pl.ds(at(s[0]), D // 2)]
        n2_rel[:, D // 2 :] = n2[:, pl.ds(other, D // 2)]

    args = (attended, w_o, tokens, vectors)
    out = (shape((T, D), f32), shape((T, D), bf16), shape((T, D), bf16))
    return call(
        kernel, out, (1,), [whole(a) for a in args], [whole(o) for o in out], offsets, args
    )


STEP = 512
UNITS = 1024
HALF = FF // 2 // UNITS


def feed_forward(n2_rel, residual, cotangent, w_in, w_out, spread, b_in, vectors, scalars):
    n_in = w_in.shape[0] // 32
    n_out = w_out.shape[0] // 32
    skip = n_out // n_in
    per = UNITS // n_out
    K_NORM = 0.7978845608028654

    def natural(j, s):
        return lax.rem(j + s[0] * HALF, 2 * HALF)

    def kernel(s, n2, res, cot, wi0, wi1, wo0, wo1, bi, vec, hid, dpre, mixed, dn2, dbi, acc, back):
        j = pl.program_id(0)
        n = natural(j, s)

        @pl.when(j == 0)
        def _():
            acc[...] = jnp.zeros_like(acc)
            back[...] = jnp.zeros_like(back)

        wo = jnp.where(j < HALF, wo0[...], wo1[...].reshape(UNITS, D))
        win = jnp.concatenate([wi0[...], wi1[...].reshape(D // 2, UNITS)], axis=0)
        pre = dot(n2[...], win) + bi[pl.ds(n, 1), :]
        d_hidden = dot_t(cot[...], wo)
        square = pre * pre
        t = jnp.tanh(K_NORM * pre * (1.0 + 0.044715 * square))
        gate_ = 0.5 * (1.0 + t)
        hidden = (pre * gate_).astype(bf16)
        slope = gate_ + (0.5 * K_NORM) * pre * (1.0 - t * t) * (1.0 + (3 * 0.044715) * square)
        d_pre = (d_hidden * slope).astype(bf16)
        hid[...] = hidden
        dpre[...] = d_pre
        dbi[pl.ds(n, 1), :] = jnp.sum(d_pre.astype(f32), axis=0, keepdims=True)
        acc[...] += dot(hidden, wo)
        back[...] += dot_t(d_pre, win)

        @pl.when(j == 2 * HALF - 1)
        def _():
            mixed[...] = (res[...] + acc[...] + row(vec, B_OUT)).astype(bf16)
            dn2[:, pl.ds(at(s[0] * (D // 2)), D // 2)] = back[:, : D // 2]
            dn2[:, pl.ds(at((1 - s[0]) * (D // 2)), D // 2)] = back[:, D // 2 :]

    out = (
        shape((T, FF), bf16),
        shape((T, FF), bf16),
        shape((T, D), bf16),
        shape((T, D), f32),
        shape((2 * HALF, UNITS), f32),
    )
    by_unit = pl.BlockSpec((T, UNITS), lambda j, s: (0, natural(j, s)))
    return call(
        kernel,
        out,
        (2 * HALF,),
        [
            whole(n2_rel),
            whole(residual),
            whole(cotangent),
            pl.BlockSpec((D // 2, UNITS), lambda j, s: (0, natural(j, s))),
            pl.BlockSpec((32, n_in, UNITS), lambda j, s: (0, skip + natural(j, s), 0)),
            pl.BlockSpec((UNITS, D), lambda j, s: (jnp.minimum(j, HALF - 1), 0)),
            pl.BlockSpec(
                (per, n_out, D), lambda j, s: (jnp.maximum(j - HALF, 0), 0, 0)
            ),
            whole(b_in),
            whole(vectors),
        ],
        [by_unit, by_unit, whole(out[2]), whole(out[3]), whole(out[4])],
        scalars,
        (n2_rel, residual, cotangent, w_in, spread, w_out, spread, b_in, vectors),
        [pltpu.VMEM((T, D), f32), pltpu.VMEM((T, D), f32)],
    )


def second_norm_back(cotangent, d_n2, residual, vectors, w_o, offsets):
    def kernel(s, cot, dn, res, vec, w, d_res, d_br, d_att, dg, db, dbo):
        xhat, r = center_scale(res[...])
        dn, wide = dn[...], cot[...].astype(f32)
        dg[...] = jnp.sum(dn * xhat, axis=0, keepdims=True)
        db[...] = jnp.sum(dn, axis=0, keepdims=True)
        dbo[...] = jnp.sum(wide, axis=0, keepdims=True)
        total = wide + norm_back(xhat, r, row(vec, LN2_G), dn)
        d_res[...] = total
        low = total.astype(bf16)
        d_br[...] = low
        natural_columns(d_att, dot_t(low, w[...]).astype(bf16), s, THIRDS)

    args = (cotangent, d_n2, residual, vectors, w_o)
    out = (
        shape((T, D), f32),
        shape((T, D), bf16),
        shape((T, D), bf16),
        shape((1, D), f32),
        shape((1, D), f32),
        shape((1, D), f32),
    )
    return call(
        kernel, out, (1,), [whole(a) for a in args], [whole(o) for o in out], offsets, args
    )


def first_norm_back(d_kv, d_q, w_kv, w_q, compressed, memory, tokens, vectors, d_res, offsets):
    steps = 4
    wide, slim = 2 * D // steps, D // steps

    def kernel(s, dkv, dq, kw, qw, comp, mem, tok, vec, dres, dtok, dg, db, acc, nat, xh, rs):
        j = pl.program_id(0)

        def product(start):
            value = dot_t(dkv[0], kw[...])
            if start:
                acc[...] = value
            else:
                acc[...] += value
            acc[2 * T :, :] += dot_t(dq[...], qw[...])

        for block, ref in enumerate((comp, mem, tok)):

            @pl.when(j == block)
            def _(block=block, ref=ref):
                product(block == 0)
                for i in range(0, T, 32):
                    xhat, r = center_scale(ref[i : i + 32, :].astype(f32))
                    xh[block * T + i : block * T + i + 32, :] = xhat
                    if block == 2:
                        rs[i : i + 32, :] = jnp.broadcast_to(r, (32, HD))

        @pl.when(j == steps - 1)
        def _():
            product(False)
            natural_columns(nat, acc, s, THIRDS)
            gain = row(vec, LN1_G)
            sum_g = jnp.zeros((8, D), f32)
            sum_b = jnp.zeros((8, D), f32)
            for i in range(0, KEYS, 32):
                dn, xhat = nat[i : i + 32, :], xh[i : i + 32, :]
                both = dn * xhat
                sum_g += (both[:8] + both[8:16]) + (both[16:24] + both[24:])
                sum_b += (dn[:8] + dn[8:16]) + (dn[16:24] + dn[24:])
                if i >= 2 * T:
                    k = i - 2 * T
                    r = rs[k : k + 32, :1]
                    dtok[k : k + 32, :] = dres[k : k + 32, :] + norm_back(xhat, r, gain, dn)
            dg[...] = jnp.sum(sum_g, axis=0, keepdims=True)
            db[...] = jnp.sum(sum_b, axis=0, keepdims=True)

    rest = (compressed, memory, tokens, vectors, d_res)
    out = (shape((T, D), f32), shape((1, D), f32), shape((1, D), f32))
    return call(
        kernel,
        out,
        (steps,),
        [
            pl.BlockSpec((1, KEYS, wide), lambda j, s: (j // (steps // 2), 0, lax.rem(j, steps // 2))),
            pl.BlockSpec((T, slim), lambda j, s: (0, j)),
            pl.BlockSpec((D, wide), lambda j, s: (0, j)),
            pl.BlockSpec((D, slim), lambda j, s: (0, j)),
        ]
        + [whole(a) for a in rest],
        [whole(o) for o in out],
        offsets,
        (d_kv, d_q, w_kv, w_q, *rest),
        [pltpu.VMEM((KEYS, D), f32)] * 3 + [pltpu.VMEM((T, HD), f32)],
    )


def compress(oldest, pieces, vectors, offsets):
    block = 256
    rows = T // 3

    def kernel(s, x, w0, w1, w2, vec, compact, normed, x_rel, natural):
        j = pl.program_id(0)

        @pl.when(j == 0)
        def _():
            x_rel[...] = relative_columns(x, s, (3 * D // 2, 3 * D // 4, 3 * D // 4))

        w = jnp.concatenate([w0[...], w1[...], w2[...]], axis=0)
        here = pl.ds(at(j * block), block)
        compact[:, here] = dot(x_rel[...], w) + vec[CONV_B : CONV_B + 1, here]

        @pl.when(j == D // block - 1)
        def _():
            xhat, r = center_scale(compact[...])
            natural[...] = (xhat * row(vec, LN1_G) + row(vec, LN1_B)).astype(bf16)
            start = 0
            for i, width in enumerate(THIRDS):
                normed[:, start : start + width] = natural[:, pl.ds(at(s[3 + i]), width)]
                start += width

    out = (shape((rows, D), f32), shape((rows, D), bf16))
    return call(
        kernel,
        out,
        (D // block,),
        [whole(oldest)]
        + [pl.BlockSpec((w.shape[0], block), lambda j, s: (0, j)) for w in pieces]
        + [whole(vectors)],
        [whole(o) for o in out],
        offsets,
        (oldest, *pieces, vectors),
        [pltpu.VMEM((rows, 3 * D), bf16), pltpu.VMEM((rows, D), bf16)],
    )


def reconstruct(queries, key_value, comp_pair, none):
    rows = T // 3
    n = 4

    def kernel(_, q, k, v, ck, cv, loss, dck, dcv):
        cuts = columns_of(n)
        asking = [(q[:, c] * FACTOR).astype(bf16) for c in cuts]
        far = [dot_t(x, k[:, c]) for x, c in zip(asking, cuts)]
        near = [dot_t(x, ck[:, c]) for x, c in zip(asking, cuts)]
        p = [softmax(x).astype(bf16) for x in far]
        gp = [softmax(x) for x in near]
        low = [x.astype(bf16) for x in gp]
        miss = [dot(p[h], v[:, c]) - dot(low[h], cv[:, c]) for h, c in enumerate(cuts)]
        total = sum(jnp.sum(x * x, axis=0, keepdims=True) for x in miss)
        d_guess = [((-2.0 / (T * D)) * x).astype(bf16) for x in miss]
        d_gp = [dot_t(x, cv[:, c]) for x, c in zip(d_guess, cuts)]
        d_gs = [
            (x * (y - jnp.sum(x * y, axis=-1, keepdims=True))).astype(bf16)
            for x, y in zip(gp, d_gp)
        ]
        for h, c in enumerate(cuts):
            dcv[:, c] = t_dot(low[h], d_guess[h]).astype(bf16)
            dck[:, c] = t_dot(d_gs[h], asking[h]).astype(bf16)

        @pl.when(pl.program_id(0) == 0)
        def _():
            loss[...] = total

        @pl.when(pl.program_id(0) > 0)
        def _():
            loss[...] += total

    return call(
        kernel,
        (shape((1, HD), f32), shape((rows, D), bf16), shape((rows, D), bf16)),
        (H // n,),
        [head(n, T), head(n, T, 1), head(n, T, 1, H), head(n, rows), head(n, rows, 0, H)],
        [pl.BlockSpec((1, HD), lambda h, s: (0, 0)), head(n, rows), head(n, rows)],
        none,
        (queries, key_value, key_value, comp_pair, comp_pair),
    )


def compress_back(dck, dcv, w_kv, compact, vectors, offsets):
    rows = T // 3

    def kernel(s, dck, dcv, w, compact, vec, d_compact, d_bias, dn):
        back = dot_t(jnp.concatenate([dck[...], dcv[...]], axis=1), w[...])
        natural_columns(dn, back, s, THIRDS)
        xhat, r = center_scale(compact[...])
        low = norm_back(xhat, r, row(vec, LN1_G), dn[...]).astype(bf16)
        d_compact[...] = low
        d_bias[...] = jnp.sum(low.astype(f32), axis=0, keepdims=True)

    args = (dck, dcv, w_kv, compact, vectors)
    out = (shape((rows, D), bf16), shape((1, D), f32))
    return call(
        kernel,
        out,
        (1,),
        [whole(a) for a in args],
        [whole(o) for o in out],
        offsets,
        args,
        [pltpu.VMEM((rows, D), f32)],
    )


def weight_grads(groups, scalars):
    in_specs, args, outs, out_specs, layout, scratch = [], [], [], [], [], []
    for ring, jobs in groups:
        first = 1 if ring == "x" else 5
        block = jobs[0][0][0].shape[1] // 8
        plan = []
        for xs, row_block, rows, dys, ready in jobs:
            width = dys[0].shape[1] // (1 if ready else 2)
            plan.append((width, rows, len(xs)))
            for x in xs:
                for y in range(2):
                    in_specs.append(
                        pl.BlockSpec(
                            (rows, block),
                            lambda q, s, r=row_block, f=first, y=y: (r, y * 4 + s[f + q]),
                        )
                    )
                    args.append(x)
            for dy in dys:
                in_specs.append(
                    pl.BlockSpec((rows, width), lambda q, s, r=ready: (0, 0 if r else s[0]))
                )
                args.append(dy)
            scratch.append(pltpu.VMEM((rows * len(xs), width), bf16))
        dims = (1, 2, block, sum(p[0] for p in plan))
        outs += [shape((2, *dims[1:]), bf16)] * 2
        out_specs += [
            pl.BlockSpec(dims, lambda q, s: (jnp.minimum(q, 1), 0, 0, 0)),
            pl.BlockSpec(dims, lambda q, s: (jnp.maximum(q - 2, 0), 0, 0, 0)),
        ]
        layout.append(plan)
    n_in, n_out = len(in_specs), len(outs)

    def kernel(s, *refs):
        ins, results, joined = refs[:n_in], refs[n_in : n_in + n_out], refs[n_in + n_out :]
        q = pl.program_id(0)

        @pl.when(q == 0)
        def _():
            place, k = 0, 0
            for plan in layout:
                for _, rows, n in plan:
                    da, db = ins[place + 2 * n], ins[place + 2 * n + 1]
                    if n == 2:
                        joined[k][:rows, :] = da[...]
                        joined[k][rows:, :] = db[...]
                    else:
                        joined[k][...] = (da[...].astype(f32) + db[...].astype(f32)).astype(bf16)
                    place += 2 * n + 2
                    k += 1

        place, k = 0, 0
        for i, plan in enumerate(layout):
            send, keep = results[2 * i : 2 * i + 2]
            block = send.shape[2]
            start = 0
            for width, rows, n in plan:
                x = jnp.concatenate([r[...] for r in ins[place : place + 2]], axis=1)
                if n == 2:
                    other = jnp.concatenate([r[...] for r in ins[place + 2 : place + 4]], axis=1)
                    x = jnp.concatenate([x, other], axis=0)
                value = t_dot(x, joined[k][...]).astype(bf16).reshape(2, block, width)
                cut = slice(start, start + width)
                send[0, :, :, cut] = jnp.where(q < 2, value, send[0, :, :, cut])
                keep[0, :, :, cut] = value
                start += width
                place += 2 * n + 2
                k += 1

    flat = call(kernel, tuple(outs), (4,), in_specs, out_specs, scalars, args, scratch)
    return [(flat[2 * i], flat[2 * i + 1]) for i in range(len(groups))]


def conv_grad(x, x_twin, dy, dy_twin, scalars):
    rows, columns = x.shape[1] // 2, D // 2

    def kernel(s, xa, xb, da, db, out):
        both = jnp.concatenate([xa[...], xb[...]], axis=0)
        total = t_dot(both, jnp.concatenate([da[...], db[...]], axis=0))
        out[...] = total.reshape(2, rows, columns)

    half = pl.BlockSpec((dy.shape[0], columns), lambda j, s: (0, s[0]))
    out = shape((2, rows, columns), f32)
    return call(
        kernel,
        out,
        (1,),
        [whole(x), whole(x_twin), half, half],
        whole(out),
        scalars,
        (x, x_twin, dy, dy_twin),
    )


def widen(gathered, plan, none):
    outs, specs, layout = [], [], []
    start = 0
    for rows, columns, ring in plan:
        u, chunks = rows // 16, columns // 2 // STEP
        outs.append(shape((4, 4, u, columns), f32))
        if ring == "x":
            specs.append(
                pl.BlockSpec((1, 4, u, chunks * STEP), lambda c, x, s: (x, 0, 0, c))
            )
        else:
            specs.append(
                pl.BlockSpec((4, 1, u, chunks * STEP), lambda c, x, s: (0, x, 0, c))
            )
        layout.append((start, u, chunks, ring))
        start += u * chunks

    def kernel(_, src, *results):
        for out, (start, u, chunks, ring) in zip(results, layout):
            for k in range(chunks):
                cut = slice(k * STEP, (k + 1) * STEP)
                for z in range(4):
                    value = src[z, start + k * u : start + (k + 1) * u, :].astype(f32)
                    if ring == "x":
                        out[0, z, :, cut] = value
                    else:
                        out[z, 0, :, cut] = value

    results = call(
        kernel,
        tuple(outs),
        (2, 4),
        [pl.BlockSpec((4, gathered.shape[1], STEP), lambda c, x, s: (c * 4 + x, 0, 0))],
        specs,
        none,
        (gathered,),
    )
    return [r.reshape(rows, columns) for r, (rows, columns, _) in zip(results, plan)]


def core_swap(v):
    return lax.ppermute(v, "c", [(0, 1), (1, 0)])


def pair_swap(v):
    return lax.ppermute(v, "yl", [(0, 1), (1, 0)])


def exchange(v, ring, masks):
    def flat(i, c):
        return (i // 2 * 2 + c) * 2 + i % 2 if ring == "y" else 2 * i + c

    pairs = [(flat(i, c), flat(i ^ masks[c], c)) for i in range(4) for c in range(2)]
    return lax.ppermute(v, RING[ring], pairs)


def pick(v, index, axis):
    return lax.dynamic_index_in_dim(v, index, axis, keepdims=False)


def quarters(place, core):
    first = jnp.where(core == 0, 1, 3)
    second = jnp.where(core == 0, 3, 1)
    return place, place ^ first, place ^ 2, place ^ second


class Flow:
    def __init__(self, ring, pair, done=None):
        self.ring, self.other = ring, "z" if ring == "x" else "x"
        self.before, self.result = None, done
        if done is None:
            send, self.keep = pair
            self.got = exchange(send, ring, (1, 3))

    def sources(self):
        return [self.keep, self.got, self.last] if self.result is None else [self.result]

    def kept(self, which):
        if self.before is None:
            dims = (1, 1, *self.keep.shape[2:])
            return [pl.BlockSpec(dims, lambda y, s: (which, y, 0, 0))], [self.keep]
        return self.before(2 + which)


def onward(flows, cuts):
    in_specs, args, counts = [], [], []
    for f in flows:
        specs, arrays = f.kept(1)
        dims = (1, 1, *f.got.shape[2:])
        in_specs += specs + [pl.BlockSpec(dims, lambda y, s: (1, y, 0, 0))]
        args += arrays + [f.got]
        counts.append(len(arrays) + 1)
    out = tuple(shape(f.got.shape[1:], bf16) for f in flows)

    def kernel(_, *refs):
        k = 0
        for i, n in enumerate(counts):
            total = sum(value_of(r) for r in refs[k : k + n])
            refs[len(args) + i][...] = total.astype(bf16)
            k += n

    sums = call(
        kernel,
        out,
        (2,),
        in_specs,
        [pl.BlockSpec((1, *o.shape[1:]), lambda y, s: (y, 0, 0)) for o in out],
        cuts,
        args,
    )
    for f, v in zip(flows, sums):
        f.last = exchange(v, f.ring, (3, 1))


def value_of(ref):
    return (ref[0] if len(ref.shape) == 4 else ref[...]).astype(f32)


def turn(flows, cuts):
    in_specs, outs, out_specs, args = [], [], [], []

    counts = []
    for f in flows:
        first = 1 if f.other == "x" else 5
        arrays = f.sources()
        rows, columns = arrays[0].shape[-2] // 4, arrays[0].shape[-1]
        four = pl.BlockSpec((1, 2, rows, columns), lambda j, s, i=first: (0, 0, s[i + j], 0))
        three = pl.BlockSpec((2, rows, columns), lambda j, s, i=first: (0, s[i + j], 0))
        in_specs += [four if a.ndim == 4 else three for a in arrays]
        args += arrays
        counts.append(len(arrays))
        dims = (1, 2, rows, columns)
        outs.append(shape((2, *dims[1:]), bf16))
        out_specs.append(pl.BlockSpec(dims, lambda j, s: (j, 0, 0, 0)))

    def kernel(_, *refs):
        k = 0
        for i, n in enumerate(counts):
            total = sum(value_of(r) for r in refs[k : k + n])
            refs[len(args) + i][0] = total.astype(bf16)
            k += n

    sends = call(kernel, tuple(outs), (2,), in_specs, out_specs, cuts, args)
    for f, send in zip(flows, sends):
        f.before = halves_of(f)
        f.ring = f.other
        f.got = exchange(send, f.ring, (1, 3))


def halves_of(f):
    arrays = f.sources()
    first = 1 if f.other == "x" else 5
    rows, columns = arrays[0].shape[-2] // 4, arrays[0].shape[-1]

    def quarter(which):
        four = pl.BlockSpec((1, 1, rows, columns), lambda y, s: (0, y, s[first + which], 0))
        three = pl.BlockSpec((1, rows, columns), lambda y, s: (y, s[first + which], 0))
        return [four if a.ndim == 4 else three for a in arrays], arrays

    return quarter


def add(a, b, none):
    def kernel(_, a, b, out):
        out[...] = (a[...].astype(f32) + b[...].astype(f32)).astype(bf16)

    out = shape(a.shape, bf16)
    return call(kernel, out, (1,), [whole(a), whole(b)], whole(out), none, (a, b))


class Finish:
    def __init__(self, flows, extra, cuts):
        in_specs, args, sizes = [], [], []
        def half(spec):
            return pl.BlockSpec(
                spec.block_shape, lambda j, s: spec.index_map(lax.rem(j + s[9], 2), s)
            )

        for f in flows:
            specs, arrays = f.kept(0)
            dims = (1, 1, *f.got.shape[2:])
            specs = specs + [
                pl.BlockSpec(dims, lambda y, s: (0, y, 0, 0)),
                pl.BlockSpec((1, *f.last.shape[1:]), lambda y, s: (y, 0, 0)),
            ]
            in_specs += [half(spec) for spec in specs]
            args += arrays + [f.got, f.last]
            sizes.append((len(arrays) + 2, f.got.shape[2], f.got.shape[3] // STEP))
        for e in extra:
            in_specs.append(half(pl.BlockSpec((1, *e.shape[1:]), lambda y, s: (y, 0, 0))))
        args += extra
        rows = sum(u * n for _, u, n in sizes) + sum(e.shape[1] for e in extra)

        def kernel(_, *refs):
            send, mine = refs[-2:]
            j = pl.program_id(0)

            def put(here, value):
                @pl.when(j == 0)
                def _():
                    mine[here, :] = value

                @pl.when(j == 1)
                def _():
                    send[here, :] = value.astype(bf16)

            start, k = 0, 0
            for count, u, n in sizes:
                v = sum(value_of(r) for r in refs[k : k + count])[0]
                for i in range(n):
                    put(slice(start, start + u), v[:, i * STEP : (i + 1) * STEP])
                    start += u
                k += count
            for ref in refs[k:-2]:
                put(slice(start, start + ref.shape[1]), ref[0])
                start += ref.shape[1]

        out = (shape((rows, STEP), bf16), shape((rows, STEP), f32))
        send, self.mine = call(
            kernel, out, (2,), in_specs, [whole(o) for o in out], cuts, args
        )
        self.got = exchange(send, "y", (1, 3))

    def second(self, none):
        self.mine = add(self.mine, self.got, none)
        self.far = lax.ppermute(self.mine, "yh", [(0, 1), (1, 0)])

    def gather(self, none):
        return lax.all_gather(add(self.mine, self.far, none), ("c", "x", "z"), axis=0)


def per_device(
    tokens,
    memory,
    compressed,
    cotangent,
    ln1_g,
    ln1_b,
    w_q,
    w_kv,
    w_r,
    bias_u,
    bias_v,
    w_o,
    ln2_g,
    ln2_b,
    w_in,
    b_in,
    w_out,
    b_out,
    conv_w,
    conv_b,
):
    line.held, line.due = [], {}
    tokens, memory, compressed, cotangent = tokens[0], memory[0], compressed[0], cotangent[0]
    yl, core = lax.axis_index("yl"), lax.axis_index("c")
    place = {"x": lax.axis_index("x"), "z": lax.axis_index("z")}
    none = jnp.zeros((1,), jnp.int32)
    ints = lambda *v: jnp.stack([jnp.asarray(i, jnp.int32) for i in v])

    def thirds(rows):
        half = rows // 2
        other = (1 - yl) * half
        return [yl * half, other + core * (half // 2), other + (1 - core) * (half // 2)]

    def both(v):
        return (v, core_swap(v))

    spot = (place["x"] * 4 + place["z"]) * 2 + core
    piece = pack(
        (ln1_g, ln1_b, bias_u, bias_v, ln2_g, ln2_b, b_out, conv_b, b_in),
        w_in,
        w_out,
        ints(spot),
    )
    piece_got = exchange(piece, "y", (1, 3))

    kv_part, small, conv_part = pack_rows(w_kv, w_q, w_r, w_o, conv_w, ints(core))
    kv_got = exchange(kv_part, "y", (1, 3))
    small_got = exchange(small, "y", (1, 3))
    conv_got = exchange(conv_part, "y", (1, 3))

    def joined(w, got, twin):
        return jnp.concatenate([w, got, twin], axis=0)

    spread = lax.all_gather(piece_got[:-16], ("x", "z", "c"), axis=0)
    thirds_d = ints(*thirds(D))
    thirds_c = ints(*thirds(3 * D), *thirds(D))
    sinus_table = sinusoid(KEYS, D).astype(bf16)
    sinus_rel = jnp.concatenate(
        [
            lax.dynamic_slice_in_dim(sinus_table, thirds_d[i], width, 1)
            for i, width in enumerate(THIRDS)
        ],
        axis=1,
    )
    line.hold(sinus_rel)
    vectors, b_in = unpack(piece, piece_got, ints(yl))

    normed, normed_rel, oldest, old_quarters = first_norm(compressed, memory, tokens, vectors, thirds_d)
    both_normed, both_cot = both(normed), both(cotangent)
    own, first, far, second = quarters(place["x"], core)
    got = exchange(
        jnp.stack([pick(old_quarters, first, 0), pick(old_quarters, far, 0)]), "x", (1, 3)
    )
    got_far = exchange(jnp.stack([pick(old_quarters, second, 0), got[1]]), "x", (3, 1))
    old_ring = jnp.concatenate([pick(old_quarters, own, 0), got[0], got_far[0], got_far[1]])
    old_twin = core_swap(old_ring)
    kv_got, small_got = gate((kv_got, small_got), normed)
    kv_twin, small_twin = core_swap(kv_got), core_swap(small_got)
    kv_whole = joined(w_kv, kv_got, kv_twin)
    q_whole, r_whole, o_whole = [
        joined(w, small_got[i], small_twin[i]) for i, w in enumerate((w_q, w_r, w_o))
    ]
    key_value = dot(normed_rel, kv_whole).astype(bf16)
    line.hold(key_value)
    queries = dot(normed_rel[2 * T :], q_whole)
    relative = dot(sinus_rel, r_whole).astype(bf16)
    line.hold(queries, relative)
    line.hold(got)
    probs, attended = attend(queries, key_value, relative, vectors, none)
    line.hold(both_normed[1], both_cot[1], got_far)
    residual, normed2, normed2_rel = out_and_norm(attended, o_whole, tokens, vectors, thirds_d)
    both_n2, both_att = both(normed2), both(attended)

    cuts, rels, twins = [], [], []
    for ring in ("x", "z"):
        own, first, far, second = quarters(place[ring], core)
        cuts += [first, far, own, second]
        rels.append([own, first, second, far])
        twins.append([own, second, first, far])
    cuts = ints(core, *cuts, yl)

    def flows(groups):
        pairs = weight_grads(groups, cuts)
        return [Flow(ring, pair) for (ring, _), pair in zip(groups, pairs)]

    line.hold(old_twin)
    hidden, d_pre, mixed_out, d_normed2, d_b_in = feed_forward(
        normed2_rel, residual, cotangent, w_in, w_out, spread, b_in, vectors, ints(yl)
    )
    both_hidden, both_pre = both(hidden), both(d_pre)
    (conv_got,) = gate((conv_got,), hidden)
    conv_pieces = (conv_w, conv_got, core_swap(conv_got))
    d_residual, d_branch, d_attended, d_ln2_g, d_ln2_b, d_b_out = second_norm_back(
        cotangent, d_normed2, residual, vectors, o_whole, thirds_d
    )
    both_branch = both(d_branch)
    large = flows(
        [
            ("x", [(both_hidden, 0, T, both_cot, False)]),
            ("z", [(both_n2, 0, T, both_pre, False), (both_att, 0, T, both_branch, False)]),
        ]
    )
    d_kv, my_kv, give_kv, d_relative, d_queries, d_bias_u, d_bias_v = attend_back(
        queries, key_value, relative, vectors, probs, d_attended, ints(core)
    )
    both_kv = (my_kv, core_swap(give_kv))
    both_q, both_rel = both(d_queries), both(d_relative)

    compact, comp_normed = compress(oldest, conv_pieces, vectors, thirds_c)
    comp_pair = dot(comp_normed, kv_whole).astype(bf16)
    compressed_next = jnp.concatenate([compressed[T // 3 :], compact], axis=0)
    loss, d_ck, d_cv = reconstruct(queries, key_value, comp_pair, none)
    recon_loss = jnp.sum(loss) / (T * D)
    line.hold(both_kv[1], both_q[1], both_rel[1])
    d_compact, d_conv_b = compress_back(d_ck, d_cv, kv_whole, compact, vectors, thirds_d)
    ring_got = exchange(d_compact, "x", (1, 3))
    line.hold(ring_got)
    onward(large, cuts)
    ring_pair = jnp.concatenate([d_compact, ring_got])
    near = flows(
        [
            ("x", [(both_normed, 0, KEYS, both_kv, True)]),
            (
                "z",
                [
                    (both_normed, 2, T, both_q, False),
                    ((sinus_table,), 0, KEYS, both_rel, False),
                ],
            ),
        ]
    )
    pair_got = exchange(ring_pair, "x", (3, 1))
    line.hold(pair_got)
    turn(large, cuts)
    compact_ring = jnp.concatenate([ring_pair, pair_got])
    d_tokens, d_ln1_g, d_ln1_b = first_norm_back(
        d_kv, d_queries, kv_whole, q_whole, compressed, memory, tokens, vectors, d_residual,
        thirds_d,
    )
    line.hold(compact_ring)
    onward(large, cuts)
    conv = Flow(
        "x", None, conv_grad(old_ring, old_twin, compact_ring, core_swap(compact_ring), cuts)
    )
    early = Finish(large, [], cuts)
    onward(near, cuts)
    early.second(none)
    late_flows = [*near, conv]
    turn(late_flows, cuts)
    early_sums = early.gather(none)
    onward(late_flows, cuts)

    total = jnp.concatenate(
        [d_ln1_g, d_ln1_b, d_bias_u, d_bias_v, d_ln2_g, d_ln2_b, d_b_out, d_conv_b]
        + [d_b_in]
    )
    total = jnp.concatenate(
        [
            total[:8].reshape(8, 2, STEP).transpose(1, 0, 2),
            total[8:].reshape(2, 4, STEP),
            jnp.zeros((2, 4, STEP), f32),
        ],
        axis=1,
    )
    late = Finish(late_flows, [total], cuts)
    late.second(none)
    line.hold(early_sums)
    late_sums = late.gather(none)

    g_out, g_in, g_o = widen(
        early_sums, [(FF // 2, D, "x"), (D // 2, FF, "z"), (D // 2, D, "z")], none
    )
    g_kv, g_q, g_r, g_conv = widen(
        late_sums,
        [(D // 2, 2 * D, "x"), (D // 2, D, "z"), (D // 2, D, "z"), (3 * D // 2, D, "x")],
        none,
    )
    half = jnp.sum(late_sums[:, 224:236].astype(f32), axis=0)
    t_ln1_g, t_ln1_b, t_bu, t_bv, t_ln2_g, t_ln2_b, t_bout, t_convb = [half[i] for i in range(8)]
    t_bin = half[8:].reshape(-1)
    return (
        mixed_out[None],
        compressed_next[None],
        recon_loss[None],
        d_tokens[None],
        t_ln1_g,
        t_ln1_b,
        g_q,
        g_kv,
        g_r,
        t_bu,
        t_bv,
        g_o,
        t_ln2_g,
        t_ln2_b,
        g_in,
        t_bin,
        g_out,
        t_bout,
        g_conv,
        t_convb,
    )


def solution(mesh):
    fine = Mesh(mesh.devices.reshape(2, 4, 4, 2, 2), AXES)
    stream = P(AXES, None, None)
    vec, mat = P("yl"), P("yl", None)
    weights = (vec, vec, mat, mat, mat, vec, vec, mat, vec, vec, mat, vec, mat, vec, mat, vec)
    return jax.shard_map(
        per_device,
        mesh=fine,
        in_specs=(stream,) * 4 + weights,
        out_specs=(stream, stream, P(AXES), stream) + weights,
        check_vma=False,
    )
```

```python
import jax
import jax.numpy as jnp
from jax import lax
from jax.experimental import pallas as pl
from jax.experimental.pallas import tpu as pltpu
from jax.sharding import Mesh, PartitionSpec as P

H = 8
HD = 128
D = 1024
T = 192
KEYS = 576
PAD = 640
FF = 4096
FACTOR = HD ** (-0.5)
f32 = jnp.float32
bf16 = jnp.bfloat16
AXES = ("yh", "x", "z", "c", "yl")
RING = {"x": ("x", "c"), "z": ("z", "c"), "y": ("yh", "c", "yl")}


def sinusoid(key_count, model_dim):
    distance = (key_count - 1 - jnp.arange(key_count)).astype(f32)
    inverse = 1.0 / 10000.0 ** (jnp.arange(0, model_dim, 2).astype(f32) / model_dim)
    angles = distance[:, None] * inverse[None, :]
    return jnp.concatenate([jnp.sin(angles), jnp.cos(angles)], axis=-1)


def dot(a, b):
    return jnp.dot(a, b, preferred_element_type=f32)


def dot_t(a, b):
    return lax.dot_general(a, b, (((1,), (1,)), ((), ())), preferred_element_type=f32)


def t_dot(a, b):
    return lax.dot_general(a, b, (((0,), (0,)), ((), ())), preferred_element_type=f32)


class Line:
    def __init__(self):
        self.held, self.due = [], {}

    def hold(self, *values):
        self.held += values

    def expect(self, gap, *values):
        self.due.setdefault(gap, []).extend(values)

    def ran(self, result):
        self.held = [result, *self.due.get(1, [])]
        self.due = {gap - 1: values for gap, values in self.due.items() if gap > 1}

    def later(self, value):
        return lax.optimization_barrier((value, *self.held))[0] if self.held else value


line = Line()


def call(kernel, out, grid, in_specs, out_specs, scalars, args, scratch=()):
    held, n = line.held, len(args)

    def body(s, *refs):
        kernel(s, *refs[:n], *refs[n + len(held) :])

    result = pl.pallas_call(
        body,
        out_shape=out,
        grid_spec=pltpu.PrefetchScalarGridSpec(
            num_scalar_prefetch=1,
            grid=grid,
            in_specs=list(in_specs) + [pl.BlockSpec(memory_space=pl.ANY)] * len(held),
            out_specs=out_specs,
            scratch_shapes=list(scratch),
        ),
        compiler_params=pltpu.CompilerParams(vmem_limit_bytes=56 << 20),
    )(scalars, *args, *held)
    line.ran(jax.tree.leaves(result)[0])
    return result


def gate(values, *after):
    n = len(values)
    anywhere = pl.BlockSpec(memory_space=pl.ANY)
    return pl.pallas_call(
        lambda *refs: None,
        out_shape=[jax.ShapeDtypeStruct(v.shape, v.dtype) for v in values],
        in_specs=[anywhere] * (n + len(after)),
        out_specs=[anywhere] * n,
        input_output_aliases={i: i for i in range(n)},
    )(*values, *after)


def whole(a):
    zeros = (0,) * a.ndim
    return pl.BlockSpec(a.shape, lambda *_: zeros)


def shape(dims, dtype):
    return jax.ShapeDtypeStruct(dims, dtype)


def at(offset):
    return pl.multiple_of(offset, 128)


def center_scale(v):
    mid = v - jnp.mean(v, axis=-1, keepdims=True)
    r = lax.rsqrt(jnp.mean(mid * mid, axis=-1, keepdims=True) + 1e-5)
    return mid * r, r


def norm_back(xhat, r, g, dn):
    gd = dn * g
    return r * (
        gd
        - jnp.mean(gd, axis=-1, keepdims=True)
        - xhat * jnp.mean(gd * xhat, axis=-1, keepdims=True)
    )


def softmax(s):
    e = jnp.exp(s - jnp.max(s, axis=-1, keepdims=True))
    return e / jnp.sum(e, axis=-1, keepdims=True)


(LN1_G, LN1_B, BIAS_U, BIAS_V, LN2_G, LN2_B, B_OUT, CONV_B) = range(8)


def row(ref, i):
    return ref[i : i + 1, :]


def pack(vectors, w_in, w_out, scalars):
    n_in, n_out = (w.shape[0] // 32 for w in (w_in, w_out))
    chunks = FF // D
    rows = n_out + n_in * chunks
    half = D // 2

    def kernel(_, *refs):
        wi, wo, piece, flat = refs[-4:]
        flat[...] = jnp.zeros_like(flat)
        for i, ref in enumerate(refs[:8]):
            flat[i : i + 1, :half] = ref[...].astype(f32).reshape(1, half)
        flat[8 : 8 + FF // 2 // D, :] = refs[8][...].astype(f32).reshape(FF // 2 // D, D)
        piece[:n_out, :] = wo[...]
        for i in range(chunks):
            piece[n_out + i * n_in : n_out + (i + 1) * n_in, :] = wi[:, i * D : (i + 1) * D]
        piece[rows:, :] = flat[...].astype(bf16)

    out = shape((rows + 16, D), bf16)
    return call(
        kernel,
        out,
        (1,),
        [whole(v) for v in vectors]
        + [
            pl.BlockSpec((w.shape[0] // 32, w.shape[1]), lambda j, s: (s[0], 0))
            for w in (w_in, w_out)
        ],
        whole(out),
        scalars,
        (*vectors, w_in, w_out),
        [pltpu.VMEM((16, D), f32)],
    )


def pack_rows(w_kv, w_q, w_r, w_o, conv_w, scalars):
    n, n_conv = w_q.shape[0] // 2, conv_w.shape[0] // 2

    def kernel(_, kv, q, r, o, conv, kv_out, out, o_out, conv_out):
        kv_out[...] = kv[...]
        out[0] = q[...]
        out[1] = r[...]
        o_out[...] = o[...]
        conv_out[...] = conv[...]

    args = (w_kv, w_q, w_r, w_o, conv_w)
    out = (
        shape((n, 2 * D), bf16),
        shape((2, n, D), bf16),
        shape((n, D), bf16),
        shape((n_conv, D), bf16),
    )
    return call(
        kernel,
        out,
        (1,),
        [pl.BlockSpec((w.shape[0] // 2, w.shape[1]), lambda j, s: (s[0], 0)) for w in args],
        [whole(o) for o in out],
        scalars,
        args,
    )


def unpack(mine, theirs, scalars):
    half = D // 2
    at_row = mine.shape[0] // 16 - 1
    tail = pl.BlockSpec((16, D), lambda j, s: (at_row, 0))

    def kernel(s, mine, theirs, vectors, b_in):
        a, b = mine[...].astype(f32), theirs[...].astype(f32)
        low = jnp.where(s[0] == 0, a, b)
        high = jnp.where(s[0] == 0, b, a)
        vectors[:, :half] = low[:8, :half]
        vectors[:, half:] = high[:8, :half]
        rows = FF // 2 // D
        b_in[:rows] = low[8 : 8 + rows]
        b_in[rows:] = high[8 : 8 + rows]

    out = (shape((8, D), f32), shape((FF // D, D), f32))
    return call(
        kernel, out, (1,), [tail, tail], [whole(o) for o in out], scalars, (mine, theirs)
    )


def relative_columns(x, s, widths):
    parts = [x[:, pl.ds(at(s[i]), width)] for i, width in enumerate(widths)]
    return jnp.concatenate(parts, axis=1)


def natural_columns(out, x, s, widths):
    start = 0
    for i, width in enumerate(widths):
        out[:, pl.ds(at(s[i]), width)] = x[:, start : start + width]
        start += width


THIRDS = (D // 2, D // 4, D // 4)


def first_norm(compressed, memory, tokens, vectors, offsets):
    def kernel(s, comp, mem, tok, vec, out, out_rel, old, old_quarters):
        gain, bias = row(vec, LN1_G), row(vec, LN1_B)

        def part(ref, base):
            for i in range(0, T, 32):
                xhat, r = center_scale(ref[i : i + 32, :].astype(f32))
                out[base + i : base + i + 32, :] = (xhat * gain + bias).astype(bf16)

        part(comp, 0)
        part(mem, T)
        part(tok, 2 * T)
        out_rel[...] = relative_columns(out, s, THIRDS)
        line_of = lax.broadcasted_iota(jnp.int32, (T // 3, T), 0)
        col = lax.broadcasted_iota(jnp.int32, (T // 3, T), 1)
        low = mem[...].astype(bf16)
        for tap in range(3):
            take = jnp.where(col == 3 * line_of + tap, 1.0, 0.0).astype(bf16)
            old[:, tap * D : (tap + 1) * D] = dot(take, low).astype(bf16)
        width = 3 * D // 8
        for q in range(4):
            for y in range(2):
                begin = y * 3 * D // 2 + q * width
                old_quarters[q, :, y * width : (y + 1) * width] = old[:, begin : begin + width]

    args = (compressed, memory, tokens, vectors)
    out = (
        shape((KEYS, D), bf16),
        shape((KEYS, D), bf16),
        shape((T // 3, 3 * D), bf16),
        shape((4, T // 3, 3 * D // 4), bf16),
    )
    return call(
        kernel, out, (1,), [whole(a) for a in args], [whole(o) for o in out], offsets, args
    )


def head(n, rows, row_block=0, first=0):
    return pl.BlockSpec((rows, n * HD), lambda h, s: (row_block, first // n + h))


def columns_of(n):
    return [slice(i * HD, (i + 1) * HD) for i in range(n)]


def attend(queries, key_value, relative, vectors, none):
    n = 2

    def kernel(_, q, k, v, rel, vec, probs, out):
        pad = jnp.zeros((PAD - KEYS, HD), bf16)
        i = lax.broadcasted_iota(jnp.int32, (T, PAD), 0)
        j = lax.broadcasted_iota(jnp.int32, (T, PAD), 1)
        seen = j <= i + (KEYS - T)
        cuts = columns_of(n)
        content = [((q[:, c] + vec[BIAS_U : BIAS_U + 1, c]) * FACTOR).astype(bf16) for c in cuts]
        located = [((q[:, c] + vec[BIAS_V : BIAS_V + 1, c]) * FACTOR).astype(bf16) for c in cuts]
        raw = [
            dot_t(x, jnp.concatenate([rel[:, c], pad], axis=0)) for x, c in zip(located, cuts)
        ]
        near = [dot_t(x, jnp.concatenate([k[:, c], pad], axis=0)) for x, c in zip(content, cuts)]
        raw = [pltpu.roll(x, PAD - T + 1, 1, stride=1, stride_axis=0) for x in raw]
        p = [softmax(jnp.where(seen, a + b, -1e30)) for a, b in zip(near, raw)]
        for h, c in enumerate(cuts):
            probs[h] = p[h]
            value = jnp.concatenate([v[:, c], pad], axis=0)
            out[:, c] = dot(p[h].astype(bf16), value).astype(bf16)

    return call(
        kernel,
        (shape((H, T, PAD), f32), shape((T, D), bf16)),
        (H // n,),
        [head(n, T), head(n, KEYS), head(n, KEYS, 0, H), head(n, KEYS), head(n, 8)],
        [pl.BlockSpec((n, T, PAD), lambda h, s: (h, 0, 0)), head(n, T)],
        none,
        (queries, key_value, key_value, relative, vectors),
    )


def attend_back(queries, key_value, relative, vectors, probs, d_attended, scalars):
    n = 2

    def kernel(s, q, k, v, rel, vec, probs, d_att, d_kv, mine, give, d_rel, d_q, d_bu, d_bv):
        pad = jnp.zeros((PAD - KEYS, HD), bf16)
        i = lax.broadcasted_iota(jnp.int32, (T, T), 0)
        j = lax.broadcasted_iota(jnp.int32, (T, T), 1)
        flip = jnp.where(i + j == T - 1, 1.0, 0.0).astype(bf16)
        cuts = columns_of(n)
        content = [((q[:, c] + vec[BIAS_U : BIAS_U + 1, c]) * FACTOR).astype(bf16) for c in cuts]
        located = [((q[:, c] + vec[BIAS_V : BIAS_V + 1, c]) * FACTOR).astype(bf16) for c in cuts]
        da = [d_att[:, c] for c in cuts]
        d_p = [dot_t(x, jnp.concatenate([v[:, c], pad], axis=0)) for x, c in zip(da, cuts)]
        d_v = [t_dot(probs[h].astype(bf16), x)[:KEYS].astype(bf16) for h, x in enumerate(da)]
        d_s = []
        for h, x in enumerate(d_p):
            p = probs[h]
            d_s.append((p * (x - jnp.sum(p * x, axis=-1, keepdims=True))).astype(bf16))
        d_raw = [dot(flip, x) for x in d_s]
        d_c = [
            dot(x, jnp.concatenate([k[:, c], pad], axis=0)) * FACTOR for x, c in zip(d_s, cuts)
        ]
        d_k = [t_dot(x, y)[:KEYS].astype(bf16) for x, y in zip(d_s, content)]
        d_raw = [pltpu.roll(x, 0, 1, stride=1, stride_axis=0).astype(bf16) for x in d_raw]
        d_raw = [dot(flip, x).astype(bf16) for x in d_raw]
        d_l = [
            dot(x, jnp.concatenate([rel[:, c], pad], axis=0)) * FACTOR for x, c in zip(d_raw, cuts)
        ]
        for h, c in enumerate(cuts):
            d_rel[:, c] = t_dot(d_raw[h], located[h])[:KEYS].astype(bf16)
            d_kv[0, :, c] = d_k[h]
            d_kv[1, :, c] = d_v[h]
            mine[:, c] = jnp.where(s[0] == 0, d_k[h], d_v[h])
            give[:, c] = jnp.where(s[0] == 0, d_v[h], d_k[h])
            d_q[:, c] = (d_c[h] + d_l[h]).astype(bf16)
            d_bu[:, c] = jnp.sum(d_c[h], axis=0, keepdims=True)
            d_bv[:, c] = jnp.sum(d_l[h], axis=0, keepdims=True)

    return call(
        kernel,
        (shape((2, KEYS, D), bf16),)
        + (shape((KEYS, D), bf16),) * 3
        + (shape((T, D), bf16), shape((1, D), f32), shape((1, D), f32)),
        (H // n,),
        [
            head(n, T),
            head(n, KEYS),
            head(n, KEYS, 0, H),
            head(n, KEYS),
            head(n, 8),
            pl.BlockSpec((n, T, PAD), lambda h, s: (h, 0, 0)),
            head(n, T),
        ],
        [
            pl.BlockSpec((2, KEYS, n * HD), lambda h, s: (0, 0, h)),
            head(n, KEYS),
            head(n, KEYS),
            head(n, KEYS),
            head(n, T),
            head(n, 1),
            head(n, 1),
        ],
        scalars,
        (queries, key_value, key_value, relative, vectors, probs, d_attended),
    )


def out_and_norm(attended, w_o, tokens, vectors, offsets):
    def kernel(s, att, w, tok, vec, res, n2, n2_rel):
        total = tok[...].astype(f32) + dot(relative_columns(att, s, THIRDS), w[...])
        res[...] = total
        xhat, r = center_scale(total)
        n2[...] = (xhat * row(vec, LN2_G) + row(vec, LN2_B)).astype(bf16)
        other = at(D // 2 - s[0])
        n2_rel[:, : D // 2] = n2[:, pl.ds(at(s[0]), D // 2)]
        n2_rel[:, D // 2 :] = n2[:, pl.ds(other, D // 2)]

    args = (attended, w_o, tokens, vectors)
    out = (shape((T, D), f32), shape((T, D), bf16), shape((T, D), bf16))
    return call(
        kernel, out, (1,), [whole(a) for a in args], [whole(o) for o in out], offsets, args
    )


STEP = 512
UNITS = 1024
HALF = FF // 2 // UNITS


def feed_forward(n2_rel, residual, cotangent, w_in, w_out, spread, b_in, vectors, scalars):
    n_in = w_in.shape[0] // 32
    n_out = w_out.shape[0] // 32
    skip = n_out // n_in
    per = UNITS // n_out
    K_NORM = 0.7978845608028654

    def natural(j, s):
        return lax.rem(j + s[0] * HALF, 2 * HALF)

    def kernel(s, n2, res, cot, wi0, wi1, wo0, wo1, bi, vec, hid, dpre, mixed, dn2, dbi, acc, back):
        j = pl.program_id(0)
        n = natural(j, s)

        @pl.when(j == 0)
        def _():
            acc[...] = jnp.zeros_like(acc)
            back[...] = jnp.zeros_like(back)

        wo = jnp.where(j < HALF, wo0[...], wo1[...].reshape(UNITS, D))
        win = jnp.concatenate([wi0[...], wi1[...].reshape(D // 2, UNITS)], axis=0)
        pre = dot(n2[...], win) + bi[pl.ds(n, 1), :]
        d_hidden = dot_t(cot[...], wo)
        square = pre * pre
        t = jnp.tanh(K_NORM * pre * (1.0 + 0.044715 * square))
        gate_ = 0.5 * (1.0 + t)
        hidden = (pre * gate_).astype(bf16)
        slope = gate_ + (0.5 * K_NORM) * pre * (1.0 - t * t) * (1.0 + (3 * 0.044715) * square)
        d_pre = (d_hidden * slope).astype(bf16)
        hid[...] = hidden
        dpre[...] = d_pre
        dbi[pl.ds(n, 1), :] = jnp.sum(d_pre.astype(f32), axis=0, keepdims=True)
        acc[...] += dot(hidden, wo)
        back[...] += dot_t(d_pre, win)

        @pl.when(j == 2 * HALF - 1)
        def _():
            mixed[...] = (res[...] + acc[...] + row(vec, B_OUT)).astype(bf16)
            dn2[:, pl.ds(at(s[0] * (D // 2)), D // 2)] = back[:, : D // 2]
            dn2[:, pl.ds(at((1 - s[0]) * (D // 2)), D // 2)] = back[:, D // 2 :]

    out = (
        shape((T, FF), bf16),
        shape((T, FF), bf16),
        shape((T, D), bf16),
        shape((T, D), f32),
        shape((2 * HALF, UNITS), f32),
    )
    by_unit = pl.BlockSpec((T, UNITS), lambda j, s: (0, natural(j, s)))
    return call(
        kernel,
        out,
        (2 * HALF,),
        [
            whole(n2_rel),
            whole(residual),
            whole(cotangent),
            pl.BlockSpec((D // 2, UNITS), lambda j, s: (0, natural(j, s))),
            pl.BlockSpec((32, n_in, UNITS), lambda j, s: (0, skip + natural(j, s), 0)),
            pl.BlockSpec((UNITS, D), lambda j, s: (jnp.minimum(j, HALF - 1), 0)),
            pl.BlockSpec(
                (per, n_out, D), lambda j, s: (jnp.maximum(j - HALF, 0), 0, 0)
            ),
            whole(b_in),
            whole(vectors),
        ],
        [by_unit, by_unit, whole(out[2]), whole(out[3]), whole(out[4])],
        scalars,
        (n2_rel, residual, cotangent, w_in, spread, w_out, spread, b_in, vectors),
        [pltpu.VMEM((T, D), f32), pltpu.VMEM((T, D), f32)],
    )


def second_norm_back(cotangent, d_n2, residual, vectors, w_o, offsets):
    def kernel(s, cot, dn, res, vec, w, d_res, d_br, d_att, dg, db, dbo):
        xhat, r = center_scale(res[...])
        dn, wide = dn[...], cot[...].astype(f32)
        dg[...] = jnp.sum(dn * xhat, axis=0, keepdims=True)
        db[...] = jnp.sum(dn, axis=0, keepdims=True)
        dbo[...] = jnp.sum(wide, axis=0, keepdims=True)
        total = wide + norm_back(xhat, r, row(vec, LN2_G), dn)
        d_res[...] = total
        low = total.astype(bf16)
        d_br[...] = low
        natural_columns(d_att, dot_t(low, w[...]).astype(bf16), s, THIRDS)

    args = (cotangent, d_n2, residual, vectors, w_o)
    out = (
        shape((T, D), f32),
        shape((T, D), bf16),
        shape((T, D), bf16),
        shape((1, D), f32),
        shape((1, D), f32),
        shape((1, D), f32),
    )
    return call(
        kernel, out, (1,), [whole(a) for a in args], [whole(o) for o in out], offsets, args
    )


def first_norm_back(d_kv, d_q, w_kv, w_q, compressed, memory, tokens, vectors, d_res, offsets):
    steps = 4
    wide, slim = 2 * D // steps, D // steps

    def kernel(s, dkv, dq, kw, qw, comp, mem, tok, vec, dres, dtok, dg, db, acc, nat, xh, rs):
        j = pl.program_id(0)

        def product(start):
            value = dot_t(dkv[0], kw[...])
            if start:
                acc[...] = value
            else:
                acc[...] += value
            acc[2 * T :, :] += dot_t(dq[...], qw[...])

        for block, ref in enumerate((comp, mem, tok)):

            @pl.when(j == block)
            def _(block=block, ref=ref):
                product(block == 0)
                for i in range(0, T, 32):
                    xhat, r = center_scale(ref[i : i + 32, :].astype(f32))
                    xh[block * T + i : block * T + i + 32, :] = xhat
                    if block == 2:
                        rs[i : i + 32, :] = jnp.broadcast_to(r, (32, HD))

        @pl.when(j == steps - 1)
        def _():
            product(False)
            natural_columns(nat, acc, s, THIRDS)
            gain = row(vec, LN1_G)
            sum_g = jnp.zeros((8, D), f32)
            sum_b = jnp.zeros((8, D), f32)
            for i in range(0, KEYS, 32):
                dn, xhat = nat[i : i + 32, :], xh[i : i + 32, :]
                both = dn * xhat
                sum_g += (both[:8] + both[8:16]) + (both[16:24] + both[24:])
                sum_b += (dn[:8] + dn[8:16]) + (dn[16:24] + dn[24:])
                if i >= 2 * T:
                    k = i - 2 * T
                    r = rs[k : k + 32, :1]
                    dtok[k : k + 32, :] = dres[k : k + 32, :] + norm_back(xhat, r, gain, dn)
            dg[...] = jnp.sum(sum_g, axis=0, keepdims=True)
            db[...] = jnp.sum(sum_b, axis=0, keepdims=True)

    rest = (compressed, memory, tokens, vectors, d_res)
    out = (shape((T, D), f32), shape((1, D), f32), shape((1, D), f32))
    return call(
        kernel,
        out,
        (steps,),
        [
            pl.BlockSpec((1, KEYS, wide), lambda j, s: (j // (steps // 2), 0, lax.rem(j, steps // 2))),
            pl.BlockSpec((T, slim), lambda j, s: (0, j)),
            pl.BlockSpec((D, wide), lambda j, s: (0, j)),
            pl.BlockSpec((D, slim), lambda j, s: (0, j)),
        ]
        + [whole(a) for a in rest],
        [whole(o) for o in out],
        offsets,
        (d_kv, d_q, w_kv, w_q, *rest),
        [pltpu.VMEM((KEYS, D), f32)] * 3 + [pltpu.VMEM((T, HD), f32)],
    )


def compress(oldest, pieces, vectors, offsets):
    block = 256
    rows = T // 3

    def kernel(s, x, w0, w1, w2, vec, compact, normed, x_rel, natural):
        j = pl.program_id(0)

        @pl.when(j == 0)
        def _():
            x_rel[...] = relative_columns(x, s, (3 * D // 2, 3 * D // 4, 3 * D // 4))

        w = jnp.concatenate([w0[...], w1[...], w2[...]], axis=0)
        here = pl.ds(at(j * block), block)
        compact[:, here] = dot(x_rel[...], w) + vec[CONV_B : CONV_B + 1, here]

        @pl.when(j == D // block - 1)
        def _():
            xhat, r = center_scale(compact[...])
            natural[...] = (xhat * row(vec, LN1_G) + row(vec, LN1_B)).astype(bf16)
            start = 0
            for i, width in enumerate(THIRDS):
                normed[:, start : start + width] = natural[:, pl.ds(at(s[3 + i]), width)]
                start += width

    out = (shape((rows, D), f32), shape((rows, D), bf16))
    return call(
        kernel,
        out,
        (D // block,),
        [whole(oldest)]
        + [pl.BlockSpec((w.shape[0], block), lambda j, s: (0, j)) for w in pieces]
        + [whole(vectors)],
        [whole(o) for o in out],
        offsets,
        (oldest, *pieces, vectors),
        [pltpu.VMEM((rows, 3 * D), bf16), pltpu.VMEM((rows, D), bf16)],
    )


def reconstruct(queries, key_value, comp_pair, none):
    rows = T // 3
    n = 4

    def kernel(_, q, k, v, ck, cv, loss, dck, dcv):
        cuts = columns_of(n)
        asking = [(q[:, c] * FACTOR).astype(bf16) for c in cuts]
        far = [dot_t(x, k[:, c]) for x, c in zip(asking, cuts)]
        near = [dot_t(x, ck[:, c]) for x, c in zip(asking, cuts)]
        p = [softmax(x).astype(bf16) for x in far]
        gp = [softmax(x) for x in near]
        low = [x.astype(bf16) for x in gp]
        miss = [dot(p[h], v[:, c]) - dot(low[h], cv[:, c]) for h, c in enumerate(cuts)]
        total = sum(jnp.sum(x * x, axis=0, keepdims=True) for x in miss)
        d_guess = [((-2.0 / (T * D)) * x).astype(bf16) for x in miss]
        d_gp = [dot_t(x, cv[:, c]) for x, c in zip(d_guess, cuts)]
        d_gs = [
            (x * (y - jnp.sum(x * y, axis=-1, keepdims=True))).astype(bf16)
            for x, y in zip(gp, d_gp)
        ]
        for h, c in enumerate(cuts):
            dcv[:, c] = t_dot(low[h], d_guess[h]).astype(bf16)
            dck[:, c] = t_dot(d_gs[h], asking[h]).astype(bf16)

        @pl.when(pl.program_id(0) == 0)
        def _():
            loss[...] = total

        @pl.when(pl.program_id(0) > 0)
        def _():
            loss[...] += total

    return call(
        kernel,
        (shape((1, HD), f32), shape((rows, D), bf16), shape((rows, D), bf16)),
        (H // n,),
        [head(n, T), head(n, T, 1), head(n, T, 1, H), head(n, rows), head(n, rows, 0, H)],
        [pl.BlockSpec((1, HD), lambda h, s: (0, 0)), head(n, rows), head(n, rows)],
        none,
        (queries, key_value, key_value, comp_pair, comp_pair),
    )


def compress_back(dck, dcv, w_kv, compact, vectors, offsets):
    rows = T // 3

    def kernel(s, dck, dcv, w, compact, vec, d_compact, d_bias, dn):
        back = dot_t(jnp.concatenate([dck[...], dcv[...]], axis=1), w[...])
        natural_columns(dn, back, s, THIRDS)
        xhat, r = center_scale(compact[...])
        low = norm_back(xhat, r, row(vec, LN1_G), dn[...]).astype(bf16)
        d_compact[...] = low
        d_bias[...] = jnp.sum(low.astype(f32), axis=0, keepdims=True)

    args = (dck, dcv, w_kv, compact, vectors)
    out = (shape((rows, D), bf16), shape((1, D), f32))
    return call(
        kernel,
        out,
        (1,),
        [whole(a) for a in args],
        [whole(o) for o in out],
        offsets,
        args,
        [pltpu.VMEM((rows, D), f32)],
    )


def weight_grads(groups, scalars):
    in_specs, args, outs, out_specs, layout, scratch = [], [], [], [], [], []
    for ring, jobs in groups:
        first = 1 if ring == "x" else 5
        block = jobs[0][0][0].shape[1] // 8
        plan = []
        for xs, row_block, rows, dys, ready in jobs:
            width = dys[0].shape[1] // (1 if ready else 2)
            plan.append((width, rows, len(xs)))
            for x in xs:
                for y in range(2):
                    in_specs.append(
                        pl.BlockSpec(
                            (rows, block),
                            lambda q, s, r=row_block, f=first, y=y: (r, y * 4 + s[f + q]),
                        )
                    )
                    args.append(x)
            for dy in dys:
                in_specs.append(
                    pl.BlockSpec((rows, width), lambda q, s, r=ready: (0, 0 if r else s[0]))
                )
                args.append(dy)
            scratch.append(pltpu.VMEM((rows * len(xs), width), bf16))
        dims = (1, 2, block, sum(p[0] for p in plan))
        outs += [shape((2, *dims[1:]), bf16)] * 2
        out_specs += [
            pl.BlockSpec(dims, lambda q, s: (jnp.minimum(q, 1), 0, 0, 0)),
            pl.BlockSpec(dims, lambda q, s: (jnp.maximum(q - 2, 0), 0, 0, 0)),
        ]
        layout.append(plan)
    n_in, n_out = len(in_specs), len(outs)

    def kernel(s, *refs):
        ins, results, joined = refs[:n_in], refs[n_in : n_in + n_out], refs[n_in + n_out :]
        q = pl.program_id(0)

        @pl.when(q == 0)
        def _():
            place, k = 0, 0
            for plan in layout:
                for _, rows, n in plan:
                    da, db = ins[place + 2 * n], ins[place + 2 * n + 1]
                    if n == 2:
                        joined[k][:rows, :] = da[...]
                        joined[k][rows:, :] = db[...]
                    else:
                        joined[k][...] = (da[...].astype(f32) + db[...].astype(f32)).astype(bf16)
                    place += 2 * n + 2
                    k += 1

        place, k = 0, 0
        for i, plan in enumerate(layout):
            send, keep = results[2 * i : 2 * i + 2]
            block = send.shape[2]
            start = 0
            for width, rows, n in plan:
                x = jnp.concatenate([r[...] for r in ins[place : place + 2]], axis=1)
                if n == 2:
                    other = jnp.concatenate([r[...] for r in ins[place + 2 : place + 4]], axis=1)
                    x = jnp.concatenate([x, other], axis=0)
                value = t_dot(x, joined[k][...]).astype(bf16).reshape(2, block, width)
                cut = slice(start, start + width)
                send[0, :, :, cut] = jnp.where(q < 2, value, send[0, :, :, cut])
                keep[0, :, :, cut] = value
                start += width
                place += 2 * n + 2
                k += 1

    flat = call(kernel, tuple(outs), (4,), in_specs, out_specs, scalars, args, scratch)
    return [(flat[2 * i], flat[2 * i + 1]) for i in range(len(groups))]


def conv_grad(x, x_twin, dy, dy_twin, scalars):
    rows, columns = x.shape[1] // 2, D // 2

    def kernel(s, xa, xb, da, db, out):
        both = jnp.concatenate([xa[...], xb[...]], axis=0)
        total = t_dot(both, jnp.concatenate([da[...], db[...]], axis=0))
        out[...] = total.reshape(2, rows, columns)

    half = pl.BlockSpec((dy.shape[0], columns), lambda j, s: (0, s[0]))
    out = shape((2, rows, columns), f32)
    return call(
        kernel,
        out,
        (1,),
        [whole(x), whole(x_twin), half, half],
        whole(out),
        scalars,
        (x, x_twin, dy, dy_twin),
    )


def widen(gathered, plan, none):
    outs, specs, layout = [], [], []
    start = 0
    for rows, columns, ring in plan:
        u, chunks = rows // 16, columns // 2 // STEP
        outs.append(shape((4, 4, u, columns), f32))
        if ring == "x":
            specs.append(
                pl.BlockSpec((1, 4, u, chunks * STEP), lambda c, x, s: (x, 0, 0, c))
            )
        else:
            specs.append(
                pl.BlockSpec((4, 1, u, chunks * STEP), lambda c, x, s: (0, x, 0, c))
            )
        layout.append((start, u, chunks, ring))
        start += u * chunks

    def kernel(_, src, *results):
        for out, (start, u, chunks, ring) in zip(results, layout):
            for k in range(chunks):
                cut = slice(k * STEP, (k + 1) * STEP)
                for z in range(4):
                    value = src[z, start + k * u : start + (k + 1) * u, :].astype(f32)
                    if ring == "x":
                        out[0, z, :, cut] = value
                    else:
                        out[z, 0, :, cut] = value

    results = call(
        kernel,
        tuple(outs),
        (2, 4),
        [pl.BlockSpec((4, gathered.shape[1], STEP), lambda c, x, s: (c * 4 + x, 0, 0))],
        specs,
        none,
        (gathered,),
    )
    return [r.reshape(rows, columns) for r, (rows, columns, _) in zip(results, plan)]


def core_swap(v):
    return lax.ppermute(v, "c", [(0, 1), (1, 0)])


def pair_swap(v):
    return lax.ppermute(v, "yl", [(0, 1), (1, 0)])


def exchange(v, ring, masks):
    def flat(i, c):
        return (i // 2 * 2 + c) * 2 + i % 2 if ring == "y" else 2 * i + c

    pairs = [(flat(i, c), flat(i ^ masks[c], c)) for i in range(4) for c in range(2)]
    return lax.ppermute(v, RING[ring], pairs)


def pick(v, index, axis):
    return lax.dynamic_index_in_dim(v, index, axis, keepdims=False)


def quarters(place, core):
    first = jnp.where(core == 0, 1, 3)
    second = jnp.where(core == 0, 3, 1)
    return place, place ^ first, place ^ 2, place ^ second


class Flow:
    def __init__(self, ring, pair, done=None):
        self.ring, self.other = ring, "z" if ring == "x" else "x"
        self.before, self.result = None, done
        if done is None:
            self.send, self.keep = pair

    def start(self):
        self.got = exchange(self.send, self.ring, (1, 3))

    def sources(self):
        return [self.keep, self.got, self.last] if self.result is None else [self.result]

    def kept(self, which):
        if self.before is None:
            dims = (1, 1, *self.keep.shape[2:])
            return [pl.BlockSpec(dims, lambda y, s: (which, y, 0, 0))], [self.keep]
        return self.before(2 + which)


def onward(flows, cuts):
    in_specs, args, counts = [], [], []
    for f in flows:
        specs, arrays = f.kept(1)
        dims = (1, 1, *f.got.shape[2:])
        in_specs += specs + [pl.BlockSpec(dims, lambda y, s: (1, y, 0, 0))]
        args += arrays + [f.got]
        counts.append(len(arrays) + 1)
    out = tuple(shape(f.got.shape[1:], bf16) for f in flows)

    def kernel(_, *refs):
        k = 0
        for i, n in enumerate(counts):
            total = sum(value_of(r) for r in refs[k : k + n])
            refs[len(args) + i][...] = total.astype(bf16)
            k += n

    sums = call(
        kernel,
        out,
        (2,),
        in_specs,
        [pl.BlockSpec((1, *o.shape[1:]), lambda y, s: (y, 0, 0)) for o in out],
        cuts,
        args,
    )
    for f, v in zip(flows, sums):
        f.last = exchange(v, f.ring, (3, 1))


def value_of(ref):
    return (ref[0] if len(ref.shape) == 4 else ref[...]).astype(f32)


def turn(flows, cuts):
    in_specs, outs, out_specs, args = [], [], [], []

    counts = []
    for f in flows:
        first = 1 if f.other == "x" else 5
        arrays = f.sources()
        rows, columns = arrays[0].shape[-2] // 4, arrays[0].shape[-1]
        four = pl.BlockSpec((1, 2, rows, columns), lambda j, s, i=first: (0, 0, s[i + j], 0))
        three = pl.BlockSpec((2, rows, columns), lambda j, s, i=first: (0, s[i + j], 0))
        in_specs += [four if a.ndim == 4 else three for a in arrays]
        args += arrays
        counts.append(len(arrays))
        dims = (1, 2, rows, columns)
        outs.append(shape((2, *dims[1:]), bf16))
        out_specs.append(pl.BlockSpec(dims, lambda j, s: (j, 0, 0, 0)))

    def kernel(_, *refs):
        k = 0
        for i, n in enumerate(counts):
            total = sum(value_of(r) for r in refs[k : k + n])
            refs[len(args) + i][0] = total.astype(bf16)
            k += n

    sends = call(kernel, tuple(outs), (2,), in_specs, out_specs, cuts, args)
    for f, send in zip(flows, sends):
        f.before = halves_of(f)
        f.ring = f.other
        f.got = exchange(send, f.ring, (1, 3))


def halves_of(f):
    arrays = f.sources()
    first = 1 if f.other == "x" else 5
    rows, columns = arrays[0].shape[-2] // 4, arrays[0].shape[-1]

    def quarter(which):
        four = pl.BlockSpec((1, 1, rows, columns), lambda y, s: (0, y, s[first + which], 0))
        three = pl.BlockSpec((1, rows, columns), lambda y, s: (y, s[first + which], 0))
        return [four if a.ndim == 4 else three for a in arrays], arrays

    return quarter


def add(a, b, none):
    def kernel(_, a, b, out):
        out[...] = (a[...].astype(f32) + b[...].astype(f32)).astype(bf16)

    out = shape(a.shape, bf16)
    return call(kernel, out, (1,), [whole(a), whole(b)], whole(out), none, (a, b))


class Finish:
    def __init__(self, flows, extra, cuts):
        in_specs, args, sizes = [], [], []
        def half(spec):
            return pl.BlockSpec(
                spec.block_shape, lambda j, s: spec.index_map(lax.rem(j + s[9], 2), s)
            )

        for f in flows:
            specs, arrays = f.kept(0)
            dims = (1, 1, *f.got.shape[2:])
            specs = specs + [
                pl.BlockSpec(dims, lambda y, s: (0, y, 0, 0)),
                pl.BlockSpec((1, *f.last.shape[1:]), lambda y, s: (y, 0, 0)),
            ]
            in_specs += [half(spec) for spec in specs]
            args += arrays + [f.got, f.last]
            sizes.append((len(arrays) + 2, f.got.shape[2], f.got.shape[3] // STEP))
        for e in extra:
            in_specs.append(half(pl.BlockSpec((1, *e.shape[1:]), lambda y, s: (y, 0, 0))))
        args += extra
        rows = sum(u * n for _, u, n in sizes) + sum(e.shape[1] for e in extra)

        def kernel(_, *refs):
            send, mine = refs[-2:]
            j = pl.program_id(0)

            def put(here, value):
                @pl.when(j == 0)
                def _():
                    mine[here, :] = value

                @pl.when(j == 1)
                def _():
                    send[here, :] = value.astype(bf16)

            start, k = 0, 0
            for count, u, n in sizes:
                v = sum(value_of(r) for r in refs[k : k + count])[0]
                for i in range(n):
                    put(slice(start, start + u), v[:, i * STEP : (i + 1) * STEP])
                    start += u
                k += count
            for ref in refs[k:-2]:
                put(slice(start, start + ref.shape[1]), ref[0])
                start += ref.shape[1]

        out = (shape((rows, STEP), bf16), shape((rows, STEP), f32))
        send, self.mine = call(
            kernel, out, (2,), in_specs, [whole(o) for o in out], cuts, args
        )
        self.got = exchange(send, "y", (1, 3))

    def second(self, none):
        self.mine = add(self.mine, self.got, none)
        self.far = lax.ppermute(self.mine, "yh", [(0, 1), (1, 0)])

    def gather(self, none):
        return lax.all_gather(add(self.mine, self.far, none), ("c", "x", "z"), axis=0)


def per_device(
    tokens,
    memory,
    compressed,
    cotangent,
    ln1_g,
    ln1_b,
    w_q,
    w_kv,
    w_r,
    bias_u,
    bias_v,
    w_o,
    ln2_g,
    ln2_b,
    w_in,
    b_in,
    w_out,
    b_out,
    conv_w,
    conv_b,
):
    line.held, line.due = [], {}
    tokens, memory, compressed, cotangent = tokens[0], memory[0], compressed[0], cotangent[0]
    yl, core = lax.axis_index("yl"), lax.axis_index("c")
    place = {"x": lax.axis_index("x"), "z": lax.axis_index("z")}
    none = jnp.zeros((1,), jnp.int32)
    ints = lambda *v: jnp.stack([jnp.asarray(i, jnp.int32) for i in v])

    def thirds(rows):
        half = rows // 2
        other = (1 - yl) * half
        return [yl * half, other + core * (half // 2), other + (1 - core) * (half // 2)]

    def both(v):
        return (v, core_swap(v))

    spot = (place["x"] * 4 + place["z"]) * 2 + core
    piece = pack(
        (ln1_g, ln1_b, bias_u, bias_v, ln2_g, ln2_b, b_out, conv_b, b_in),
        w_in,
        w_out,
        ints(spot),
    )
    piece_got = exchange(piece, "y", (1, 3))

    kv_part, small, o_part, conv_part = pack_rows(w_kv, w_q, w_r, w_o, conv_w, ints(core))
    kv_got = exchange(kv_part, "y", (1, 3))
    small_got = exchange(small, "y", (1, 3))
    o_got = exchange(o_part, "y", (1, 3))
    conv_got = exchange(conv_part, "y", (1, 3))

    def joined(w, got, twin):
        return jnp.concatenate([w, got, twin], axis=0)

    spread = lax.all_gather(piece_got[:-16], ("x", "z", "c"), axis=0)
    thirds_d = ints(*thirds(D))
    thirds_c = ints(*thirds(3 * D), *thirds(D))
    sinus_table = sinusoid(KEYS, D).astype(bf16)
    sinus_rel = jnp.concatenate(
        [
            lax.dynamic_slice_in_dim(sinus_table, thirds_d[i], width, 1)
            for i, width in enumerate(THIRDS)
        ],
        axis=1,
    )
    line.hold(sinus_rel)
    vectors, b_in = unpack(piece, piece_got, ints(yl))

    normed, normed_rel, oldest, old_quarters = first_norm(compressed, memory, tokens, vectors, thirds_d)
    both_normed, both_cot = both(normed), both(cotangent)
    own, first, far, second = quarters(place["x"], core)
    got = exchange(
        jnp.stack([pick(old_quarters, first, 0), pick(old_quarters, far, 0)]), "x", (1, 3)
    )
    got_far = exchange(jnp.stack([pick(old_quarters, second, 0), got[1]]), "x", (3, 1))
    old_ring = jnp.concatenate([pick(old_quarters, own, 0), got[0], got_far[0], got_far[1]])
    old_twin = core_swap(old_ring)
    kv_got, small_got = gate((kv_got, small_got), normed)
    kv_twin, small_twin = core_swap(kv_got), core_swap(small_got)
    kv_whole = joined(w_kv, kv_got, kv_twin)
    q_whole, r_whole = [
        joined(w, small_got[i], small_twin[i]) for i, w in enumerate((w_q, w_r))
    ]
    key_value = dot(normed_rel, kv_whole).astype(bf16)
    line.hold(key_value)
    queries = dot(normed_rel[2 * T :], q_whole)
    relative = dot(sinus_rel, r_whole).astype(bf16)
    (o_got,) = gate((o_got,), key_value, queries, relative)
    o_whole = joined(w_o, o_got, core_swap(o_got))
    line.hold(queries, relative)
    line.hold(got)
    probs, attended = attend(queries, key_value, relative, vectors, none)
    line.hold(both_normed[1], both_cot[1], got_far)
    residual, normed2, normed2_rel = out_and_norm(attended, o_whole, tokens, vectors, thirds_d)
    both_n2, both_att = both(normed2), both(attended)

    cuts, rels, twins = [], [], []
    for ring in ("x", "z"):
        own, first, far, second = quarters(place[ring], core)
        cuts += [first, far, own, second]
        rels.append([own, first, second, far])
        twins.append([own, second, first, far])
    cuts = ints(core, *cuts, yl)

    def flows(groups):
        pairs = weight_grads(groups, cuts)
        return [Flow(ring, pair) for (ring, _), pair in zip(groups, pairs)]

    def start(some):
        for f in some:
            f.start()

    line.hold(old_twin)
    hidden, d_pre, mixed_out, d_normed2, d_b_in = feed_forward(
        normed2_rel, residual, cotangent, w_in, w_out, spread, b_in, vectors, ints(yl)
    )
    both_hidden, both_pre = both(hidden), both(d_pre)
    (conv_got,) = gate((conv_got,), hidden)
    conv_pieces = (conv_w, conv_got, core_swap(conv_got))
    d_residual, d_branch, d_attended, d_ln2_g, d_ln2_b, d_b_out = second_norm_back(
        cotangent, d_normed2, residual, vectors, o_whole, thirds_d
    )
    both_branch = both(d_branch)
    large = flows(
        [
            ("x", [(both_hidden, 0, T, both_cot, False)]),
            ("z", [(both_n2, 0, T, both_pre, False), (both_att, 0, T, both_branch, False)]),
        ]
    )
    start(large)
    d_kv, my_kv, give_kv, d_relative, d_queries, d_bias_u, d_bias_v = attend_back(
        queries, key_value, relative, vectors, probs, d_attended, ints(core)
    )
    both_kv = (my_kv, core_swap(give_kv))
    both_q, both_rel = both(d_queries), both(d_relative)

    compact, comp_normed = compress(oldest, conv_pieces, vectors, thirds_c)
    comp_pair = dot(comp_normed, kv_whole).astype(bf16)
    compressed_next = jnp.concatenate([compressed[T // 3 :], compact], axis=0)
    near = flows(
        [
            ("x", [(both_normed, 0, KEYS, both_kv, True)]),
            (
                "z",
                [
                    (both_normed, 2, T, both_q, False),
                    ((sinus_table,), 0, KEYS, both_rel, False),
                ],
            ),
        ]
    )
    onward(large, cuts)
    sends = gate([f.send for f in near], line.held[0])
    for f, send in zip(near, sends):
        f.send = send
    start(near)
    loss, d_ck, d_cv = reconstruct(queries, key_value, comp_pair, none)
    recon_loss = jnp.sum(loss) / (T * D)
    d_compact, d_conv_b = compress_back(d_ck, d_cv, kv_whole, compact, vectors, thirds_d)
    ring_got = exchange(d_compact, "x", (1, 3))
    turn(large, cuts)
    d_tokens, d_ln1_g, d_ln1_b = first_norm_back(
        d_kv, d_queries, kv_whole, q_whole, compressed, memory, tokens, vectors, d_residual,
        thirds_d,
    )
    line.hold(ring_got)
    onward(large, cuts)
    ring_pair = jnp.concatenate([d_compact, ring_got])
    pair_got = exchange(ring_pair, "x", (3, 1))
    onward(near, cuts)
    line.expect(2, *[f.last for f in near])
    early = Finish(large, [], cuts)
    line.hold(pair_got)
    compact_ring = jnp.concatenate([ring_pair, pair_got])
    compact_twin = core_swap(compact_ring)
    early.second(none)
    conv = Flow("x", None, conv_grad(old_ring, old_twin, compact_ring, compact_twin, cuts))
    late_flows = [*near, conv]
    early_sums = early.gather(none)
    turn(late_flows, cuts)
    onward(late_flows, cuts)

    total = jnp.concatenate(
        [d_ln1_g, d_ln1_b, d_bias_u, d_bias_v, d_ln2_g, d_ln2_b, d_b_out, d_conv_b]
        + [d_b_in]
    )
    total = jnp.concatenate(
        [
            total[:8].reshape(8, 2, STEP).transpose(1, 0, 2),
            total[8:].reshape(2, 4, STEP),
            jnp.zeros((2, 4, STEP), f32),
        ],
        axis=1,
    )
    late = Finish(late_flows, [total], cuts)
    late.second(none)
    line.hold(early_sums)
    late_sums = late.gather(none)

    g_out, g_in, g_o = widen(
        early_sums, [(FF // 2, D, "x"), (D // 2, FF, "z"), (D // 2, D, "z")], none
    )
    g_kv, g_q, g_r, g_conv = widen(
        late_sums,
        [(D // 2, 2 * D, "x"), (D // 2, D, "z"), (D // 2, D, "z"), (3 * D // 2, D, "x")],
        none,
    )
    half = jnp.sum(late_sums[:, 224:236].astype(f32), axis=0)
    t_ln1_g, t_ln1_b, t_bu, t_bv, t_ln2_g, t_ln2_b, t_bout, t_convb = [half[i] for i in range(8)]
    t_bin = half[8:].reshape(-1)
    return (
        mixed_out[None],
        compressed_next[None],
        recon_loss[None],
        d_tokens[None],
        t_ln1_g,
        t_ln1_b,
        g_q,
        g_kv,
        g_r,
        t_bu,
        t_bv,
        g_o,
        t_ln2_g,
        t_ln2_b,
        g_in,
        t_bin,
        g_out,
        t_bout,
        g_conv,
        t_convb,
    )


def solution(mesh):
    fine = Mesh(mesh.devices.reshape(2, 4, 4, 2, 2), AXES)
    stream = P(AXES, None, None)
    vec, mat = P("yl"), P("yl", None)
    weights = (vec, vec, mat, mat, mat, vec, vec, mat, vec, vec, mat, vec, mat, vec, mat, vec)
    return jax.shard_map(
        per_device,
        mesh=fine,
        in_specs=(stream,) * 4 + weights,
        out_specs=(stream, stream, P(AXES), stream) + weights,
        check_vma=False,
    )
```

```python
import jax
import jax.numpy as jnp
from jax import lax
from jax.experimental import pallas as pl
from jax.experimental.pallas import tpu as pltpu
from jax.sharding import Mesh, PartitionSpec as P

H = 8
HD = 128
D = 1024
T = 192
KEYS = 576
PAD = 640
FF = 4096
FACTOR = HD ** (-0.5)
f32 = jnp.float32
bf16 = jnp.bfloat16
AXES = ("yh", "x", "z", "c", "yl")
RING = {"x": ("x", "c"), "z": ("z", "c"), "y": ("yh", "c", "yl")}


def sinusoid(key_count, model_dim):
    distance = (key_count - 1 - jnp.arange(key_count)).astype(f32)
    inverse = 1.0 / 10000.0 ** (jnp.arange(0, model_dim, 2).astype(f32) / model_dim)
    angles = distance[:, None] * inverse[None, :]
    return jnp.concatenate([jnp.sin(angles), jnp.cos(angles)], axis=-1)


def dot(a, b):
    return jnp.dot(a, b, preferred_element_type=f32)


def dot_t(a, b):
    return lax.dot_general(a, b, (((1,), (1,)), ((), ())), preferred_element_type=f32)


def t_dot(a, b):
    return lax.dot_general(a, b, (((0,), (0,)), ((), ())), preferred_element_type=f32)


class Line:
    def __init__(self):
        self.held, self.due = [], {}

    def hold(self, *values):
        self.held += values

    def expect(self, gap, *values):
        self.due.setdefault(gap, []).extend(values)

    def ran(self, result):
        self.held = [result, *self.due.get(1, [])]
        self.due = {gap - 1: values for gap, values in self.due.items() if gap > 1}

    def later(self, value):
        return lax.optimization_barrier((value, *self.held))[0] if self.held else value


line = Line()


def call(kernel, out, grid, in_specs, out_specs, scalars, args, scratch=()):
    held, n = line.held, len(args)

    def body(s, *refs):
        kernel(s, *refs[:n], *refs[n + len(held) :])

    result = pl.pallas_call(
        body,
        out_shape=out,
        grid_spec=pltpu.PrefetchScalarGridSpec(
            num_scalar_prefetch=1,
            grid=grid,
            in_specs=list(in_specs) + [pl.BlockSpec(memory_space=pl.ANY)] * len(held),
            out_specs=out_specs,
            scratch_shapes=list(scratch),
        ),
        compiler_params=pltpu.CompilerParams(vmem_limit_bytes=56 << 20),
    )(scalars, *args, *held)
    line.ran(jax.tree.leaves(result)[0])
    return result


def gate(values, *after):
    n = len(values)
    anywhere = pl.BlockSpec(memory_space=pl.ANY)
    return pl.pallas_call(
        lambda *refs: None,
        out_shape=[jax.ShapeDtypeStruct(v.shape, v.dtype) for v in values],
        in_specs=[anywhere] * (n + len(after)),
        out_specs=[anywhere] * n,
        input_output_aliases={i: i for i in range(n)},
    )(*values, *after)


def whole(a):
    zeros = (0,) * a.ndim
    return pl.BlockSpec(a.shape, lambda *_: zeros)


def shape(dims, dtype):
    return jax.ShapeDtypeStruct(dims, dtype)


def at(offset):
    return pl.multiple_of(offset, 128)


def center_scale(v):
    mid = v - jnp.mean(v, axis=-1, keepdims=True)
    r = lax.rsqrt(jnp.mean(mid * mid, axis=-1, keepdims=True) + 1e-5)
    return mid * r, r


def norm_back(xhat, r, g, dn):
    gd = dn * g
    return r * (
        gd
        - jnp.mean(gd, axis=-1, keepdims=True)
        - xhat * jnp.mean(gd * xhat, axis=-1, keepdims=True)
    )


def softmax(s):
    e = jnp.exp(s - jnp.max(s, axis=-1, keepdims=True))
    return e / jnp.sum(e, axis=-1, keepdims=True)


(LN1_G, LN1_B, BIAS_U, BIAS_V, LN2_G, LN2_B, B_OUT, CONV_B) = range(8)


def row(ref, i):
    return ref[i : i + 1, :]


def pack(vectors, w_in, w_out, scalars):
    n_in, n_out = (w.shape[0] // 32 for w in (w_in, w_out))
    chunks = FF // D
    rows = n_out + n_in * chunks
    half = D // 2

    def kernel(_, *refs):
        wi, wo, piece, flat = refs[-4:]
        flat[...] = jnp.zeros_like(flat)
        for i, ref in enumerate(refs[:8]):
            flat[i : i + 1, :half] = ref[...].astype(f32).reshape(1, half)
        flat[8 : 8 + FF // 2 // D, :] = refs[8][...].astype(f32).reshape(FF // 2 // D, D)
        piece[:n_out, :] = wo[...]
        for i in range(chunks):
            piece[n_out + i * n_in : n_out + (i + 1) * n_in, :] = wi[:, i * D : (i + 1) * D]
        piece[rows:, :] = flat[...].astype(bf16)

    out = shape((rows + 16, D), bf16)
    return call(
        kernel,
        out,
        (1,),
        [whole(v) for v in vectors]
        + [
            pl.BlockSpec((w.shape[0] // 32, w.shape[1]), lambda j, s: (s[0], 0))
            for w in (w_in, w_out)
        ],
        whole(out),
        scalars,
        (*vectors, w_in, w_out),
        [pltpu.VMEM((16, D), f32)],
    )


def pack_rows(w_kv, w_q, w_r, w_o, conv_w, scalars):
    n, n_conv = w_q.shape[0] // 2, conv_w.shape[0] // 2

    def kernel(_, kv, q, r, o, conv, kv_out, out, o_out, conv_out):
        kv_out[...] = kv[...]
        out[0] = q[...]
        out[1] = r[...]
        o_out[...] = o[...]
        conv_out[...] = conv[...]

    args = (w_kv, w_q, w_r, w_o, conv_w)
    out = (
        shape((n, 2 * D), bf16),
        shape((2, n, D), bf16),
        shape((n, D), bf16),
        shape((n_conv, D), bf16),
    )
    return call(
        kernel,
        out,
        (1,),
        [pl.BlockSpec((w.shape[0] // 2, w.shape[1]), lambda j, s: (s[0], 0)) for w in args],
        [whole(o) for o in out],
        scalars,
        args,
    )


def unpack(mine, theirs, scalars):
    half = D // 2
    at_row = mine.shape[0] // 16 - 1
    tail = pl.BlockSpec((16, D), lambda j, s: (at_row, 0))

    def kernel(s, mine, theirs, vectors, b_in):
        a, b = mine[...].astype(f32), theirs[...].astype(f32)
        low = jnp.where(s[0] == 0, a, b)
        high = jnp.where(s[0] == 0, b, a)
        vectors[:, :half] = low[:8, :half]
        vectors[:, half:] = high[:8, :half]
        rows = FF // 2 // D
        b_in[:rows] = low[8 : 8 + rows]
        b_in[rows:] = high[8 : 8 + rows]

    out = (shape((8, D), f32), shape((FF // D, D), f32))
    return call(
        kernel, out, (1,), [tail, tail], [whole(o) for o in out], scalars, (mine, theirs)
    )


def relative_columns(x, s, widths):
    parts = [x[:, pl.ds(at(s[i]), width)] for i, width in enumerate(widths)]
    return jnp.concatenate(parts, axis=1)


def natural_columns(out, x, s, widths):
    start = 0
    for i, width in enumerate(widths):
        out[:, pl.ds(at(s[i]), width)] = x[:, start : start + width]
        start += width


THIRDS = (D // 2, D // 4, D // 4)


def first_norm(compressed, memory, tokens, vectors, offsets):
    def kernel(s, comp, mem, tok, vec, out, out_rel, old, old_quarters):
        gain, bias = row(vec, LN1_G), row(vec, LN1_B)

        def part(ref, base):
            for i in range(0, T, 32):
                xhat, r = center_scale(ref[i : i + 32, :].astype(f32))
                out[base + i : base + i + 32, :] = (xhat * gain + bias).astype(bf16)

        part(comp, 0)
        part(mem, T)
        part(tok, 2 * T)
        out_rel[...] = relative_columns(out, s, THIRDS)
        line_of = lax.broadcasted_iota(jnp.int32, (T // 3, T), 0)
        col = lax.broadcasted_iota(jnp.int32, (T // 3, T), 1)
        low = mem[...].astype(bf16)
        for tap in range(3):
            take = jnp.where(col == 3 * line_of + tap, 1.0, 0.0).astype(bf16)
            old[:, tap * D : (tap + 1) * D] = dot(take, low).astype(bf16)
        width = 3 * D // 8
        for q in range(4):
            for y in range(2):
                begin = y * 3 * D // 2 + q * width
                old_quarters[q, :, y * width : (y + 1) * width] = old[:, begin : begin + width]

    args = (compressed, memory, tokens, vectors)
    out = (
        shape((KEYS, D), bf16),
        shape((KEYS, D), bf16),
        shape((T // 3, 3 * D), bf16),
        shape((4, T // 3, 3 * D // 4), bf16),
    )
    return call(
        kernel, out, (1,), [whole(a) for a in args], [whole(o) for o in out], offsets, args
    )


def head(n, rows, row_block=0, first=0):
    return pl.BlockSpec((rows, n * HD), lambda h, s: (row_block, first // n + h))


def columns_of(n):
    return [slice(i * HD, (i + 1) * HD) for i in range(n)]


def attend(queries, key_value, relative, vectors, none):
    n = 2

    def kernel(_, q, k, v, rel, vec, probs, out):
        pad = jnp.zeros((PAD - KEYS, HD), bf16)
        i = lax.broadcasted_iota(jnp.int32, (T, PAD), 0)
        j = lax.broadcasted_iota(jnp.int32, (T, PAD), 1)
        seen = j <= i + (KEYS - T)
        cuts = columns_of(n)
        content = [((q[:, c] + vec[BIAS_U : BIAS_U + 1, c]) * FACTOR).astype(bf16) for c in cuts]
        located = [((q[:, c] + vec[BIAS_V : BIAS_V + 1, c]) * FACTOR).astype(bf16) for c in cuts]
        raw = [
            dot_t(x, jnp.concatenate([rel[:, c], pad], axis=0)) for x, c in zip(located, cuts)
        ]
        near = [dot_t(x, jnp.concatenate([k[:, c], pad], axis=0)) for x, c in zip(content, cuts)]
        raw = [pltpu.roll(x, PAD - T + 1, 1, stride=1, stride_axis=0) for x in raw]
        p = [softmax(jnp.where(seen, a + b, -1e30)) for a, b in zip(near, raw)]
        for h, c in enumerate(cuts):
            probs[h] = p[h]
            value = jnp.concatenate([v[:, c], pad], axis=0)
            out[:, c] = dot(p[h].astype(bf16), value).astype(bf16)

    return call(
        kernel,
        (shape((H, T, PAD), f32), shape((T, D), bf16)),
        (H // n,),
        [head(n, T), head(n, KEYS), head(n, KEYS, 0, H), head(n, KEYS), head(n, 8)],
        [pl.BlockSpec((n, T, PAD), lambda h, s: (h, 0, 0)), head(n, T)],
        none,
        (queries, key_value, key_value, relative, vectors),
    )


def attend_back(queries, key_value, relative, vectors, probs, d_attended, scalars):
    n = 2

    def kernel(s, q, k, v, rel, vec, probs, d_att, d_kv, mine, give, d_rel, d_q, d_bu, d_bv):
        pad = jnp.zeros((PAD - KEYS, HD), bf16)
        i = lax.broadcasted_iota(jnp.int32, (T, T), 0)
        j = lax.broadcasted_iota(jnp.int32, (T, T), 1)
        flip = jnp.where(i + j == T - 1, 1.0, 0.0).astype(bf16)
        cuts = columns_of(n)
        content = [((q[:, c] + vec[BIAS_U : BIAS_U + 1, c]) * FACTOR).astype(bf16) for c in cuts]
        located = [((q[:, c] + vec[BIAS_V : BIAS_V + 1, c]) * FACTOR).astype(bf16) for c in cuts]
        da = [d_att[:, c] for c in cuts]
        d_p = [dot_t(x, jnp.concatenate([v[:, c], pad], axis=0)) for x, c in zip(da, cuts)]
        d_v = [t_dot(probs[h].astype(bf16), x)[:KEYS].astype(bf16) for h, x in enumerate(da)]
        d_s = []
        for h, x in enumerate(d_p):
            p = probs[h]
            d_s.append((p * (x - jnp.sum(p * x, axis=-1, keepdims=True))).astype(bf16))
        d_raw = [dot(flip, x) for x in d_s]
        d_c = [
            dot(x, jnp.concatenate([k[:, c], pad], axis=0)) * FACTOR for x, c in zip(d_s, cuts)
        ]
        d_k = [t_dot(x, y)[:KEYS].astype(bf16) for x, y in zip(d_s, content)]
        d_raw = [pltpu.roll(x, 0, 1, stride=1, stride_axis=0).astype(bf16) for x in d_raw]
        d_raw = [dot(flip, x).astype(bf16) for x in d_raw]
        d_l = [
            dot(x, jnp.concatenate([rel[:, c], pad], axis=0)) * FACTOR for x, c in zip(d_raw, cuts)
        ]
        for h, c in enumerate(cuts):
            d_rel[:, c] = t_dot(d_raw[h], located[h])[:KEYS].astype(bf16)
            d_kv[0, :, c] = d_k[h]
            d_kv[1, :, c] = d_v[h]
            mine[:, c] = jnp.where(s[0] == 0, d_k[h], d_v[h])
            give[:, c] = jnp.where(s[0] == 0, d_v[h], d_k[h])
            d_q[:, c] = (d_c[h] + d_l[h]).astype(bf16)
            d_bu[:, c] = jnp.sum(d_c[h], axis=0, keepdims=True)
            d_bv[:, c] = jnp.sum(d_l[h], axis=0, keepdims=True)

    return call(
        kernel,
        (shape((2, KEYS, D), bf16),)
        + (shape((KEYS, D), bf16),) * 3
        + (shape((T, D), bf16), shape((1, D), f32), shape((1, D), f32)),
        (H // n,),
        [
            head(n, T),
            head(n, KEYS),
            head(n, KEYS, 0, H),
            head(n, KEYS),
            head(n, 8),
            pl.BlockSpec((n, T, PAD), lambda h, s: (h, 0, 0)),
            head(n, T),
        ],
        [
            pl.BlockSpec((2, KEYS, n * HD), lambda h, s: (0, 0, h)),
            head(n, KEYS),
            head(n, KEYS),
            head(n, KEYS),
            head(n, T),
            head(n, 1),
            head(n, 1),
        ],
        scalars,
        (queries, key_value, key_value, relative, vectors, probs, d_attended),
    )


def out_and_norm(attended, w_o, tokens, vectors, offsets):
    def kernel(s, att, w, tok, vec, res, n2, n2_rel):
        total = tok[...].astype(f32) + dot(relative_columns(att, s, THIRDS), w[...])
        res[...] = total
        xhat, r = center_scale(total)
        n2[...] = (xhat * row(vec, LN2_G) + row(vec, LN2_B)).astype(bf16)
        other = at(D // 2 - s[0])
        n2_rel[:, : D // 2] = n2[:, pl.ds(at(s[0]), D // 2)]
        n2_rel[:, D // 2 :] = n2[:, pl.ds(other, D // 2)]

    args = (attended, w_o, tokens, vectors)
    out = (shape((T, D), f32), shape((T, D), bf16), shape((T, D), bf16))
    return call(
        kernel, out, (1,), [whole(a) for a in args], [whole(o) for o in out], offsets, args
    )


STEP = 512
UNITS = 1024
HALF = FF // 2 // UNITS


def feed_forward(n2_rel, residual, cotangent, w_in, w_out, spread, b_in, vectors, scalars):
    n_in = w_in.shape[0] // 32
    n_out = w_out.shape[0] // 32
    skip = n_out // n_in
    per = UNITS // n_out
    K_NORM = 0.7978845608028654

    def natural(j, s):
        return lax.rem(j + s[0] * HALF, 2 * HALF)

    def kernel(s, n2, res, cot, wi0, wi1, wo0, wo1, bi, vec, hid, dpre, mixed, dn2, dbi, acc, back):
        j = pl.program_id(0)
        n = natural(j, s)

        @pl.when(j == 0)
        def _():
            acc[...] = jnp.zeros_like(acc)
            back[...] = jnp.zeros_like(back)

        wo = jnp.where(j < HALF, wo0[...], wo1[...].reshape(UNITS, D))
        win = jnp.concatenate([wi0[...], wi1[...].reshape(D // 2, UNITS)], axis=0)
        pre = dot(n2[...], win) + bi[pl.ds(n, 1), :]
        d_hidden = dot_t(cot[...], wo)
        square = pre * pre
        t = jnp.tanh(K_NORM * pre * (1.0 + 0.044715 * square))
        gate_ = 0.5 * (1.0 + t)
        hidden = (pre * gate_).astype(bf16)
        slope = gate_ + (0.5 * K_NORM) * pre * (1.0 - t * t) * (1.0 + (3 * 0.044715) * square)
        d_pre = (d_hidden * slope).astype(bf16)
        hid[...] = hidden
        dpre[...] = d_pre
        dbi[pl.ds(n, 1), :] = jnp.sum(d_pre.astype(f32), axis=0, keepdims=True)
        acc[...] += dot(hidden, wo)
        back[...] += dot_t(d_pre, win)

        @pl.when(j == 2 * HALF - 1)
        def _():
            mixed[...] = (res[...] + acc[...] + row(vec, B_OUT)).astype(bf16)
            dn2[:, pl.ds(at(s[0] * (D // 2)), D // 2)] = back[:, : D // 2]
            dn2[:, pl.ds(at((1 - s[0]) * (D // 2)), D // 2)] = back[:, D // 2 :]

    out = (
        shape((T, FF), bf16),
        shape((T, FF), bf16),
        shape((T, D), bf16),
        shape((T, D), f32),
        shape((2 * HALF, UNITS), f32),
    )
    by_unit = pl.BlockSpec((T, UNITS), lambda j, s: (0, natural(j, s)))
    return call(
        kernel,
        out,
        (2 * HALF,),
        [
            whole(n2_rel),
            whole(residual),
            whole(cotangent),
            pl.BlockSpec((D // 2, UNITS), lambda j, s: (0, natural(j, s))),
            pl.BlockSpec((32, n_in, UNITS), lambda j, s: (0, skip + natural(j, s), 0)),
            pl.BlockSpec((UNITS, D), lambda j, s: (jnp.minimum(j, HALF - 1), 0)),
            pl.BlockSpec(
                (per, n_out, D), lambda j, s: (jnp.maximum(j - HALF, 0), 0, 0)
            ),
            whole(b_in),
            whole(vectors),
        ],
        [by_unit, by_unit, whole(out[2]), whole(out[3]), whole(out[4])],
        scalars,
        (n2_rel, residual, cotangent, w_in, spread, w_out, spread, b_in, vectors),
        [pltpu.VMEM((T, D), f32), pltpu.VMEM((T, D), f32)],
    )


def second_norm_back(cotangent, d_n2, residual, vectors, w_o, offsets):
    def kernel(s, cot, dn, res, vec, w, d_res, d_br, d_att, dg, db, dbo):
        xhat, r = center_scale(res[...])
        dn, wide = dn[...], cot[...].astype(f32)
        dg[...] = jnp.sum(dn * xhat, axis=0, keepdims=True)
        db[...] = jnp.sum(dn, axis=0, keepdims=True)
        dbo[...] = jnp.sum(wide, axis=0, keepdims=True)
        total = wide + norm_back(xhat, r, row(vec, LN2_G), dn)
        d_res[...] = total
        low = total.astype(bf16)
        d_br[...] = low
        natural_columns(d_att, dot_t(low, w[...]).astype(bf16), s, THIRDS)

    args = (cotangent, d_n2, residual, vectors, w_o)
    out = (
        shape((T, D), f32),
        shape((T, D), bf16),
        shape((T, D), bf16),
        shape((1, D), f32),
        shape((1, D), f32),
        shape((1, D), f32),
    )
    return call(
        kernel, out, (1,), [whole(a) for a in args], [whole(o) for o in out], offsets, args
    )


def first_norm_back(d_kv, d_q, w_kv, w_q, compressed, memory, tokens, vectors, d_res, offsets):
    steps = 4
    wide, slim = 2 * D // steps, D // steps

    def kernel(s, dkv, dq, kw, qw, comp, mem, tok, vec, dres, dtok, dg, db, acc, nat, xh, rs):
        j = pl.program_id(0)

        def product(start):
            value = dot_t(dkv[0], kw[...])
            if start:
                acc[...] = value
            else:
                acc[...] += value
            acc[2 * T :, :] += dot_t(dq[...], qw[...])

        for block, ref in enumerate((comp, mem, tok)):

            @pl.when(j == block)
            def _(block=block, ref=ref):
                product(block == 0)
                for i in range(0, T, 32):
                    xhat, r = center_scale(ref[i : i + 32, :].astype(f32))
                    xh[block * T + i : block * T + i + 32, :] = xhat
                    if block == 2:
                        rs[i : i + 32, :] = jnp.broadcast_to(r, (32, HD))

        @pl.when(j == steps - 1)
        def _():
            product(False)
            natural_columns(nat, acc, s, THIRDS)
            gain = row(vec, LN1_G)
            sum_g = jnp.zeros((8, D), f32)
            sum_b = jnp.zeros((8, D), f32)
            for i in range(0, KEYS, 32):
                dn, xhat = nat[i : i + 32, :], xh[i : i + 32, :]
                both = dn * xhat
                sum_g += (both[:8] + both[8:16]) + (both[16:24] + both[24:])
                sum_b += (dn[:8] + dn[8:16]) + (dn[16:24] + dn[24:])
                if i >= 2 * T:
                    k = i - 2 * T
                    r = rs[k : k + 32, :1]
                    dtok[k : k + 32, :] = dres[k : k + 32, :] + norm_back(xhat, r, gain, dn)
            dg[...] = jnp.sum(sum_g, axis=0, keepdims=True)
            db[...] = jnp.sum(sum_b, axis=0, keepdims=True)

    rest = (compressed, memory, tokens, vectors, d_res)
    out = (shape((T, D), f32), shape((1, D), f32), shape((1, D), f32))
    return call(
        kernel,
        out,
        (steps,),
        [
            pl.BlockSpec((1, KEYS, wide), lambda j, s: (j // (steps // 2), 0, lax.rem(j, steps // 2))),
            pl.BlockSpec((T, slim), lambda j, s: (0, j)),
            pl.BlockSpec((D, wide), lambda j, s: (0, j)),
            pl.BlockSpec((D, slim), lambda j, s: (0, j)),
        ]
        + [whole(a) for a in rest],
        [whole(o) for o in out],
        offsets,
        (d_kv, d_q, w_kv, w_q, *rest),
        [pltpu.VMEM((KEYS, D), f32)] * 3 + [pltpu.VMEM((T, HD), f32)],
    )


def compress(oldest, pieces, vectors, offsets):
    block = 256
    rows = T // 3

    def kernel(s, x, w0, w1, w2, vec, compact, normed, x_rel, natural):
        j = pl.program_id(0)

        @pl.when(j == 0)
        def _():
            x_rel[...] = relative_columns(x, s, (3 * D // 2, 3 * D // 4, 3 * D // 4))

        w = jnp.concatenate([w0[...], w1[...], w2[...]], axis=0)
        here = pl.ds(at(j * block), block)
        compact[:, here] = dot(x_rel[...], w) + vec[CONV_B : CONV_B + 1, here]

        @pl.when(j == D // block - 1)
        def _():
            xhat, r = center_scale(compact[...])
            natural[...] = (xhat * row(vec, LN1_G) + row(vec, LN1_B)).astype(bf16)
            start = 0
            for i, width in enumerate(THIRDS):
                normed[:, start : start + width] = natural[:, pl.ds(at(s[3 + i]), width)]
                start += width

    out = (shape((rows, D), f32), shape((rows, D), bf16))
    return call(
        kernel,
        out,
        (D // block,),
        [whole(oldest)]
        + [pl.BlockSpec((w.shape[0], block), lambda j, s: (0, j)) for w in pieces]
        + [whole(vectors)],
        [whole(o) for o in out],
        offsets,
        (oldest, *pieces, vectors),
        [pltpu.VMEM((rows, 3 * D), bf16), pltpu.VMEM((rows, D), bf16)],
    )


def reconstruct(queries, key_value, comp_pair, none):
    rows = T // 3
    n = 4

    def kernel(_, q, k, v, ck, cv, loss, dck, dcv):
        cuts = columns_of(n)
        asking = [(q[:, c] * FACTOR).astype(bf16) for c in cuts]
        far = [dot_t(x, k[:, c]) for x, c in zip(asking, cuts)]
        near = [dot_t(x, ck[:, c]) for x, c in zip(asking, cuts)]
        p = [softmax(x).astype(bf16) for x in far]
        gp = [softmax(x) for x in near]
        low = [x.astype(bf16) for x in gp]
        miss = [dot(p[h], v[:, c]) - dot(low[h], cv[:, c]) for h, c in enumerate(cuts)]
        total = sum(jnp.sum(x * x, axis=0, keepdims=True) for x in miss)
        d_guess = [((-2.0 / (T * D)) * x).astype(bf16) for x in miss]
        d_gp = [dot_t(x, cv[:, c]) for x, c in zip(d_guess, cuts)]
        d_gs = [
            (x * (y - jnp.sum(x * y, axis=-1, keepdims=True))).astype(bf16)
            for x, y in zip(gp, d_gp)
        ]
        for h, c in enumerate(cuts):
            dcv[:, c] = t_dot(low[h], d_guess[h]).astype(bf16)
            dck[:, c] = t_dot(d_gs[h], asking[h]).astype(bf16)

        @pl.when(pl.program_id(0) == 0)
        def _():
            loss[...] = total

        @pl.when(pl.program_id(0) > 0)
        def _():
            loss[...] += total

    return call(
        kernel,
        (shape((1, HD), f32), shape((rows, D), bf16), shape((rows, D), bf16)),
        (H // n,),
        [head(n, T), head(n, T, 1), head(n, T, 1, H), head(n, rows), head(n, rows, 0, H)],
        [pl.BlockSpec((1, HD), lambda h, s: (0, 0)), head(n, rows), head(n, rows)],
        none,
        (queries, key_value, key_value, comp_pair, comp_pair),
    )


def compress_back(dck, dcv, w_kv, compact, vectors, offsets):
    rows = T // 3

    def kernel(s, dck, dcv, w, compact, vec, d_compact, d_bias, dn):
        back = dot_t(jnp.concatenate([dck[...], dcv[...]], axis=1), w[...])
        natural_columns(dn, back, s, THIRDS)
        xhat, r = center_scale(compact[...])
        low = norm_back(xhat, r, row(vec, LN1_G), dn[...]).astype(bf16)
        d_compact[...] = low
        d_bias[...] = jnp.sum(low.astype(f32), axis=0, keepdims=True)

    args = (dck, dcv, w_kv, compact, vectors)
    out = (shape((rows, D), bf16), shape((1, D), f32))
    return call(
        kernel,
        out,
        (1,),
        [whole(a) for a in args],
        [whole(o) for o in out],
        offsets,
        args,
        [pltpu.VMEM((rows, D), f32)],
    )


def weight_grads(groups, scalars):
    in_specs, args, outs, out_specs, layout, scratch = [], [], [], [], [], []
    for ring, jobs in groups:
        first = 1 if ring == "x" else 5
        block = jobs[0][0][0].shape[1] // 8
        plan = []
        for xs, row_block, rows, dys, ready in jobs:
            width = dys[0].shape[1] // (1 if ready else 2)
            plan.append((width, rows, len(xs)))
            for x in xs:
                for y in range(2):
                    in_specs.append(
                        pl.BlockSpec(
                            (rows, block),
                            lambda q, s, r=row_block, f=first, y=y: (r, y * 4 + s[f + q]),
                        )
                    )
                    args.append(x)
            for dy in dys:
                in_specs.append(
                    pl.BlockSpec((rows, width), lambda q, s, r=ready: (0, 0 if r else s[0]))
                )
                args.append(dy)
            scratch.append(pltpu.VMEM((rows * len(xs), width), bf16))
        dims = (1, 2, block, sum(p[0] for p in plan))
        outs += [shape((2, *dims[1:]), bf16)] * 2
        out_specs += [
            pl.BlockSpec(dims, lambda q, s: (jnp.minimum(q, 1), 0, 0, 0)),
            pl.BlockSpec(dims, lambda q, s: (jnp.maximum(q - 2, 0), 0, 0, 0)),
        ]
        layout.append(plan)
    n_in, n_out = len(in_specs), len(outs)

    def kernel(s, *refs):
        ins, results, joined = refs[:n_in], refs[n_in : n_in + n_out], refs[n_in + n_out :]
        q = pl.program_id(0)

        @pl.when(q == 0)
        def _():
            place, k = 0, 0
            for plan in layout:
                for _, rows, n in plan:
                    da, db = ins[place + 2 * n], ins[place + 2 * n + 1]
                    if n == 2:
                        joined[k][:rows, :] = da[...]
                        joined[k][rows:, :] = db[...]
                    else:
                        joined[k][...] = (da[...].astype(f32) + db[...].astype(f32)).astype(bf16)
                    place += 2 * n + 2
                    k += 1

        place, k = 0, 0
        for i, plan in enumerate(layout):
            send, keep = results[2 * i : 2 * i + 2]
            block = send.shape[2]
            start = 0
            for width, rows, n in plan:
                x = jnp.concatenate([r[...] for r in ins[place : place + 2]], axis=1)
                if n == 2:
                    other = jnp.concatenate([r[...] for r in ins[place + 2 : place + 4]], axis=1)
                    x = jnp.concatenate([x, other], axis=0)
                value = t_dot(x, joined[k][...]).astype(bf16).reshape(2, block, width)
                cut = slice(start, start + width)
                send[0, :, :, cut] = jnp.where(q < 2, value, send[0, :, :, cut])
                keep[0, :, :, cut] = value
                start += width
                place += 2 * n + 2
                k += 1

    flat = call(kernel, tuple(outs), (4,), in_specs, out_specs, scalars, args, scratch)
    return [(flat[2 * i], flat[2 * i + 1]) for i in range(len(groups))]


def conv_grad(x, x_twin, dy, dy_twin, scalars):
    rows, columns = x.shape[1] // 2, D // 2

    def kernel(s, xa, xb, da, db, out):
        both = jnp.concatenate([xa[...], xb[...]], axis=0)
        total = t_dot(both, jnp.concatenate([da[...], db[...]], axis=0))
        out[...] = total.reshape(2, rows, columns)

    half = pl.BlockSpec((dy.shape[0], columns), lambda j, s: (0, s[0]))
    out = shape((2, rows, columns), f32)
    return call(
        kernel,
        out,
        (1,),
        [whole(x), whole(x_twin), half, half],
        whole(out),
        scalars,
        (x, x_twin, dy, dy_twin),
    )


def widen(gathered, plan, none):
    outs, specs, layout = [], [], []
    start = 0
    for rows, columns, ring in plan:
        u, chunks = rows // 16, columns // 2 // STEP
        outs.append(shape((4, 4, u, columns), f32))
        if ring == "x":
            specs.append(
                pl.BlockSpec((1, 4, u, chunks * STEP), lambda c, x, s: (x, 0, 0, c))
            )
        else:
            specs.append(
                pl.BlockSpec((4, 1, u, chunks * STEP), lambda c, x, s: (0, x, 0, c))
            )
        layout.append((start, u, chunks, ring))
        start += u * chunks

    def kernel(_, src, *results):
        for out, (start, u, chunks, ring) in zip(results, layout):
            for k in range(chunks):
                cut = slice(k * STEP, (k + 1) * STEP)
                for z in range(4):
                    value = src[z, start + k * u : start + (k + 1) * u, :].astype(f32)
                    if ring == "x":
                        out[0, z, :, cut] = value
                    else:
                        out[z, 0, :, cut] = value

    results = call(
        kernel,
        tuple(outs),
        (2, 4),
        [pl.BlockSpec((4, gathered.shape[1], STEP), lambda c, x, s: (c * 4 + x, 0, 0))],
        specs,
        none,
        (gathered,),
    )
    return [r.reshape(rows, columns) for r, (rows, columns, _) in zip(results, plan)]


def core_swap(v):
    return lax.ppermute(v, "c", [(0, 1), (1, 0)])


def pair_swap(v):
    return lax.ppermute(v, "yl", [(0, 1), (1, 0)])


def exchange(v, ring, masks):
    def flat(i, c):
        return (i // 2 * 2 + c) * 2 + i % 2 if ring == "y" else 2 * i + c

    pairs = [(flat(i, c), flat(i ^ masks[c], c)) for i in range(4) for c in range(2)]
    return lax.ppermute(v, RING[ring], pairs)


def pick(v, index, axis):
    return lax.dynamic_index_in_dim(v, index, axis, keepdims=False)


def quarters(place, core):
    first = jnp.where(core == 0, 1, 3)
    second = jnp.where(core == 0, 3, 1)
    return place, place ^ first, place ^ 2, place ^ second


class Flow:
    def __init__(self, ring, pair, done=None):
        self.ring, self.other = ring, "z" if ring == "x" else "x"
        self.before, self.result = None, done
        if done is None:
            self.send, self.keep = pair

    def start(self):
        self.got = exchange(self.send, self.ring, (1, 3))

    def sources(self):
        return [self.keep, self.got, self.last] if self.result is None else [self.result]

    def kept(self, which):
        if self.before is None:
            dims = (1, 1, *self.keep.shape[2:])
            return [pl.BlockSpec(dims, lambda y, s: (which, y, 0, 0))], [self.keep]
        return self.before(2 + which)


def onward(flows, cuts):
    in_specs, args, counts = [], [], []
    for f in flows:
        specs, arrays = f.kept(1)
        dims = (1, 1, *f.got.shape[2:])
        in_specs += specs + [pl.BlockSpec(dims, lambda y, s: (1, y, 0, 0))]
        args += arrays + [f.got]
        counts.append(len(arrays) + 1)
    out = tuple(shape(f.got.shape[1:], bf16) for f in flows)

    def kernel(_, *refs):
        k = 0
        for i, n in enumerate(counts):
            total = sum(value_of(r) for r in refs[k : k + n])
            refs[len(args) + i][...] = total.astype(bf16)
            k += n

    sums = call(
        kernel,
        out,
        (2,),
        in_specs,
        [pl.BlockSpec((1, *o.shape[1:]), lambda y, s: (y, 0, 0)) for o in out],
        cuts,
        args,
    )
    for f, v in zip(flows, sums):
        f.last = exchange(v, f.ring, (3, 1))


def value_of(ref):
    return (ref[0] if len(ref.shape) == 4 else ref[...]).astype(f32)


def turn(flows, cuts):
    in_specs, outs, out_specs, args = [], [], [], []

    counts = []
    for f in flows:
        first = 1 if f.other == "x" else 5
        arrays = f.sources()
        rows, columns = arrays[0].shape[-2] // 4, arrays[0].shape[-1]
        four = pl.BlockSpec((1, 2, rows, columns), lambda j, s, i=first: (0, 0, s[i + j], 0))
        three = pl.BlockSpec((2, rows, columns), lambda j, s, i=first: (0, s[i + j], 0))
        in_specs += [four if a.ndim == 4 else three for a in arrays]
        args += arrays
        counts.append(len(arrays))
        dims = (1, 2, rows, columns)
        outs.append(shape((2, *dims[1:]), bf16))
        out_specs.append(pl.BlockSpec(dims, lambda j, s: (j, 0, 0, 0)))

    def kernel(_, *refs):
        k = 0
        for i, n in enumerate(counts):
            total = sum(value_of(r) for r in refs[k : k + n])
            refs[len(args) + i][0] = total.astype(bf16)
            k += n

    sends = call(kernel, tuple(outs), (2,), in_specs, out_specs, cuts, args)
    for f, send in zip(flows, sends):
        f.before = halves_of(f)
        f.ring = f.other
        f.got = exchange(send, f.ring, (1, 3))


def halves_of(f):
    arrays = f.sources()
    first = 1 if f.other == "x" else 5
    rows, columns = arrays[0].shape[-2] // 4, arrays[0].shape[-1]

    def quarter(which):
        four = pl.BlockSpec((1, 1, rows, columns), lambda y, s: (0, y, s[first + which], 0))
        three = pl.BlockSpec((1, rows, columns), lambda y, s: (y, s[first + which], 0))
        return [four if a.ndim == 4 else three for a in arrays], arrays

    return quarter


def add(a, b, none):
    def kernel(_, a, b, out):
        out[...] = (a[...].astype(f32) + b[...].astype(f32)).astype(bf16)

    out = shape(a.shape, bf16)
    return call(kernel, out, (1,), [whole(a), whole(b)], whole(out), none, (a, b))


class Finish:
    def __init__(self, flows, extra, cuts):
        in_specs, args, sizes = [], [], []
        def half(spec):
            return pl.BlockSpec(
                spec.block_shape, lambda j, s: spec.index_map(lax.rem(j + s[9], 2), s)
            )

        for f in flows:
            specs, arrays = f.kept(0)
            dims = (1, 1, *f.got.shape[2:])
            specs = specs + [
                pl.BlockSpec(dims, lambda y, s: (0, y, 0, 0)),
                pl.BlockSpec((1, *f.last.shape[1:]), lambda y, s: (y, 0, 0)),
            ]
            in_specs += [half(spec) for spec in specs]
            args += arrays + [f.got, f.last]
            sizes.append((len(arrays) + 2, f.got.shape[2], f.got.shape[3] // STEP))
        for e in extra:
            in_specs.append(half(pl.BlockSpec((1, *e.shape[1:]), lambda y, s: (y, 0, 0))))
        args += extra
        rows = sum(u * n for _, u, n in sizes) + sum(e.shape[1] for e in extra)

        def kernel(_, *refs):
            send, mine = refs[-2:]
            j = pl.program_id(0)

            def put(here, value):
                @pl.when(j == 0)
                def _():
                    mine[here, :] = value

                @pl.when(j == 1)
                def _():
                    send[here, :] = value.astype(bf16)

            start, k = 0, 0
            for count, u, n in sizes:
                v = sum(value_of(r) for r in refs[k : k + count])[0]
                for i in range(n):
                    put(slice(start, start + u), v[:, i * STEP : (i + 1) * STEP])
                    start += u
                k += count
            for ref in refs[k:-2]:
                put(slice(start, start + ref.shape[1]), ref[0])
                start += ref.shape[1]

        out = (shape((rows, STEP), bf16), shape((rows, STEP), f32))
        send, self.mine = call(
            kernel, out, (2,), in_specs, [whole(o) for o in out], cuts, args
        )
        self.got = exchange(send, "y", (1, 3))

    def second(self, none):
        self.mine = add(self.mine, self.got, none)
        self.far = lax.ppermute(self.mine, "yh", [(0, 1), (1, 0)])

    def gather(self, none):
        return lax.all_gather(add(self.mine, self.far, none), ("c", "x", "z"), axis=0)


def per_device(
    tokens,
    memory,
    compressed,
    cotangent,
    ln1_g,
    ln1_b,
    w_q,
    w_kv,
    w_r,
    bias_u,
    bias_v,
    w_o,
    ln2_g,
    ln2_b,
    w_in,
    b_in,
    w_out,
    b_out,
    conv_w,
    conv_b,
):
    line.held, line.due = [], {}
    tokens, memory, compressed, cotangent = tokens[0], memory[0], compressed[0], cotangent[0]
    yl, core = lax.axis_index("yl"), lax.axis_index("c")
    place = {"x": lax.axis_index("x"), "z": lax.axis_index("z")}
    none = jnp.zeros((1,), jnp.int32)
    ints = lambda *v: jnp.stack([jnp.asarray(i, jnp.int32) for i in v])

    def thirds(rows):
        half = rows // 2
        other = (1 - yl) * half
        return [yl * half, other + core * (half // 2), other + (1 - core) * (half // 2)]

    def both(v):
        return (v, core_swap(v))

    spot = (place["x"] * 4 + place["z"]) * 2 + core
    piece = pack(
        (ln1_g, ln1_b, bias_u, bias_v, ln2_g, ln2_b, b_out, conv_b, b_in),
        w_in,
        w_out,
        ints(spot),
    )
    piece_got = exchange(piece, "y", (1, 3))

    kv_part, small, o_part, conv_part = pack_rows(w_kv, w_q, w_r, w_o, conv_w, ints(core))
    kv_got = exchange(kv_part, "y", (1, 3))
    small_got = exchange(small, "y", (1, 3))
    o_got = exchange(o_part, "y", (1, 3))
    conv_got = exchange(conv_part, "y", (1, 3))

    def joined(w, got, twin):
        return jnp.concatenate([w, got, twin], axis=0)

    spread = lax.all_gather(piece_got[:-16], ("x", "z", "c"), axis=0)
    thirds_d = ints(*thirds(D))
    thirds_c = ints(*thirds(3 * D), *thirds(D))
    sinus_table = sinusoid(KEYS, D).astype(bf16)
    sinus_rel = jnp.concatenate(
        [
            lax.dynamic_slice_in_dim(sinus_table, thirds_d[i], width, 1)
            for i, width in enumerate(THIRDS)
        ],
        axis=1,
    )
    line.hold(sinus_rel)
    vectors, b_in = unpack(piece, piece_got, ints(yl))

    normed, normed_rel, oldest, old_quarters = first_norm(compressed, memory, tokens, vectors, thirds_d)
    both_normed, both_cot = both(normed), both(cotangent)
    own, first, far, second = quarters(place["x"], core)
    got = exchange(
        jnp.stack([pick(old_quarters, first, 0), pick(old_quarters, far, 0)]), "x", (1, 3)
    )
    got_far = exchange(jnp.stack([pick(old_quarters, second, 0), got[1]]), "x", (3, 1))
    old_ring = jnp.concatenate([pick(old_quarters, own, 0), got[0], got_far[0], got_far[1]])
    old_twin = core_swap(old_ring)
    kv_got, small_got = gate((kv_got, small_got), normed)
    kv_twin, small_twin = core_swap(kv_got), core_swap(small_got)
    kv_whole = joined(w_kv, kv_got, kv_twin)
    q_whole, r_whole = [
        joined(w, small_got[i], small_twin[i]) for i, w in enumerate((w_q, w_r))
    ]
    key_value = dot(normed_rel, kv_whole).astype(bf16)
    line.hold(key_value)
    queries = dot(normed_rel[2 * T :], q_whole)
    relative = dot(sinus_rel, r_whole).astype(bf16)
    (o_got,) = gate((o_got,), key_value, queries, relative)
    o_whole = joined(w_o, o_got, core_swap(o_got))
    line.hold(queries, relative)
    line.hold(got)
    probs, attended = attend(queries, key_value, relative, vectors, none)
    line.hold(both_normed[1], both_cot[1], got_far)
    residual, normed2, normed2_rel = out_and_norm(attended, o_whole, tokens, vectors, thirds_d)
    both_n2, both_att = both(normed2), both(attended)

    cuts, rels, twins = [], [], []
    for ring in ("x", "z"):
        own, first, far, second = quarters(place[ring], core)
        cuts += [first, far, own, second]
        rels.append([own, first, second, far])
        twins.append([own, second, first, far])
    cuts = ints(core, *cuts, yl)

    def flows(groups):
        pairs = weight_grads(groups, cuts)
        return [Flow(ring, pair) for (ring, _), pair in zip(groups, pairs)]

    def start(some):
        for f in some:
            f.start()

    line.hold(old_twin)
    hidden, d_pre, mixed_out, d_normed2, d_b_in = feed_forward(
        normed2_rel, residual, cotangent, w_in, w_out, spread, b_in, vectors, ints(yl)
    )
    both_hidden, both_pre = both(hidden), both(d_pre)
    (conv_got,) = gate((conv_got,), hidden)
    conv_pieces = (conv_w, conv_got, core_swap(conv_got))
    d_residual, d_branch, d_attended, d_ln2_g, d_ln2_b, d_b_out = second_norm_back(
        cotangent, d_normed2, residual, vectors, o_whole, thirds_d
    )
    both_branch = both(d_branch)
    large = flows(
        [
            ("x", [(both_hidden, 0, T, both_cot, False)]),
            ("z", [(both_n2, 0, T, both_pre, False), (both_att, 0, T, both_branch, False)]),
        ]
    )
    start(large)
    d_kv, my_kv, give_kv, d_relative, d_queries, d_bias_u, d_bias_v = attend_back(
        queries, key_value, relative, vectors, probs, d_attended, ints(core)
    )
    both_kv = (my_kv, core_swap(give_kv))
    both_q, both_rel = both(d_queries), both(d_relative)

    compact, comp_normed = compress(oldest, conv_pieces, vectors, thirds_c)
    comp_pair = dot(comp_normed, kv_whole).astype(bf16)
    compressed_next = jnp.concatenate([compressed[T // 3 :], compact], axis=0)
    near = flows(
        [
            ("x", [(both_normed, 0, KEYS, both_kv, True)]),
            (
                "z",
                [
                    (both_normed, 2, T, both_q, False),
                    ((sinus_table,), 0, KEYS, both_rel, False),
                ],
            ),
        ]
    )
    onward(large, cuts)
    loss, d_ck, d_cv = reconstruct(queries, key_value, comp_pair, none)
    recon_loss = jnp.sum(loss) / (T * D)
    sends = gate([f.send for f in near], loss)
    for f, send in zip(near, sends):
        f.send = send
    start(near)
    d_compact, d_conv_b = compress_back(d_ck, d_cv, kv_whole, compact, vectors, thirds_d)
    ring_got = exchange(d_compact, "x", (1, 3))
    line.hold(ring_got)
    turn(large, cuts)
    ring_pair = jnp.concatenate([d_compact, ring_got])
    pair_got = exchange(ring_pair, "x", (3, 1))
    d_tokens, d_ln1_g, d_ln1_b = first_norm_back(
        d_kv, d_queries, kv_whole, q_whole, compressed, memory, tokens, vectors, d_residual,
        thirds_d,
    )
    (pair_got,) = gate((pair_got,), d_ln1_g)
    onward(large, cuts)
    compact_ring = jnp.concatenate([ring_pair, pair_got])
    compact_twin = core_swap(compact_ring)
    onward(near, cuts)
    line.expect(1, *[f.last for f in near])
    line.hold(compact_twin)
    early = Finish(large, [], cuts)
    conv = Flow("x", None, conv_grad(old_ring, old_twin, compact_ring, compact_twin, cuts))
    early.second(none)
    late_flows = [*near, conv]
    turn(late_flows, cuts)
    early_sums = early.gather(none)
    onward(late_flows, cuts)

    total = jnp.concatenate(
        [d_ln1_g, d_ln1_b, d_bias_u, d_bias_v, d_ln2_g, d_ln2_b, d_b_out, d_conv_b]
        + [d_b_in]
    )
    total = jnp.concatenate(
        [
            total[:8].reshape(8, 2, STEP).transpose(1, 0, 2),
            total[8:].reshape(2, 4, STEP),
            jnp.zeros((2, 4, STEP), f32),
        ],
        axis=1,
    )
    late = Finish(late_flows, [total], cuts)
    late.second(none)
    line.hold(early_sums)
    late_sums = late.gather(none)

    g_out, g_in, g_o = widen(
        early_sums, [(FF // 2, D, "x"), (D // 2, FF, "z"), (D // 2, D, "z")], none
    )
    g_kv, g_q, g_r, g_conv = widen(
        late_sums,
        [(D // 2, 2 * D, "x"), (D // 2, D, "z"), (D // 2, D, "z"), (3 * D // 2, D, "x")],
        none,
    )
    half = jnp.sum(late_sums[:, 224:236].astype(f32), axis=0)
    t_ln1_g, t_ln1_b, t_bu, t_bv, t_ln2_g, t_ln2_b, t_bout, t_convb = [half[i] for i in range(8)]
    t_bin = half[8:].reshape(-1)
    return (
        mixed_out[None],
        compressed_next[None],
        recon_loss[None],
        d_tokens[None],
        t_ln1_g,
        t_ln1_b,
        g_q,
        g_kv,
        g_r,
        t_bu,
        t_bv,
        g_o,
        t_ln2_g,
        t_ln2_b,
        g_in,
        t_bin,
        g_out,
        t_bout,
        g_conv,
        t_convb,
    )


def solution(mesh):
    fine = Mesh(mesh.devices.reshape(2, 4, 4, 2, 2), AXES)
    stream = P(AXES, None, None)
    vec, mat = P("yl"), P("yl", None)
    weights = (vec, vec, mat, mat, mat, vec, vec, mat, vec, vec, mat, vec, mat, vec, mat, vec)
    return jax.shard_map(
        per_device,
        mesh=fine,
        in_specs=(stream,) * 4 + weights,
        out_specs=(stream, stream, P(AXES), stream) + weights,
        check_vma=False,
    )
```

```python
import jax
import jax.numpy as jnp
from jax import lax
from jax.experimental import pallas as pl
from jax.experimental.pallas import tpu as pltpu
from jax.sharding import Mesh, PartitionSpec as P

H = 8
HD = 128
D = 1024
T = 192
KEYS = 576
PAD = 640
FF = 4096
FACTOR = HD ** (-0.5)
f32 = jnp.float32
bf16 = jnp.bfloat16
AXES = ("yh", "x", "z", "c", "yl")
RING = {"x": ("x", "c"), "z": ("z", "c"), "y": ("yh", "c", "yl")}


def sinusoid(key_count, model_dim):
    distance = (key_count - 1 - jnp.arange(key_count)).astype(f32)
    inverse = 1.0 / 10000.0 ** (jnp.arange(0, model_dim, 2).astype(f32) / model_dim)
    angles = distance[:, None] * inverse[None, :]
    return jnp.concatenate([jnp.sin(angles), jnp.cos(angles)], axis=-1)


def dot(a, b):
    return jnp.dot(a, b, preferred_element_type=f32)


def dot_t(a, b):
    return lax.dot_general(a, b, (((1,), (1,)), ((), ())), preferred_element_type=f32)


def t_dot(a, b):
    return lax.dot_general(a, b, (((0,), (0,)), ((), ())), preferred_element_type=f32)


class Line:
    def __init__(self):
        self.held, self.due = [], {}

    def hold(self, *values):
        self.held += values

    def expect(self, gap, *values):
        self.due.setdefault(gap, []).extend(values)

    def ran(self, result):
        self.held = [result, *self.due.get(1, [])]
        self.due = {gap - 1: values for gap, values in self.due.items() if gap > 1}

    def later(self, value):
        return lax.optimization_barrier((value, *self.held))[0] if self.held else value


line = Line()


def call(kernel, out, grid, in_specs, out_specs, scalars, args, scratch=()):
    held, n = line.held, len(args)

    def body(s, *refs):
        kernel(s, *refs[:n], *refs[n + len(held) :])

    result = pl.pallas_call(
        body,
        out_shape=out,
        grid_spec=pltpu.PrefetchScalarGridSpec(
            num_scalar_prefetch=1,
            grid=grid,
            in_specs=list(in_specs) + [pl.BlockSpec(memory_space=pl.ANY)] * len(held),
            out_specs=out_specs,
            scratch_shapes=list(scratch),
        ),
        compiler_params=pltpu.CompilerParams(vmem_limit_bytes=56 << 20),
    )(scalars, *args, *held)
    line.ran(jax.tree.leaves(result)[0])
    return result


def gate(values, *after):
    n = len(values)
    anywhere = pl.BlockSpec(memory_space=pl.ANY)
    return pl.pallas_call(
        lambda *refs: None,
        out_shape=[jax.ShapeDtypeStruct(v.shape, v.dtype) for v in values],
        in_specs=[anywhere] * (n + len(after)),
        out_specs=[anywhere] * n,
        input_output_aliases={i: i for i in range(n)},
    )(*values, *after)


def whole(a):
    zeros = (0,) * a.ndim
    return pl.BlockSpec(a.shape, lambda *_: zeros)


def shape(dims, dtype):
    return jax.ShapeDtypeStruct(dims, dtype)


def at(offset):
    return pl.multiple_of(offset, 128)


def center_scale(v):
    mid = v - jnp.mean(v, axis=-1, keepdims=True)
    r = lax.rsqrt(jnp.mean(mid * mid, axis=-1, keepdims=True) + 1e-5)
    return mid * r, r


def norm_back(xhat, r, g, dn):
    gd = dn * g
    return r * (
        gd
        - jnp.mean(gd, axis=-1, keepdims=True)
        - xhat * jnp.mean(gd * xhat, axis=-1, keepdims=True)
    )


def softmax(s):
    e = jnp.exp(s - jnp.max(s, axis=-1, keepdims=True))
    return e / jnp.sum(e, axis=-1, keepdims=True)


(LN1_G, LN1_B, BIAS_U, BIAS_V, LN2_G, LN2_B, B_OUT, CONV_B) = range(8)


def row(ref, i):
    return ref[i : i + 1, :]


def pack(vectors, w_in, w_out, scalars):
    n_in, n_out = (w.shape[0] // 32 for w in (w_in, w_out))
    chunks = FF // D
    rows = n_out + n_in * chunks
    half = D // 2

    def kernel(_, *refs):
        wi, wo, piece, flat = refs[-4:]
        flat[...] = jnp.zeros_like(flat)
        for i, ref in enumerate(refs[:8]):
            flat[i : i + 1, :half] = ref[...].astype(f32).reshape(1, half)
        flat[8 : 8 + FF // 2 // D, :] = refs[8][...].astype(f32).reshape(FF // 2 // D, D)
        piece[:n_out, :] = wo[...]
        for i in range(chunks):
            piece[n_out + i * n_in : n_out + (i + 1) * n_in, :] = wi[:, i * D : (i + 1) * D]
        piece[rows:, :] = flat[...].astype(bf16)

    out = shape((rows + 16, D), bf16)
    return call(
        kernel,
        out,
        (1,),
        [whole(v) for v in vectors]
        + [
            pl.BlockSpec((w.shape[0] // 32, w.shape[1]), lambda j, s: (s[0], 0))
            for w in (w_in, w_out)
        ],
        whole(out),
        scalars,
        (*vectors, w_in, w_out),
        [pltpu.VMEM((16, D), f32)],
    )


def half_rows(w, scalars):
    n = w.shape[0] // 2

    def kernel(_, w, out):
        out[...] = w[...]

    out = shape((n, w.shape[1]), w.dtype)
    spec = pl.BlockSpec((n, w.shape[1]), lambda j, s: (s[0], 0))
    return call(kernel, out, (1,), [spec], whole(out), scalars, (w,))


def pack_rows(w_kv, w_q, w_r, w_o, scalars):
    n = w_q.shape[0] // 2

    def kernel(_, kv, q, r, o, kv_out, out, o_out):
        kv_out[...] = kv[...]
        out[0] = q[...]
        out[1] = r[...]
        o_out[...] = o[...]

    args = (w_kv, w_q, w_r, w_o)
    out = (shape((n, 2 * D), bf16), shape((2, n, D), bf16), shape((n, D), bf16))
    return call(
        kernel,
        out,
        (1,),
        [pl.BlockSpec((w.shape[0] // 2, w.shape[1]), lambda j, s: (s[0], 0)) for w in args],
        [whole(o) for o in out],
        scalars,
        args,
    )


def unpack(mine, theirs, scalars):
    half = D // 2
    at_row = mine.shape[0] // 16 - 1
    tail = pl.BlockSpec((16, D), lambda j, s: (at_row, 0))

    def kernel(s, mine, theirs, vectors, b_in):
        a, b = mine[...].astype(f32), theirs[...].astype(f32)
        low = jnp.where(s[0] == 0, a, b)
        high = jnp.where(s[0] == 0, b, a)
        vectors[:, :half] = low[:8, :half]
        vectors[:, half:] = high[:8, :half]
        rows = FF // 2 // D
        b_in[:rows] = low[8 : 8 + rows]
        b_in[rows:] = high[8 : 8 + rows]

    out = (shape((8, D), f32), shape((FF // D, D), f32))
    return call(
        kernel, out, (1,), [tail, tail], [whole(o) for o in out], scalars, (mine, theirs)
    )


def relative_columns(x, s, widths):
    parts = [x[:, pl.ds(at(s[i]), width)] for i, width in enumerate(widths)]
    return jnp.concatenate(parts, axis=1)


def natural_columns(out, x, s, widths):
    start = 0
    for i, width in enumerate(widths):
        out[:, pl.ds(at(s[i]), width)] = x[:, start : start + width]
        start += width


THIRDS = (D // 2, D // 4, D // 4)


def first_norm(compressed, memory, tokens, vectors, offsets):
    def kernel(s, comp, mem, tok, vec, out, out_rel, old, old_quarters):
        gain, bias = row(vec, LN1_G), row(vec, LN1_B)

        def part(ref, base):
            for i in range(0, T, 32):
                xhat, r = center_scale(ref[i : i + 32, :].astype(f32))
                out[base + i : base + i + 32, :] = (xhat * gain + bias).astype(bf16)

        part(comp, 0)
        part(mem, T)
        part(tok, 2 * T)
        out_rel[...] = relative_columns(out, s, THIRDS)
        line_of = lax.broadcasted_iota(jnp.int32, (T // 3, T), 0)
        col = lax.broadcasted_iota(jnp.int32, (T // 3, T), 1)
        low = mem[...].astype(bf16)
        for tap in range(3):
            take = jnp.where(col == 3 * line_of + tap, 1.0, 0.0).astype(bf16)
            old[:, tap * D : (tap + 1) * D] = dot(take, low).astype(bf16)
        width = 3 * D // 8
        for q in range(4):
            for y in range(2):
                begin = y * 3 * D // 2 + q * width
                old_quarters[q, :, y * width : (y + 1) * width] = old[:, begin : begin + width]

    args = (compressed, memory, tokens, vectors)
    out = (
        shape((KEYS, D), bf16),
        shape((KEYS, D), bf16),
        shape((T // 3, 3 * D), bf16),
        shape((4, T // 3, 3 * D // 4), bf16),
    )
    return call(
        kernel, out, (1,), [whole(a) for a in args], [whole(o) for o in out], offsets, args
    )


def head(n, rows, row_block=0, first=0):
    return pl.BlockSpec((rows, n * HD), lambda h, s: (row_block, first // n + h))


def columns_of(n):
    return [slice(i * HD, (i + 1) * HD) for i in range(n)]


def attend(queries, key_value, relative, vectors, none):
    n = 2

    def kernel(_, q, k, v, rel, vec, probs, out):
        pad = jnp.zeros((PAD - KEYS, HD), bf16)
        i = lax.broadcasted_iota(jnp.int32, (T, PAD), 0)
        j = lax.broadcasted_iota(jnp.int32, (T, PAD), 1)
        seen = j <= i + (KEYS - T)
        cuts = columns_of(n)
        content = [((q[:, c] + vec[BIAS_U : BIAS_U + 1, c]) * FACTOR).astype(bf16) for c in cuts]
        located = [((q[:, c] + vec[BIAS_V : BIAS_V + 1, c]) * FACTOR).astype(bf16) for c in cuts]
        raw = [
            dot_t(x, jnp.concatenate([rel[:, c], pad], axis=0)) for x, c in zip(located, cuts)
        ]
        near = [dot_t(x, jnp.concatenate([k[:, c], pad], axis=0)) for x, c in zip(content, cuts)]
        raw = [pltpu.roll(x, PAD - T + 1, 1, stride=1, stride_axis=0) for x in raw]
        p = [softmax(jnp.where(seen, a + b, -1e30)) for a, b in zip(near, raw)]
        for h, c in enumerate(cuts):
            probs[h] = p[h]
            value = jnp.concatenate([v[:, c], pad], axis=0)
            out[:, c] = dot(p[h].astype(bf16), value).astype(bf16)

    return call(
        kernel,
        (shape((H, T, PAD), f32), shape((T, D), bf16)),
        (H // n,),
        [head(n, T), head(n, KEYS), head(n, KEYS, 0, H), head(n, KEYS), head(n, 8)],
        [pl.BlockSpec((n, T, PAD), lambda h, s: (h, 0, 0)), head(n, T)],
        none,
        (queries, key_value, key_value, relative, vectors),
    )


def attend_back(queries, key_value, relative, vectors, probs, d_attended, scalars):
    n = 2

    def kernel(s, q, k, v, rel, vec, probs, d_att, d_kv, mine, give, d_rel, d_q, d_bu, d_bv):
        pad = jnp.zeros((PAD - KEYS, HD), bf16)
        i = lax.broadcasted_iota(jnp.int32, (T, T), 0)
        j = lax.broadcasted_iota(jnp.int32, (T, T), 1)
        flip = jnp.where(i + j == T - 1, 1.0, 0.0).astype(bf16)
        cuts = columns_of(n)
        content = [((q[:, c] + vec[BIAS_U : BIAS_U + 1, c]) * FACTOR).astype(bf16) for c in cuts]
        located = [((q[:, c] + vec[BIAS_V : BIAS_V + 1, c]) * FACTOR).astype(bf16) for c in cuts]
        da = [d_att[:, c] for c in cuts]
        d_p = [dot_t(x, jnp.concatenate([v[:, c], pad], axis=0)) for x, c in zip(da, cuts)]
        d_v = [t_dot(probs[h].astype(bf16), x)[:KEYS].astype(bf16) for h, x in enumerate(da)]
        d_s = []
        for h, x in enumerate(d_p):
            p = probs[h]
            d_s.append((p * (x - jnp.sum(p * x, axis=-1, keepdims=True))).astype(bf16))
        d_raw = [dot(flip, x) for x in d_s]
        d_c = [
            dot(x, jnp.concatenate([k[:, c], pad], axis=0)) * FACTOR for x, c in zip(d_s, cuts)
        ]
        d_k = [t_dot(x, y)[:KEYS].astype(bf16) for x, y in zip(d_s, content)]
        d_raw = [pltpu.roll(x, 0, 1, stride=1, stride_axis=0).astype(bf16) for x in d_raw]
        d_raw = [dot(flip, x).astype(bf16) for x in d_raw]
        d_l = [
            dot(x, jnp.concatenate([rel[:, c], pad], axis=0)) * FACTOR for x, c in zip(d_raw, cuts)
        ]
        for h, c in enumerate(cuts):
            d_rel[:, c] = t_dot(d_raw[h], located[h])[:KEYS].astype(bf16)
            d_kv[0, :, c] = d_k[h]
            d_kv[1, :, c] = d_v[h]
            mine[:, c] = jnp.where(s[0] == 0, d_k[h], d_v[h])
            give[:, c] = jnp.where(s[0] == 0, d_v[h], d_k[h])
            d_q[:, c] = (d_c[h] + d_l[h]).astype(bf16)
            d_bu[:, c] = jnp.sum(d_c[h], axis=0, keepdims=True)
            d_bv[:, c] = jnp.sum(d_l[h], axis=0, keepdims=True)

    return call(
        kernel,
        (shape((2, KEYS, D), bf16),)
        + (shape((KEYS, D), bf16),) * 3
        + (shape((T, D), bf16), shape((1, D), f32), shape((1, D), f32)),
        (H // n,),
        [
            head(n, T),
            head(n, KEYS),
            head(n, KEYS, 0, H),
            head(n, KEYS),
            head(n, 8),
            pl.BlockSpec((n, T, PAD), lambda h, s: (h, 0, 0)),
            head(n, T),
        ],
        [
            pl.BlockSpec((2, KEYS, n * HD), lambda h, s: (0, 0, h)),
            head(n, KEYS),
            head(n, KEYS),
            head(n, KEYS),
            head(n, T),
            head(n, 1),
            head(n, 1),
        ],
        scalars,
        (queries, key_value, key_value, relative, vectors, probs, d_attended),
    )


def out_and_norm(attended, w_o, tokens, vectors, offsets):
    def kernel(s, att, w, tok, vec, res, n2, n2_rel):
        total = tok[...].astype(f32) + dot(relative_columns(att, s, THIRDS), w[...])
        res[...] = total
        xhat, r = center_scale(total)
        n2[...] = (xhat * row(vec, LN2_G) + row(vec, LN2_B)).astype(bf16)
        other = at(D // 2 - s[0])
        n2_rel[:, : D // 2] = n2[:, pl.ds(at(s[0]), D // 2)]
        n2_rel[:, D // 2 :] = n2[:, pl.ds(other, D // 2)]

    args = (attended, w_o, tokens, vectors)
    out = (shape((T, D), f32), shape((T, D), bf16), shape((T, D), bf16))
    return call(
        kernel, out, (1,), [whole(a) for a in args], [whole(o) for o in out], offsets, args
    )


STEP = 512
UNITS = 1024
HALF = FF // 2 // UNITS


def feed_forward(n2_rel, residual, cotangent, w_in, w_out, spread, b_in, vectors, scalars):
    n_in = w_in.shape[0] // 32
    n_out = w_out.shape[0] // 32
    skip = n_out // n_in
    per = UNITS // n_out
    K_NORM = 0.7978845608028654

    def natural(j, s):
        return lax.rem(j + s[0] * HALF, 2 * HALF)

    def kernel(s, n2, res, cot, wi0, wi1, wo0, wo1, bi, vec, hid, dpre, mixed, dn2, dbi, acc, back):
        j = pl.program_id(0)
        n = natural(j, s)

        @pl.when(j == 0)
        def _():
            acc[...] = jnp.zeros_like(acc)
            back[...] = jnp.zeros_like(back)

        wo = jnp.where(j < HALF, wo0[...], wo1[...].reshape(UNITS, D))
        win = jnp.concatenate([wi0[...], wi1[...].reshape(D // 2, UNITS)], axis=0)
        pre = dot(n2[...], win) + bi[pl.ds(n, 1), :]
        d_hidden = dot_t(cot[...], wo)
        square = pre * pre
        t = jnp.tanh(K_NORM * pre * (1.0 + 0.044715 * square))
        gate_ = 0.5 * (1.0 + t)
        hidden = (pre * gate_).astype(bf16)
        slope = gate_ + (0.5 * K_NORM) * pre * (1.0 - t * t) * (1.0 + (3 * 0.044715) * square)
        d_pre = (d_hidden * slope).astype(bf16)
        hid[...] = hidden
        dpre[...] = d_pre
        dbi[pl.ds(n, 1), :] = jnp.sum(d_pre.astype(f32), axis=0, keepdims=True)
        acc[...] += dot(hidden, wo)
        back[...] += dot_t(d_pre, win)

        @pl.when(j == 2 * HALF - 1)
        def _():
            mixed[...] = (res[...] + acc[...] + row(vec, B_OUT)).astype(bf16)
            dn2[:, pl.ds(at(s[0] * (D // 2)), D // 2)] = back[:, : D // 2]
            dn2[:, pl.ds(at((1 - s[0]) * (D // 2)), D // 2)] = back[:, D // 2 :]

    out = (
        shape((T, FF), bf16),
        shape((T, FF), bf16),
        shape((T, D), bf16),
        shape((T, D), f32),
        shape((2 * HALF, UNITS), f32),
    )
    by_unit = pl.BlockSpec((T, UNITS), lambda j, s: (0, natural(j, s)))
    return call(
        kernel,
        out,
        (2 * HALF,),
        [
            whole(n2_rel),
            whole(residual),
            whole(cotangent),
            pl.BlockSpec((D // 2, UNITS), lambda j, s: (0, natural(j, s))),
            pl.BlockSpec((32, n_in, UNITS), lambda j, s: (0, skip + natural(j, s), 0)),
            pl.BlockSpec((UNITS, D), lambda j, s: (jnp.minimum(j, HALF - 1), 0)),
            pl.BlockSpec(
                (per, n_out, D), lambda j, s: (jnp.maximum(j - HALF, 0), 0, 0)
            ),
            whole(b_in),
            whole(vectors),
        ],
        [by_unit, by_unit, whole(out[2]), whole(out[3]), whole(out[4])],
        scalars,
        (n2_rel, residual, cotangent, w_in, spread, w_out, spread, b_in, vectors),
        [pltpu.VMEM((T, D), f32), pltpu.VMEM((T, D), f32)],
    )


def second_norm_back(cotangent, d_n2, residual, vectors, w_o, offsets):
    def kernel(s, cot, dn, res, vec, w, d_res, d_br, d_att, dg, db, dbo):
        xhat, r = center_scale(res[...])
        dn, wide = dn[...], cot[...].astype(f32)
        dg[...] = jnp.sum(dn * xhat, axis=0, keepdims=True)
        db[...] = jnp.sum(dn, axis=0, keepdims=True)
        dbo[...] = jnp.sum(wide, axis=0, keepdims=True)
        total = wide + norm_back(xhat, r, row(vec, LN2_G), dn)
        d_res[...] = total
        low = total.astype(bf16)
        d_br[...] = low
        natural_columns(d_att, dot_t(low, w[...]).astype(bf16), s, THIRDS)

    args = (cotangent, d_n2, residual, vectors, w_o)
    out = (
        shape((T, D), f32),
        shape((T, D), bf16),
        shape((T, D), bf16),
        shape((1, D), f32),
        shape((1, D), f32),
        shape((1, D), f32),
    )
    return call(
        kernel, out, (1,), [whole(a) for a in args], [whole(o) for o in out], offsets, args
    )


def first_norm_back(d_kv, d_q, w_kv, w_q, compressed, memory, tokens, vectors, d_res, offsets):
    steps = 4
    wide, slim = 2 * D // steps, D // steps

    def kernel(s, dkv, dq, kw, qw, comp, mem, tok, vec, dres, dtok, dg, db, acc, nat, xh, rs):
        j = pl.program_id(0)

        def product(start):
            value = dot_t(dkv[0], kw[...])
            if start:
                acc[...] = value
            else:
                acc[...] += value
            acc[2 * T :, :] += dot_t(dq[...], qw[...])

        for block, ref in enumerate((comp, mem, tok)):

            @pl.when(j == block)
            def _(block=block, ref=ref):
                product(block == 0)
                for i in range(0, T, 32):
                    xhat, r = center_scale(ref[i : i + 32, :].astype(f32))
                    xh[block * T + i : block * T + i + 32, :] = xhat
                    if block == 2:
                        rs[i : i + 32, :] = jnp.broadcast_to(r, (32, HD))

        @pl.when(j == steps - 1)
        def _():
            product(False)
            natural_columns(nat, acc, s, THIRDS)
            gain = row(vec, LN1_G)
            sum_g = jnp.zeros((8, D), f32)
            sum_b = jnp.zeros((8, D), f32)
            for i in range(0, KEYS, 32):
                dn, xhat = nat[i : i + 32, :], xh[i : i + 32, :]
                both = dn * xhat
                sum_g += (both[:8] + both[8:16]) + (both[16:24] + both[24:])
                sum_b += (dn[:8] + dn[8:16]) + (dn[16:24] + dn[24:])
                if i >= 2 * T:
                    k = i - 2 * T
                    r = rs[k : k + 32, :1]
                    dtok[k : k + 32, :] = dres[k : k + 32, :] + norm_back(xhat, r, gain, dn)
            dg[...] = jnp.sum(sum_g, axis=0, keepdims=True)
            db[...] = jnp.sum(sum_b, axis=0, keepdims=True)

    rest = (compressed, memory, tokens, vectors, d_res)
    out = (shape((T, D), f32), shape((1, D), f32), shape((1, D), f32))
    return call(
        kernel,
        out,
        (steps,),
        [
            pl.BlockSpec((1, KEYS, wide), lambda j, s: (j // (steps // 2), 0, lax.rem(j, steps // 2))),
            pl.BlockSpec((T, slim), lambda j, s: (0, j)),
            pl.BlockSpec((D, wide), lambda j, s: (0, j)),
            pl.BlockSpec((D, slim), lambda j, s: (0, j)),
        ]
        + [whole(a) for a in rest],
        [whole(o) for o in out],
        offsets,
        (d_kv, d_q, w_kv, w_q, *rest),
        [pltpu.VMEM((KEYS, D), f32)] * 3 + [pltpu.VMEM((T, HD), f32)],
    )


def compress(oldest, pieces, vectors, offsets):
    block = 256
    rows = T // 3

    def kernel(s, x, w0, w1, w2, vec, compact, normed, x_rel, natural):
        j = pl.program_id(0)

        @pl.when(j == 0)
        def _():
            x_rel[...] = relative_columns(x, s, (3 * D // 2, 3 * D // 4, 3 * D // 4))

        w = jnp.concatenate([w0[...], w1[...], w2[...]], axis=0)
        here = pl.ds(at(j * block), block)
        compact[:, here] = dot(x_rel[...], w) + vec[CONV_B : CONV_B + 1, here]

        @pl.when(j == D // block - 1)
        def _():
            xhat, r = center_scale(compact[...])
            natural[...] = (xhat * row(vec, LN1_G) + row(vec, LN1_B)).astype(bf16)
            start = 0
            for i, width in enumerate(THIRDS):
                normed[:, start : start + width] = natural[:, pl.ds(at(s[3 + i]), width)]
                start += width

    out = (shape((rows, D), f32), shape((rows, D), bf16))
    return call(
        kernel,
        out,
        (D // block,),
        [whole(oldest)]
        + [pl.BlockSpec((w.shape[0], block), lambda j, s: (0, j)) for w in pieces]
        + [whole(vectors)],
        [whole(o) for o in out],
        offsets,
        (oldest, *pieces, vectors),
        [pltpu.VMEM((rows, 3 * D), bf16), pltpu.VMEM((rows, D), bf16)],
    )


def reconstruct(queries, key_value, comp_pair, none):
    rows = T // 3
    n = 4

    def kernel(_, q, k, v, ck, cv, loss, dck, dcv):
        cuts = columns_of(n)
        asking = [(q[:, c] * FACTOR).astype(bf16) for c in cuts]
        far = [dot_t(x, k[:, c]) for x, c in zip(asking, cuts)]
        near = [dot_t(x, ck[:, c]) for x, c in zip(asking, cuts)]
        p = [softmax(x).astype(bf16) for x in far]
        gp = [softmax(x) for x in near]
        low = [x.astype(bf16) for x in gp]
        miss = [dot(p[h], v[:, c]) - dot(low[h], cv[:, c]) for h, c in enumerate(cuts)]
        total = sum(jnp.sum(x * x, axis=0, keepdims=True) for x in miss)
        d_guess = [((-2.0 / (T * D)) * x).astype(bf16) for x in miss]
        d_gp = [dot_t(x, cv[:, c]) for x, c in zip(d_guess, cuts)]
        d_gs = [
            (x * (y - jnp.sum(x * y, axis=-1, keepdims=True))).astype(bf16)
            for x, y in zip(gp, d_gp)
        ]
        for h, c in enumerate(cuts):
            dcv[:, c] = t_dot(low[h], d_guess[h]).astype(bf16)
            dck[:, c] = t_dot(d_gs[h], asking[h]).astype(bf16)

        @pl.when(pl.program_id(0) == 0)
        def _():
            loss[...] = total

        @pl.when(pl.program_id(0) > 0)
        def _():
            loss[...] += total

    return call(
        kernel,
        (shape((1, HD), f32), shape((rows, D), bf16), shape((rows, D), bf16)),
        (H // n,),
        [head(n, T), head(n, T, 1), head(n, T, 1, H), head(n, rows), head(n, rows, 0, H)],
        [pl.BlockSpec((1, HD), lambda h, s: (0, 0)), head(n, rows), head(n, rows)],
        none,
        (queries, key_value, key_value, comp_pair, comp_pair),
    )


def compress_back(dck, dcv, w_kv, compact, vectors, offsets):
    rows = T // 3

    def kernel(s, dck, dcv, w, compact, vec, d_compact, d_bias, dn):
        back = dot_t(jnp.concatenate([dck[...], dcv[...]], axis=1), w[...])
        natural_columns(dn, back, s, THIRDS)
        xhat, r = center_scale(compact[...])
        low = norm_back(xhat, r, row(vec, LN1_G), dn[...]).astype(bf16)
        d_compact[...] = low
        d_bias[...] = jnp.sum(low.astype(f32), axis=0, keepdims=True)

    args = (dck, dcv, w_kv, compact, vectors)
    out = (shape((rows, D), bf16), shape((1, D), f32))
    return call(
        kernel,
        out,
        (1,),
        [whole(a) for a in args],
        [whole(o) for o in out],
        offsets,
        args,
        [pltpu.VMEM((rows, D), f32)],
    )


def weight_grads(groups, scalars):
    in_specs, args, outs, out_specs, layout, scratch = [], [], [], [], [], []
    for ring, jobs in groups:
        first = 1 if ring == "x" else 5
        block = jobs[0][0][0].shape[1] // 8
        plan = []
        for xs, row_block, rows, dys, ready in jobs:
            width = dys[0].shape[1] // (1 if ready else 2)
            plan.append((width, rows, len(xs)))
            for x in xs:
                for y in range(2):
                    in_specs.append(
                        pl.BlockSpec(
                            (rows, block),
                            lambda q, s, r=row_block, f=first, y=y: (r, y * 4 + s[f + q]),
                        )
                    )
                    args.append(x)
            for dy in dys:
                in_specs.append(
                    pl.BlockSpec((rows, width), lambda q, s, r=ready: (0, 0 if r else s[0]))
                )
                args.append(dy)
            scratch.append(pltpu.VMEM((rows * len(xs), width), bf16))
        dims = (1, 2, block, sum(p[0] for p in plan))
        outs += [shape((2, *dims[1:]), bf16)] * 2
        out_specs += [
            pl.BlockSpec(dims, lambda q, s: (jnp.minimum(q, 1), 0, 0, 0)),
            pl.BlockSpec(dims, lambda q, s: (jnp.maximum(q - 2, 0), 0, 0, 0)),
        ]
        layout.append(plan)
    n_in, n_out = len(in_specs), len(outs)

    def kernel(s, *refs):
        ins, results, joined = refs[:n_in], refs[n_in : n_in + n_out], refs[n_in + n_out :]
        q = pl.program_id(0)

        @pl.when(q == 0)
        def _():
            place, k = 0, 0
            for plan in layout:
                for _, rows, n in plan:
                    da, db = ins[place + 2 * n], ins[place + 2 * n + 1]
                    if n == 2:
                        joined[k][:rows, :] = da[...]
                        joined[k][rows:, :] = db[...]
                    else:
                        joined[k][...] = (da[...].astype(f32) + db[...].astype(f32)).astype(bf16)
                    place += 2 * n + 2
                    k += 1

        place, k = 0, 0
        for i, plan in enumerate(layout):
            send, keep = results[2 * i : 2 * i + 2]
            block = send.shape[2]
            start = 0
            for width, rows, n in plan:
                x = jnp.concatenate([r[...] for r in ins[place : place + 2]], axis=1)
                if n == 2:
                    other = jnp.concatenate([r[...] for r in ins[place + 2 : place + 4]], axis=1)
                    x = jnp.concatenate([x, other], axis=0)
                value = t_dot(x, joined[k][...]).astype(bf16).reshape(2, block, width)
                cut = slice(start, start + width)
                send[0, :, :, cut] = jnp.where(q < 2, value, send[0, :, :, cut])
                keep[0, :, :, cut] = value
                start += width
                place += 2 * n + 2
                k += 1

    flat = call(kernel, tuple(outs), (4,), in_specs, out_specs, scalars, args, scratch)
    return [(flat[2 * i], flat[2 * i + 1]) for i in range(len(groups))]


def conv_grad(x, x_twin, dy, dy_twin, scalars):
    rows, columns = x.shape[1] // 2, D // 2

    def kernel(s, xa, xb, da, db, out):
        both = jnp.concatenate([xa[...], xb[...]], axis=0)
        total = t_dot(both, jnp.concatenate([da[...], db[...]], axis=0))
        out[...] = total.reshape(2, rows, columns)

    half = pl.BlockSpec((dy.shape[0], columns), lambda j, s: (0, s[0]))
    out = shape((2, rows, columns), f32)
    return call(
        kernel,
        out,
        (1,),
        [whole(x), whole(x_twin), half, half],
        whole(out),
        scalars,
        (x, x_twin, dy, dy_twin),
    )


def widen(gathered, plan, none):
    outs, specs, layout = [], [], []
    start = 0
    for rows, columns, ring in plan:
        u, chunks = rows // 16, columns // 2 // STEP
        outs.append(shape((4, 4, u, columns), f32))
        if ring == "x":
            specs.append(
                pl.BlockSpec((1, 4, u, chunks * STEP), lambda c, x, s: (x, 0, 0, c))
            )
        else:
            specs.append(
                pl.BlockSpec((4, 1, u, chunks * STEP), lambda c, x, s: (0, x, 0, c))
            )
        layout.append((start, u, chunks, ring))
        start += u * chunks

    def kernel(_, src, *results):
        for out, (start, u, chunks, ring) in zip(results, layout):
            for k in range(chunks):
                cut = slice(k * STEP, (k + 1) * STEP)
                for z in range(4):
                    value = src[z, start + k * u : start + (k + 1) * u, :].astype(f32)
                    if ring == "x":
                        out[0, z, :, cut] = value
                    else:
                        out[z, 0, :, cut] = value

    results = call(
        kernel,
        tuple(outs),
        (2, 4),
        [pl.BlockSpec((4, gathered.shape[1], STEP), lambda c, x, s: (c * 4 + x, 0, 0))],
        specs,
        none,
        (gathered,),
    )
    return [r.reshape(rows, columns) for r, (rows, columns, _) in zip(results, plan)]


def core_swap(v):
    return lax.ppermute(v, "c", [(0, 1), (1, 0)])


def pair_swap(v):
    return lax.ppermute(v, "yl", [(0, 1), (1, 0)])


def exchange(v, ring, masks):
    def flat(i, c):
        return (i // 2 * 2 + c) * 2 + i % 2 if ring == "y" else 2 * i + c

    pairs = [(flat(i, c), flat(i ^ masks[c], c)) for i in range(4) for c in range(2)]
    return lax.ppermute(v, RING[ring], pairs)


def pick(v, index, axis):
    return lax.dynamic_index_in_dim(v, index, axis, keepdims=False)


def quarters(place, core):
    first = jnp.where(core == 0, 1, 3)
    second = jnp.where(core == 0, 3, 1)
    return place, place ^ first, place ^ 2, place ^ second


class Flow:
    def __init__(self, ring, pair, done=None):
        self.ring, self.other = ring, "z" if ring == "x" else "x"
        self.before, self.result = None, done
        if done is None:
            self.send, self.keep = pair

    def start(self):
        self.got = exchange(self.send, self.ring, (1, 3))

    def sources(self):
        return [self.keep, self.got, self.last] if self.result is None else [self.result]

    def kept(self, which):
        if self.before is None:
            dims = (1, 1, *self.keep.shape[2:])
            return [pl.BlockSpec(dims, lambda y, s: (which, y, 0, 0))], [self.keep]
        return self.before(2 + which)


def onward(flows, cuts):
    in_specs, args, counts = [], [], []
    for f in flows:
        specs, arrays = f.kept(1)
        dims = (1, 1, *f.got.shape[2:])
        in_specs += specs + [pl.BlockSpec(dims, lambda y, s: (1, y, 0, 0))]
        args += arrays + [f.got]
        counts.append(len(arrays) + 1)
    out = tuple(shape(f.got.shape[1:], bf16) for f in flows)

    def kernel(_, *refs):
        k = 0
        for i, n in enumerate(counts):
            total = sum(value_of(r) for r in refs[k : k + n])
            refs[len(args) + i][...] = total.astype(bf16)
            k += n

    sums = call(
        kernel,
        out,
        (2,),
        in_specs,
        [pl.BlockSpec((1, *o.shape[1:]), lambda y, s: (y, 0, 0)) for o in out],
        cuts,
        args,
    )
    for f, v in zip(flows, sums):
        f.last = exchange(v, f.ring, (3, 1))


def value_of(ref):
    return (ref[0] if len(ref.shape) == 4 else ref[...]).astype(f32)


def turn(flows, cuts):
    in_specs, outs, out_specs, args = [], [], [], []

    counts = []
    for f in flows:
        first = 1 if f.other == "x" else 5
        arrays = f.sources()
        rows, columns = arrays[0].shape[-2] // 4, arrays[0].shape[-1]
        four = pl.BlockSpec((1, 2, rows, columns), lambda j, s, i=first: (0, 0, s[i + j], 0))
        three = pl.BlockSpec((2, rows, columns), lambda j, s, i=first: (0, s[i + j], 0))
        in_specs += [four if a.ndim == 4 else three for a in arrays]
        args += arrays
        counts.append(len(arrays))
        dims = (1, 2, rows, columns)
        outs.append(shape((2, *dims[1:]), bf16))
        out_specs.append(pl.BlockSpec(dims, lambda j, s: (j, 0, 0, 0)))

    def kernel(_, *refs):
        k = 0
        for i, n in enumerate(counts):
            total = sum(value_of(r) for r in refs[k : k + n])
            refs[len(args) + i][0] = total.astype(bf16)
            k += n

    sends = call(kernel, tuple(outs), (2,), in_specs, out_specs, cuts, args)
    for f, send in zip(flows, sends):
        f.before = halves_of(f)
        f.ring = f.other
        f.got = exchange(send, f.ring, (1, 3))


def halves_of(f):
    arrays = f.sources()
    first = 1 if f.other == "x" else 5
    rows, columns = arrays[0].shape[-2] // 4, arrays[0].shape[-1]

    def quarter(which):
        four = pl.BlockSpec((1, 1, rows, columns), lambda y, s: (0, y, s[first + which], 0))
        three = pl.BlockSpec((1, rows, columns), lambda y, s: (y, s[first + which], 0))
        return [four if a.ndim == 4 else three for a in arrays], arrays

    return quarter


def add(a, b, none):
    def kernel(_, a, b, out):
        out[...] = (a[...].astype(f32) + b[...].astype(f32)).astype(bf16)

    out = shape(a.shape, bf16)
    return call(kernel, out, (1,), [whole(a), whole(b)], whole(out), none, (a, b))


class Finish:
    def __init__(self, flows, extra, cuts):
        in_specs, args, sizes = [], [], []
        def half(spec):
            return pl.BlockSpec(
                spec.block_shape, lambda j, s: spec.index_map(lax.rem(j + s[9], 2), s)
            )

        for f in flows:
            specs, arrays = f.kept(0)
            dims = (1, 1, *f.got.shape[2:])
            specs = specs + [
                pl.BlockSpec(dims, lambda y, s: (0, y, 0, 0)),
                pl.BlockSpec((1, *f.last.shape[1:]), lambda y, s: (y, 0, 0)),
            ]
            in_specs += [half(spec) for spec in specs]
            args += arrays + [f.got, f.last]
            sizes.append((len(arrays) + 2, f.got.shape[2], f.got.shape[3] // STEP))
        for e in extra:
            in_specs.append(half(pl.BlockSpec((1, *e.shape[1:]), lambda y, s: (y, 0, 0))))
        args += extra
        rows = sum(u * n for _, u, n in sizes) + sum(e.shape[1] for e in extra)

        def kernel(_, *refs):
            send, mine = refs[-2:]
            j = pl.program_id(0)

            def put(here, value):
                @pl.when(j == 0)
                def _():
                    mine[here, :] = value

                @pl.when(j == 1)
                def _():
                    send[here, :] = value.astype(bf16)

            start, k = 0, 0
            for count, u, n in sizes:
                v = sum(value_of(r) for r in refs[k : k + count])[0]
                for i in range(n):
                    put(slice(start, start + u), v[:, i * STEP : (i + 1) * STEP])
                    start += u
                k += count
            for ref in refs[k:-2]:
                put(slice(start, start + ref.shape[1]), ref[0])
                start += ref.shape[1]

        out = (shape((rows, STEP), bf16), shape((rows, STEP), f32))
        send, self.mine = call(
            kernel, out, (2,), in_specs, [whole(o) for o in out], cuts, args
        )
        self.got = exchange(send, "y", (1, 3))

    def second(self, none):
        self.mine = add(self.mine, self.got, none)
        self.far = lax.ppermute(self.mine, "yh", [(0, 1), (1, 0)])

    def gather(self, none):
        return lax.all_gather(add(self.mine, self.far, none), ("c", "x", "z"), axis=0)


def per_device(
    tokens,
    memory,
    compressed,
    cotangent,
    ln1_g,
    ln1_b,
    w_q,
    w_kv,
    w_r,
    bias_u,
    bias_v,
    w_o,
    ln2_g,
    ln2_b,
    w_in,
    b_in,
    w_out,
    b_out,
    conv_w,
    conv_b,
):
    line.held, line.due = [], {}
    tokens, memory, compressed, cotangent = tokens[0], memory[0], compressed[0], cotangent[0]
    yl, core = lax.axis_index("yl"), lax.axis_index("c")
    place = {"x": lax.axis_index("x"), "z": lax.axis_index("z")}
    none = jnp.zeros((1,), jnp.int32)
    ints = lambda *v: jnp.stack([jnp.asarray(i, jnp.int32) for i in v])

    def thirds(rows):
        half = rows // 2
        other = (1 - yl) * half
        return [yl * half, other + core * (half // 2), other + (1 - core) * (half // 2)]

    def both(v):
        return (v, core_swap(v))

    spot = (place["x"] * 4 + place["z"]) * 2 + core
    piece = pack(
        (ln1_g, ln1_b, bias_u, bias_v, ln2_g, ln2_b, b_out, conv_b, b_in),
        w_in,
        w_out,
        ints(spot),
    )
    piece_got = exchange(piece, "y", (1, 3))

    kv_part, small, o_part = pack_rows(w_kv, w_q, w_r, w_o, ints(core))
    (piece_got,) = gate((piece_got,), kv_part)
    kv_got = exchange(kv_part, "y", (1, 3))
    small_got = exchange(small, "y", (1, 3))
    o_got = exchange(o_part, "y", (1, 3))

    def joined(w, got, twin):
        return jnp.concatenate([w, got, twin], axis=0)

    spread = lax.all_gather(piece_got[:-16], ("x", "z", "c"), axis=0)
    thirds_d = ints(*thirds(D))
    thirds_c = ints(*thirds(3 * D), *thirds(D))
    sinus_table = sinusoid(KEYS, D).astype(bf16)
    sinus_rel = jnp.concatenate(
        [
            lax.dynamic_slice_in_dim(sinus_table, thirds_d[i], width, 1)
            for i, width in enumerate(THIRDS)
        ],
        axis=1,
    )
    line.hold(sinus_rel)
    vectors, b_in = unpack(piece, piece_got, ints(yl))

    normed, normed_rel, oldest, old_quarters = first_norm(compressed, memory, tokens, vectors, thirds_d)
    both_normed, both_cot = both(normed), both(cotangent)
    own, first, far, second = quarters(place["x"], core)
    got = exchange(
        jnp.stack([pick(old_quarters, first, 0), pick(old_quarters, far, 0)]), "x", (1, 3)
    )
    got_far = exchange(jnp.stack([pick(old_quarters, second, 0), got[1]]), "x", (3, 1))
    old_ring = jnp.concatenate([pick(old_quarters, own, 0), got[0], got_far[0], got_far[1]])
    old_twin = core_swap(old_ring)
    kv_got, small_got = gate((kv_got, small_got), normed)
    kv_twin, small_twin = core_swap(kv_got), core_swap(small_got)
    kv_whole = joined(w_kv, kv_got, kv_twin)
    q_whole, r_whole = [
        joined(w, small_got[i], small_twin[i]) for i, w in enumerate((w_q, w_r))
    ]
    key_value = dot(normed_rel, kv_whole).astype(bf16)
    line.hold(key_value)
    queries = dot(normed_rel[2 * T :], q_whole)
    relative = dot(sinus_rel, r_whole).astype(bf16)
    (o_got,) = gate((o_got,), key_value, queries, relative)
    o_whole = joined(w_o, o_got, core_swap(o_got))
    line.hold(queries, relative)
    line.hold(got)
    probs, attended = attend(queries, key_value, relative, vectors, none)
    line.hold(both_normed[1], both_cot[1], got_far)
    residual, normed2, normed2_rel = out_and_norm(attended, o_whole, tokens, vectors, thirds_d)
    both_n2, both_att = both(normed2), both(attended)

    cuts, rels, twins = [], [], []
    for ring in ("x", "z"):
        own, first, far, second = quarters(place[ring], core)
        cuts += [first, far, own, second]
        rels.append([own, first, second, far])
        twins.append([own, second, first, far])
    cuts = ints(core, *cuts, yl)

    def flows(groups):
        pairs = weight_grads(groups, cuts)
        return [Flow(ring, pair) for (ring, _), pair in zip(groups, pairs)]

    def start(some):
        for f in some:
            f.start()

    line.hold(old_twin)
    hidden, d_pre, mixed_out, d_normed2, d_b_in = feed_forward(
        normed2_rel, residual, cotangent, w_in, w_out, spread, b_in, vectors, ints(yl)
    )
    both_hidden, both_pre = both(hidden), both(d_pre)
    conv_got = exchange(half_rows(conv_w, ints(core)), "y", (1, 3))
    d_residual, d_branch, d_attended, d_ln2_g, d_ln2_b, d_b_out = second_norm_back(
        cotangent, d_normed2, residual, vectors, o_whole, thirds_d
    )
    both_branch = both(d_branch)
    large = flows(
        [
            ("x", [(both_hidden, 0, T, both_cot, False)]),
            ("z", [(both_n2, 0, T, both_pre, False), (both_att, 0, T, both_branch, False)]),
        ]
    )
    start(large)
    line.hold(conv_got)
    conv_pieces = (conv_w, conv_got, core_swap(conv_got))
    d_kv, my_kv, give_kv, d_relative, d_queries, d_bias_u, d_bias_v = attend_back(
        queries, key_value, relative, vectors, probs, d_attended, ints(core)
    )
    both_kv = (my_kv, core_swap(give_kv))
    both_q, both_rel = both(d_queries), both(d_relative)

    compact, comp_normed = compress(oldest, conv_pieces, vectors, thirds_c)
    comp_pair = dot(comp_normed, kv_whole).astype(bf16)
    compressed_next = jnp.concatenate([compressed[T // 3 :], compact], axis=0)
    near = flows(
        [
            ("x", [(both_normed, 0, KEYS, both_kv, True)]),
            (
                "z",
                [
                    (both_normed, 2, T, both_q, False),
                    ((sinus_table,), 0, KEYS, both_rel, False),
                ],
            ),
        ]
    )
    onward(large, cuts)
    loss, d_ck, d_cv = reconstruct(queries, key_value, comp_pair, none)
    recon_loss = jnp.sum(loss) / (T * D)
    d_compact, d_conv_b = compress_back(d_ck, d_cv, kv_whole, compact, vectors, thirds_d)
    ring_got = exchange(d_compact, "x", (1, 3))
    sends = gate([f.send for f in near], ring_got)
    for f, send in zip(near, sends):
        f.send = send
    start(near)
    line.hold(ring_got)
    turn(large, cuts)
    ring_pair = jnp.concatenate([d_compact, ring_got])
    pair_got = exchange(ring_pair, "x", (3, 1))
    d_tokens, d_ln1_g, d_ln1_b = first_norm_back(
        d_kv, d_queries, kv_whole, q_whole, compressed, memory, tokens, vectors, d_residual,
        thirds_d,
    )
    (pair_got,) = gate((pair_got,), d_ln1_g)
    onward(large, cuts)
    compact_ring = jnp.concatenate([ring_pair, pair_got])
    compact_twin = core_swap(compact_ring)
    onward(near, cuts)
    line.expect(1, *[f.last for f in near])
    line.hold(compact_twin)
    early = Finish(large, [], cuts)
    conv = Flow("x", None, conv_grad(old_ring, old_twin, compact_ring, compact_twin, cuts))
    early.second(none)
    late_flows = [*near, conv]
    turn(late_flows, cuts)
    early_sums = early.gather(none)
    onward(late_flows, cuts)

    total = jnp.concatenate(
        [d_ln1_g, d_ln1_b, d_bias_u, d_bias_v, d_ln2_g, d_ln2_b, d_b_out, d_conv_b]
        + [d_b_in]
    )
    total = jnp.concatenate(
        [
            total[:8].reshape(8, 2, STEP).transpose(1, 0, 2),
            total[8:].reshape(2, 4, STEP),
            jnp.zeros((2, 4, STEP), f32),
        ],
        axis=1,
    )
    late = Finish(late_flows, [total], cuts)
    late.second(none)
    line.hold(early_sums)
    late_sums = late.gather(none)

    g_out, g_in, g_o = widen(
        early_sums, [(FF // 2, D, "x"), (D // 2, FF, "z"), (D // 2, D, "z")], none
    )
    g_kv, g_q, g_r, g_conv = widen(
        late_sums,
        [(D // 2, 2 * D, "x"), (D // 2, D, "z"), (D // 2, D, "z"), (3 * D // 2, D, "x")],
        none,
    )
    half = jnp.sum(late_sums[:, 224:236].astype(f32), axis=0)
    t_ln1_g, t_ln1_b, t_bu, t_bv, t_ln2_g, t_ln2_b, t_bout, t_convb = [half[i] for i in range(8)]
    t_bin = half[8:].reshape(-1)
    return (
        mixed_out[None],
        compressed_next[None],
        recon_loss[None],
        d_tokens[None],
        t_ln1_g,
        t_ln1_b,
        g_q,
        g_kv,
        g_r,
        t_bu,
        t_bv,
        g_o,
        t_ln2_g,
        t_ln2_b,
        g_in,
        t_bin,
        g_out,
        t_bout,
        g_conv,
        t_convb,
    )


def solution(mesh):
    fine = Mesh(mesh.devices.reshape(2, 4, 4, 2, 2), AXES)
    stream = P(AXES, None, None)
    vec, mat = P("yl"), P("yl", None)
    weights = (vec, vec, mat, mat, mat, vec, vec, mat, vec, vec, mat, vec, mat, vec, mat, vec)
    return jax.shard_map(
        per_device,
        mesh=fine,
        in_specs=(stream,) * 4 + weights,
        out_specs=(stream, stream, P(AXES), stream) + weights,
        check_vma=False,
    )
```

```python
import jax
import jax.numpy as jnp
from jax import lax
from jax.experimental import pallas as pl
from jax.experimental.pallas import tpu as pltpu
from jax.sharding import Mesh, PartitionSpec as P

H = 8
HD = 128
D = 1024
T = 192
KEYS = 576
PAD = 640
FF = 4096
FACTOR = HD ** (-0.5)
f32 = jnp.float32
bf16 = jnp.bfloat16
AXES = ("yh", "x", "z", "c", "yl")
RING = {"x": ("x", "c"), "z": ("z", "c"), "y": ("yh", "c", "yl")}


def sinusoid(key_count, model_dim):
    distance = (key_count - 1 - jnp.arange(key_count)).astype(f32)
    inverse = 1.0 / 10000.0 ** (jnp.arange(0, model_dim, 2).astype(f32) / model_dim)
    angles = distance[:, None] * inverse[None, :]
    return jnp.concatenate([jnp.sin(angles), jnp.cos(angles)], axis=-1)


def dot(a, b):
    return jnp.dot(a, b, preferred_element_type=f32)


def dot_t(a, b):
    return lax.dot_general(a, b, (((1,), (1,)), ((), ())), preferred_element_type=f32)


def t_dot(a, b):
    return lax.dot_general(a, b, (((0,), (0,)), ((), ())), preferred_element_type=f32)


class Line:
    def __init__(self):
        self.held, self.due = [], {}

    def hold(self, *values):
        self.held += values

    def expect(self, gap, *values):
        self.due.setdefault(gap, []).extend(values)

    def ran(self, result):
        self.held = [result, *self.due.get(1, [])]
        self.due = {gap - 1: values for gap, values in self.due.items() if gap > 1}

    def later(self, value):
        return lax.optimization_barrier((value, *self.held))[0] if self.held else value


line = Line()


def call(kernel, out, grid, in_specs, out_specs, scalars, args, scratch=()):
    held, n = line.held, len(args)

    def body(s, *refs):
        kernel(s, *refs[:n], *refs[n + len(held) :])

    result = pl.pallas_call(
        body,
        out_shape=out,
        grid_spec=pltpu.PrefetchScalarGridSpec(
            num_scalar_prefetch=1,
            grid=grid,
            in_specs=list(in_specs) + [pl.BlockSpec(memory_space=pl.ANY)] * len(held),
            out_specs=out_specs,
            scratch_shapes=list(scratch),
        ),
        compiler_params=pltpu.CompilerParams(vmem_limit_bytes=56 << 20),
    )(scalars, *args, *held)
    line.ran(jax.tree.leaves(result)[0])
    return result


def gate(values, *after):
    n = len(values)
    anywhere = pl.BlockSpec(memory_space=pl.ANY)
    return pl.pallas_call(
        lambda *refs: None,
        out_shape=[jax.ShapeDtypeStruct(v.shape, v.dtype) for v in values],
        in_specs=[anywhere] * (n + len(after)),
        out_specs=[anywhere] * n,
        input_output_aliases={i: i for i in range(n)},
    )(*values, *after)


def whole(a):
    zeros = (0,) * a.ndim
    return pl.BlockSpec(a.shape, lambda *_: zeros)


def shape(dims, dtype):
    return jax.ShapeDtypeStruct(dims, dtype)


def at(offset):
    return pl.multiple_of(offset, 128)


def center_scale(v):
    mid = v - jnp.mean(v, axis=-1, keepdims=True)
    r = lax.rsqrt(jnp.mean(mid * mid, axis=-1, keepdims=True) + 1e-5)
    return mid * r, r


def norm_back(xhat, r, g, dn):
    gd = dn * g
    return r * (
        gd
        - jnp.mean(gd, axis=-1, keepdims=True)
        - xhat * jnp.mean(gd * xhat, axis=-1, keepdims=True)
    )


def softmax(s):
    e = jnp.exp(s - jnp.max(s, axis=-1, keepdims=True))
    return e / jnp.sum(e, axis=-1, keepdims=True)


(LN1_G, LN1_B, BIAS_U, BIAS_V, LN2_G, LN2_B, B_OUT, CONV_B) = range(8)


def row(ref, i):
    return ref[i : i + 1, :]


def pack(vectors, w_in, w_out, scalars):
    n_in, n_out = (w.shape[0] // 32 for w in (w_in, w_out))
    chunks = FF // D
    rows = n_out + n_in * chunks
    half = D // 2

    def kernel(_, *refs):
        wi, wo, piece, flat = refs[-4:]
        flat[...] = jnp.zeros_like(flat)
        for i, ref in enumerate(refs[:8]):
            flat[i : i + 1, :half] = ref[...].astype(f32).reshape(1, half)
        flat[8 : 8 + FF // 2 // D, :] = refs[8][...].astype(f32).reshape(FF // 2 // D, D)
        piece[:n_out, :] = wo[...]
        for i in range(chunks):
            piece[n_out + i * n_in : n_out + (i + 1) * n_in, :] = wi[:, i * D : (i + 1) * D]
        piece[rows:, :] = flat[...].astype(bf16)

    out = shape((rows + 16, D), bf16)
    return call(
        kernel,
        out,
        (1,),
        [whole(v) for v in vectors]
        + [
            pl.BlockSpec((w.shape[0] // 32, w.shape[1]), lambda j, s: (s[0], 0))
            for w in (w_in, w_out)
        ],
        whole(out),
        scalars,
        (*vectors, w_in, w_out),
        [pltpu.VMEM((16, D), f32)],
    )


def half_rows(w, scalars):
    n = w.shape[0] // 2

    def kernel(_, w, out):
        out[...] = w[...]

    out = shape((n, w.shape[1]), w.dtype)
    spec = pl.BlockSpec((n, w.shape[1]), lambda j, s: (s[0], 0))
    return call(kernel, out, (1,), [spec], whole(out), scalars, (w,))


def pack_rows(w_kv, w_q, w_r, w_o, scalars):
    n = w_q.shape[0] // 2

    def kernel(_, kv, q, r, o, kv_out, out, o_out):
        kv_out[...] = kv[...]
        out[0] = q[...]
        out[1] = r[...]
        o_out[...] = o[...]

    args = (w_kv, w_q, w_r, w_o)
    out = (shape((n, 2 * D), bf16), shape((2, n, D), bf16), shape((n, D), bf16))
    return call(
        kernel,
        out,
        (1,),
        [pl.BlockSpec((w.shape[0] // 2, w.shape[1]), lambda j, s: (s[0], 0)) for w in args],
        [whole(o) for o in out],
        scalars,
        args,
    )


def unpack(mine, theirs, scalars):
    half = D // 2
    at_row = mine.shape[0] // 16 - 1
    tail = pl.BlockSpec((16, D), lambda j, s: (at_row, 0))

    def kernel(s, mine, theirs, vectors, b_in):
        a, b = mine[...].astype(f32), theirs[...].astype(f32)
        low = jnp.where(s[0] == 0, a, b)
        high = jnp.where(s[0] == 0, b, a)
        vectors[:, :half] = low[:8, :half]
        vectors[:, half:] = high[:8, :half]
        rows = FF // 2 // D
        b_in[:rows] = low[8 : 8 + rows]
        b_in[rows:] = high[8 : 8 + rows]

    out = (shape((8, D), f32), shape((FF // D, D), f32))
    return call(
        kernel, out, (1,), [tail, tail], [whole(o) for o in out], scalars, (mine, theirs)
    )


def relative_columns(x, s, widths):
    parts = [x[:, pl.ds(at(s[i]), width)] for i, width in enumerate(widths)]
    return jnp.concatenate(parts, axis=1)


def natural_columns(out, x, s, widths):
    start = 0
    for i, width in enumerate(widths):
        out[:, pl.ds(at(s[i]), width)] = x[:, start : start + width]
        start += width


THIRDS = (D // 2, D // 4, D // 4)


def first_norm(compressed, memory, tokens, vectors, offsets):
    def kernel(s, comp, mem, tok, vec, out, out_rel, old, old_quarters):
        gain, bias = row(vec, LN1_G), row(vec, LN1_B)

        def part(ref, base):
            for i in range(0, T, 32):
                xhat, r = center_scale(ref[i : i + 32, :].astype(f32))
                out[base + i : base + i + 32, :] = (xhat * gain + bias).astype(bf16)

        part(comp, 0)
        part(mem, T)
        part(tok, 2 * T)
        out_rel[...] = relative_columns(out, s, THIRDS)
        line_of = lax.broadcasted_iota(jnp.int32, (T // 3, T), 0)
        col = lax.broadcasted_iota(jnp.int32, (T // 3, T), 1)
        low = mem[...].astype(bf16)
        for tap in range(3):
            take = jnp.where(col == 3 * line_of + tap, 1.0, 0.0).astype(bf16)
            old[:, tap * D : (tap + 1) * D] = dot(take, low).astype(bf16)
        width = 3 * D // 8
        for q in range(4):
            for y in range(2):
                begin = y * 3 * D // 2 + q * width
                old_quarters[q, :, y * width : (y + 1) * width] = old[:, begin : begin + width]

    args = (compressed, memory, tokens, vectors)
    out = (
        shape((KEYS, D), bf16),
        shape((KEYS, D), bf16),
        shape((T // 3, 3 * D), bf16),
        shape((4, T // 3, 3 * D // 4), bf16),
    )
    return call(
        kernel, out, (1,), [whole(a) for a in args], [whole(o) for o in out], offsets, args
    )


def head(n, rows, row_block=0, first=0):
    return pl.BlockSpec((rows, n * HD), lambda h, s: (row_block, first // n + h))


def columns_of(n):
    return [slice(i * HD, (i + 1) * HD) for i in range(n)]


def attend(queries, key_value, relative, vectors, none):
    n = 2

    def kernel(_, q, k, v, rel, vec, probs, out):
        pad = jnp.zeros((PAD - KEYS, HD), bf16)
        i = lax.broadcasted_iota(jnp.int32, (T, PAD), 0)
        j = lax.broadcasted_iota(jnp.int32, (T, PAD), 1)
        seen = j <= i + (KEYS - T)
        cuts = columns_of(n)
        content = [((q[:, c] + vec[BIAS_U : BIAS_U + 1, c]) * FACTOR).astype(bf16) for c in cuts]
        located = [((q[:, c] + vec[BIAS_V : BIAS_V + 1, c]) * FACTOR).astype(bf16) for c in cuts]
        raw = [
            dot_t(x, jnp.concatenate([rel[:, c], pad], axis=0)) for x, c in zip(located, cuts)
        ]
        near = [dot_t(x, jnp.concatenate([k[:, c], pad], axis=0)) for x, c in zip(content, cuts)]
        raw = [pltpu.roll(x, PAD - T + 1, 1, stride=1, stride_axis=0) for x in raw]
        p = [softmax(jnp.where(seen, a + b, -1e30)) for a, b in zip(near, raw)]
        for h, c in enumerate(cuts):
            probs[h] = p[h]
            value = jnp.concatenate([v[:, c], pad], axis=0)
            out[:, c] = dot(p[h].astype(bf16), value).astype(bf16)

    return call(
        kernel,
        (shape((H, T, PAD), f32), shape((T, D), bf16)),
        (H // n,),
        [head(n, T), head(n, KEYS), head(n, KEYS, 0, H), head(n, KEYS), head(n, 8)],
        [pl.BlockSpec((n, T, PAD), lambda h, s: (h, 0, 0)), head(n, T)],
        none,
        (queries, key_value, key_value, relative, vectors),
    )


def attend_back(queries, key_value, relative, vectors, probs, d_attended, scalars):
    n = 2

    def kernel(s, q, k, v, rel, vec, probs, d_att, d_kv, mine, give, d_rel, d_q, d_bu, d_bv):
        pad = jnp.zeros((PAD - KEYS, HD), bf16)
        i = lax.broadcasted_iota(jnp.int32, (T, T), 0)
        j = lax.broadcasted_iota(jnp.int32, (T, T), 1)
        flip = jnp.where(i + j == T - 1, 1.0, 0.0).astype(bf16)
        cuts = columns_of(n)
        content = [((q[:, c] + vec[BIAS_U : BIAS_U + 1, c]) * FACTOR).astype(bf16) for c in cuts]
        located = [((q[:, c] + vec[BIAS_V : BIAS_V + 1, c]) * FACTOR).astype(bf16) for c in cuts]
        da = [d_att[:, c] for c in cuts]
        d_p = [dot_t(x, jnp.concatenate([v[:, c], pad], axis=0)) for x, c in zip(da, cuts)]
        d_v = [t_dot(probs[h].astype(bf16), x)[:KEYS].astype(bf16) for h, x in enumerate(da)]
        d_s = []
        for h, x in enumerate(d_p):
            p = probs[h]
            d_s.append((p * (x - jnp.sum(p * x, axis=-1, keepdims=True))).astype(bf16))
        d_raw = [dot(flip, x) for x in d_s]
        d_c = [
            dot(x, jnp.concatenate([k[:, c], pad], axis=0)) * FACTOR for x, c in zip(d_s, cuts)
        ]
        d_k = [t_dot(x, y)[:KEYS].astype(bf16) for x, y in zip(d_s, content)]
        d_raw = [pltpu.roll(x, 0, 1, stride=1, stride_axis=0).astype(bf16) for x in d_raw]
        d_raw = [dot(flip, x).astype(bf16) for x in d_raw]
        d_l = [
            dot(x, jnp.concatenate([rel[:, c], pad], axis=0)) * FACTOR for x, c in zip(d_raw, cuts)
        ]
        for h, c in enumerate(cuts):
            d_rel[:, c] = t_dot(d_raw[h], located[h])[:KEYS].astype(bf16)
            d_kv[0, :, c] = d_k[h]
            d_kv[1, :, c] = d_v[h]
            mine[:, c] = jnp.where(s[0] == 0, d_k[h], d_v[h])
            give[:, c] = jnp.where(s[0] == 0, d_v[h], d_k[h])
            d_q[:, c] = (d_c[h] + d_l[h]).astype(bf16)
            d_bu[:, c] = jnp.sum(d_c[h], axis=0, keepdims=True)
            d_bv[:, c] = jnp.sum(d_l[h], axis=0, keepdims=True)

    return call(
        kernel,
        (shape((2, KEYS, D), bf16),)
        + (shape((KEYS, D), bf16),) * 3
        + (shape((T, D), bf16), shape((1, D), f32), shape((1, D), f32)),
        (H // n,),
        [
            head(n, T),
            head(n, KEYS),
            head(n, KEYS, 0, H),
            head(n, KEYS),
            head(n, 8),
            pl.BlockSpec((n, T, PAD), lambda h, s: (h, 0, 0)),
            head(n, T),
        ],
        [
            pl.BlockSpec((2, KEYS, n * HD), lambda h, s: (0, 0, h)),
            head(n, KEYS),
            head(n, KEYS),
            head(n, KEYS),
            head(n, T),
            head(n, 1),
            head(n, 1),
        ],
        scalars,
        (queries, key_value, key_value, relative, vectors, probs, d_attended),
    )


def out_and_norm(attended, w_o, tokens, vectors, offsets):
    def kernel(s, att, w, tok, vec, res, n2, n2_rel):
        total = tok[...].astype(f32) + dot(relative_columns(att, s, THIRDS), w[...])
        res[...] = total
        xhat, r = center_scale(total)
        n2[...] = (xhat * row(vec, LN2_G) + row(vec, LN2_B)).astype(bf16)
        other = at(D // 2 - s[0])
        n2_rel[:, : D // 2] = n2[:, pl.ds(at(s[0]), D // 2)]
        n2_rel[:, D // 2 :] = n2[:, pl.ds(other, D // 2)]

    args = (attended, w_o, tokens, vectors)
    out = (shape((T, D), f32), shape((T, D), bf16), shape((T, D), bf16))
    return call(
        kernel, out, (1,), [whole(a) for a in args], [whole(o) for o in out], offsets, args
    )


STEP = 512
UNITS = 1024
HALF = FF // 2 // UNITS


def feed_forward(n2_rel, residual, cotangent, w_in, w_out, spread, b_in, vectors, scalars):
    n_in = w_in.shape[0] // 32
    n_out = w_out.shape[0] // 32
    skip = n_out // n_in
    per = UNITS // n_out
    K_NORM = 0.7978845608028654

    def natural(j, s):
        return lax.rem(j + s[0] * HALF, 2 * HALF)

    def kernel(s, n2, res, cot, wi0, wi1, wo0, wo1, bi, vec, hid, dpre, mixed, dn2, dbi, acc, back):
        j = pl.program_id(0)
        n = natural(j, s)

        @pl.when(j == 0)
        def _():
            acc[...] = jnp.zeros_like(acc)
            back[...] = jnp.zeros_like(back)

        wo = jnp.where(j < HALF, wo0[...], wo1[...].reshape(UNITS, D))
        win = jnp.concatenate([wi0[...], wi1[...].reshape(D // 2, UNITS)], axis=0)
        pre = dot(n2[...], win) + bi[pl.ds(n, 1), :]
        d_hidden = dot_t(cot[...], wo)
        square = pre * pre
        t = jnp.tanh(K_NORM * pre * (1.0 + 0.044715 * square))
        gate_ = 0.5 * (1.0 + t)
        hidden = (pre * gate_).astype(bf16)
        slope = gate_ + (0.5 * K_NORM) * pre * (1.0 - t * t) * (1.0 + (3 * 0.044715) * square)
        d_pre = (d_hidden * slope).astype(bf16)
        hid[...] = hidden
        dpre[...] = d_pre
        dbi[pl.ds(n, 1), :] = jnp.sum(d_pre.astype(f32), axis=0, keepdims=True)
        acc[...] += dot(hidden, wo)
        back[...] += dot_t(d_pre, win)

        @pl.when(j == 2 * HALF - 1)
        def _():
            mixed[...] = (res[...] + acc[...] + row(vec, B_OUT)).astype(bf16)
            dn2[:, pl.ds(at(s[0] * (D // 2)), D // 2)] = back[:, : D // 2]
            dn2[:, pl.ds(at((1 - s[0]) * (D // 2)), D // 2)] = back[:, D // 2 :]

    out = (
        shape((T, FF), bf16),
        shape((T, FF), bf16),
        shape((T, D), bf16),
        shape((T, D), f32),
        shape((2 * HALF, UNITS), f32),
    )
    by_unit = pl.BlockSpec((T, UNITS), lambda j, s: (0, natural(j, s)))
    return call(
        kernel,
        out,
        (2 * HALF,),
        [
            whole(n2_rel),
            whole(residual),
            whole(cotangent),
            pl.BlockSpec((D // 2, UNITS), lambda j, s: (0, natural(j, s))),
            pl.BlockSpec((32, n_in, UNITS), lambda j, s: (0, skip + natural(j, s), 0)),
            pl.BlockSpec((UNITS, D), lambda j, s: (jnp.minimum(j, HALF - 1), 0)),
            pl.BlockSpec(
                (per, n_out, D), lambda j, s: (jnp.maximum(j - HALF, 0), 0, 0)
            ),
            whole(b_in),
            whole(vectors),
        ],
        [by_unit, by_unit, whole(out[2]), whole(out[3]), whole(out[4])],
        scalars,
        (n2_rel, residual, cotangent, w_in, spread, w_out, spread, b_in, vectors),
        [pltpu.VMEM((T, D), f32), pltpu.VMEM((T, D), f32)],
    )


def second_norm_back(cotangent, d_n2, residual, vectors, w_o, offsets):
    def kernel(s, cot, dn, res, vec, w, d_res, d_br, d_att, dg, db, dbo):
        xhat, r = center_scale(res[...])
        dn, wide = dn[...], cot[...].astype(f32)
        dg[...] = jnp.sum(dn * xhat, axis=0, keepdims=True)
        db[...] = jnp.sum(dn, axis=0, keepdims=True)
        dbo[...] = jnp.sum(wide, axis=0, keepdims=True)
        total = wide + norm_back(xhat, r, row(vec, LN2_G), dn)
        d_res[...] = total
        low = total.astype(bf16)
        d_br[...] = low
        natural_columns(d_att, dot_t(low, w[...]).astype(bf16), s, THIRDS)

    args = (cotangent, d_n2, residual, vectors, w_o)
    out = (
        shape((T, D), f32),
        shape((T, D), bf16),
        shape((T, D), bf16),
        shape((1, D), f32),
        shape((1, D), f32),
        shape((1, D), f32),
    )
    return call(
        kernel, out, (1,), [whole(a) for a in args], [whole(o) for o in out], offsets, args
    )


def first_norm_back(d_kv, d_q, w_kv, w_q, compressed, memory, tokens, vectors, d_res, offsets):
    steps = 4
    wide, slim = 2 * D // steps, D // steps

    def kernel(s, dkv, dq, kw, qw, comp, mem, tok, vec, dres, dtok, dg, db, acc, nat, xh, rs):
        j = pl.program_id(0)

        def product(start):
            value = dot_t(dkv[0], kw[...])
            if start:
                acc[...] = value
            else:
                acc[...] += value
            acc[2 * T :, :] += dot_t(dq[...], qw[...])

        for block, ref in enumerate((comp, mem, tok)):

            @pl.when(j == block)
            def _(block=block, ref=ref):
                product(block == 0)
                for i in range(0, T, 32):
                    xhat, r = center_scale(ref[i : i + 32, :].astype(f32))
                    xh[block * T + i : block * T + i + 32, :] = xhat
                    if block == 2:
                        rs[i : i + 32, :] = jnp.broadcast_to(r, (32, HD))

        @pl.when(j == steps - 1)
        def _():
            product(False)
            natural_columns(nat, acc, s, THIRDS)
            gain = row(vec, LN1_G)
            sum_g = jnp.zeros((8, D), f32)
            sum_b = jnp.zeros((8, D), f32)
            for i in range(0, KEYS, 32):
                dn, xhat = nat[i : i + 32, :], xh[i : i + 32, :]
                both = dn * xhat
                sum_g += (both[:8] + both[8:16]) + (both[16:24] + both[24:])
                sum_b += (dn[:8] + dn[8:16]) + (dn[16:24] + dn[24:])
                if i >= 2 * T:
                    k = i - 2 * T
                    r = rs[k : k + 32, :1]
                    dtok[k : k + 32, :] = dres[k : k + 32, :] + norm_back(xhat, r, gain, dn)
            dg[...] = jnp.sum(sum_g, axis=0, keepdims=True)
            db[...] = jnp.sum(sum_b, axis=0, keepdims=True)

    rest = (compressed, memory, tokens, vectors, d_res)
    out = (shape((T, D), f32), shape((1, D), f32), shape((1, D), f32))
    return call(
        kernel,
        out,
        (steps,),
        [
            pl.BlockSpec((1, KEYS, wide), lambda j, s: (j // (steps // 2), 0, lax.rem(j, steps // 2))),
            pl.BlockSpec((T, slim), lambda j, s: (0, j)),
            pl.BlockSpec((D, wide), lambda j, s: (0, j)),
            pl.BlockSpec((D, slim), lambda j, s: (0, j)),
        ]
        + [whole(a) for a in rest],
        [whole(o) for o in out],
        offsets,
        (d_kv, d_q, w_kv, w_q, *rest),
        [pltpu.VMEM((KEYS, D), f32)] * 3 + [pltpu.VMEM((T, HD), f32)],
    )


def compress(oldest, pieces, vectors, offsets):
    block = 256
    rows = T // 3

    def kernel(s, x, w0, w1, w2, vec, compact, normed, x_rel, natural):
        j = pl.program_id(0)

        @pl.when(j == 0)
        def _():
            x_rel[...] = relative_columns(x, s, (3 * D // 2, 3 * D // 4, 3 * D // 4))

        w = jnp.concatenate([w0[...], w1[...], w2[...]], axis=0)
        here = pl.ds(at(j * block), block)
        compact[:, here] = dot(x_rel[...], w) + vec[CONV_B : CONV_B + 1, here]

        @pl.when(j == D // block - 1)
        def _():
            xhat, r = center_scale(compact[...])
            natural[...] = (xhat * row(vec, LN1_G) + row(vec, LN1_B)).astype(bf16)
            start = 0
            for i, width in enumerate(THIRDS):
                normed[:, start : start + width] = natural[:, pl.ds(at(s[3 + i]), width)]
                start += width

    out = (shape((rows, D), f32), shape((rows, D), bf16))
    return call(
        kernel,
        out,
        (D // block,),
        [whole(oldest)]
        + [pl.BlockSpec((w.shape[0], block), lambda j, s: (0, j)) for w in pieces]
        + [whole(vectors)],
        [whole(o) for o in out],
        offsets,
        (oldest, *pieces, vectors),
        [pltpu.VMEM((rows, 3 * D), bf16), pltpu.VMEM((rows, D), bf16)],
    )


def reconstruct(queries, key_value, comp_pair, none):
    rows = T // 3
    n = 4

    def kernel(_, q, k, v, ck, cv, loss, dck, dcv):
        cuts = columns_of(n)
        asking = [(q[:, c] * FACTOR).astype(bf16) for c in cuts]
        far = [dot_t(x, k[:, c]) for x, c in zip(asking, cuts)]
        near = [dot_t(x, ck[:, c]) for x, c in zip(asking, cuts)]
        p = [softmax(x).astype(bf16) for x in far]
        gp = [softmax(x) for x in near]
        low = [x.astype(bf16) for x in gp]
        miss = [dot(p[h], v[:, c]) - dot(low[h], cv[:, c]) for h, c in enumerate(cuts)]
        total = sum(jnp.sum(x * x, axis=0, keepdims=True) for x in miss)
        d_guess = [((-2.0 / (T * D)) * x).astype(bf16) for x in miss]
        d_gp = [dot_t(x, cv[:, c]) for x, c in zip(d_guess, cuts)]
        d_gs = [
            (x * (y - jnp.sum(x * y, axis=-1, keepdims=True))).astype(bf16)
            for x, y in zip(gp, d_gp)
        ]
        for h, c in enumerate(cuts):
            dcv[:, c] = t_dot(low[h], d_guess[h]).astype(bf16)
            dck[:, c] = t_dot(d_gs[h], asking[h]).astype(bf16)

        @pl.when(pl.program_id(0) == 0)
        def _():
            loss[...] = total

        @pl.when(pl.program_id(0) > 0)
        def _():
            loss[...] += total

    return call(
        kernel,
        (shape((1, HD), f32), shape((rows, D), bf16), shape((rows, D), bf16)),
        (H // n,),
        [head(n, T), head(n, T, 1), head(n, T, 1, H), head(n, rows), head(n, rows, 0, H)],
        [pl.BlockSpec((1, HD), lambda h, s: (0, 0)), head(n, rows), head(n, rows)],
        none,
        (queries, key_value, key_value, comp_pair, comp_pair),
    )


def compress_back(dck, dcv, w_kv, compact, vectors, offsets):
    rows = T // 3

    def kernel(s, dck, dcv, w, compact, vec, d_compact, d_bias, dn):
        back = dot_t(jnp.concatenate([dck[...], dcv[...]], axis=1), w[...])
        natural_columns(dn, back, s, THIRDS)
        xhat, r = center_scale(compact[...])
        low = norm_back(xhat, r, row(vec, LN1_G), dn[...]).astype(bf16)
        d_compact[...] = low
        d_bias[...] = jnp.sum(low.astype(f32), axis=0, keepdims=True)

    args = (dck, dcv, w_kv, compact, vectors)
    out = (shape((rows, D), bf16), shape((1, D), f32))
    return call(
        kernel,
        out,
        (1,),
        [whole(a) for a in args],
        [whole(o) for o in out],
        offsets,
        args,
        [pltpu.VMEM((rows, D), f32)],
    )


def weight_grads(groups, scalars):
    in_specs, args, outs, out_specs, layout, scratch = [], [], [], [], [], []
    for ring, jobs in groups:
        first = 1 if ring == "x" else 5
        block = jobs[0][0][0].shape[1] // 8
        plan = []
        for xs, row_block, rows, dys, ready in jobs:
            width = dys[0].shape[1] // (1 if ready else 2)
            plan.append((width, rows, len(xs)))
            for x in xs:
                for y in range(2):
                    in_specs.append(
                        pl.BlockSpec(
                            (rows, block),
                            lambda q, s, r=row_block, f=first, y=y: (r, y * 4 + s[f + q]),
                        )
                    )
                    args.append(x)
            for dy in dys:
                in_specs.append(
                    pl.BlockSpec((rows, width), lambda q, s, r=ready: (0, 0 if r else s[0]))
                )
                args.append(dy)
            scratch.append(pltpu.VMEM((rows * len(xs), width), bf16))
        dims = (1, 2, block, sum(p[0] for p in plan))
        outs += [shape((2, *dims[1:]), bf16)] * 2
        out_specs += [
            pl.BlockSpec(dims, lambda q, s: (jnp.minimum(q, 1), 0, 0, 0)),
            pl.BlockSpec(dims, lambda q, s: (jnp.maximum(q - 2, 0), 0, 0, 0)),
        ]
        layout.append(plan)
    n_in, n_out = len(in_specs), len(outs)

    def kernel(s, *refs):
        ins, results, joined = refs[:n_in], refs[n_in : n_in + n_out], refs[n_in + n_out :]
        q = pl.program_id(0)

        @pl.when(q == 0)
        def _():
            place, k = 0, 0
            for plan in layout:
                for _, rows, n in plan:
                    da, db = ins[place + 2 * n], ins[place + 2 * n + 1]
                    if n == 2:
                        joined[k][:rows, :] = da[...]
                        joined[k][rows:, :] = db[...]
                    else:
                        joined[k][...] = (da[...].astype(f32) + db[...].astype(f32)).astype(bf16)
                    place += 2 * n + 2
                    k += 1

        place, k = 0, 0
        for i, plan in enumerate(layout):
            send, keep = results[2 * i : 2 * i + 2]
            block = send.shape[2]
            start = 0
            for width, rows, n in plan:
                x = jnp.concatenate([r[...] for r in ins[place : place + 2]], axis=1)
                if n == 2:
                    other = jnp.concatenate([r[...] for r in ins[place + 2 : place + 4]], axis=1)
                    x = jnp.concatenate([x, other], axis=0)
                value = t_dot(x, joined[k][...]).astype(bf16).reshape(2, block, width)
                cut = slice(start, start + width)
                send[0, :, :, cut] = jnp.where(q < 2, value, send[0, :, :, cut])
                keep[0, :, :, cut] = value
                start += width
                place += 2 * n + 2
                k += 1

    flat = call(kernel, tuple(outs), (4,), in_specs, out_specs, scalars, args, scratch)
    return [(flat[2 * i], flat[2 * i + 1]) for i in range(len(groups))]


def conv_grad(x, x_twin, dy, dy_twin, scalars):
    rows, columns = x.shape[1] // 2, D // 2

    def kernel(s, xa, xb, da, db, out):
        both = jnp.concatenate([xa[...], xb[...]], axis=0)
        total = t_dot(both, jnp.concatenate([da[...], db[...]], axis=0))
        out[...] = total.reshape(2, rows, columns)

    half = pl.BlockSpec((dy.shape[0], columns), lambda j, s: (0, s[0]))
    out = shape((2, rows, columns), f32)
    return call(
        kernel,
        out,
        (1,),
        [whole(x), whole(x_twin), half, half],
        whole(out),
        scalars,
        (x, x_twin, dy, dy_twin),
    )


def widen(gathered, plan, none):
    outs, specs, layout = [], [], []
    start = 0
    for rows, columns, ring in plan:
        u, chunks = rows // 16, columns // 2 // STEP
        outs.append(shape((4, 4, u, columns), f32))
        if ring == "x":
            specs.append(
                pl.BlockSpec((1, 4, u, chunks * STEP), lambda c, x, s: (x, 0, 0, c))
            )
        else:
            specs.append(
                pl.BlockSpec((4, 1, u, chunks * STEP), lambda c, x, s: (0, x, 0, c))
            )
        layout.append((start, u, chunks, ring))
        start += u * chunks

    def kernel(_, src, *results):
        for out, (start, u, chunks, ring) in zip(results, layout):
            for k in range(chunks):
                cut = slice(k * STEP, (k + 1) * STEP)
                for z in range(4):
                    value = src[z, start + k * u : start + (k + 1) * u, :].astype(f32)
                    if ring == "x":
                        out[0, z, :, cut] = value
                    else:
                        out[z, 0, :, cut] = value

    results = call(
        kernel,
        tuple(outs),
        (2, 4),
        [pl.BlockSpec((4, gathered.shape[1], STEP), lambda c, x, s: (c * 4 + x, 0, 0))],
        specs,
        none,
        (gathered,),
    )
    return [r.reshape(rows, columns) for r, (rows, columns, _) in zip(results, plan)]


def core_swap(v):
    return lax.ppermute(v, "c", [(0, 1), (1, 0)])


def pair_swap(v):
    return lax.ppermute(v, "yl", [(0, 1), (1, 0)])


def exchange(v, ring, masks):
    def flat(i, c):
        return (i // 2 * 2 + c) * 2 + i % 2 if ring == "y" else 2 * i + c

    pairs = [(flat(i, c), flat(i ^ masks[c], c)) for i in range(4) for c in range(2)]
    return lax.ppermute(v, RING[ring], pairs)


def pick(v, index, axis):
    return lax.dynamic_index_in_dim(v, index, axis, keepdims=False)


def quarters(place, core):
    first = jnp.where(core == 0, 1, 3)
    second = jnp.where(core == 0, 3, 1)
    return place, place ^ first, place ^ 2, place ^ second


class Flow:
    def __init__(self, ring, pair, done=None):
        self.ring, self.other = ring, "z" if ring == "x" else "x"
        self.before, self.result = None, done
        if done is None:
            self.send, self.keep = pair

    def start(self):
        self.got = exchange(self.send, self.ring, (1, 3))

    def sources(self):
        return [self.keep, self.got, self.last] if self.result is None else [self.result]

    def kept(self, which):
        if self.before is None:
            dims = (1, 1, *self.keep.shape[2:])
            return [pl.BlockSpec(dims, lambda y, s: (which, y, 0, 0))], [self.keep]
        return self.before(2 + which)


def onward(flows, cuts):
    in_specs, args, counts = [], [], []
    for f in flows:
        specs, arrays = f.kept(1)
        dims = (1, 1, *f.got.shape[2:])
        in_specs += specs + [pl.BlockSpec(dims, lambda y, s: (1, y, 0, 0))]
        args += arrays + [f.got]
        counts.append(len(arrays) + 1)
    out = tuple(shape(f.got.shape[1:], bf16) for f in flows)

    def kernel(_, *refs):
        k = 0
        for i, n in enumerate(counts):
            total = sum(value_of(r) for r in refs[k : k + n])
            refs[len(args) + i][...] = total.astype(bf16)
            k += n

    sums = call(
        kernel,
        out,
        (2,),
        in_specs,
        [pl.BlockSpec((1, *o.shape[1:]), lambda y, s: (y, 0, 0)) for o in out],
        cuts,
        args,
    )
    for f, v in zip(flows, sums):
        f.last = exchange(v, f.ring, (3, 1))


def value_of(ref):
    return (ref[0] if len(ref.shape) == 4 else ref[...]).astype(f32)


def turn(flows, cuts):
    in_specs, outs, out_specs, args = [], [], [], []

    counts = []
    for f in flows:
        first = 1 if f.other == "x" else 5
        arrays = f.sources()
        rows, columns = arrays[0].shape[-2] // 4, arrays[0].shape[-1]
        four = pl.BlockSpec((1, 2, rows, columns), lambda j, s, i=first: (0, 0, s[i + j], 0))
        three = pl.BlockSpec((2, rows, columns), lambda j, s, i=first: (0, s[i + j], 0))
        in_specs += [four if a.ndim == 4 else three for a in arrays]
        args += arrays
        counts.append(len(arrays))
        dims = (1, 2, rows, columns)
        outs.append(shape((2, *dims[1:]), bf16))
        out_specs.append(pl.BlockSpec(dims, lambda j, s: (j, 0, 0, 0)))

    def kernel(_, *refs):
        k = 0
        for i, n in enumerate(counts):
            total = sum(value_of(r) for r in refs[k : k + n])
            refs[len(args) + i][0] = total.astype(bf16)
            k += n

    sends = call(kernel, tuple(outs), (2,), in_specs, out_specs, cuts, args)
    for f, send in zip(flows, sends):
        f.before = halves_of(f)
        f.ring = f.other
        f.got = exchange(send, f.ring, (1, 3))


def halves_of(f):
    arrays = f.sources()
    first = 1 if f.other == "x" else 5
    rows, columns = arrays[0].shape[-2] // 4, arrays[0].shape[-1]

    def quarter(which):
        four = pl.BlockSpec((1, 1, rows, columns), lambda y, s: (0, y, s[first + which], 0))
        three = pl.BlockSpec((1, rows, columns), lambda y, s: (y, s[first + which], 0))
        return [four if a.ndim == 4 else three for a in arrays], arrays

    return quarter


def add(a, b, none):
    def kernel(_, a, b, out):
        out[...] = (a[...].astype(f32) + b[...].astype(f32)).astype(bf16)

    out = shape(a.shape, bf16)
    return call(kernel, out, (1,), [whole(a), whole(b)], whole(out), none, (a, b))


class Finish:
    def __init__(self, flows, extra, cuts):
        in_specs, args, sizes = [], [], []
        def half(spec):
            return pl.BlockSpec(
                spec.block_shape, lambda j, s: spec.index_map(lax.rem(j + s[9], 2), s)
            )

        for f in flows:
            specs, arrays = f.kept(0)
            dims = (1, 1, *f.got.shape[2:])
            specs = specs + [
                pl.BlockSpec(dims, lambda y, s: (0, y, 0, 0)),
                pl.BlockSpec((1, *f.last.shape[1:]), lambda y, s: (y, 0, 0)),
            ]
            in_specs += [half(spec) for spec in specs]
            args += arrays + [f.got, f.last]
            sizes.append((len(arrays) + 2, f.got.shape[2], f.got.shape[3] // STEP))
        for e in extra:
            in_specs.append(half(pl.BlockSpec((1, *e.shape[1:]), lambda y, s: (y, 0, 0))))
        args += extra
        rows = sum(u * n for _, u, n in sizes) + sum(e.shape[1] for e in extra)

        def kernel(_, *refs):
            send, mine = refs[-2:]
            j = pl.program_id(0)

            def put(here, value):
                @pl.when(j == 0)
                def _():
                    mine[here, :] = value

                @pl.when(j == 1)
                def _():
                    send[here, :] = value.astype(bf16)

            start, k = 0, 0
            for count, u, n in sizes:
                v = sum(value_of(r) for r in refs[k : k + count])[0]
                for i in range(n):
                    put(slice(start, start + u), v[:, i * STEP : (i + 1) * STEP])
                    start += u
                k += count
            for ref in refs[k:-2]:
                put(slice(start, start + ref.shape[1]), ref[0])
                start += ref.shape[1]

        out = (shape((rows, STEP), bf16), shape((rows, STEP), f32))
        send, self.mine = call(
            kernel, out, (2,), in_specs, [whole(o) for o in out], cuts, args
        )
        self.got = exchange(send, "y", (1, 3))

    def second(self, none):
        self.mine = add(self.mine, self.got, none)
        self.far = lax.ppermute(self.mine, "yh", [(0, 1), (1, 0)])

    def gather(self, none):
        return lax.all_gather(add(self.mine, self.far, none), ("c", "x", "z"), axis=0)


def per_device(
    tokens,
    memory,
    compressed,
    cotangent,
    ln1_g,
    ln1_b,
    w_q,
    w_kv,
    w_r,
    bias_u,
    bias_v,
    w_o,
    ln2_g,
    ln2_b,
    w_in,
    b_in,
    w_out,
    b_out,
    conv_w,
    conv_b,
):
    line.held, line.due = [], {}
    tokens, memory, compressed, cotangent = tokens[0], memory[0], compressed[0], cotangent[0]
    yl, core = lax.axis_index("yl"), lax.axis_index("c")
    place = {"x": lax.axis_index("x"), "z": lax.axis_index("z")}
    none = jnp.zeros((1,), jnp.int32)
    ints = lambda *v: jnp.stack([jnp.asarray(i, jnp.int32) for i in v])

    def thirds(rows):
        half = rows // 2
        other = (1 - yl) * half
        return [yl * half, other + core * (half // 2), other + (1 - core) * (half // 2)]

    def both(v):
        return (v, core_swap(v))

    spot = (place["x"] * 4 + place["z"]) * 2 + core
    piece = pack(
        (ln1_g, ln1_b, bias_u, bias_v, ln2_g, ln2_b, b_out, conv_b, b_in),
        w_in,
        w_out,
        ints(spot),
    )
    piece_got = exchange(piece, "y", (1, 3))

    kv_part, small, o_part = pack_rows(w_kv, w_q, w_r, w_o, ints(core))
    (piece_got,) = gate((piece_got,), kv_part)
    kv_got = exchange(kv_part, "y", (1, 3))
    small_got = exchange(small, "y", (1, 3))
    o_got = exchange(o_part, "y", (1, 3))

    def joined(w, got, twin):
        return jnp.concatenate([w, got, twin], axis=0)

    spread = lax.all_gather(piece_got[:-16], ("x", "z", "c"), axis=0)
    thirds_d = ints(*thirds(D))
    thirds_c = ints(*thirds(3 * D), *thirds(D))
    sinus_table = sinusoid(KEYS, D).astype(bf16)
    sinus_rel = jnp.concatenate(
        [
            lax.dynamic_slice_in_dim(sinus_table, thirds_d[i], width, 1)
            for i, width in enumerate(THIRDS)
        ],
        axis=1,
    )
    line.hold(sinus_rel)
    vectors, b_in = unpack(piece, piece_got, ints(yl))

    normed, normed_rel, oldest, old_quarters = first_norm(compressed, memory, tokens, vectors, thirds_d)
    conv_part = half_rows(conv_w, ints(core))
    both_normed, both_cot = both(normed), both(cotangent)
    own, first, far, second = quarters(place["x"], core)
    got = exchange(
        jnp.stack([pick(old_quarters, first, 0), pick(old_quarters, far, 0)]), "x", (1, 3)
    )
    got_far = exchange(jnp.stack([pick(old_quarters, second, 0), got[1]]), "x", (3, 1))
    old_ring = jnp.concatenate([pick(old_quarters, own, 0), got[0], got_far[0], got_far[1]])
    old_twin = core_swap(old_ring)
    kv_got, small_got = gate((kv_got, small_got), normed)
    kv_twin, small_twin = core_swap(kv_got), core_swap(small_got)
    kv_whole = joined(w_kv, kv_got, kv_twin)
    q_whole, r_whole = [
        joined(w, small_got[i], small_twin[i]) for i, w in enumerate((w_q, w_r))
    ]
    key_value = dot(normed_rel, kv_whole).astype(bf16)
    line.hold(key_value)
    queries = dot(normed_rel[2 * T :], q_whole)
    relative = dot(sinus_rel, r_whole).astype(bf16)
    (o_got,) = gate((o_got,), key_value, queries, relative)
    o_whole = joined(w_o, o_got, core_swap(o_got))
    line.hold(queries, relative)
    line.hold(got)
    probs, attended = attend(queries, key_value, relative, vectors, none)
    line.hold(both_normed[1], both_cot[1], got_far)
    residual, normed2, normed2_rel = out_and_norm(attended, o_whole, tokens, vectors, thirds_d)
    both_n2, both_att = both(normed2), both(attended)

    cuts, rels, twins = [], [], []
    for ring in ("x", "z"):
        own, first, far, second = quarters(place[ring], core)
        cuts += [first, far, own, second]
        rels.append([own, first, second, far])
        twins.append([own, second, first, far])
    cuts = ints(core, *cuts, yl)

    def flows(groups):
        pairs = weight_grads(groups, cuts)
        return [Flow(ring, pair) for (ring, _), pair in zip(groups, pairs)]

    def start(some):
        for f in some:
            f.start()

    line.hold(old_twin)
    hidden, d_pre, mixed_out, d_normed2, d_b_in = feed_forward(
        normed2_rel, residual, cotangent, w_in, w_out, spread, b_in, vectors, ints(yl)
    )
    both_hidden, both_pre = both(hidden), both(d_pre)
    conv_got = exchange(conv_part, "y", (1, 3))
    d_residual, d_branch, d_attended, d_ln2_g, d_ln2_b, d_b_out = second_norm_back(
        cotangent, d_normed2, residual, vectors, o_whole, thirds_d
    )
    both_branch = both(d_branch)
    large = flows(
        [
            ("x", [(both_hidden, 0, T, both_cot, False)]),
            ("z", [(both_n2, 0, T, both_pre, False)]),
        ]
    )
    start(large)
    line.hold(conv_got)
    conv_pieces = (conv_w, conv_got, core_swap(conv_got))
    d_kv, my_kv, give_kv, d_relative, d_queries, d_bias_u, d_bias_v = attend_back(
        queries, key_value, relative, vectors, probs, d_attended, ints(core)
    )
    both_kv = (my_kv, core_swap(give_kv))
    both_q, both_rel = both(d_queries), both(d_relative)
    near = flows(
        [
            (
                "x",
                [(both_normed, 0, KEYS, both_kv, True), (both_att, 0, T, both_branch, False)],
            ),
            (
                "z",
                [
                    (both_normed, 2, T, both_q, False),
                    ((sinus_table,), 0, KEYS, both_rel, False),
                ],
            ),
        ]
    )
    onward(large, cuts)

    compact, comp_normed = compress(oldest, conv_pieces, vectors, thirds_c)
    comp_pair = dot(comp_normed, kv_whole).astype(bf16)
    compressed_next = jnp.concatenate([compressed[T // 3 :], compact], axis=0)
    sends = gate([f.send for f in near], compact)
    for f, send in zip(near, sends):
        f.send = send
    start(near)
    line.hold(*sends)
    loss, d_ck, d_cv = reconstruct(queries, key_value, comp_pair, none)
    recon_loss = jnp.sum(loss) / (T * D)
    turn(large, cuts)
    d_compact, d_conv_b = compress_back(d_ck, d_cv, kv_whole, compact, vectors, thirds_d)
    ring_got = exchange(d_compact, "x", (1, 3))
    d_tokens, d_ln1_g, d_ln1_b = first_norm_back(
        d_kv, d_queries, kv_whole, q_whole, compressed, memory, tokens, vectors, d_residual,
        thirds_d,
    )
    line.hold(ring_got, *[f.got for f in near])
    onward(large, cuts)
    ring_pair = jnp.concatenate([d_compact, ring_got])
    pair_got = exchange(ring_pair, "x", (3, 1))
    early = Finish(large, [], cuts)
    onward(near, cuts)
    line.hold(pair_got)
    early.second(none)
    compact_ring = jnp.concatenate([ring_pair, pair_got])
    compact_twin = core_swap(compact_ring)
    conv = Flow("x", None, conv_grad(old_ring, old_twin, compact_ring, compact_twin, cuts))
    early_sums = early.gather(none)
    late_flows = [*near, conv]
    turn(late_flows, cuts)
    onward(late_flows, cuts)

    total = jnp.concatenate(
        [d_ln1_g, d_ln1_b, d_bias_u, d_bias_v, d_ln2_g, d_ln2_b, d_b_out, d_conv_b]
        + [d_b_in]
    )
    total = jnp.concatenate(
        [
            total[:8].reshape(8, 2, STEP).transpose(1, 0, 2),
            total[8:].reshape(2, 4, STEP),
            jnp.zeros((2, 4, STEP), f32),
        ],
        axis=1,
    )
    late = Finish(late_flows, [total], cuts)
    late.second(none)
    line.hold(early_sums)
    late_sums = late.gather(none)

    g_out, g_in = widen(early_sums, [(FF // 2, D, "x"), (D // 2, FF, "z")], none)
    g_kv, g_o, g_q, g_r, g_conv = widen(
        late_sums,
        [
            (D // 2, 2 * D, "x"),
            (D // 2, D, "x"),
            (D // 2, D, "z"),
            (D // 2, D, "z"),
            (3 * D // 2, D, "x"),
        ],
        none,
    )
    half = jnp.sum(late_sums[:, 256:268].astype(f32), axis=0)
    t_ln1_g, t_ln1_b, t_bu, t_bv, t_ln2_g, t_ln2_b, t_bout, t_convb = [half[i] for i in range(8)]
    t_bin = half[8:].reshape(-1)
    return (
        mixed_out[None],
        compressed_next[None],
        recon_loss[None],
        d_tokens[None],
        t_ln1_g,
        t_ln1_b,
        g_q,
        g_kv,
        g_r,
        t_bu,
        t_bv,
        g_o,
        t_ln2_g,
        t_ln2_b,
        g_in,
        t_bin,
        g_out,
        t_bout,
        g_conv,
        t_convb,
    )


def solution(mesh):
    fine = Mesh(mesh.devices.reshape(2, 4, 4, 2, 2), AXES)
    stream = P(AXES, None, None)
    vec, mat = P("yl"), P("yl", None)
    weights = (vec, vec, mat, mat, mat, vec, vec, mat, vec, vec, mat, vec, mat, vec, mat, vec)
    return jax.shard_map(
        per_device,
        mesh=fine,
        in_specs=(stream,) * 4 + weights,
        out_specs=(stream, stream, P(AXES), stream) + weights,
        check_vma=False,
    )
```

```python
import jax
import jax.numpy as jnp
from jax import lax
from jax.experimental import pallas as pl
from jax.experimental.pallas import tpu as pltpu
from jax.sharding import Mesh, PartitionSpec as P

H = 8
HD = 128
D = 1024
T = 192
KEYS = 576
PAD = 640
FF = 4096
FACTOR = HD ** (-0.5)
f32 = jnp.float32
bf16 = jnp.bfloat16
AXES = ("yh", "x", "z", "c", "yl")
RING = {"x": ("x", "c"), "z": ("z", "c"), "y": ("yh", "c", "yl")}


def sinusoid(key_count, model_dim):
    distance = (key_count - 1 - jnp.arange(key_count)).astype(f32)
    inverse = 1.0 / 10000.0 ** (jnp.arange(0, model_dim, 2).astype(f32) / model_dim)
    angles = distance[:, None] * inverse[None, :]
    return jnp.concatenate([jnp.sin(angles), jnp.cos(angles)], axis=-1)


def dot(a, b):
    return jnp.dot(a, b, preferred_element_type=f32)


def dot_t(a, b):
    return lax.dot_general(a, b, (((1,), (1,)), ((), ())), preferred_element_type=f32)


def t_dot(a, b):
    return lax.dot_general(a, b, (((0,), (0,)), ((), ())), preferred_element_type=f32)


class Line:
    def __init__(self):
        self.held, self.due = [], {}

    def hold(self, *values):
        self.held += values

    def expect(self, gap, *values):
        self.due.setdefault(gap, []).extend(values)

    def ran(self, result):
        self.held = [result, *self.due.get(1, [])]
        self.due = {gap - 1: values for gap, values in self.due.items() if gap > 1}

    def later(self, value):
        return lax.optimization_barrier((value, *self.held))[0] if self.held else value


line = Line()


def call(kernel, out, grid, in_specs, out_specs, scalars, args, scratch=()):
    held, n = line.held, len(args)

    def body(s, *refs):
        kernel(s, *refs[:n], *refs[n + len(held) :])

    result = pl.pallas_call(
        body,
        out_shape=out,
        grid_spec=pltpu.PrefetchScalarGridSpec(
            num_scalar_prefetch=1,
            grid=grid,
            in_specs=list(in_specs) + [pl.BlockSpec(memory_space=pl.ANY)] * len(held),
            out_specs=out_specs,
            scratch_shapes=list(scratch),
        ),
        compiler_params=pltpu.CompilerParams(vmem_limit_bytes=56 << 20),
    )(scalars, *args, *held)
    line.ran(jax.tree.leaves(result)[0])
    return result


def gate(values, *after):
    n = len(values)
    anywhere = pl.BlockSpec(memory_space=pl.ANY)
    return pl.pallas_call(
        lambda *refs: None,
        out_shape=[jax.ShapeDtypeStruct(v.shape, v.dtype) for v in values],
        in_specs=[anywhere] * (n + len(after)),
        out_specs=[anywhere] * n,
        input_output_aliases={i: i for i in range(n)},
    )(*values, *after)


def whole(a):
    zeros = (0,) * a.ndim
    return pl.BlockSpec(a.shape, lambda *_: zeros)


def shape(dims, dtype):
    return jax.ShapeDtypeStruct(dims, dtype)


def at(offset):
    return pl.multiple_of(offset, 128)


def center_scale(v):
    mid = v - jnp.mean(v, axis=-1, keepdims=True)
    r = lax.rsqrt(jnp.mean(mid * mid, axis=-1, keepdims=True) + 1e-5)
    return mid * r, r


def norm_back(xhat, r, g, dn):
    gd = dn * g
    return r * (
        gd
        - jnp.mean(gd, axis=-1, keepdims=True)
        - xhat * jnp.mean(gd * xhat, axis=-1, keepdims=True)
    )


def softmax(s):
    e = jnp.exp(s - jnp.max(s, axis=-1, keepdims=True))
    return e / jnp.sum(e, axis=-1, keepdims=True)


(LN1_G, LN1_B, BIAS_U, BIAS_V, LN2_G, LN2_B, B_OUT, CONV_B) = range(8)


def row(ref, i):
    return ref[i : i + 1, :]


def pack(vectors, w_in, w_out, scalars):
    n_in, n_out = (w.shape[0] // 32 for w in (w_in, w_out))
    chunks = FF // D
    rows = n_out + n_in * chunks
    half = D // 2

    def kernel(_, *refs):
        wi, wo, piece, flat = refs[-4:]
        flat[...] = jnp.zeros_like(flat)
        for i, ref in enumerate(refs[:8]):
            flat[i : i + 1, :half] = ref[...].astype(f32).reshape(1, half)
        flat[8 : 8 + FF // 2 // D, :] = refs[8][...].astype(f32).reshape(FF // 2 // D, D)
        piece[:n_out, :] = wo[...]
        for i in range(chunks):
            piece[n_out + i * n_in : n_out + (i + 1) * n_in, :] = wi[:, i * D : (i + 1) * D]
        piece[rows:, :] = flat[...].astype(bf16)

    out = shape((rows + 16, D), bf16)
    return call(
        kernel,
        out,
        (1,),
        [whole(v) for v in vectors]
        + [
            pl.BlockSpec((w.shape[0] // 32, w.shape[1]), lambda j, s: (s[0], 0))
            for w in (w_in, w_out)
        ],
        whole(out),
        scalars,
        (*vectors, w_in, w_out),
        [pltpu.VMEM((16, D), f32)],
    )


def half_rows(w, scalars):
    n = w.shape[0] // 2

    def kernel(_, w, out):
        out[...] = w[...]

    out = shape((n, w.shape[1]), w.dtype)
    spec = pl.BlockSpec((n, w.shape[1]), lambda j, s: (s[0], 0))
    return call(kernel, out, (1,), [spec], whole(out), scalars, (w,))


def pack_rows(w_kv, w_q, w_r, w_o, scalars):
    n = w_q.shape[0] // 2

    def kernel(_, kv, q, r, o, kv_out, out, o_out):
        kv_out[...] = kv[...]
        out[0] = q[...]
        out[1] = r[...]
        o_out[...] = o[...]

    args = (w_kv, w_q, w_r, w_o)
    out = (shape((n, 2 * D), bf16), shape((2, n, D), bf16), shape((n, D), bf16))
    return call(
        kernel,
        out,
        (1,),
        [pl.BlockSpec((w.shape[0] // 2, w.shape[1]), lambda j, s: (s[0], 0)) for w in args],
        [whole(o) for o in out],
        scalars,
        args,
    )


def unpack(mine, theirs, scalars):
    half = D // 2
    at_row = mine.shape[0] // 16 - 1
    tail = pl.BlockSpec((16, D), lambda j, s: (at_row, 0))

    def kernel(s, mine, theirs, vectors, b_in):
        a, b = mine[...].astype(f32), theirs[...].astype(f32)
        low = jnp.where(s[0] == 0, a, b)
        high = jnp.where(s[0] == 0, b, a)
        vectors[:, :half] = low[:8, :half]
        vectors[:, half:] = high[:8, :half]
        rows = FF // 2 // D
        b_in[:rows] = low[8 : 8 + rows]
        b_in[rows:] = high[8 : 8 + rows]

    out = (shape((8, D), f32), shape((FF // D, D), f32))
    return call(
        kernel, out, (1,), [tail, tail], [whole(o) for o in out], scalars, (mine, theirs)
    )


def relative_columns(x, s, widths):
    parts = [x[:, pl.ds(at(s[i]), width)] for i, width in enumerate(widths)]
    return jnp.concatenate(parts, axis=1)


def natural_columns(out, x, s, widths):
    start = 0
    for i, width in enumerate(widths):
        out[:, pl.ds(at(s[i]), width)] = x[:, start : start + width]
        start += width


THIRDS = (D // 2, D // 4, D // 4)


def first_norm(compressed, memory, tokens, vectors, offsets):
    def kernel(s, comp, mem, tok, vec, out, out_rel, old, old_quarters):
        gain, bias = row(vec, LN1_G), row(vec, LN1_B)

        def part(ref, base):
            for i in range(0, T, 32):
                xhat, r = center_scale(ref[i : i + 32, :].astype(f32))
                out[base + i : base + i + 32, :] = (xhat * gain + bias).astype(bf16)

        part(comp, 0)
        part(mem, T)
        part(tok, 2 * T)
        out_rel[...] = relative_columns(out, s, THIRDS)
        line_of = lax.broadcasted_iota(jnp.int32, (T // 3, T), 0)
        col = lax.broadcasted_iota(jnp.int32, (T // 3, T), 1)
        low = mem[...].astype(bf16)
        for tap in range(3):
            take = jnp.where(col == 3 * line_of + tap, 1.0, 0.0).astype(bf16)
            old[:, tap * D : (tap + 1) * D] = dot(take, low).astype(bf16)
        width = 3 * D // 8
        for q in range(4):
            for y in range(2):
                begin = y * 3 * D // 2 + q * width
                old_quarters[q, :, y * width : (y + 1) * width] = old[:, begin : begin + width]

    args = (compressed, memory, tokens, vectors)
    out = (
        shape((KEYS, D), bf16),
        shape((KEYS, D), bf16),
        shape((T // 3, 3 * D), bf16),
        shape((4, T // 3, 3 * D // 4), bf16),
    )
    return call(
        kernel, out, (1,), [whole(a) for a in args], [whole(o) for o in out], offsets, args
    )


def head(n, rows, row_block=0, first=0):
    return pl.BlockSpec((rows, n * HD), lambda h, s: (row_block, first // n + h))


def columns_of(n):
    return [slice(i * HD, (i + 1) * HD) for i in range(n)]


def attend(queries, key_value, relative, vectors, none):
    n = 2

    def kernel(_, q, k, v, rel, vec, probs, out):
        pad = jnp.zeros((PAD - KEYS, HD), bf16)
        i = lax.broadcasted_iota(jnp.int32, (T, PAD), 0)
        j = lax.broadcasted_iota(jnp.int32, (T, PAD), 1)
        seen = j <= i + (KEYS - T)
        cuts = columns_of(n)
        content = [((q[:, c] + vec[BIAS_U : BIAS_U + 1, c]) * FACTOR).astype(bf16) for c in cuts]
        located = [((q[:, c] + vec[BIAS_V : BIAS_V + 1, c]) * FACTOR).astype(bf16) for c in cuts]
        raw = [
            dot_t(x, jnp.concatenate([rel[:, c], pad], axis=0)) for x, c in zip(located, cuts)
        ]
        near = [dot_t(x, jnp.concatenate([k[:, c], pad], axis=0)) for x, c in zip(content, cuts)]
        raw = [pltpu.roll(x, PAD - T + 1, 1, stride=1, stride_axis=0) for x in raw]
        p = [softmax(jnp.where(seen, a + b, -1e30)) for a, b in zip(near, raw)]
        for h, c in enumerate(cuts):
            probs[h] = p[h]
            value = jnp.concatenate([v[:, c], pad], axis=0)
            out[:, c] = dot(p[h].astype(bf16), value).astype(bf16)

    return call(
        kernel,
        (shape((H, T, PAD), f32), shape((T, D), bf16)),
        (H // n,),
        [head(n, T), head(n, KEYS), head(n, KEYS, 0, H), head(n, KEYS), head(n, 8)],
        [pl.BlockSpec((n, T, PAD), lambda h, s: (h, 0, 0)), head(n, T)],
        none,
        (queries, key_value, key_value, relative, vectors),
    )


def attend_back(queries, key_value, relative, vectors, probs, d_attended, scalars):
    n = 2

    def kernel(s, q, k, v, rel, vec, probs, d_att, d_kv, mine, give, d_rel, d_q, d_bu, d_bv):
        pad = jnp.zeros((PAD - KEYS, HD), bf16)
        i = lax.broadcasted_iota(jnp.int32, (T, T), 0)
        j = lax.broadcasted_iota(jnp.int32, (T, T), 1)
        flip = jnp.where(i + j == T - 1, 1.0, 0.0).astype(bf16)
        cuts = columns_of(n)
        content = [((q[:, c] + vec[BIAS_U : BIAS_U + 1, c]) * FACTOR).astype(bf16) for c in cuts]
        located = [((q[:, c] + vec[BIAS_V : BIAS_V + 1, c]) * FACTOR).astype(bf16) for c in cuts]
        da = [d_att[:, c] for c in cuts]
        d_p = [dot_t(x, jnp.concatenate([v[:, c], pad], axis=0)) for x, c in zip(da, cuts)]
        d_v = [t_dot(probs[h].astype(bf16), x)[:KEYS].astype(bf16) for h, x in enumerate(da)]
        d_s = []
        for h, x in enumerate(d_p):
            p = probs[h]
            d_s.append((p * (x - jnp.sum(p * x, axis=-1, keepdims=True))).astype(bf16))
        d_raw = [dot(flip, x) for x in d_s]
        d_c = [
            dot(x, jnp.concatenate([k[:, c], pad], axis=0)) * FACTOR for x, c in zip(d_s, cuts)
        ]
        d_k = [t_dot(x, y)[:KEYS].astype(bf16) for x, y in zip(d_s, content)]
        d_raw = [pltpu.roll(x, 0, 1, stride=1, stride_axis=0).astype(bf16) for x in d_raw]
        d_raw = [dot(flip, x).astype(bf16) for x in d_raw]
        d_l = [
            dot(x, jnp.concatenate([rel[:, c], pad], axis=0)) * FACTOR for x, c in zip(d_raw, cuts)
        ]
        for h, c in enumerate(cuts):
            d_rel[:, c] = t_dot(d_raw[h], located[h])[:KEYS].astype(bf16)
            d_kv[0, :, c] = d_k[h]
            d_kv[1, :, c] = d_v[h]
            mine[:, c] = jnp.where(s[0] == 0, d_k[h], d_v[h])
            give[:, c] = jnp.where(s[0] == 0, d_v[h], d_k[h])
            d_q[:, c] = (d_c[h] + d_l[h]).astype(bf16)
            d_bu[:, c] = jnp.sum(d_c[h], axis=0, keepdims=True)
            d_bv[:, c] = jnp.sum(d_l[h], axis=0, keepdims=True)

    return call(
        kernel,
        (shape((2, KEYS, D), bf16),)
        + (shape((KEYS, D), bf16),) * 3
        + (shape((T, D), bf16), shape((1, D), f32), shape((1, D), f32)),
        (H // n,),
        [
            head(n, T),
            head(n, KEYS),
            head(n, KEYS, 0, H),
            head(n, KEYS),
            head(n, 8),
            pl.BlockSpec((n, T, PAD), lambda h, s: (h, 0, 0)),
            head(n, T),
        ],
        [
            pl.BlockSpec((2, KEYS, n * HD), lambda h, s: (0, 0, h)),
            head(n, KEYS),
            head(n, KEYS),
            head(n, KEYS),
            head(n, T),
            head(n, 1),
            head(n, 1),
        ],
        scalars,
        (queries, key_value, key_value, relative, vectors, probs, d_attended),
    )


def out_and_norm(attended, w_o, tokens, vectors, offsets):
    def kernel(s, att, w, tok, vec, res, n2, n2_rel):
        total = tok[...].astype(f32) + dot(relative_columns(att, s, THIRDS), w[...])
        res[...] = total
        xhat, r = center_scale(total)
        n2[...] = (xhat * row(vec, LN2_G) + row(vec, LN2_B)).astype(bf16)
        other = at(D // 2 - s[0])
        n2_rel[:, : D // 2] = n2[:, pl.ds(at(s[0]), D // 2)]
        n2_rel[:, D // 2 :] = n2[:, pl.ds(other, D // 2)]

    args = (attended, w_o, tokens, vectors)
    out = (shape((T, D), f32), shape((T, D), bf16), shape((T, D), bf16))
    return call(
        kernel, out, (1,), [whole(a) for a in args], [whole(o) for o in out], offsets, args
    )


STEP = 512
UNITS = 1024
HALF = FF // 2 // UNITS


def feed_forward(n2_rel, residual, cotangent, w_in, w_out, spread, b_in, vectors, scalars):
    n_in = w_in.shape[0] // 32
    n_out = w_out.shape[0] // 32
    skip = n_out // n_in
    per = UNITS // n_out
    K_NORM = 0.7978845608028654

    def natural(j, s):
        return lax.rem(j + s[0] * HALF, 2 * HALF)

    def kernel(s, n2, res, cot, wi0, wi1, wo0, wo1, bi, vec, hid, dpre, mixed, dn2, dbi, acc, back):
        j = pl.program_id(0)
        n = natural(j, s)

        @pl.when(j == 0)
        def _():
            acc[...] = jnp.zeros_like(acc)
            back[...] = jnp.zeros_like(back)

        wo = jnp.where(j < HALF, wo0[...], wo1[...].reshape(UNITS, D))
        win = jnp.concatenate([wi0[...], wi1[...].reshape(D // 2, UNITS)], axis=0)
        pre = dot(n2[...], win) + bi[pl.ds(n, 1), :]
        d_hidden = dot_t(cot[...], wo)
        square = pre * pre
        t = jnp.tanh(K_NORM * pre * (1.0 + 0.044715 * square))
        gate_ = 0.5 * (1.0 + t)
        hidden = (pre * gate_).astype(bf16)
        slope = gate_ + (0.5 * K_NORM) * pre * (1.0 - t * t) * (1.0 + (3 * 0.044715) * square)
        d_pre = (d_hidden * slope).astype(bf16)
        hid[...] = hidden
        dpre[...] = d_pre
        dbi[pl.ds(n, 1), :] = jnp.sum(d_pre.astype(f32), axis=0, keepdims=True)
        acc[...] += dot(hidden, wo)
        back[...] += dot_t(d_pre, win)

        @pl.when(j == 2 * HALF - 1)
        def _():
            mixed[...] = (res[...] + acc[...] + row(vec, B_OUT)).astype(bf16)
            dn2[:, pl.ds(at(s[0] * (D // 2)), D // 2)] = back[:, : D // 2]
            dn2[:, pl.ds(at((1 - s[0]) * (D // 2)), D // 2)] = back[:, D // 2 :]

    out = (
        shape((T, FF), bf16),
        shape((T, FF), bf16),
        shape((T, D), bf16),
        shape((T, D), f32),
        shape((2 * HALF, UNITS), f32),
    )
    by_unit = pl.BlockSpec((T, UNITS), lambda j, s: (0, natural(j, s)))
    return call(
        kernel,
        out,
        (2 * HALF,),
        [
            whole(n2_rel),
            whole(residual),
            whole(cotangent),
            pl.BlockSpec((D // 2, UNITS), lambda j, s: (0, natural(j, s))),
            pl.BlockSpec((32, n_in, UNITS), lambda j, s: (0, skip + natural(j, s), 0)),
            pl.BlockSpec((UNITS, D), lambda j, s: (jnp.minimum(j, HALF - 1), 0)),
            pl.BlockSpec(
                (per, n_out, D), lambda j, s: (jnp.maximum(j - HALF, 0), 0, 0)
            ),
            whole(b_in),
            whole(vectors),
        ],
        [by_unit, by_unit, whole(out[2]), whole(out[3]), whole(out[4])],
        scalars,
        (n2_rel, residual, cotangent, w_in, spread, w_out, spread, b_in, vectors),
        [pltpu.VMEM((T, D), f32), pltpu.VMEM((T, D), f32)],
    )


def second_norm_back(cotangent, d_n2, residual, vectors, w_o, offsets):
    def kernel(s, cot, dn, res, vec, w, d_res, d_br, d_att, dg, db, dbo):
        xhat, r = center_scale(res[...])
        dn, wide = dn[...], cot[...].astype(f32)
        dg[...] = jnp.sum(dn * xhat, axis=0, keepdims=True)
        db[...] = jnp.sum(dn, axis=0, keepdims=True)
        dbo[...] = jnp.sum(wide, axis=0, keepdims=True)
        total = wide + norm_back(xhat, r, row(vec, LN2_G), dn)
        d_res[...] = total
        low = total.astype(bf16)
        d_br[...] = low
        natural_columns(d_att, dot_t(low, w[...]).astype(bf16), s, THIRDS)

    args = (cotangent, d_n2, residual, vectors, w_o)
    out = (
        shape((T, D), f32),
        shape((T, D), bf16),
        shape((T, D), bf16),
        shape((1, D), f32),
        shape((1, D), f32),
        shape((1, D), f32),
    )
    return call(
        kernel, out, (1,), [whole(a) for a in args], [whole(o) for o in out], offsets, args
    )


def first_norm_back(d_kv, d_q, w_kv, w_q, compressed, memory, tokens, vectors, d_res, offsets):
    steps = 4
    wide, slim = 2 * D // steps, D // steps

    def kernel(s, dkv, dq, kw, qw, comp, mem, tok, vec, dres, dtok, dg, db, acc, nat, xh, rs):
        j = pl.program_id(0)

        def product(start):
            value = dot_t(dkv[0], kw[...])
            if start:
                acc[...] = value
            else:
                acc[...] += value
            acc[2 * T :, :] += dot_t(dq[...], qw[...])

        for block, ref in enumerate((comp, mem, tok)):

            @pl.when(j == block)
            def _(block=block, ref=ref):
                product(block == 0)
                for i in range(0, T, 32):
                    xhat, r = center_scale(ref[i : i + 32, :].astype(f32))
                    xh[block * T + i : block * T + i + 32, :] = xhat
                    if block == 2:
                        rs[i : i + 32, :] = jnp.broadcast_to(r, (32, HD))

        @pl.when(j == steps - 1)
        def _():
            product(False)
            natural_columns(nat, acc, s, THIRDS)
            gain = row(vec, LN1_G)
            sum_g = jnp.zeros((8, D), f32)
            sum_b = jnp.zeros((8, D), f32)
            for i in range(0, KEYS, 32):
                dn, xhat = nat[i : i + 32, :], xh[i : i + 32, :]
                both = dn * xhat
                sum_g += (both[:8] + both[8:16]) + (both[16:24] + both[24:])
                sum_b += (dn[:8] + dn[8:16]) + (dn[16:24] + dn[24:])
                if i >= 2 * T:
                    k = i - 2 * T
                    r = rs[k : k + 32, :1]
                    dtok[k : k + 32, :] = dres[k : k + 32, :] + norm_back(xhat, r, gain, dn)
            dg[...] = jnp.sum(sum_g, axis=0, keepdims=True)
            db[...] = jnp.sum(sum_b, axis=0, keepdims=True)

    rest = (compressed, memory, tokens, vectors, d_res)
    out = (shape((T, D), f32), shape((1, D), f32), shape((1, D), f32))
    return call(
        kernel,
        out,
        (steps,),
        [
            pl.BlockSpec((1, KEYS, wide), lambda j, s: (j // (steps // 2), 0, lax.rem(j, steps // 2))),
            pl.BlockSpec((T, slim), lambda j, s: (0, j)),
            pl.BlockSpec((D, wide), lambda j, s: (0, j)),
            pl.BlockSpec((D, slim), lambda j, s: (0, j)),
        ]
        + [whole(a) for a in rest],
        [whole(o) for o in out],
        offsets,
        (d_kv, d_q, w_kv, w_q, *rest),
        [pltpu.VMEM((KEYS, D), f32)] * 3 + [pltpu.VMEM((T, HD), f32)],
    )


def compress(oldest, pieces, vectors, offsets):
    block = 256
    rows = T // 3

    def kernel(s, x, w0, w1, w2, vec, compact, normed, x_rel, natural):
        j = pl.program_id(0)

        @pl.when(j == 0)
        def _():
            x_rel[...] = relative_columns(x, s, (3 * D // 2, 3 * D // 4, 3 * D // 4))

        w = jnp.concatenate([w0[...], w1[...], w2[...]], axis=0)
        here = pl.ds(at(j * block), block)
        compact[:, here] = dot(x_rel[...], w) + vec[CONV_B : CONV_B + 1, here]

        @pl.when(j == D // block - 1)
        def _():
            xhat, r = center_scale(compact[...])
            natural[...] = (xhat * row(vec, LN1_G) + row(vec, LN1_B)).astype(bf16)
            start = 0
            for i, width in enumerate(THIRDS):
                normed[:, start : start + width] = natural[:, pl.ds(at(s[3 + i]), width)]
                start += width

    out = (shape((rows, D), f32), shape((rows, D), bf16))
    return call(
        kernel,
        out,
        (D // block,),
        [whole(oldest)]
        + [pl.BlockSpec((w.shape[0], block), lambda j, s: (0, j)) for w in pieces]
        + [whole(vectors)],
        [whole(o) for o in out],
        offsets,
        (oldest, *pieces, vectors),
        [pltpu.VMEM((rows, 3 * D), bf16), pltpu.VMEM((rows, D), bf16)],
    )


def reconstruct(queries, key_value, comp_pair, none):
    rows = T // 3
    n = 4

    def kernel(_, q, k, v, ck, cv, loss, dck, dcv):
        cuts = columns_of(n)
        asking = [(q[:, c] * FACTOR).astype(bf16) for c in cuts]
        far = [dot_t(x, k[:, c]) for x, c in zip(asking, cuts)]
        near = [dot_t(x, ck[:, c]) for x, c in zip(asking, cuts)]
        p = [softmax(x).astype(bf16) for x in far]
        gp = [softmax(x) for x in near]
        low = [x.astype(bf16) for x in gp]
        miss = [dot(p[h], v[:, c]) - dot(low[h], cv[:, c]) for h, c in enumerate(cuts)]
        total = sum(jnp.sum(x * x, axis=0, keepdims=True) for x in miss)
        d_guess = [((-2.0 / (T * D)) * x).astype(bf16) for x in miss]
        d_gp = [dot_t(x, cv[:, c]) for x, c in zip(d_guess, cuts)]
        d_gs = [
            (x * (y - jnp.sum(x * y, axis=-1, keepdims=True))).astype(bf16)
            for x, y in zip(gp, d_gp)
        ]
        for h, c in enumerate(cuts):
            dcv[:, c] = t_dot(low[h], d_guess[h]).astype(bf16)
            dck[:, c] = t_dot(d_gs[h], asking[h]).astype(bf16)

        @pl.when(pl.program_id(0) == 0)
        def _():
            loss[...] = total

        @pl.when(pl.program_id(0) > 0)
        def _():
            loss[...] += total

    return call(
        kernel,
        (shape((1, HD), f32), shape((rows, D), bf16), shape((rows, D), bf16)),
        (H // n,),
        [head(n, T), head(n, T, 1), head(n, T, 1, H), head(n, rows), head(n, rows, 0, H)],
        [pl.BlockSpec((1, HD), lambda h, s: (0, 0)), head(n, rows), head(n, rows)],
        none,
        (queries, key_value, key_value, comp_pair, comp_pair),
    )


def compress_back(dck, dcv, w_kv, compact, vectors, offsets):
    rows = T // 3

    def kernel(s, dck, dcv, w, compact, vec, d_compact, d_bias, dn):
        back = dot_t(jnp.concatenate([dck[...], dcv[...]], axis=1), w[...])
        natural_columns(dn, back, s, THIRDS)
        xhat, r = center_scale(compact[...])
        low = norm_back(xhat, r, row(vec, LN1_G), dn[...]).astype(bf16)
        d_compact[...] = low
        d_bias[...] = jnp.sum(low.astype(f32), axis=0, keepdims=True)

    args = (dck, dcv, w_kv, compact, vectors)
    out = (shape((rows, D), bf16), shape((1, D), f32))
    return call(
        kernel,
        out,
        (1,),
        [whole(a) for a in args],
        [whole(o) for o in out],
        offsets,
        args,
        [pltpu.VMEM((rows, D), f32)],
    )


def weight_grads(groups, scalars):
    in_specs, args, outs, out_specs, layout, scratch = [], [], [], [], [], []
    for ring, jobs in groups:
        first = 1 if ring == "x" else 5
        block = jobs[0][0][0].shape[1] // 8
        plan = []
        for xs, row_block, rows, dys, ready in jobs:
            width = dys[0].shape[1] // (1 if ready else 2)
            plan.append((width, rows, len(xs)))
            for x in xs:
                for y in range(2):
                    in_specs.append(
                        pl.BlockSpec(
                            (rows, block),
                            lambda q, s, r=row_block, f=first, y=y: (r, y * 4 + s[f + q]),
                        )
                    )
                    args.append(x)
            for dy in dys:
                in_specs.append(
                    pl.BlockSpec((rows, width), lambda q, s, r=ready: (0, 0 if r else s[0]))
                )
                args.append(dy)
            scratch.append(pltpu.VMEM((rows * len(xs), width), bf16))
        dims = (1, 2, block, sum(p[0] for p in plan))
        outs += [shape((2, *dims[1:]), bf16)] * 2
        out_specs += [
            pl.BlockSpec(dims, lambda q, s: (jnp.minimum(q, 1), 0, 0, 0)),
            pl.BlockSpec(dims, lambda q, s: (jnp.maximum(q - 2, 0), 0, 0, 0)),
        ]
        layout.append(plan)
    n_in, n_out = len(in_specs), len(outs)

    def kernel(s, *refs):
        ins, results, joined = refs[:n_in], refs[n_in : n_in + n_out], refs[n_in + n_out :]
        q = pl.program_id(0)

        @pl.when(q == 0)
        def _():
            place, k = 0, 0
            for plan in layout:
                for _, rows, n in plan:
                    da, db = ins[place + 2 * n], ins[place + 2 * n + 1]
                    if n == 2:
                        joined[k][:rows, :] = da[...]
                        joined[k][rows:, :] = db[...]
                    else:
                        joined[k][...] = (da[...].astype(f32) + db[...].astype(f32)).astype(bf16)
                    place += 2 * n + 2
                    k += 1

        place, k = 0, 0
        for i, plan in enumerate(layout):
            send, keep = results[2 * i : 2 * i + 2]
            block = send.shape[2]
            start = 0
            for width, rows, n in plan:
                x = jnp.concatenate([r[...] for r in ins[place : place + 2]], axis=1)
                if n == 2:
                    other = jnp.concatenate([r[...] for r in ins[place + 2 : place + 4]], axis=1)
                    x = jnp.concatenate([x, other], axis=0)
                value = t_dot(x, joined[k][...]).astype(bf16).reshape(2, block, width)
                cut = slice(start, start + width)
                send[0, :, :, cut] = jnp.where(q < 2, value, send[0, :, :, cut])
                keep[0, :, :, cut] = value
                start += width
                place += 2 * n + 2
                k += 1

    flat = call(kernel, tuple(outs), (4,), in_specs, out_specs, scalars, args, scratch)
    return [(flat[2 * i], flat[2 * i + 1]) for i in range(len(groups))]


def conv_grad(x, x_twin, dy, dy_twin, scalars):
    rows, columns = x.shape[1] // 2, D // 2

    def kernel(s, xa, xb, da, db, out):
        both = jnp.concatenate([xa[...], xb[...]], axis=0)
        total = t_dot(both, jnp.concatenate([da[...], db[...]], axis=0))
        out[...] = total.reshape(2, rows, columns)

    half = pl.BlockSpec((dy.shape[0], columns), lambda j, s: (0, s[0]))
    out = shape((2, rows, columns), f32)
    return call(
        kernel,
        out,
        (1,),
        [whole(x), whole(x_twin), half, half],
        whole(out),
        scalars,
        (x, x_twin, dy, dy_twin),
    )


def widen(gathered, plan, none):
    outs, specs, layout = [], [], []
    start = 0
    for rows, columns, ring in plan:
        u, chunks = rows // 16, columns // 2 // STEP
        outs.append(shape((4, 4, u, columns), f32))
        if ring == "x":
            specs.append(
                pl.BlockSpec((1, 4, u, chunks * STEP), lambda c, x, s: (x, 0, 0, c))
            )
        else:
            specs.append(
                pl.BlockSpec((4, 1, u, chunks * STEP), lambda c, x, s: (0, x, 0, c))
            )
        layout.append((start, u, chunks, ring))
        start += u * chunks

    def kernel(_, src, *results):
        for out, (start, u, chunks, ring) in zip(results, layout):
            for k in range(chunks):
                cut = slice(k * STEP, (k + 1) * STEP)
                for z in range(4):
                    value = src[z, start + k * u : start + (k + 1) * u, :].astype(f32)
                    if ring == "x":
                        out[0, z, :, cut] = value
                    else:
                        out[z, 0, :, cut] = value

    results = call(
        kernel,
        tuple(outs),
        (2, 4),
        [pl.BlockSpec((4, gathered.shape[1], STEP), lambda c, x, s: (c * 4 + x, 0, 0))],
        specs,
        none,
        (gathered,),
    )
    return [r.reshape(rows, columns) for r, (rows, columns, _) in zip(results, plan)]


def core_swap(v):
    return lax.ppermute(v, "c", [(0, 1), (1, 0)])


def pair_swap(v):
    return lax.ppermute(v, "yl", [(0, 1), (1, 0)])


def exchange(v, ring, masks):
    def flat(i, c):
        return (i // 2 * 2 + c) * 2 + i % 2 if ring == "y" else 2 * i + c

    pairs = [(flat(i, c), flat(i ^ masks[c], c)) for i in range(4) for c in range(2)]
    return lax.ppermute(v, RING[ring], pairs)


def pick(v, index, axis):
    return lax.dynamic_index_in_dim(v, index, axis, keepdims=False)


def quarters(place, core):
    first = jnp.where(core == 0, 1, 3)
    second = jnp.where(core == 0, 3, 1)
    return place, place ^ first, place ^ 2, place ^ second


class Flow:
    def __init__(self, ring, pair, done=None):
        self.ring, self.other = ring, "z" if ring == "x" else "x"
        self.before, self.result = None, done
        if done is None:
            self.send, self.keep = pair

    def start(self):
        self.got = exchange(self.send, self.ring, (1, 3))

    def sources(self):
        return [self.keep, self.got, self.last] if self.result is None else [self.result]

    def kept(self, which):
        if self.before is None:
            dims = (1, 1, *self.keep.shape[2:])
            return [pl.BlockSpec(dims, lambda y, s: (which, y, 0, 0))], [self.keep]
        return self.before(2 + which)


def onward(flows, cuts):
    in_specs, args, counts = [], [], []
    for f in flows:
        specs, arrays = f.kept(1)
        dims = (1, 1, *f.got.shape[2:])
        in_specs += specs + [pl.BlockSpec(dims, lambda y, s: (1, y, 0, 0))]
        args += arrays + [f.got]
        counts.append(len(arrays) + 1)
    out = tuple(shape(f.got.shape[1:], bf16) for f in flows)

    def kernel(_, *refs):
        k = 0
        for i, n in enumerate(counts):
            total = sum(value_of(r) for r in refs[k : k + n])
            refs[len(args) + i][...] = total.astype(bf16)
            k += n

    sums = call(
        kernel,
        out,
        (2,),
        in_specs,
        [pl.BlockSpec((1, *o.shape[1:]), lambda y, s: (y, 0, 0)) for o in out],
        cuts,
        args,
    )
    for f, v in zip(flows, sums):
        f.last = exchange(v, f.ring, (3, 1))


def value_of(ref):
    return (ref[0] if len(ref.shape) == 4 else ref[...]).astype(f32)


def turn(flows, cuts):
    in_specs, outs, out_specs, args = [], [], [], []

    counts = []
    for f in flows:
        first = 1 if f.other == "x" else 5
        arrays = f.sources()
        rows, columns = arrays[0].shape[-2] // 4, arrays[0].shape[-1]
        four = pl.BlockSpec((1, 2, rows, columns), lambda j, s, i=first: (0, 0, s[i + j], 0))
        three = pl.BlockSpec((2, rows, columns), lambda j, s, i=first: (0, s[i + j], 0))
        in_specs += [four if a.ndim == 4 else three for a in arrays]
        args += arrays
        counts.append(len(arrays))
        dims = (1, 2, rows, columns)
        outs.append(shape((2, *dims[1:]), bf16))
        out_specs.append(pl.BlockSpec(dims, lambda j, s: (j, 0, 0, 0)))

    def kernel(_, *refs):
        k = 0
        for i, n in enumerate(counts):
            total = sum(value_of(r) for r in refs[k : k + n])
            refs[len(args) + i][0] = total.astype(bf16)
            k += n

    sends = call(kernel, tuple(outs), (2,), in_specs, out_specs, cuts, args)
    for f, send in zip(flows, sends):
        f.before = halves_of(f)
        f.ring = f.other
        f.got = exchange(send, f.ring, (1, 3))


def halves_of(f):
    arrays = f.sources()
    first = 1 if f.other == "x" else 5
    rows, columns = arrays[0].shape[-2] // 4, arrays[0].shape[-1]

    def quarter(which):
        four = pl.BlockSpec((1, 1, rows, columns), lambda y, s: (0, y, s[first + which], 0))
        three = pl.BlockSpec((1, rows, columns), lambda y, s: (y, s[first + which], 0))
        return [four if a.ndim == 4 else three for a in arrays], arrays

    return quarter


def add(a, b, none):
    def kernel(_, a, b, out):
        out[...] = (a[...].astype(f32) + b[...].astype(f32)).astype(bf16)

    out = shape(a.shape, bf16)
    return call(kernel, out, (1,), [whole(a), whole(b)], whole(out), none, (a, b))


class Finish:
    def __init__(self, flows, extra, cuts):
        in_specs, args, sizes = [], [], []
        def half(spec):
            return pl.BlockSpec(
                spec.block_shape, lambda j, s: spec.index_map(lax.rem(j + s[9], 2), s)
            )

        for f in flows:
            specs, arrays = f.kept(0)
            dims = (1, 1, *f.got.shape[2:])
            specs = specs + [
                pl.BlockSpec(dims, lambda y, s: (0, y, 0, 0)),
                pl.BlockSpec((1, *f.last.shape[1:]), lambda y, s: (y, 0, 0)),
            ]
            in_specs += [half(spec) for spec in specs]
            args += arrays + [f.got, f.last]
            sizes.append((len(arrays) + 2, f.got.shape[2], f.got.shape[3] // STEP))
        for e in extra:
            in_specs.append(half(pl.BlockSpec((1, *e.shape[1:]), lambda y, s: (y, 0, 0))))
        args += extra
        rows = sum(u * n for _, u, n in sizes) + sum(e.shape[1] for e in extra)

        def kernel(_, *refs):
            send, mine = refs[-2:]
            j = pl.program_id(0)

            def put(here, value):
                @pl.when(j == 0)
                def _():
                    mine[here, :] = value

                @pl.when(j == 1)
                def _():
                    send[here, :] = value.astype(bf16)

            start, k = 0, 0
            for count, u, n in sizes:
                v = sum(value_of(r) for r in refs[k : k + count])[0]
                for i in range(n):
                    put(slice(start, start + u), v[:, i * STEP : (i + 1) * STEP])
                    start += u
                k += count
            for ref in refs[k:-2]:
                put(slice(start, start + ref.shape[1]), ref[0])
                start += ref.shape[1]

        out = (shape((rows, STEP), bf16), shape((rows, STEP), f32))
        send, self.mine = call(
            kernel, out, (2,), in_specs, [whole(o) for o in out], cuts, args
        )
        self.got = exchange(send, "y", (1, 3))

    def second(self, none):
        self.mine = add(self.mine, self.got, none)
        self.far = lax.ppermute(self.mine, "yh", [(0, 1), (1, 0)])

    def gather(self, none):
        return lax.all_gather(add(self.mine, self.far, none), ("c", "x", "z"), axis=0)


def per_device(
    tokens,
    memory,
    compressed,
    cotangent,
    ln1_g,
    ln1_b,
    w_q,
    w_kv,
    w_r,
    bias_u,
    bias_v,
    w_o,
    ln2_g,
    ln2_b,
    w_in,
    b_in,
    w_out,
    b_out,
    conv_w,
    conv_b,
):
    line.held, line.due = [], {}
    tokens, memory, compressed, cotangent = tokens[0], memory[0], compressed[0], cotangent[0]
    yl, core = lax.axis_index("yl"), lax.axis_index("c")
    place = {"x": lax.axis_index("x"), "z": lax.axis_index("z")}
    none = jnp.zeros((1,), jnp.int32)
    ints = lambda *v: jnp.stack([jnp.asarray(i, jnp.int32) for i in v])

    def thirds(rows):
        half = rows // 2
        other = (1 - yl) * half
        return [yl * half, other + core * (half // 2), other + (1 - core) * (half // 2)]

    def both(v):
        return (v, core_swap(v))

    spot = (place["x"] * 4 + place["z"]) * 2 + core
    piece = pack(
        (ln1_g, ln1_b, bias_u, bias_v, ln2_g, ln2_b, b_out, conv_b, b_in),
        w_in,
        w_out,
        ints(spot),
    )
    piece_got = exchange(piece, "y", (1, 3))

    kv_part, small, o_part = pack_rows(w_kv, w_q, w_r, w_o, ints(core))
    (piece_got,) = gate((piece_got,), kv_part)
    kv_got = exchange(kv_part, "y", (1, 3))
    small_got = exchange(small, "y", (1, 3))
    o_got = exchange(o_part, "y", (1, 3))

    def joined(w, got, twin):
        return jnp.concatenate([w, got, twin], axis=0)

    spread = lax.all_gather(piece_got[:-16], ("x", "z", "c"), axis=0)
    thirds_d = ints(*thirds(D))
    thirds_c = ints(*thirds(3 * D), *thirds(D))
    sinus_table = sinusoid(KEYS, D).astype(bf16)
    sinus_rel = jnp.concatenate(
        [
            lax.dynamic_slice_in_dim(sinus_table, thirds_d[i], width, 1)
            for i, width in enumerate(THIRDS)
        ],
        axis=1,
    )
    line.hold(sinus_rel)
    vectors, b_in = unpack(piece, piece_got, ints(yl))

    normed, normed_rel, oldest, old_quarters = first_norm(compressed, memory, tokens, vectors, thirds_d)
    conv_part = half_rows(conv_w, ints(core))
    both_normed, both_cot = both(normed), both(cotangent)
    own, first, far, second = quarters(place["x"], core)
    got = exchange(
        jnp.stack([pick(old_quarters, first, 0), pick(old_quarters, far, 0)]), "x", (1, 3)
    )
    got_far = exchange(jnp.stack([pick(old_quarters, second, 0), got[1]]), "x", (3, 1))
    old_ring = jnp.concatenate([pick(old_quarters, own, 0), got[0], got_far[0], got_far[1]])
    old_twin = core_swap(old_ring)
    kv_got, small_got = gate((kv_got, small_got), normed, conv_part)
    kv_twin, small_twin = core_swap(kv_got), core_swap(small_got)
    kv_whole = joined(w_kv, kv_got, kv_twin)
    q_whole, r_whole = [
        joined(w, small_got[i], small_twin[i]) for i, w in enumerate((w_q, w_r))
    ]
    key_value = dot(normed_rel, kv_whole).astype(bf16)
    line.hold(key_value)
    queries = dot(normed_rel[2 * T :], q_whole)
    relative = dot(sinus_rel, r_whole).astype(bf16)
    (o_got,) = gate((o_got,), key_value, queries, relative)
    o_whole = joined(w_o, o_got, core_swap(o_got))
    line.hold(queries, relative)
    line.hold(got)
    probs, attended = attend(queries, key_value, relative, vectors, none)
    line.hold(both_normed[1], both_cot[1], got_far)
    residual, normed2, normed2_rel = out_and_norm(attended, o_whole, tokens, vectors, thirds_d)
    both_n2, both_att = both(normed2), both(attended)

    cuts, rels, twins = [], [], []
    for ring in ("x", "z"):
        own, first, far, second = quarters(place[ring], core)
        cuts += [first, far, own, second]
        rels.append([own, first, second, far])
        twins.append([own, second, first, far])
    cuts = ints(core, *cuts, yl)

    def flows(groups):
        pairs = weight_grads(groups, cuts)
        return [Flow(ring, pair) for (ring, _), pair in zip(groups, pairs)]

    def start(some):
        for f in some:
            f.start()

    line.hold(old_twin)
    hidden, d_pre, mixed_out, d_normed2, d_b_in = feed_forward(
        normed2_rel, residual, cotangent, w_in, w_out, spread, b_in, vectors, ints(yl)
    )
    both_hidden, both_pre = both(hidden), both(d_pre)
    conv_got = exchange(conv_part, "y", (1, 3))
    d_residual, d_branch, d_attended, d_ln2_g, d_ln2_b, d_b_out = second_norm_back(
        cotangent, d_normed2, residual, vectors, o_whole, thirds_d
    )
    both_branch = both(d_branch)
    large = flows(
        [
            ("x", [(both_hidden, 0, T, both_cot, False)]),
            ("z", [(both_n2, 0, T, both_pre, False), (both_att, 0, T, both_branch, False)]),
        ]
    )
    start(large)
    line.hold(conv_got)
    conv_pieces = (conv_w, conv_got, core_swap(conv_got))
    d_kv, my_kv, give_kv, d_relative, d_queries, d_bias_u, d_bias_v = attend_back(
        queries, key_value, relative, vectors, probs, d_attended, ints(core)
    )
    both_kv = (my_kv, core_swap(give_kv))
    both_q, both_rel = both(d_queries), both(d_relative)

    compact, comp_normed = compress(oldest, conv_pieces, vectors, thirds_c)
    comp_pair = dot(comp_normed, kv_whole).astype(bf16)
    compressed_next = jnp.concatenate([compressed[T // 3 :], compact], axis=0)
    near = flows(
        [
            ("x", [(both_normed, 0, KEYS, both_kv, True)]),
            (
                "z",
                [
                    (both_normed, 2, T, both_q, False),
                    ((sinus_table,), 0, KEYS, both_rel, False),
                ],
            ),
        ]
    )
    onward(large, cuts)
    loss, d_ck, d_cv = reconstruct(queries, key_value, comp_pair, none)
    recon_loss = jnp.sum(loss) / (T * D)
    d_compact, d_conv_b = compress_back(d_ck, d_cv, kv_whole, compact, vectors, thirds_d)
    ring_got = exchange(d_compact, "x", (1, 3))
    sends = gate([f.send for f in near], ring_got)
    for f, send in zip(near, sends):
        f.send = send
    start(near)
    line.hold(ring_got)
    turn(large, cuts)
    ring_pair = jnp.concatenate([d_compact, ring_got])
    pair_got = exchange(ring_pair, "x", (3, 1))
    d_tokens, d_ln1_g, d_ln1_b = first_norm_back(
        d_kv, d_queries, kv_whole, q_whole, compressed, memory, tokens, vectors, d_residual,
        thirds_d,
    )
    (pair_got,) = gate((pair_got,), d_ln1_g)
    onward(large, cuts)
    compact_ring = jnp.concatenate([ring_pair, pair_got])
    compact_twin = core_swap(compact_ring)
    onward(near, cuts)
    line.hold(compact_twin)
    conv = Flow("x", None, conv_grad(old_ring, old_twin, compact_ring, compact_twin, cuts))
    late_flows = [*near, conv]
    line.hold(*[f.last for f in large])
    turn(late_flows, cuts)
    onward(late_flows, cuts)

    total = jnp.concatenate(
        [d_ln1_g, d_ln1_b, d_bias_u, d_bias_v, d_ln2_g, d_ln2_b, d_b_out, d_conv_b]
        + [d_b_in]
    )
    total = jnp.concatenate(
        [
            total[:8].reshape(8, 2, STEP).transpose(1, 0, 2),
            total[8:].reshape(2, 4, STEP),
            jnp.zeros((2, 4, STEP), f32),
        ],
        axis=1,
    )
    sums = Finish([*large, *late_flows], [total], cuts)
    sums.second(none)
    gathered = sums.gather(none)

    g_out, g_in, g_o, g_kv, g_q, g_r, g_conv = widen(
        gathered,
        [
            (FF // 2, D, "x"),
            (D // 2, FF, "z"),
            (D // 2, D, "z"),
            (D // 2, 2 * D, "x"),
            (D // 2, D, "z"),
            (D // 2, D, "z"),
            (3 * D // 2, D, "x"),
        ],
        none,
    )
    half = jnp.sum(gathered[:, 512:524].astype(f32), axis=0)
    t_ln1_g, t_ln1_b, t_bu, t_bv, t_ln2_g, t_ln2_b, t_bout, t_convb = [half[i] for i in range(8)]
    t_bin = half[8:].reshape(-1)
    return (
        mixed_out[None],
        compressed_next[None],
        recon_loss[None],
        d_tokens[None],
        t_ln1_g,
        t_ln1_b,
        g_q,
        g_kv,
        g_r,
        t_bu,
        t_bv,
        g_o,
        t_ln2_g,
        t_ln2_b,
        g_in,
        t_bin,
        g_out,
        t_bout,
        g_conv,
        t_convb,
    )


def solution(mesh):
    fine = Mesh(mesh.devices.reshape(2, 4, 4, 2, 2), AXES)
    stream = P(AXES, None, None)
    vec, mat = P("yl"), P("yl", None)
    weights = (vec, vec, mat, mat, mat, vec, vec, mat, vec, vec, mat, vec, mat, vec, mat, vec)
    return jax.shard_map(
        per_device,
        mesh=fine,
        in_specs=(stream,) * 4 + weights,
        out_specs=(stream, stream, P(AXES), stream) + weights,
        check_vma=False,
    )
```

```python
import jax
import jax.numpy as jnp
from jax import lax
from jax.experimental import pallas as pl
from jax.experimental.pallas import tpu as pltpu
from jax.sharding import Mesh, PartitionSpec as P

H = 8
HD = 128
D = 1024
T = 192
KEYS = 576
PAD = 640
FF = 4096
FACTOR = HD ** (-0.5)
f32 = jnp.float32
bf16 = jnp.bfloat16
AXES = ("yh", "x", "z", "c", "yl")
RING = {"x": ("x", "c"), "z": ("z", "c"), "y": ("yh", "c", "yl")}


def sinusoid(key_count, model_dim):
    distance = (key_count - 1 - jnp.arange(key_count)).astype(f32)
    inverse = 1.0 / 10000.0 ** (jnp.arange(0, model_dim, 2).astype(f32) / model_dim)
    angles = distance[:, None] * inverse[None, :]
    return jnp.concatenate([jnp.sin(angles), jnp.cos(angles)], axis=-1)


def dot(a, b):
    return jnp.dot(a, b, preferred_element_type=f32)


def dot_t(a, b):
    return lax.dot_general(a, b, (((1,), (1,)), ((), ())), preferred_element_type=f32)


def t_dot(a, b):
    return lax.dot_general(a, b, (((0,), (0,)), ((), ())), preferred_element_type=f32)


class Line:
    def __init__(self):
        self.held, self.due = [], {}

    def hold(self, *values):
        self.held += values

    def expect(self, gap, *values):
        self.due.setdefault(gap, []).extend(values)

    def ran(self, result):
        self.held = [result, *self.due.get(1, [])]
        self.due = {gap - 1: values for gap, values in self.due.items() if gap > 1}

    def later(self, value):
        return lax.optimization_barrier((value, *self.held))[0] if self.held else value


line = Line()


def call(kernel, out, grid, in_specs, out_specs, scalars, args, scratch=()):
    held, n = line.held, len(args)

    def body(s, *refs):
        kernel(s, *refs[:n], *refs[n + len(held) :])

    result = pl.pallas_call(
        body,
        out_shape=out,
        grid_spec=pltpu.PrefetchScalarGridSpec(
            num_scalar_prefetch=1,
            grid=grid,
            in_specs=list(in_specs) + [pl.BlockSpec(memory_space=pl.ANY)] * len(held),
            out_specs=out_specs,
            scratch_shapes=list(scratch),
        ),
        compiler_params=pltpu.CompilerParams(vmem_limit_bytes=56 << 20),
    )(scalars, *args, *held)
    line.ran(jax.tree.leaves(result)[0])
    return result


def gate(values, *after):
    n = len(values)
    anywhere = pl.BlockSpec(memory_space=pl.ANY)
    return pl.pallas_call(
        lambda *refs: None,
        out_shape=[jax.ShapeDtypeStruct(v.shape, v.dtype) for v in values],
        in_specs=[anywhere] * (n + len(after)),
        out_specs=[anywhere] * n,
        input_output_aliases={i: i for i in range(n)},
    )(*values, *after)


def whole(a):
    zeros = (0,) * a.ndim
    return pl.BlockSpec(a.shape, lambda *_: zeros)


def shape(dims, dtype):
    return jax.ShapeDtypeStruct(dims, dtype)


def at(offset):
    return pl.multiple_of(offset, 128)


def center_scale(v):
    mid = v - jnp.mean(v, axis=-1, keepdims=True)
    r = lax.rsqrt(jnp.mean(mid * mid, axis=-1, keepdims=True) + 1e-5)
    return mid * r, r


def norm_back(xhat, r, g, dn):
    gd = dn * g
    return r * (
        gd
        - jnp.mean(gd, axis=-1, keepdims=True)
        - xhat * jnp.mean(gd * xhat, axis=-1, keepdims=True)
    )


def softmax(s):
    e = jnp.exp(s - jnp.max(s, axis=-1, keepdims=True))
    return e / jnp.sum(e, axis=-1, keepdims=True)


(LN1_G, LN1_B, BIAS_U, BIAS_V, LN2_G, LN2_B, B_OUT, CONV_B) = range(8)


def row(ref, i):
    return ref[i : i + 1, :]


def pack(vectors, w_in, w_out, scalars):
    n_in, n_out = (w.shape[0] // 32 for w in (w_in, w_out))
    chunks = FF // D
    rows = n_out + n_in * chunks
    half = D // 2

    def kernel(_, *refs):
        wi, wo, piece, flat = refs[-4:]
        flat[...] = jnp.zeros_like(flat)
        for i, ref in enumerate(refs[:8]):
            flat[i : i + 1, :half] = ref[...].astype(f32).reshape(1, half)
        flat[8 : 8 + FF // 2 // D, :] = refs[8][...].astype(f32).reshape(FF // 2 // D, D)
        piece[:n_out, :] = wo[...]
        for i in range(chunks):
            piece[n_out + i * n_in : n_out + (i + 1) * n_in, :] = wi[:, i * D : (i + 1) * D]
        piece[rows:, :] = flat[...].astype(bf16)

    out = shape((rows + 16, D), bf16)
    return call(
        kernel,
        out,
        (1,),
        [whole(v) for v in vectors]
        + [
            pl.BlockSpec((w.shape[0] // 32, w.shape[1]), lambda j, s: (s[0], 0))
            for w in (w_in, w_out)
        ],
        whole(out),
        scalars,
        (*vectors, w_in, w_out),
        [pltpu.VMEM((16, D), f32)],
    )


def half_rows(w, scalars):
    n = w.shape[0] // 2

    def kernel(_, w, out):
        out[...] = w[...]

    out = shape((n, w.shape[1]), w.dtype)
    spec = pl.BlockSpec((n, w.shape[1]), lambda j, s: (s[0], 0))
    return call(kernel, out, (1,), [spec], whole(out), scalars, (w,))


def pack_rows(w_kv, w_q, w_r, w_o, scalars):
    n = w_q.shape[0] // 2

    def kernel(_, kv, q, r, o, kv_out, out, o_out):
        kv_out[...] = kv[...]
        out[0] = q[...]
        out[1] = r[...]
        o_out[...] = o[...]

    args = (w_kv, w_q, w_r, w_o)
    out = (shape((n, 2 * D), bf16), shape((2, n, D), bf16), shape((n, D), bf16))
    return call(
        kernel,
        out,
        (1,),
        [pl.BlockSpec((w.shape[0] // 2, w.shape[1]), lambda j, s: (s[0], 0)) for w in args],
        [whole(o) for o in out],
        scalars,
        args,
    )


def unpack(mine, theirs, scalars):
    half = D // 2
    at_row = mine.shape[0] // 16 - 1
    tail = pl.BlockSpec((16, D), lambda j, s: (at_row, 0))

    def kernel(s, mine, theirs, vectors, b_in):
        a, b = mine[...].astype(f32), theirs[...].astype(f32)
        low = jnp.where(s[0] == 0, a, b)
        high = jnp.where(s[0] == 0, b, a)
        vectors[:, :half] = low[:8, :half]
        vectors[:, half:] = high[:8, :half]
        rows = FF // 2 // D
        b_in[:rows] = low[8 : 8 + rows]
        b_in[rows:] = high[8 : 8 + rows]

    out = (shape((8, D), f32), shape((FF // D, D), f32))
    return call(
        kernel, out, (1,), [tail, tail], [whole(o) for o in out], scalars, (mine, theirs)
    )


def relative_columns(x, s, widths):
    parts = [x[:, pl.ds(at(s[i]), width)] for i, width in enumerate(widths)]
    return jnp.concatenate(parts, axis=1)


def natural_columns(out, x, s, widths):
    start = 0
    for i, width in enumerate(widths):
        out[:, pl.ds(at(s[i]), width)] = x[:, start : start + width]
        start += width


THIRDS = (D // 2, D // 4, D // 4)


def first_norm(compressed, memory, tokens, vectors, offsets):
    def kernel(s, comp, mem, tok, vec, out, out_rel, old, old_quarters):
        gain, bias = row(vec, LN1_G), row(vec, LN1_B)

        def part(ref, base):
            for i in range(0, T, 32):
                xhat, r = center_scale(ref[i : i + 32, :].astype(f32))
                out[base + i : base + i + 32, :] = (xhat * gain + bias).astype(bf16)

        part(comp, 0)
        part(mem, T)
        part(tok, 2 * T)
        out_rel[...] = relative_columns(out, s, THIRDS)
        line_of = lax.broadcasted_iota(jnp.int32, (T // 3, T), 0)
        col = lax.broadcasted_iota(jnp.int32, (T // 3, T), 1)
        low = mem[...].astype(bf16)
        for tap in range(3):
            take = jnp.where(col == 3 * line_of + tap, 1.0, 0.0).astype(bf16)
            old[:, tap * D : (tap + 1) * D] = dot(take, low).astype(bf16)
        width = 3 * D // 8
        for q in range(4):
            for y in range(2):
                begin = y * 3 * D // 2 + q * width
                old_quarters[q, :, y * width : (y + 1) * width] = old[:, begin : begin + width]

    args = (compressed, memory, tokens, vectors)
    out = (
        shape((KEYS, D), bf16),
        shape((KEYS, D), bf16),
        shape((T // 3, 3 * D), bf16),
        shape((4, T // 3, 3 * D // 4), bf16),
    )
    return call(
        kernel, out, (1,), [whole(a) for a in args], [whole(o) for o in out], offsets, args
    )


def head(n, rows, row_block=0, first=0):
    return pl.BlockSpec((rows, n * HD), lambda h, s: (row_block, first // n + h))


def columns_of(n):
    return [slice(i * HD, (i + 1) * HD) for i in range(n)]


def attend(queries, key_value, relative, vectors, none):
    n = 2

    def kernel(_, q, k, v, rel, vec, probs, out):
        pad = jnp.zeros((PAD - KEYS, HD), bf16)
        i = lax.broadcasted_iota(jnp.int32, (T, PAD), 0)
        j = lax.broadcasted_iota(jnp.int32, (T, PAD), 1)
        seen = j <= i + (KEYS - T)
        cuts = columns_of(n)
        content = [((q[:, c] + vec[BIAS_U : BIAS_U + 1, c]) * FACTOR).astype(bf16) for c in cuts]
        located = [((q[:, c] + vec[BIAS_V : BIAS_V + 1, c]) * FACTOR).astype(bf16) for c in cuts]
        raw = [
            dot_t(x, jnp.concatenate([rel[:, c], pad], axis=0)) for x, c in zip(located, cuts)
        ]
        near = [dot_t(x, jnp.concatenate([k[:, c], pad], axis=0)) for x, c in zip(content, cuts)]
        raw = [pltpu.roll(x, PAD - T + 1, 1, stride=1, stride_axis=0) for x in raw]
        p = [softmax(jnp.where(seen, a + b, -1e30)) for a, b in zip(near, raw)]
        for h, c in enumerate(cuts):
            probs[h] = p[h]
            value = jnp.concatenate([v[:, c], pad], axis=0)
            out[:, c] = dot(p[h].astype(bf16), value).astype(bf16)

    return call(
        kernel,
        (shape((H, T, PAD), f32), shape((T, D), bf16)),
        (H // n,),
        [head(n, T), head(n, KEYS), head(n, KEYS, 0, H), head(n, KEYS), head(n, 8)],
        [pl.BlockSpec((n, T, PAD), lambda h, s: (h, 0, 0)), head(n, T)],
        none,
        (queries, key_value, key_value, relative, vectors),
    )


def attend_back(queries, key_value, relative, vectors, probs, d_attended, scalars):
    n = 2

    def kernel(s, q, k, v, rel, vec, probs, d_att, d_kv, mine, give, d_rel, d_q, d_bu, d_bv):
        pad = jnp.zeros((PAD - KEYS, HD), bf16)
        i = lax.broadcasted_iota(jnp.int32, (T, T), 0)
        j = lax.broadcasted_iota(jnp.int32, (T, T), 1)
        flip = jnp.where(i + j == T - 1, 1.0, 0.0).astype(bf16)
        cuts = columns_of(n)
        content = [((q[:, c] + vec[BIAS_U : BIAS_U + 1, c]) * FACTOR).astype(bf16) for c in cuts]
        located = [((q[:, c] + vec[BIAS_V : BIAS_V + 1, c]) * FACTOR).astype(bf16) for c in cuts]
        da = [d_att[:, c] for c in cuts]
        d_p = [dot_t(x, jnp.concatenate([v[:, c], pad], axis=0)) for x, c in zip(da, cuts)]
        d_v = [t_dot(probs[h].astype(bf16), x)[:KEYS].astype(bf16) for h, x in enumerate(da)]
        d_s = []
        for h, x in enumerate(d_p):
            p = probs[h]
            d_s.append((p * (x - jnp.sum(p * x, axis=-1, keepdims=True))).astype(bf16))
        d_raw = [dot(flip, x) for x in d_s]
        d_c = [
            dot(x, jnp.concatenate([k[:, c], pad], axis=0)) * FACTOR for x, c in zip(d_s, cuts)
        ]
        d_k = [t_dot(x, y)[:KEYS].astype(bf16) for x, y in zip(d_s, content)]
        d_raw = [pltpu.roll(x, 0, 1, stride=1, stride_axis=0).astype(bf16) for x in d_raw]
        d_raw = [dot(flip, x).astype(bf16) for x in d_raw]
        d_l = [
            dot(x, jnp.concatenate([rel[:, c], pad], axis=0)) * FACTOR for x, c in zip(d_raw, cuts)
        ]
        for h, c in enumerate(cuts):
            d_rel[:, c] = t_dot(d_raw[h], located[h])[:KEYS].astype(bf16)
            d_kv[0, :, c] = d_k[h]
            d_kv[1, :, c] = d_v[h]
            mine[:, c] = jnp.where(s[0] == 0, d_k[h], d_v[h])
            give[:, c] = jnp.where(s[0] == 0, d_v[h], d_k[h])
            d_q[:, c] = (d_c[h] + d_l[h]).astype(bf16)
            d_bu[:, c] = jnp.sum(d_c[h], axis=0, keepdims=True)
            d_bv[:, c] = jnp.sum(d_l[h], axis=0, keepdims=True)

    return call(
        kernel,
        (shape((2, KEYS, D), bf16),)
        + (shape((KEYS, D), bf16),) * 3
        + (shape((T, D), bf16), shape((1, D), f32), shape((1, D), f32)),
        (H // n,),
        [
            head(n, T),
            head(n, KEYS),
            head(n, KEYS, 0, H),
            head(n, KEYS),
            head(n, 8),
            pl.BlockSpec((n, T, PAD), lambda h, s: (h, 0, 0)),
            head(n, T),
        ],
        [
            pl.BlockSpec((2, KEYS, n * HD), lambda h, s: (0, 0, h)),
            head(n, KEYS),
            head(n, KEYS),
            head(n, KEYS),
            head(n, T),
            head(n, 1),
            head(n, 1),
        ],
        scalars,
        (queries, key_value, key_value, relative, vectors, probs, d_attended),
    )


def out_and_norm(attended, w_o, tokens, vectors, offsets):
    def kernel(s, att, w, tok, vec, res, n2, n2_rel):
        total = tok[...].astype(f32) + dot(relative_columns(att, s, THIRDS), w[...])
        res[...] = total
        xhat, r = center_scale(total)
        n2[...] = (xhat * row(vec, LN2_G) + row(vec, LN2_B)).astype(bf16)
        other = at(D // 2 - s[0])
        n2_rel[:, : D // 2] = n2[:, pl.ds(at(s[0]), D // 2)]
        n2_rel[:, D // 2 :] = n2[:, pl.ds(other, D // 2)]

    args = (attended, w_o, tokens, vectors)
    out = (shape((T, D), f32), shape((T, D), bf16), shape((T, D), bf16))
    return call(
        kernel, out, (1,), [whole(a) for a in args], [whole(o) for o in out], offsets, args
    )


STEP = 512
UNITS = 1024
HALF = FF // 2 // UNITS


def feed_forward(n2_rel, residual, cotangent, w_in, w_out, spread, b_in, vectors, scalars):
    n_in = w_in.shape[0] // 32
    n_out = w_out.shape[0] // 32
    skip = n_out // n_in
    per = UNITS // n_out
    K_NORM = 0.7978845608028654

    def natural(j, s):
        return lax.rem(j + s[0] * HALF, 2 * HALF)

    def kernel(s, n2, res, cot, wi0, wi1, wo0, wo1, bi, vec, hid, dpre, mixed, dn2, dbi, acc, back):
        j = pl.program_id(0)
        n = natural(j, s)

        @pl.when(j == 0)
        def _():
            acc[...] = jnp.zeros_like(acc)
            back[...] = jnp.zeros_like(back)

        wo = jnp.where(j < HALF, wo0[...], wo1[...].reshape(UNITS, D))
        win = jnp.concatenate([wi0[...], wi1[...].reshape(D // 2, UNITS)], axis=0)
        pre = dot(n2[...], win) + bi[pl.ds(n, 1), :]
        d_hidden = dot_t(cot[...], wo)
        square = pre * pre
        t = jnp.tanh(K_NORM * pre * (1.0 + 0.044715 * square))
        gate_ = 0.5 * (1.0 + t)
        hidden = (pre * gate_).astype(bf16)
        slope = gate_ + (0.5 * K_NORM) * pre * (1.0 - t * t) * (1.0 + (3 * 0.044715) * square)
        d_pre = (d_hidden * slope).astype(bf16)
        hid[...] = hidden
        dpre[...] = d_pre
        dbi[pl.ds(n, 1), :] = jnp.sum(d_pre.astype(f32), axis=0, keepdims=True)
        acc[...] += dot(hidden, wo)
        back[...] += dot_t(d_pre, win)

        @pl.when(j == 2 * HALF - 1)
        def _():
            mixed[...] = (res[...] + acc[...] + row(vec, B_OUT)).astype(bf16)
            dn2[:, pl.ds(at(s[0] * (D // 2)), D // 2)] = back[:, : D // 2]
            dn2[:, pl.ds(at((1 - s[0]) * (D // 2)), D // 2)] = back[:, D // 2 :]

    out = (
        shape((T, FF), bf16),
        shape((T, FF), bf16),
        shape((T, D), bf16),
        shape((T, D), f32),
        shape((2 * HALF, UNITS), f32),
    )
    by_unit = pl.BlockSpec((T, UNITS), lambda j, s: (0, natural(j, s)))
    return call(
        kernel,
        out,
        (2 * HALF,),
        [
            whole(n2_rel),
            whole(residual),
            whole(cotangent),
            pl.BlockSpec((D // 2, UNITS), lambda j, s: (0, natural(j, s))),
            pl.BlockSpec((32, n_in, UNITS), lambda j, s: (0, skip + natural(j, s), 0)),
            pl.BlockSpec((UNITS, D), lambda j, s: (jnp.minimum(j, HALF - 1), 0)),
            pl.BlockSpec(
                (per, n_out, D), lambda j, s: (jnp.maximum(j - HALF, 0), 0, 0)
            ),
            whole(b_in),
            whole(vectors),
        ],
        [by_unit, by_unit, whole(out[2]), whole(out[3]), whole(out[4])],
        scalars,
        (n2_rel, residual, cotangent, w_in, spread, w_out, spread, b_in, vectors),
        [pltpu.VMEM((T, D), f32), pltpu.VMEM((T, D), f32)],
    )


def second_norm_back(cotangent, d_n2, residual, vectors, w_o, offsets):
    def kernel(s, cot, dn, res, vec, w, d_res, d_br, d_att, dg, db, dbo):
        xhat, r = center_scale(res[...])
        dn, wide = dn[...], cot[...].astype(f32)
        dg[...] = jnp.sum(dn * xhat, axis=0, keepdims=True)
        db[...] = jnp.sum(dn, axis=0, keepdims=True)
        dbo[...] = jnp.sum(wide, axis=0, keepdims=True)
        total = wide + norm_back(xhat, r, row(vec, LN2_G), dn)
        d_res[...] = total
        low = total.astype(bf16)
        d_br[...] = low
        natural_columns(d_att, dot_t(low, w[...]).astype(bf16), s, THIRDS)

    args = (cotangent, d_n2, residual, vectors, w_o)
    out = (
        shape((T, D), f32),
        shape((T, D), bf16),
        shape((T, D), bf16),
        shape((1, D), f32),
        shape((1, D), f32),
        shape((1, D), f32),
    )
    return call(
        kernel, out, (1,), [whole(a) for a in args], [whole(o) for o in out], offsets, args
    )


def first_norm_back(d_kv, d_q, w_kv, w_q, compressed, memory, tokens, vectors, d_res, offsets):
    steps = 4
    wide, slim = 2 * D // steps, D // steps

    def kernel(s, dkv, dq, kw, qw, comp, mem, tok, vec, dres, dtok, dg, db, acc, nat, xh, rs):
        j = pl.program_id(0)

        def product(start):
            value = dot_t(dkv[0], kw[...])
            if start:
                acc[...] = value
            else:
                acc[...] += value
            acc[2 * T :, :] += dot_t(dq[...], qw[...])

        for block, ref in enumerate((comp, mem, tok)):

            @pl.when(j == block)
            def _(block=block, ref=ref):
                product(block == 0)
                for i in range(0, T, 32):
                    xhat, r = center_scale(ref[i : i + 32, :].astype(f32))
                    xh[block * T + i : block * T + i + 32, :] = xhat
                    if block == 2:
                        rs[i : i + 32, :] = jnp.broadcast_to(r, (32, HD))

        @pl.when(j == steps - 1)
        def _():
            product(False)
            natural_columns(nat, acc, s, THIRDS)
            gain = row(vec, LN1_G)
            sum_g = jnp.zeros((8, D), f32)
            sum_b = jnp.zeros((8, D), f32)
            for i in range(0, KEYS, 32):
                dn, xhat = nat[i : i + 32, :], xh[i : i + 32, :]
                both = dn * xhat
                sum_g += (both[:8] + both[8:16]) + (both[16:24] + both[24:])
                sum_b += (dn[:8] + dn[8:16]) + (dn[16:24] + dn[24:])
                if i >= 2 * T:
                    k = i - 2 * T
                    r = rs[k : k + 32, :1]
                    dtok[k : k + 32, :] = dres[k : k + 32, :] + norm_back(xhat, r, gain, dn)
            dg[...] = jnp.sum(sum_g, axis=0, keepdims=True)
            db[...] = jnp.sum(sum_b, axis=0, keepdims=True)

    rest = (compressed, memory, tokens, vectors, d_res)
    out = (shape((T, D), f32), shape((1, D), f32), shape((1, D), f32))
    return call(
        kernel,
        out,
        (steps,),
        [
            pl.BlockSpec((1, KEYS, wide), lambda j, s: (j // (steps // 2), 0, lax.rem(j, steps // 2))),
            pl.BlockSpec((T, slim), lambda j, s: (0, j)),
            pl.BlockSpec((D, wide), lambda j, s: (0, j)),
            pl.BlockSpec((D, slim), lambda j, s: (0, j)),
        ]
        + [whole(a) for a in rest],
        [whole(o) for o in out],
        offsets,
        (d_kv, d_q, w_kv, w_q, *rest),
        [pltpu.VMEM((KEYS, D), f32)] * 3 + [pltpu.VMEM((T, HD), f32)],
    )


def compress(oldest, pieces, vectors, offsets):
    block = 256
    rows = T // 3

    def kernel(s, x, w0, w1, w2, vec, compact, normed, x_rel, natural):
        j = pl.program_id(0)

        @pl.when(j == 0)
        def _():
            x_rel[...] = relative_columns(x, s, (3 * D // 2, 3 * D // 4, 3 * D // 4))

        w = jnp.concatenate([w0[...], w1[...], w2[...]], axis=0)
        here = pl.ds(at(j * block), block)
        compact[:, here] = dot(x_rel[...], w) + vec[CONV_B : CONV_B + 1, here]

        @pl.when(j == D // block - 1)
        def _():
            xhat, r = center_scale(compact[...])
            natural[...] = (xhat * row(vec, LN1_G) + row(vec, LN1_B)).astype(bf16)
            start = 0
            for i, width in enumerate(THIRDS):
                normed[:, start : start + width] = natural[:, pl.ds(at(s[3 + i]), width)]
                start += width

    out = (shape((rows, D), f32), shape((rows, D), bf16))
    return call(
        kernel,
        out,
        (D // block,),
        [whole(oldest)]
        + [pl.BlockSpec((w.shape[0], block), lambda j, s: (0, j)) for w in pieces]
        + [whole(vectors)],
        [whole(o) for o in out],
        offsets,
        (oldest, *pieces, vectors),
        [pltpu.VMEM((rows, 3 * D), bf16), pltpu.VMEM((rows, D), bf16)],
    )


def reconstruct(queries, key_value, comp_pair, none):
    rows = T // 3
    n = 4

    def kernel(_, q, k, v, ck, cv, loss, dck, dcv):
        cuts = columns_of(n)
        asking = [(q[:, c] * FACTOR).astype(bf16) for c in cuts]
        far = [dot_t(x, k[:, c]) for x, c in zip(asking, cuts)]
        near = [dot_t(x, ck[:, c]) for x, c in zip(asking, cuts)]
        p = [softmax(x).astype(bf16) for x in far]
        gp = [softmax(x) for x in near]
        low = [x.astype(bf16) for x in gp]
        miss = [dot(p[h], v[:, c]) - dot(low[h], cv[:, c]) for h, c in enumerate(cuts)]
        total = sum(jnp.sum(x * x, axis=0, keepdims=True) for x in miss)
        d_guess = [((-2.0 / (T * D)) * x).astype(bf16) for x in miss]
        d_gp = [dot_t(x, cv[:, c]) for x, c in zip(d_guess, cuts)]
        d_gs = [
            (x * (y - jnp.sum(x * y, axis=-1, keepdims=True))).astype(bf16)
            for x, y in zip(gp, d_gp)
        ]
        for h, c in enumerate(cuts):
            dcv[:, c] = t_dot(low[h], d_guess[h]).astype(bf16)
            dck[:, c] = t_dot(d_gs[h], asking[h]).astype(bf16)

        @pl.when(pl.program_id(0) == 0)
        def _():
            loss[...] = total

        @pl.when(pl.program_id(0) > 0)
        def _():
            loss[...] += total

    return call(
        kernel,
        (shape((1, HD), f32), shape((rows, D), bf16), shape((rows, D), bf16)),
        (H // n,),
        [head(n, T), head(n, T, 1), head(n, T, 1, H), head(n, rows), head(n, rows, 0, H)],
        [pl.BlockSpec((1, HD), lambda h, s: (0, 0)), head(n, rows), head(n, rows)],
        none,
        (queries, key_value, key_value, comp_pair, comp_pair),
    )


def compress_back(dck, dcv, w_kv, compact, vectors, offsets):
    rows = T // 3

    def kernel(s, dck, dcv, w, compact, vec, d_compact, d_bias, dn):
        back = dot_t(jnp.concatenate([dck[...], dcv[...]], axis=1), w[...])
        natural_columns(dn, back, s, THIRDS)
        xhat, r = center_scale(compact[...])
        low = norm_back(xhat, r, row(vec, LN1_G), dn[...]).astype(bf16)
        d_compact[...] = low
        d_bias[...] = jnp.sum(low.astype(f32), axis=0, keepdims=True)

    args = (dck, dcv, w_kv, compact, vectors)
    out = (shape((rows, D), bf16), shape((1, D), f32))
    return call(
        kernel,
        out,
        (1,),
        [whole(a) for a in args],
        [whole(o) for o in out],
        offsets,
        args,
        [pltpu.VMEM((rows, D), f32)],
    )


def weight_grads(groups, scalars):
    in_specs, args, outs, out_specs, layout, scratch = [], [], [], [], [], []
    for ring, jobs in groups:
        first = 1 if ring == "x" else 5
        block = jobs[0][0][0].shape[1] // 8
        plan = []
        for xs, row_block, rows, dys, ready in jobs:
            width = dys[0].shape[1] // (1 if ready else 2)
            plan.append((width, rows, len(xs)))
            for x in xs:
                for y in range(2):
                    in_specs.append(
                        pl.BlockSpec(
                            (rows, block),
                            lambda q, s, r=row_block, f=first, y=y: (r, y * 4 + s[f + q]),
                        )
                    )
                    args.append(x)
            for dy in dys:
                in_specs.append(
                    pl.BlockSpec((rows, width), lambda q, s, r=ready: (0, 0 if r else s[0]))
                )
                args.append(dy)
            scratch.append(pltpu.VMEM((rows * len(xs), width), bf16))
        dims = (1, 2, block, sum(p[0] for p in plan))
        outs += [shape((2, *dims[1:]), bf16)] * 2
        out_specs += [
            pl.BlockSpec(dims, lambda q, s: (jnp.minimum(q, 1), 0, 0, 0)),
            pl.BlockSpec(dims, lambda q, s: (jnp.maximum(q - 2, 0), 0, 0, 0)),
        ]
        layout.append(plan)
    n_in, n_out = len(in_specs), len(outs)

    def kernel(s, *refs):
        ins, results, joined = refs[:n_in], refs[n_in : n_in + n_out], refs[n_in + n_out :]
        q = pl.program_id(0)

        @pl.when(q == 0)
        def _():
            place, k = 0, 0
            for plan in layout:
                for _, rows, n in plan:
                    da, db = ins[place + 2 * n], ins[place + 2 * n + 1]
                    if n == 2:
                        joined[k][:rows, :] = da[...]
                        joined[k][rows:, :] = db[...]
                    else:
                        joined[k][...] = (da[...].astype(f32) + db[...].astype(f32)).astype(bf16)
                    place += 2 * n + 2
                    k += 1

        place, k = 0, 0
        for i, plan in enumerate(layout):
            send, keep = results[2 * i : 2 * i + 2]
            block = send.shape[2]
            start = 0
            for width, rows, n in plan:
                x = jnp.concatenate([r[...] for r in ins[place : place + 2]], axis=1)
                if n == 2:
                    other = jnp.concatenate([r[...] for r in ins[place + 2 : place + 4]], axis=1)
                    x = jnp.concatenate([x, other], axis=0)
                value = t_dot(x, joined[k][...]).astype(bf16).reshape(2, block, width)
                cut = slice(start, start + width)
                send[0, :, :, cut] = jnp.where(q < 2, value, send[0, :, :, cut])
                keep[0, :, :, cut] = value
                start += width
                place += 2 * n + 2
                k += 1

    flat = call(kernel, tuple(outs), (4,), in_specs, out_specs, scalars, args, scratch)
    return [(flat[2 * i], flat[2 * i + 1]) for i in range(len(groups))]


def conv_grad(x, x_twin, dy, dy_twin, scalars):
    rows, columns = x.shape[1] // 2, D // 2

    def kernel(s, xa, xb, da, db, out):
        both = jnp.concatenate([xa[...], xb[...]], axis=0)
        total = t_dot(both, jnp.concatenate([da[...], db[...]], axis=0))
        out[...] = total.reshape(2, rows, columns)

    half = pl.BlockSpec((dy.shape[0], columns), lambda j, s: (0, s[0]))
    out = shape((2, rows, columns), f32)
    return call(
        kernel,
        out,
        (1,),
        [whole(x), whole(x_twin), half, half],
        whole(out),
        scalars,
        (x, x_twin, dy, dy_twin),
    )


def widen(gathered, plan, none):
    outs, specs, layout = [], [], []
    start = 0
    for rows, columns, ring in plan:
        u, chunks = rows // 16, columns // 2 // STEP
        outs.append(shape((4, 4, u, columns), f32))
        if ring == "x":
            specs.append(
                pl.BlockSpec((1, 4, u, chunks * STEP), lambda c, x, s: (x, 0, 0, c))
            )
        else:
            specs.append(
                pl.BlockSpec((4, 1, u, chunks * STEP), lambda c, x, s: (0, x, 0, c))
            )
        layout.append((start, u, chunks, ring))
        start += u * chunks

    def kernel(_, src, *results):
        for out, (start, u, chunks, ring) in zip(results, layout):
            for k in range(chunks):
                cut = slice(k * STEP, (k + 1) * STEP)
                for z in range(4):
                    value = src[z, start + k * u : start + (k + 1) * u, :].astype(f32)
                    if ring == "x":
                        out[0, z, :, cut] = value
                    else:
                        out[z, 0, :, cut] = value

    results = call(
        kernel,
        tuple(outs),
        (2, 4),
        [pl.BlockSpec((4, gathered.shape[1], STEP), lambda c, x, s: (c * 4 + x, 0, 0))],
        specs,
        none,
        (gathered,),
    )
    return [r.reshape(rows, columns) for r, (rows, columns, _) in zip(results, plan)]


def core_swap(v):
    return lax.ppermute(v, "c", [(0, 1), (1, 0)])


def pair_swap(v):
    return lax.ppermute(v, "yl", [(0, 1), (1, 0)])


def exchange(v, ring, masks):
    def flat(i, c):
        return (i // 2 * 2 + c) * 2 + i % 2 if ring == "y" else 2 * i + c

    pairs = [(flat(i, c), flat(i ^ masks[c], c)) for i in range(4) for c in range(2)]
    return lax.ppermute(v, RING[ring], pairs)


def pick(v, index, axis):
    return lax.dynamic_index_in_dim(v, index, axis, keepdims=False)


def quarters(place, core):
    first = jnp.where(core == 0, 1, 3)
    second = jnp.where(core == 0, 3, 1)
    return place, place ^ first, place ^ 2, place ^ second


class Flow:
    def __init__(self, ring, pair, done=None):
        self.ring, self.other = ring, "z" if ring == "x" else "x"
        self.before, self.result = None, done
        if done is None:
            self.send, self.keep = pair

    def start(self):
        self.got = exchange(self.send, self.ring, (1, 3))

    def sources(self):
        return [self.keep, self.got, self.last] if self.result is None else [self.result]

    def kept(self, which):
        if self.before is None:
            dims = (1, 1, *self.keep.shape[2:])
            return [pl.BlockSpec(dims, lambda y, s: (which, y, 0, 0))], [self.keep]
        return self.before(2 + which)


def onward(flows, cuts):
    in_specs, args, counts = [], [], []
    for f in flows:
        specs, arrays = f.kept(1)
        dims = (1, 1, *f.got.shape[2:])
        in_specs += specs + [pl.BlockSpec(dims, lambda y, s: (1, y, 0, 0))]
        args += arrays + [f.got]
        counts.append(len(arrays) + 1)
    out = tuple(shape(f.got.shape[1:], bf16) for f in flows)

    def kernel(_, *refs):
        k = 0
        for i, n in enumerate(counts):
            total = sum(value_of(r) for r in refs[k : k + n])
            refs[len(args) + i][...] = total.astype(bf16)
            k += n

    sums = call(
        kernel,
        out,
        (2,),
        in_specs,
        [pl.BlockSpec((1, *o.shape[1:]), lambda y, s: (y, 0, 0)) for o in out],
        cuts,
        args,
    )
    for f, v in zip(flows, sums):
        f.last = exchange(v, f.ring, (3, 1))


def value_of(ref):
    return (ref[0] if len(ref.shape) == 4 else ref[...]).astype(f32)


def turn(flows, cuts):
    in_specs, outs, out_specs, args = [], [], [], []

    counts = []
    for f in flows:
        first = 1 if f.other == "x" else 5
        arrays = f.sources()
        rows, columns = arrays[0].shape[-2] // 4, arrays[0].shape[-1]
        four = pl.BlockSpec((1, 2, rows, columns), lambda j, s, i=first: (0, 0, s[i + j], 0))
        three = pl.BlockSpec((2, rows, columns), lambda j, s, i=first: (0, s[i + j], 0))
        in_specs += [four if a.ndim == 4 else three for a in arrays]
        args += arrays
        counts.append(len(arrays))
        dims = (1, 2, rows, columns)
        outs.append(shape((2, *dims[1:]), bf16))
        out_specs.append(pl.BlockSpec(dims, lambda j, s: (j, 0, 0, 0)))

    def kernel(_, *refs):
        k = 0
        for i, n in enumerate(counts):
            total = sum(value_of(r) for r in refs[k : k + n])
            refs[len(args) + i][0] = total.astype(bf16)
            k += n

    sends = call(kernel, tuple(outs), (2,), in_specs, out_specs, cuts, args)
    for f, send in zip(flows, sends):
        f.before = halves_of(f)
        f.ring = f.other
        f.got = exchange(send, f.ring, (1, 3))


def halves_of(f):
    arrays = f.sources()
    first = 1 if f.other == "x" else 5
    rows, columns = arrays[0].shape[-2] // 4, arrays[0].shape[-1]

    def quarter(which):
        four = pl.BlockSpec((1, 1, rows, columns), lambda y, s: (0, y, s[first + which], 0))
        three = pl.BlockSpec((1, rows, columns), lambda y, s: (y, s[first + which], 0))
        return [four if a.ndim == 4 else three for a in arrays], arrays

    return quarter


def add(a, b, none):
    def kernel(_, a, b, out):
        out[...] = (a[...].astype(f32) + b[...].astype(f32)).astype(bf16)

    out = shape(a.shape, bf16)
    return call(kernel, out, (1,), [whole(a), whole(b)], whole(out), none, (a, b))


class Finish:
    def __init__(self, flows, extra, cuts):
        in_specs, args, sizes = [], [], []
        def half(spec):
            return pl.BlockSpec(
                spec.block_shape, lambda j, s: spec.index_map(lax.rem(j + s[9], 2), s)
            )

        for f in flows:
            specs, arrays = f.kept(0)
            dims = (1, 1, *f.got.shape[2:])
            specs = specs + [
                pl.BlockSpec(dims, lambda y, s: (0, y, 0, 0)),
                pl.BlockSpec((1, *f.last.shape[1:]), lambda y, s: (y, 0, 0)),
            ]
            in_specs += [half(spec) for spec in specs]
            args += arrays + [f.got, f.last]
            sizes.append((len(arrays) + 2, f.got.shape[2], f.got.shape[3] // STEP))
        for e in extra:
            in_specs.append(half(pl.BlockSpec((1, *e.shape[1:]), lambda y, s: (y, 0, 0))))
        args += extra
        rows = sum(u * n for _, u, n in sizes) + sum(e.shape[1] for e in extra)

        def kernel(_, *refs):
            send, mine = refs[-2:]
            j = pl.program_id(0)

            def put(here, value):
                @pl.when(j == 0)
                def _():
                    mine[here, :] = value

                @pl.when(j == 1)
                def _():
                    send[here, :] = value.astype(bf16)

            start, k = 0, 0
            for count, u, n in sizes:
                v = sum(value_of(r) for r in refs[k : k + count])[0]
                for i in range(n):
                    put(slice(start, start + u), v[:, i * STEP : (i + 1) * STEP])
                    start += u
                k += count
            for ref in refs[k:-2]:
                put(slice(start, start + ref.shape[1]), ref[0])
                start += ref.shape[1]

        out = (shape((rows, STEP), bf16), shape((rows, STEP), f32))
        send, self.mine = call(
            kernel, out, (2,), in_specs, [whole(o) for o in out], cuts, args
        )
        self.got = exchange(send, "y", (1, 3))

    def second(self, none):
        self.mine = add(self.mine, self.got, none)
        self.far = lax.ppermute(self.mine, "yh", [(0, 1), (1, 0)])

    def gather(self, none, *after):
        done = add(self.mine, self.far, none)
        if after:
            (done,) = gate((done,), *after)
            line.hold(done)
        return lax.all_gather(done, ("c", "x", "z"), axis=0)


def per_device(
    tokens,
    memory,
    compressed,
    cotangent,
    ln1_g,
    ln1_b,
    w_q,
    w_kv,
    w_r,
    bias_u,
    bias_v,
    w_o,
    ln2_g,
    ln2_b,
    w_in,
    b_in,
    w_out,
    b_out,
    conv_w,
    conv_b,
):
    line.held, line.due = [], {}
    tokens, memory, compressed, cotangent = tokens[0], memory[0], compressed[0], cotangent[0]
    yl, core = lax.axis_index("yl"), lax.axis_index("c")
    place = {"x": lax.axis_index("x"), "z": lax.axis_index("z")}
    none = jnp.zeros((1,), jnp.int32)
    ints = lambda *v: jnp.stack([jnp.asarray(i, jnp.int32) for i in v])

    def thirds(rows):
        half = rows // 2
        other = (1 - yl) * half
        return [yl * half, other + core * (half // 2), other + (1 - core) * (half // 2)]

    def both(v):
        return (v, core_swap(v))

    spot = (place["x"] * 4 + place["z"]) * 2 + core
    piece = pack(
        (ln1_g, ln1_b, bias_u, bias_v, ln2_g, ln2_b, b_out, conv_b, b_in),
        w_in,
        w_out,
        ints(spot),
    )
    piece_got = exchange(piece, "y", (1, 3))

    kv_part, small, o_part = pack_rows(w_kv, w_q, w_r, w_o, ints(core))
    (piece_got,) = gate((piece_got,), kv_part)
    kv_got = exchange(kv_part, "y", (1, 3))
    small_got = exchange(small, "y", (1, 3))
    o_got = exchange(o_part, "y", (1, 3))

    def joined(w, got, twin):
        return jnp.concatenate([w, got, twin], axis=0)

    spread = lax.all_gather(piece_got[:-16], ("x", "z", "c"), axis=0)
    thirds_d = ints(*thirds(D))
    thirds_c = ints(*thirds(3 * D), *thirds(D))
    sinus_table = sinusoid(KEYS, D).astype(bf16)
    sinus_rel = jnp.concatenate(
        [
            lax.dynamic_slice_in_dim(sinus_table, thirds_d[i], width, 1)
            for i, width in enumerate(THIRDS)
        ],
        axis=1,
    )
    line.hold(sinus_rel)
    vectors, b_in = unpack(piece, piece_got, ints(yl))

    normed, normed_rel, oldest, old_quarters = first_norm(compressed, memory, tokens, vectors, thirds_d)
    conv_part = half_rows(conv_w, ints(core))
    both_normed, both_cot = both(normed), both(cotangent)
    own, first, far, second = quarters(place["x"], core)
    got = exchange(
        jnp.stack([pick(old_quarters, first, 0), pick(old_quarters, far, 0)]), "x", (1, 3)
    )
    got_far = exchange(jnp.stack([pick(old_quarters, second, 0), got[1]]), "x", (3, 1))
    old_ring = jnp.concatenate([pick(old_quarters, own, 0), got[0], got_far[0], got_far[1]])
    old_twin = core_swap(old_ring)
    kv_got, small_got = gate((kv_got, small_got), normed, conv_part)
    kv_twin, small_twin = core_swap(kv_got), core_swap(small_got)
    kv_whole = joined(w_kv, kv_got, kv_twin)
    q_whole, r_whole = [
        joined(w, small_got[i], small_twin[i]) for i, w in enumerate((w_q, w_r))
    ]
    key_value = dot(normed_rel, kv_whole).astype(bf16)
    line.hold(key_value)
    queries = dot(normed_rel[2 * T :], q_whole)
    relative = dot(sinus_rel, r_whole).astype(bf16)
    (o_got,) = gate((o_got,), key_value, queries, relative)
    o_whole = joined(w_o, o_got, core_swap(o_got))
    line.hold(queries, relative)
    line.hold(got)
    probs, attended = attend(queries, key_value, relative, vectors, none)
    line.hold(both_normed[1], both_cot[1], got_far)
    residual, normed2, normed2_rel = out_and_norm(attended, o_whole, tokens, vectors, thirds_d)
    both_n2, both_att = both(normed2), both(attended)

    cuts, rels, twins = [], [], []
    for ring in ("x", "z"):
        own, first, far, second = quarters(place[ring], core)
        cuts += [first, far, own, second]
        rels.append([own, first, second, far])
        twins.append([own, second, first, far])
    cuts = ints(core, *cuts, yl)

    def flows(groups):
        pairs = weight_grads(groups, cuts)
        return [Flow(ring, pair) for (ring, _), pair in zip(groups, pairs)]

    def start(some):
        for f in some:
            f.start()

    line.hold(old_twin)
    hidden, d_pre, mixed_out, d_normed2, d_b_in = feed_forward(
        normed2_rel, residual, cotangent, w_in, w_out, spread, b_in, vectors, ints(yl)
    )
    both_hidden, both_pre = both(hidden), both(d_pre)
    conv_got = exchange(conv_part, "y", (1, 3))
    d_residual, d_branch, d_attended, d_ln2_g, d_ln2_b, d_b_out = second_norm_back(
        cotangent, d_normed2, residual, vectors, o_whole, thirds_d
    )
    both_branch = both(d_branch)
    large = flows(
        [
            ("x", [(both_hidden, 0, T, both_cot, False)]),
            ("z", [(both_n2, 0, T, both_pre, False), (both_att, 0, T, both_branch, False)]),
        ]
    )
    start(large)
    line.hold(conv_got)
    conv_pieces = (conv_w, conv_got, core_swap(conv_got))
    d_kv, my_kv, give_kv, d_relative, d_queries, d_bias_u, d_bias_v = attend_back(
        queries, key_value, relative, vectors, probs, d_attended, ints(core)
    )
    both_kv = (my_kv, core_swap(give_kv))
    both_q, both_rel = both(d_queries), both(d_relative)

    compact, comp_normed = compress(oldest, conv_pieces, vectors, thirds_c)
    comp_pair = dot(comp_normed, kv_whole).astype(bf16)
    compressed_next = jnp.concatenate([compressed[T // 3 :], compact], axis=0)
    near = flows(
        [
            ("x", [(both_normed, 0, KEYS, both_kv, True)]),
            (
                "z",
                [
                    (both_normed, 2, T, both_q, False),
                    ((sinus_table,), 0, KEYS, both_rel, False),
                ],
            ),
        ]
    )
    onward(large, cuts)
    loss, d_ck, d_cv = reconstruct(queries, key_value, comp_pair, none)
    recon_loss = jnp.sum(loss) / (T * D)
    d_compact, d_conv_b = compress_back(d_ck, d_cv, kv_whole, compact, vectors, thirds_d)
    turn(large, cuts)
    ring_got = exchange(d_compact, "x", (1, 3))
    d_tokens, d_ln1_g, d_ln1_b = first_norm_back(
        d_kv, d_queries, kv_whole, q_whole, compressed, memory, tokens, vectors, d_residual,
        thirds_d,
    )
    sends = gate([f.send for f in near], ring_got, d_ln1_g, *[f.got for f in large])
    for f, send in zip(near, sends):
        f.send = send
    start(near)
    line.hold(*sends)
    onward(large, cuts)
    ring_pair = jnp.concatenate([d_compact, ring_got])
    pair_got = exchange(ring_pair, "x", (3, 1))
    onward(near, cuts)
    early = Finish(large, [], cuts)
    early.second(none)
    line.hold(pair_got)
    early_sums = early.gather(none)
    compact_ring = jnp.concatenate([ring_pair, pair_got])
    compact_twin = core_swap(compact_ring)
    conv = Flow("x", None, conv_grad(old_ring, old_twin, compact_ring, compact_twin, cuts))
    late_flows = [*near, conv]
    turn(late_flows, cuts)
    onward(late_flows, cuts)

    total = jnp.concatenate(
        [d_ln1_g, d_ln1_b, d_bias_u, d_bias_v, d_ln2_g, d_ln2_b, d_b_out, d_conv_b]
        + [d_b_in]
    )
    total = jnp.concatenate(
        [
            total[:8].reshape(8, 2, STEP).transpose(1, 0, 2),
            total[8:].reshape(2, 4, STEP),
            jnp.zeros((2, 4, STEP), f32),
        ],
        axis=1,
    )
    late = Finish(late_flows, [total], cuts)
    late.second(none)
    late_sums = late.gather(none, early_sums)

    g_out, g_in, g_o = widen(
        early_sums, [(FF // 2, D, "x"), (D // 2, FF, "z"), (D // 2, D, "z")], none
    )
    g_kv, g_q, g_r, g_conv = widen(
        late_sums,
        [(D // 2, 2 * D, "x"), (D // 2, D, "z"), (D // 2, D, "z"), (3 * D // 2, D, "x")],
        none,
    )
    half = jnp.sum(late_sums[:, 224:236].astype(f32), axis=0)
    t_ln1_g, t_ln1_b, t_bu, t_bv, t_ln2_g, t_ln2_b, t_bout, t_convb = [half[i] for i in range(8)]
    t_bin = half[8:].reshape(-1)
    return (
        mixed_out[None],
        compressed_next[None],
        recon_loss[None],
        d_tokens[None],
        t_ln1_g,
        t_ln1_b,
        g_q,
        g_kv,
        g_r,
        t_bu,
        t_bv,
        g_o,
        t_ln2_g,
        t_ln2_b,
        g_in,
        t_bin,
        g_out,
        t_bout,
        g_conv,
        t_convb,
    )


def solution(mesh):
    fine = Mesh(mesh.devices.reshape(2, 4, 4, 2, 2), AXES)
    stream = P(AXES, None, None)
    vec, mat = P("yl"), P("yl", None)
    weights = (vec, vec, mat, mat, mat, vec, vec, mat, vec, vec, mat, vec, mat, vec, mat, vec)
    return jax.shard_map(
        per_device,
        mesh=fine,
        in_specs=(stream,) * 4 + weights,
        out_specs=(stream, stream, P(AXES), stream) + weights,
        check_vma=False,
    )
```

```python
import jax
import jax.numpy as jnp
from jax import lax
from jax.experimental import pallas as pl
from jax.experimental.pallas import tpu as pltpu
from jax.sharding import Mesh, PartitionSpec as P

H = 8
HD = 128
D = 1024
T = 192
KEYS = 576
PAD = 640
FF = 4096
FACTOR = HD ** (-0.5)
f32 = jnp.float32
bf16 = jnp.bfloat16
AXES = ("yh", "x", "z", "c", "yl")
RING = {"x": ("x", "c"), "z": ("z", "c"), "y": ("yh", "c", "yl")}


def sinusoid(key_count, model_dim):
    distance = (key_count - 1 - jnp.arange(key_count)).astype(f32)
    inverse = 1.0 / 10000.0 ** (jnp.arange(0, model_dim, 2).astype(f32) / model_dim)
    angles = distance[:, None] * inverse[None, :]
    return jnp.concatenate([jnp.sin(angles), jnp.cos(angles)], axis=-1)


def dot(a, b):
    return jnp.dot(a, b, preferred_element_type=f32)


def dot_t(a, b):
    return lax.dot_general(a, b, (((1,), (1,)), ((), ())), preferred_element_type=f32)


def t_dot(a, b):
    return lax.dot_general(a, b, (((0,), (0,)), ((), ())), preferred_element_type=f32)


class Line:
    def __init__(self):
        self.held, self.due = [], {}

    def hold(self, *values):
        self.held += values

    def expect(self, gap, *values):
        self.due.setdefault(gap, []).extend(values)

    def ran(self, result):
        self.held = [result, *self.due.get(1, [])]
        self.due = {gap - 1: values for gap, values in self.due.items() if gap > 1}

    def later(self, value):
        return lax.optimization_barrier((value, *self.held))[0] if self.held else value


line = Line()


def call(kernel, out, grid, in_specs, out_specs, scalars, args, scratch=()):
    held, n = line.held, len(args)

    def body(s, *refs):
        kernel(s, *refs[:n], *refs[n + len(held) :])

    result = pl.pallas_call(
        body,
        out_shape=out,
        grid_spec=pltpu.PrefetchScalarGridSpec(
            num_scalar_prefetch=1,
            grid=grid,
            in_specs=list(in_specs) + [pl.BlockSpec(memory_space=pl.ANY)] * len(held),
            out_specs=out_specs,
            scratch_shapes=list(scratch),
        ),
        compiler_params=pltpu.CompilerParams(vmem_limit_bytes=56 << 20),
    )(scalars, *args, *held)
    line.ran(jax.tree.leaves(result)[0])
    return result


def gate(values, *after):
    n = len(values)
    anywhere = pl.BlockSpec(memory_space=pl.ANY)
    return pl.pallas_call(
        lambda *refs: None,
        out_shape=[jax.ShapeDtypeStruct(v.shape, v.dtype) for v in values],
        in_specs=[anywhere] * (n + len(after)),
        out_specs=[anywhere] * n,
        input_output_aliases={i: i for i in range(n)},
    )(*values, *after)


def whole(a):
    zeros = (0,) * a.ndim
    return pl.BlockSpec(a.shape, lambda *_: zeros)


def shape(dims, dtype):
    return jax.ShapeDtypeStruct(dims, dtype)


def at(offset):
    return pl.multiple_of(offset, 128)


def center_scale(v):
    mid = v - jnp.mean(v, axis=-1, keepdims=True)
    r = lax.rsqrt(jnp.mean(mid * mid, axis=-1, keepdims=True) + 1e-5)
    return mid * r, r


def norm_back(xhat, r, g, dn):
    gd = dn * g
    return r * (
        gd
        - jnp.mean(gd, axis=-1, keepdims=True)
        - xhat * jnp.mean(gd * xhat, axis=-1, keepdims=True)
    )


def softmax(s):
    e = jnp.exp(s - jnp.max(s, axis=-1, keepdims=True))
    return e / jnp.sum(e, axis=-1, keepdims=True)


(LN1_G, LN1_B, BIAS_U, BIAS_V, LN2_G, LN2_B, B_OUT, CONV_B) = range(8)


def row(ref, i):
    return ref[i : i + 1, :]


def pack(vectors, w_in, w_out, scalars):
    n_in, n_out = (w.shape[0] // 32 for w in (w_in, w_out))
    chunks = FF // D
    rows = n_out + n_in * chunks
    half = D // 2

    def kernel(_, *refs):
        wi, wo, piece, flat = refs[-4:]
        flat[...] = jnp.zeros_like(flat)
        for i, ref in enumerate(refs[:8]):
            flat[i : i + 1, :half] = ref[...].astype(f32).reshape(1, half)
        flat[8 : 8 + FF // 2 // D, :] = refs[8][...].astype(f32).reshape(FF // 2 // D, D)
        piece[:n_out, :] = wo[...]
        for i in range(chunks):
            piece[n_out + i * n_in : n_out + (i + 1) * n_in, :] = wi[:, i * D : (i + 1) * D]
        piece[rows:, :] = flat[...].astype(bf16)

    out = shape((rows + 16, D), bf16)
    return call(
        kernel,
        out,
        (1,),
        [whole(v) for v in vectors]
        + [
            pl.BlockSpec((w.shape[0] // 32, w.shape[1]), lambda j, s: (s[0], 0))
            for w in (w_in, w_out)
        ],
        whole(out),
        scalars,
        (*vectors, w_in, w_out),
        [pltpu.VMEM((16, D), f32)],
    )


def half_rows(w, scalars):
    n = w.shape[0] // 2

    def kernel(_, w, out):
        out[...] = w[...]

    out = shape((n, w.shape[1]), w.dtype)
    spec = pl.BlockSpec((n, w.shape[1]), lambda j, s: (s[0], 0))
    return call(kernel, out, (1,), [spec], whole(out), scalars, (w,))


def pack_rows(w_kv, w_q, w_r, w_o, scalars):
    n = w_q.shape[0] // 2

    def kernel(_, kv, q, r, o, kv_out, out, o_out):
        kv_out[...] = kv[...]
        out[0] = q[...]
        out[1] = r[...]
        o_out[...] = o[...]

    args = (w_kv, w_q, w_r, w_o)
    out = (shape((n, 2 * D), bf16), shape((2, n, D), bf16), shape((n, D), bf16))
    return call(
        kernel,
        out,
        (1,),
        [pl.BlockSpec((w.shape[0] // 2, w.shape[1]), lambda j, s: (s[0], 0)) for w in args],
        [whole(o) for o in out],
        scalars,
        args,
    )


def unpack(mine, theirs, scalars):
    half = D // 2
    at_row = mine.shape[0] // 16 - 1
    tail = pl.BlockSpec((16, D), lambda j, s: (at_row, 0))

    def kernel(s, mine, theirs, vectors, b_in):
        a, b = mine[...].astype(f32), theirs[...].astype(f32)
        low = jnp.where(s[0] == 0, a, b)
        high = jnp.where(s[0] == 0, b, a)
        vectors[:, :half] = low[:8, :half]
        vectors[:, half:] = high[:8, :half]
        rows = FF // 2 // D
        b_in[:rows] = low[8 : 8 + rows]
        b_in[rows:] = high[8 : 8 + rows]

    out = (shape((8, D), f32), shape((FF // D, D), f32))
    return call(
        kernel, out, (1,), [tail, tail], [whole(o) for o in out], scalars, (mine, theirs)
    )


def relative_columns(x, s, widths):
    parts = [x[:, pl.ds(at(s[i]), width)] for i, width in enumerate(widths)]
    return jnp.concatenate(parts, axis=1)


def natural_columns(out, x, s, widths):
    start = 0
    for i, width in enumerate(widths):
        out[:, pl.ds(at(s[i]), width)] = x[:, start : start + width]
        start += width


THIRDS = (D // 2, D // 4, D // 4)


def first_norm(compressed, memory, tokens, vectors, offsets):
    def kernel(s, comp, mem, tok, vec, out, out_rel, old, old_quarters):
        gain, bias = row(vec, LN1_G), row(vec, LN1_B)

        def part(ref, base):
            for i in range(0, T, 32):
                xhat, r = center_scale(ref[i : i + 32, :].astype(f32))
                out[base + i : base + i + 32, :] = (xhat * gain + bias).astype(bf16)

        part(comp, 0)
        part(mem, T)
        part(tok, 2 * T)
        out_rel[...] = relative_columns(out, s, THIRDS)
        line_of = lax.broadcasted_iota(jnp.int32, (T // 3, T), 0)
        col = lax.broadcasted_iota(jnp.int32, (T // 3, T), 1)
        low = mem[...].astype(bf16)
        for tap in range(3):
            take = jnp.where(col == 3 * line_of + tap, 1.0, 0.0).astype(bf16)
            old[:, tap * D : (tap + 1) * D] = dot(take, low).astype(bf16)
        width = 3 * D // 8
        for q in range(4):
            for y in range(2):
                begin = y * 3 * D // 2 + q * width
                old_quarters[q, :, y * width : (y + 1) * width] = old[:, begin : begin + width]

    args = (compressed, memory, tokens, vectors)
    out = (
        shape((KEYS, D), bf16),
        shape((KEYS, D), bf16),
        shape((T // 3, 3 * D), bf16),
        shape((4, T // 3, 3 * D // 4), bf16),
    )
    return call(
        kernel, out, (1,), [whole(a) for a in args], [whole(o) for o in out], offsets, args
    )


def head(n, rows, row_block=0, first=0):
    return pl.BlockSpec((rows, n * HD), lambda h, s: (row_block, first // n + h))


def columns_of(n):
    return [slice(i * HD, (i + 1) * HD) for i in range(n)]


def attend(queries, key_value, relative, vectors, none):
    n = 2

    def kernel(_, q, k, v, rel, vec, probs, out):
        pad = jnp.zeros((PAD - KEYS, HD), bf16)
        i = lax.broadcasted_iota(jnp.int32, (T, PAD), 0)
        j = lax.broadcasted_iota(jnp.int32, (T, PAD), 1)
        seen = j <= i + (KEYS - T)
        cuts = columns_of(n)
        content = [((q[:, c] + vec[BIAS_U : BIAS_U + 1, c]) * FACTOR).astype(bf16) for c in cuts]
        located = [((q[:, c] + vec[BIAS_V : BIAS_V + 1, c]) * FACTOR).astype(bf16) for c in cuts]
        raw = [
            dot_t(x, jnp.concatenate([rel[:, c], pad], axis=0)) for x, c in zip(located, cuts)
        ]
        near = [dot_t(x, jnp.concatenate([k[:, c], pad], axis=0)) for x, c in zip(content, cuts)]
        raw = [pltpu.roll(x, PAD - T + 1, 1, stride=1, stride_axis=0) for x in raw]
        p = [softmax(jnp.where(seen, a + b, -1e30)) for a, b in zip(near, raw)]
        for h, c in enumerate(cuts):
            probs[h] = p[h]
            value = jnp.concatenate([v[:, c], pad], axis=0)
            out[:, c] = dot(p[h].astype(bf16), value).astype(bf16)

    return call(
        kernel,
        (shape((H, T, PAD), f32), shape((T, D), bf16)),
        (H // n,),
        [head(n, T), head(n, KEYS), head(n, KEYS, 0, H), head(n, KEYS), head(n, 8)],
        [pl.BlockSpec((n, T, PAD), lambda h, s: (h, 0, 0)), head(n, T)],
        none,
        (queries, key_value, key_value, relative, vectors),
    )


def attend_back(queries, key_value, relative, vectors, probs, d_attended, scalars):
    n = 2

    def kernel(s, q, k, v, rel, vec, probs, d_att, d_kv, mine, give, d_rel, d_q, d_bu, d_bv):
        pad = jnp.zeros((PAD - KEYS, HD), bf16)
        i = lax.broadcasted_iota(jnp.int32, (T, T), 0)
        j = lax.broadcasted_iota(jnp.int32, (T, T), 1)
        flip = jnp.where(i + j == T - 1, 1.0, 0.0).astype(bf16)
        cuts = columns_of(n)
        content = [((q[:, c] + vec[BIAS_U : BIAS_U + 1, c]) * FACTOR).astype(bf16) for c in cuts]
        located = [((q[:, c] + vec[BIAS_V : BIAS_V + 1, c]) * FACTOR).astype(bf16) for c in cuts]
        da = [d_att[:, c] for c in cuts]
        d_p = [dot_t(x, jnp.concatenate([v[:, c], pad], axis=0)) for x, c in zip(da, cuts)]
        d_v = [t_dot(probs[h].astype(bf16), x)[:KEYS].astype(bf16) for h, x in enumerate(da)]
        d_s = []
        for h, x in enumerate(d_p):
            p = probs[h]
            d_s.append((p * (x - jnp.sum(p * x, axis=-1, keepdims=True))).astype(bf16))
        d_raw = [dot(flip, x) for x in d_s]
        d_c = [
            dot(x, jnp.concatenate([k[:, c], pad], axis=0)) * FACTOR for x, c in zip(d_s, cuts)
        ]
        d_k = [t_dot(x, y)[:KEYS].astype(bf16) for x, y in zip(d_s, content)]
        d_raw = [pltpu.roll(x, 0, 1, stride=1, stride_axis=0).astype(bf16) for x in d_raw]
        d_raw = [dot(flip, x).astype(bf16) for x in d_raw]
        d_l = [
            dot(x, jnp.concatenate([rel[:, c], pad], axis=0)) * FACTOR for x, c in zip(d_raw, cuts)
        ]
        for h, c in enumerate(cuts):
            d_rel[:, c] = t_dot(d_raw[h], located[h])[:KEYS].astype(bf16)
            d_kv[0, :, c] = d_k[h]
            d_kv[1, :, c] = d_v[h]
            mine[:, c] = jnp.where(s[0] == 0, d_k[h], d_v[h])
            give[:, c] = jnp.where(s[0] == 0, d_v[h], d_k[h])
            d_q[:, c] = (d_c[h] + d_l[h]).astype(bf16)
            d_bu[:, c] = jnp.sum(d_c[h], axis=0, keepdims=True)
            d_bv[:, c] = jnp.sum(d_l[h], axis=0, keepdims=True)

    return call(
        kernel,
        (shape((2, KEYS, D), bf16),)
        + (shape((KEYS, D), bf16),) * 3
        + (shape((T, D), bf16), shape((1, D), f32), shape((1, D), f32)),
        (H // n,),
        [
            head(n, T),
            head(n, KEYS),
            head(n, KEYS, 0, H),
            head(n, KEYS),
            head(n, 8),
            pl.BlockSpec((n, T, PAD), lambda h, s: (h, 0, 0)),
            head(n, T),
        ],
        [
            pl.BlockSpec((2, KEYS, n * HD), lambda h, s: (0, 0, h)),
            head(n, KEYS),
            head(n, KEYS),
            head(n, KEYS),
            head(n, T),
            head(n, 1),
            head(n, 1),
        ],
        scalars,
        (queries, key_value, key_value, relative, vectors, probs, d_attended),
    )


def out_and_norm(attended, w_o, tokens, vectors, offsets):
    def kernel(s, att, w, tok, vec, res, n2, n2_rel):
        total = tok[...].astype(f32) + dot(relative_columns(att, s, THIRDS), w[...])
        res[...] = total
        xhat, r = center_scale(total)
        n2[...] = (xhat * row(vec, LN2_G) + row(vec, LN2_B)).astype(bf16)
        other = at(D // 2 - s[0])
        n2_rel[:, : D // 2] = n2[:, pl.ds(at(s[0]), D // 2)]
        n2_rel[:, D // 2 :] = n2[:, pl.ds(other, D // 2)]

    args = (attended, w_o, tokens, vectors)
    out = (shape((T, D), f32), shape((T, D), bf16), shape((T, D), bf16))
    return call(
        kernel, out, (1,), [whole(a) for a in args], [whole(o) for o in out], offsets, args
    )


STEP = 512
UNITS = 1024
HALF = FF // 2 // UNITS


def feed_forward(n2_rel, residual, cotangent, w_in, w_out, spread, b_in, vectors, scalars):
    n_in = w_in.shape[0] // 32
    n_out = w_out.shape[0] // 32
    skip = n_out // n_in
    per = UNITS // n_out
    K_NORM = 0.7978845608028654

    def natural(j, s):
        return lax.rem(j + s[0] * HALF, 2 * HALF)

    def kernel(s, n2, res, cot, wi0, wi1, wo0, wo1, bi, vec, hid, dpre, mixed, dn2, dbi, acc, back):
        j = pl.program_id(0)
        n = natural(j, s)

        @pl.when(j == 0)
        def _():
            acc[...] = jnp.zeros_like(acc)
            back[...] = jnp.zeros_like(back)

        wo = jnp.where(j < HALF, wo0[...], wo1[...].reshape(UNITS, D))
        win = jnp.concatenate([wi0[...], wi1[...].reshape(D // 2, UNITS)], axis=0)
        pre = dot(n2[...], win) + bi[pl.ds(n, 1), :]
        d_hidden = dot_t(cot[...], wo)
        square = pre * pre
        t = jnp.tanh(K_NORM * pre * (1.0 + 0.044715 * square))
        gate_ = 0.5 * (1.0 + t)
        hidden = (pre * gate_).astype(bf16)
        slope = gate_ + (0.5 * K_NORM) * pre * (1.0 - t * t) * (1.0 + (3 * 0.044715) * square)
        d_pre = (d_hidden * slope).astype(bf16)
        hid[...] = hidden
        dpre[...] = d_pre
        dbi[pl.ds(n, 1), :] = jnp.sum(d_pre.astype(f32), axis=0, keepdims=True)
        acc[...] += dot(hidden, wo)
        back[...] += dot_t(d_pre, win)

        @pl.when(j == 2 * HALF - 1)
        def _():
            mixed[...] = (res[...] + acc[...] + row(vec, B_OUT)).astype(bf16)
            dn2[:, pl.ds(at(s[0] * (D // 2)), D // 2)] = back[:, : D // 2]
            dn2[:, pl.ds(at((1 - s[0]) * (D // 2)), D // 2)] = back[:, D // 2 :]

    out = (
        shape((T, FF), bf16),
        shape((T, FF), bf16),
        shape((T, D), bf16),
        shape((T, D), f32),
        shape((2 * HALF, UNITS), f32),
    )
    by_unit = pl.BlockSpec((T, UNITS), lambda j, s: (0, natural(j, s)))
    return call(
        kernel,
        out,
        (2 * HALF,),
        [
            whole(n2_rel),
            whole(residual),
            whole(cotangent),
            pl.BlockSpec((D // 2, UNITS), lambda j, s: (0, natural(j, s))),
            pl.BlockSpec((32, n_in, UNITS), lambda j, s: (0, skip + natural(j, s), 0)),
            pl.BlockSpec((UNITS, D), lambda j, s: (jnp.minimum(j, HALF - 1), 0)),
            pl.BlockSpec(
                (per, n_out, D), lambda j, s: (jnp.maximum(j - HALF, 0), 0, 0)
            ),
            whole(b_in),
            whole(vectors),
        ],
        [by_unit, by_unit, whole(out[2]), whole(out[3]), whole(out[4])],
        scalars,
        (n2_rel, residual, cotangent, w_in, spread, w_out, spread, b_in, vectors),
        [pltpu.VMEM((T, D), f32), pltpu.VMEM((T, D), f32)],
    )


def second_norm_back(cotangent, d_n2, residual, vectors, w_o, offsets):
    def kernel(s, cot, dn, res, vec, w, d_res, d_br, d_att, dg, db, dbo):
        xhat, r = center_scale(res[...])
        dn, wide = dn[...], cot[...].astype(f32)
        dg[...] = jnp.sum(dn * xhat, axis=0, keepdims=True)
        db[...] = jnp.sum(dn, axis=0, keepdims=True)
        dbo[...] = jnp.sum(wide, axis=0, keepdims=True)
        total = wide + norm_back(xhat, r, row(vec, LN2_G), dn)
        d_res[...] = total
        low = total.astype(bf16)
        d_br[...] = low
        natural_columns(d_att, dot_t(low, w[...]).astype(bf16), s, THIRDS)

    args = (cotangent, d_n2, residual, vectors, w_o)
    out = (
        shape((T, D), f32),
        shape((T, D), bf16),
        shape((T, D), bf16),
        shape((1, D), f32),
        shape((1, D), f32),
        shape((1, D), f32),
    )
    return call(
        kernel, out, (1,), [whole(a) for a in args], [whole(o) for o in out], offsets, args
    )


def first_norm_back(d_kv, d_q, w_kv, w_q, compressed, memory, tokens, vectors, d_res, offsets):
    steps = 4
    wide, slim = 2 * D // steps, D // steps

    def kernel(s, dkv, dq, kw, qw, comp, mem, tok, vec, dres, dtok, dg, db, acc, nat, xh, rs):
        j = pl.program_id(0)

        def product(start):
            value = dot_t(dkv[0], kw[...])
            if start:
                acc[...] = value
            else:
                acc[...] += value
            acc[2 * T :, :] += dot_t(dq[...], qw[...])

        for block, ref in enumerate((comp, mem, tok)):

            @pl.when(j == block)
            def _(block=block, ref=ref):
                product(block == 0)
                for i in range(0, T, 32):
                    xhat, r = center_scale(ref[i : i + 32, :].astype(f32))
                    xh[block * T + i : block * T + i + 32, :] = xhat
                    if block == 2:
                        rs[i : i + 32, :] = jnp.broadcast_to(r, (32, HD))

        @pl.when(j == steps - 1)
        def _():
            product(False)
            natural_columns(nat, acc, s, THIRDS)
            gain = row(vec, LN1_G)
            sum_g = jnp.zeros((8, D), f32)
            sum_b = jnp.zeros((8, D), f32)
            for i in range(0, KEYS, 32):
                dn, xhat = nat[i : i + 32, :], xh[i : i + 32, :]
                both = dn * xhat
                sum_g += (both[:8] + both[8:16]) + (both[16:24] + both[24:])
                sum_b += (dn[:8] + dn[8:16]) + (dn[16:24] + dn[24:])
                if i >= 2 * T:
                    k = i - 2 * T
                    r = rs[k : k + 32, :1]
                    dtok[k : k + 32, :] = dres[k : k + 32, :] + norm_back(xhat, r, gain, dn)
            dg[...] = jnp.sum(sum_g, axis=0, keepdims=True)
            db[...] = jnp.sum(sum_b, axis=0, keepdims=True)

    rest = (compressed, memory, tokens, vectors, d_res)
    out = (shape((T, D), f32), shape((1, D), f32), shape((1, D), f32))
    return call(
        kernel,
        out,
        (steps,),
        [
            pl.BlockSpec((1, KEYS, wide), lambda j, s: (j // (steps // 2), 0, lax.rem(j, steps // 2))),
            pl.BlockSpec((T, slim), lambda j, s: (0, j)),
            pl.BlockSpec((D, wide), lambda j, s: (0, j)),
            pl.BlockSpec((D, slim), lambda j, s: (0, j)),
        ]
        + [whole(a) for a in rest],
        [whole(o) for o in out],
        offsets,
        (d_kv, d_q, w_kv, w_q, *rest),
        [pltpu.VMEM((KEYS, D), f32)] * 3 + [pltpu.VMEM((T, HD), f32)],
    )


def compress(oldest, pieces, vectors, offsets):
    block = 256
    rows = T // 3

    def kernel(s, x, w0, w1, w2, vec, compact, normed, x_rel, natural):
        j = pl.program_id(0)

        @pl.when(j == 0)
        def _():
            x_rel[...] = relative_columns(x, s, (3 * D // 2, 3 * D // 4, 3 * D // 4))

        w = jnp.concatenate([w0[...], w1[...], w2[...]], axis=0)
        here = pl.ds(at(j * block), block)
        compact[:, here] = dot(x_rel[...], w) + vec[CONV_B : CONV_B + 1, here]

        @pl.when(j == D // block - 1)
        def _():
            xhat, r = center_scale(compact[...])
            natural[...] = (xhat * row(vec, LN1_G) + row(vec, LN1_B)).astype(bf16)
            start = 0
            for i, width in enumerate(THIRDS):
                normed[:, start : start + width] = natural[:, pl.ds(at(s[3 + i]), width)]
                start += width

    out = (shape((rows, D), f32), shape((rows, D), bf16))
    return call(
        kernel,
        out,
        (D // block,),
        [whole(oldest)]
        + [pl.BlockSpec((w.shape[0], block), lambda j, s: (0, j)) for w in pieces]
        + [whole(vectors)],
        [whole(o) for o in out],
        offsets,
        (oldest, *pieces, vectors),
        [pltpu.VMEM((rows, 3 * D), bf16), pltpu.VMEM((rows, D), bf16)],
    )


def reconstruct(queries, key_value, comp_pair, none):
    rows = T // 3
    n = 4

    def kernel(_, q, k, v, ck, cv, loss, dck, dcv):
        cuts = columns_of(n)
        asking = [(q[:, c] * FACTOR).astype(bf16) for c in cuts]
        far = [dot_t(x, k[:, c]) for x, c in zip(asking, cuts)]
        near = [dot_t(x, ck[:, c]) for x, c in zip(asking, cuts)]
        p = [softmax(x).astype(bf16) for x in far]
        gp = [softmax(x) for x in near]
        low = [x.astype(bf16) for x in gp]
        miss = [dot(p[h], v[:, c]) - dot(low[h], cv[:, c]) for h, c in enumerate(cuts)]
        total = sum(jnp.sum(x * x, axis=0, keepdims=True) for x in miss)
        d_guess = [((-2.0 / (T * D)) * x).astype(bf16) for x in miss]
        d_gp = [dot_t(x, cv[:, c]) for x, c in zip(d_guess, cuts)]
        d_gs = [
            (x * (y - jnp.sum(x * y, axis=-1, keepdims=True))).astype(bf16)
            for x, y in zip(gp, d_gp)
        ]
        for h, c in enumerate(cuts):
            dcv[:, c] = t_dot(low[h], d_guess[h]).astype(bf16)
            dck[:, c] = t_dot(d_gs[h], asking[h]).astype(bf16)

        @pl.when(pl.program_id(0) == 0)
        def _():
            loss[...] = total

        @pl.when(pl.program_id(0) > 0)
        def _():
            loss[...] += total

    return call(
        kernel,
        (shape((1, HD), f32), shape((rows, D), bf16), shape((rows, D), bf16)),
        (H // n,),
        [head(n, T), head(n, T, 1), head(n, T, 1, H), head(n, rows), head(n, rows, 0, H)],
        [pl.BlockSpec((1, HD), lambda h, s: (0, 0)), head(n, rows), head(n, rows)],
        none,
        (queries, key_value, key_value, comp_pair, comp_pair),
    )


def compress_back(dck, dcv, w_kv, compact, vectors, offsets):
    rows = T // 3

    def kernel(s, dck, dcv, w, compact, vec, d_compact, d_bias, dn):
        back = dot_t(jnp.concatenate([dck[...], dcv[...]], axis=1), w[...])
        natural_columns(dn, back, s, THIRDS)
        xhat, r = center_scale(compact[...])
        low = norm_back(xhat, r, row(vec, LN1_G), dn[...]).astype(bf16)
        d_compact[...] = low
        d_bias[...] = jnp.sum(low.astype(f32), axis=0, keepdims=True)

    args = (dck, dcv, w_kv, compact, vectors)
    out = (shape((rows, D), bf16), shape((1, D), f32))
    return call(
        kernel,
        out,
        (1,),
        [whole(a) for a in args],
        [whole(o) for o in out],
        offsets,
        args,
        [pltpu.VMEM((rows, D), f32)],
    )


def weight_grads(groups, scalars):
    in_specs, args, outs, out_specs, layout, scratch = [], [], [], [], [], []
    for ring, jobs in groups:
        first = 1 if ring == "x" else 5
        block = jobs[0][0][0].shape[1] // 8
        plan = []
        for xs, row_block, rows, dys, ready in jobs:
            width = dys[0].shape[1] // (1 if ready else 2)
            plan.append((width, rows, len(xs)))
            for x in xs:
                for y in range(2):
                    in_specs.append(
                        pl.BlockSpec(
                            (rows, block),
                            lambda q, s, r=row_block, f=first, y=y: (r, y * 4 + s[f + q]),
                        )
                    )
                    args.append(x)
            for dy in dys:
                in_specs.append(
                    pl.BlockSpec((rows, width), lambda q, s, r=ready: (0, 0 if r else s[0]))
                )
                args.append(dy)
            scratch.append(pltpu.VMEM((rows * len(xs), width), bf16))
        dims = (1, 2, block, sum(p[0] for p in plan))
        outs += [shape((2, *dims[1:]), bf16)] * 2
        out_specs += [
            pl.BlockSpec(dims, lambda q, s: (jnp.minimum(q, 1), 0, 0, 0)),
            pl.BlockSpec(dims, lambda q, s: (jnp.maximum(q - 2, 0), 0, 0, 0)),
        ]
        layout.append(plan)
    n_in, n_out = len(in_specs), len(outs)

    def kernel(s, *refs):
        ins, results, joined = refs[:n_in], refs[n_in : n_in + n_out], refs[n_in + n_out :]
        q = pl.program_id(0)

        @pl.when(q == 0)
        def _():
            place, k = 0, 0
            for plan in layout:
                for _, rows, n in plan:
                    da, db = ins[place + 2 * n], ins[place + 2 * n + 1]
                    if n == 2:
                        joined[k][:rows, :] = da[...]
                        joined[k][rows:, :] = db[...]
                    else:
                        joined[k][...] = (da[...].astype(f32) + db[...].astype(f32)).astype(bf16)
                    place += 2 * n + 2
                    k += 1

        place, k = 0, 0
        for i, plan in enumerate(layout):
            send, keep = results[2 * i : 2 * i + 2]
            block = send.shape[2]
            start = 0
            for width, rows, n in plan:
                x = jnp.concatenate([r[...] for r in ins[place : place + 2]], axis=1)
                if n == 2:
                    other = jnp.concatenate([r[...] for r in ins[place + 2 : place + 4]], axis=1)
                    x = jnp.concatenate([x, other], axis=0)
                value = t_dot(x, joined[k][...]).astype(bf16).reshape(2, block, width)
                cut = slice(start, start + width)
                send[0, :, :, cut] = jnp.where(q < 2, value, send[0, :, :, cut])
                keep[0, :, :, cut] = value
                start += width
                place += 2 * n + 2
                k += 1

    flat = call(kernel, tuple(outs), (4,), in_specs, out_specs, scalars, args, scratch)
    return [(flat[2 * i], flat[2 * i + 1]) for i in range(len(groups))]


def conv_grad(x, x_twin, dy, dy_twin, scalars):
    rows, columns = x.shape[1] // 2, D // 2

    def kernel(s, xa, xb, da, db, out):
        both = jnp.concatenate([xa[...], xb[...]], axis=0)
        total = t_dot(both, jnp.concatenate([da[...], db[...]], axis=0))
        out[...] = total.reshape(2, rows, columns)

    half = pl.BlockSpec((dy.shape[0], columns), lambda j, s: (0, s[0]))
    out = shape((2, rows, columns), f32)
    return call(
        kernel,
        out,
        (1,),
        [whole(x), whole(x_twin), half, half],
        whole(out),
        scalars,
        (x, x_twin, dy, dy_twin),
    )


def widen(gathered, plan, none):
    outs, specs, layout = [], [], []
    start = 0
    for rows, columns, ring in plan:
        u, chunks = rows // 16, columns // 2 // STEP
        outs.append(shape((4, 4, u, columns), f32))
        if ring == "x":
            specs.append(
                pl.BlockSpec((1, 4, u, chunks * STEP), lambda c, x, s: (x, 0, 0, c))
            )
        else:
            specs.append(
                pl.BlockSpec((4, 1, u, chunks * STEP), lambda c, x, s: (0, x, 0, c))
            )
        layout.append((start, u, chunks, ring))
        start += u * chunks

    def kernel(_, src, *results):
        for out, (start, u, chunks, ring) in zip(results, layout):
            for k in range(chunks):
                cut = slice(k * STEP, (k + 1) * STEP)
                for z in range(4):
                    value = src[z, start + k * u : start + (k + 1) * u, :].astype(f32)
                    if ring == "x":
                        out[0, z, :, cut] = value
                    else:
                        out[z, 0, :, cut] = value

    results = call(
        kernel,
        tuple(outs),
        (2, 4),
        [pl.BlockSpec((4, gathered.shape[1], STEP), lambda c, x, s: (c * 4 + x, 0, 0))],
        specs,
        none,
        (gathered,),
    )
    return [r.reshape(rows, columns) for r, (rows, columns, _) in zip(results, plan)]


def core_swap(v):
    return lax.ppermute(v, "c", [(0, 1), (1, 0)])


def pair_swap(v):
    return lax.ppermute(v, "yl", [(0, 1), (1, 0)])


def exchange(v, ring, masks):
    def flat(i, c):
        return (i // 2 * 2 + c) * 2 + i % 2 if ring == "y" else 2 * i + c

    pairs = [(flat(i, c), flat(i ^ masks[c], c)) for i in range(4) for c in range(2)]
    return lax.ppermute(v, RING[ring], pairs)


def pick(v, index, axis):
    return lax.dynamic_index_in_dim(v, index, axis, keepdims=False)


def quarters(place, core):
    first = jnp.where(core == 0, 1, 3)
    second = jnp.where(core == 0, 3, 1)
    return place, place ^ first, place ^ 2, place ^ second


class Flow:
    def __init__(self, ring, pair, done=None):
        self.ring, self.other = ring, "z" if ring == "x" else "x"
        self.before, self.result = None, done
        if done is None:
            self.send, self.keep = pair

    def start(self):
        self.got = exchange(self.send, self.ring, (1, 3))

    def sources(self):
        return [self.keep, self.got, self.last] if self.result is None else [self.result]

    def kept(self, which):
        if self.before is None:
            dims = (1, 1, *self.keep.shape[2:])
            return [pl.BlockSpec(dims, lambda y, s: (which, y, 0, 0))], [self.keep]
        return self.before(2 + which)


def onward(flows, cuts):
    in_specs, args, counts = [], [], []
    for f in flows:
        specs, arrays = f.kept(1)
        dims = (1, 1, *f.got.shape[2:])
        in_specs += specs + [pl.BlockSpec(dims, lambda y, s: (1, y, 0, 0))]
        args += arrays + [f.got]
        counts.append(len(arrays) + 1)
    out = tuple(shape(f.got.shape[1:], bf16) for f in flows)

    def kernel(_, *refs):
        k = 0
        for i, n in enumerate(counts):
            total = sum(value_of(r) for r in refs[k : k + n])
            refs[len(args) + i][...] = total.astype(bf16)
            k += n

    sums = call(
        kernel,
        out,
        (2,),
        in_specs,
        [pl.BlockSpec((1, *o.shape[1:]), lambda y, s: (y, 0, 0)) for o in out],
        cuts,
        args,
    )
    for f, v in zip(flows, sums):
        f.last = exchange(v, f.ring, (3, 1))


def value_of(ref):
    return (ref[0] if len(ref.shape) == 4 else ref[...]).astype(f32)


def turn(flows, cuts):
    in_specs, outs, out_specs, args = [], [], [], []

    counts = []
    for f in flows:
        first = 1 if f.other == "x" else 5
        arrays = f.sources()
        rows, columns = arrays[0].shape[-2] // 4, arrays[0].shape[-1]
        four = pl.BlockSpec((1, 2, rows, columns), lambda j, s, i=first: (0, 0, s[i + j], 0))
        three = pl.BlockSpec((2, rows, columns), lambda j, s, i=first: (0, s[i + j], 0))
        in_specs += [four if a.ndim == 4 else three for a in arrays]
        args += arrays
        counts.append(len(arrays))
        dims = (1, 2, rows, columns)
        outs.append(shape((2, *dims[1:]), bf16))
        out_specs.append(pl.BlockSpec(dims, lambda j, s: (j, 0, 0, 0)))

    def kernel(_, *refs):
        k = 0
        for i, n in enumerate(counts):
            total = sum(value_of(r) for r in refs[k : k + n])
            refs[len(args) + i][0] = total.astype(bf16)
            k += n

    sends = call(kernel, tuple(outs), (2,), in_specs, out_specs, cuts, args)
    for f, send in zip(flows, sends):
        f.before = halves_of(f)
        f.ring = f.other
        f.got = exchange(send, f.ring, (1, 3))


def halves_of(f):
    arrays = f.sources()
    first = 1 if f.other == "x" else 5
    rows, columns = arrays[0].shape[-2] // 4, arrays[0].shape[-1]

    def quarter(which):
        four = pl.BlockSpec((1, 1, rows, columns), lambda y, s: (0, y, s[first + which], 0))
        three = pl.BlockSpec((1, rows, columns), lambda y, s: (y, s[first + which], 0))
        return [four if a.ndim == 4 else three for a in arrays], arrays

    return quarter


def add(a, b, none):
    def kernel(_, a, b, out):
        out[...] = (a[...].astype(f32) + b[...].astype(f32)).astype(bf16)

    out = shape(a.shape, bf16)
    return call(kernel, out, (1,), [whole(a), whole(b)], whole(out), none, (a, b))


class Finish:
    def __init__(self, flows, extra, cuts):
        in_specs, args, sizes = [], [], []
        def half(spec):
            return pl.BlockSpec(
                spec.block_shape, lambda j, s: spec.index_map(lax.rem(j + s[9], 2), s)
            )

        for f in flows:
            specs, arrays = f.kept(0)
            dims = (1, 1, *f.got.shape[2:])
            specs = specs + [
                pl.BlockSpec(dims, lambda y, s: (0, y, 0, 0)),
                pl.BlockSpec((1, *f.last.shape[1:]), lambda y, s: (y, 0, 0)),
            ]
            in_specs += [half(spec) for spec in specs]
            args += arrays + [f.got, f.last]
            sizes.append((len(arrays) + 2, f.got.shape[2], f.got.shape[3] // STEP))
        for e in extra:
            in_specs.append(half(pl.BlockSpec((1, *e.shape[1:]), lambda y, s: (y, 0, 0))))
        args += extra
        rows = sum(u * n for _, u, n in sizes) + sum(e.shape[1] for e in extra)

        def kernel(_, *refs):
            send, mine = refs[-2:]
            j = pl.program_id(0)

            def put(here, value):
                @pl.when(j == 0)
                def _():
                    mine[here, :] = value

                @pl.when(j == 1)
                def _():
                    send[here, :] = value.astype(bf16)

            start, k = 0, 0
            for count, u, n in sizes:
                v = sum(value_of(r) for r in refs[k : k + count])[0]
                for i in range(n):
                    put(slice(start, start + u), v[:, i * STEP : (i + 1) * STEP])
                    start += u
                k += count
            for ref in refs[k:-2]:
                put(slice(start, start + ref.shape[1]), ref[0])
                start += ref.shape[1]

        out = (shape((rows, STEP), bf16), shape((rows, STEP), f32))
        send, self.mine = call(
            kernel, out, (2,), in_specs, [whole(o) for o in out], cuts, args
        )
        self.got = exchange(send, "y", (1, 3))

    def second(self, none):
        self.mine = add(self.mine, self.got, none)
        self.far = lax.ppermute(self.mine, "yh", [(0, 1), (1, 0)])

    def gather(self, none, *after):
        done = add(self.mine, self.far, none)
        if after:
            (done,) = gate((done,), *after)
            line.hold(done)
        return lax.all_gather(done, ("c", "x", "z"), axis=0)


def per_device(
    tokens,
    memory,
    compressed,
    cotangent,
    ln1_g,
    ln1_b,
    w_q,
    w_kv,
    w_r,
    bias_u,
    bias_v,
    w_o,
    ln2_g,
    ln2_b,
    w_in,
    b_in,
    w_out,
    b_out,
    conv_w,
    conv_b,
):
    line.held, line.due = [], {}
    tokens, memory, compressed, cotangent = tokens[0], memory[0], compressed[0], cotangent[0]
    yl, core = lax.axis_index("yl"), lax.axis_index("c")
    place = {"x": lax.axis_index("x"), "z": lax.axis_index("z")}
    none = jnp.zeros((1,), jnp.int32)
    ints = lambda *v: jnp.stack([jnp.asarray(i, jnp.int32) for i in v])

    def thirds(rows):
        half = rows // 2
        other = (1 - yl) * half
        return [yl * half, other + core * (half // 2), other + (1 - core) * (half // 2)]

    def both(v):
        return (v, core_swap(v))

    spot = (place["x"] * 4 + place["z"]) * 2 + core
    piece = pack(
        (ln1_g, ln1_b, bias_u, bias_v, ln2_g, ln2_b, b_out, conv_b, b_in),
        w_in,
        w_out,
        ints(spot),
    )
    piece_got = exchange(piece, "y", (1, 3))

    kv_part, small, o_part = pack_rows(w_kv, w_q, w_r, w_o, ints(core))
    (piece_got,) = gate((piece_got,), kv_part)
    kv_got = exchange(kv_part, "y", (1, 3))
    small_got = exchange(small, "y", (1, 3))
    o_got = exchange(o_part, "y", (1, 3))

    def joined(w, got, twin):
        return jnp.concatenate([w, got, twin], axis=0)

    spread = lax.all_gather(piece_got[:-16], ("x", "z", "c"), axis=0)
    thirds_d = ints(*thirds(D))
    thirds_c = ints(*thirds(3 * D), *thirds(D))
    sinus_table = sinusoid(KEYS, D).astype(bf16)
    sinus_rel = jnp.concatenate(
        [
            lax.dynamic_slice_in_dim(sinus_table, thirds_d[i], width, 1)
            for i, width in enumerate(THIRDS)
        ],
        axis=1,
    )
    line.hold(sinus_rel)
    vectors, b_in = unpack(piece, piece_got, ints(yl))

    normed, normed_rel, oldest, old_quarters = first_norm(compressed, memory, tokens, vectors, thirds_d)
    conv_part = half_rows(conv_w, ints(core))
    both_normed, both_cot = both(normed), both(cotangent)
    own, first, far, second = quarters(place["x"], core)
    got = exchange(
        jnp.stack([pick(old_quarters, first, 0), pick(old_quarters, far, 0)]), "x", (1, 3)
    )
    got_far = exchange(jnp.stack([pick(old_quarters, second, 0), got[1]]), "x", (3, 1))
    old_ring = jnp.concatenate([pick(old_quarters, own, 0), got[0], got_far[0], got_far[1]])
    old_twin = core_swap(old_ring)
    kv_got, small_got = gate((kv_got, small_got), normed, conv_part)
    kv_twin, small_twin = core_swap(kv_got), core_swap(small_got)
    kv_whole = joined(w_kv, kv_got, kv_twin)
    q_whole, r_whole = [
        joined(w, small_got[i], small_twin[i]) for i, w in enumerate((w_q, w_r))
    ]
    key_value = dot(normed_rel, kv_whole).astype(bf16)
    line.hold(key_value)
    queries = dot(normed_rel[2 * T :], q_whole)
    relative = dot(sinus_rel, r_whole).astype(bf16)
    (o_got,) = gate((o_got,), key_value, queries, relative)
    o_whole = joined(w_o, o_got, core_swap(o_got))
    line.hold(queries, relative)
    line.hold(got)
    probs, attended = attend(queries, key_value, relative, vectors, none)
    line.hold(both_normed[1], both_cot[1], got_far)
    residual, normed2, normed2_rel = out_and_norm(attended, o_whole, tokens, vectors, thirds_d)
    both_n2, both_att = both(normed2), both(attended)

    cuts, rels, twins = [], [], []
    for ring in ("x", "z"):
        own, first, far, second = quarters(place[ring], core)
        cuts += [first, far, own, second]
        rels.append([own, first, second, far])
        twins.append([own, second, first, far])
    cuts = ints(core, *cuts, yl)

    def flows(groups):
        pairs = weight_grads(groups, cuts)
        return [Flow(ring, pair) for (ring, _), pair in zip(groups, pairs)]

    def start(some):
        for f in some:
            f.start()

    line.hold(old_twin)
    hidden, d_pre, mixed_out, d_normed2, d_b_in = feed_forward(
        normed2_rel, residual, cotangent, w_in, w_out, spread, b_in, vectors, ints(yl)
    )
    both_hidden, both_pre = both(hidden), both(d_pre)
    conv_got = exchange(conv_part, "y", (1, 3))
    d_residual, d_branch, d_attended, d_ln2_g, d_ln2_b, d_b_out = second_norm_back(
        cotangent, d_normed2, residual, vectors, o_whole, thirds_d
    )
    both_branch = both(d_branch)
    large = flows(
        [
            ("x", [(both_hidden, 0, T, both_cot, False)]),
            ("z", [(both_n2, 0, T, both_pre, False), (both_att, 0, T, both_branch, False)]),
        ]
    )
    start(large)
    line.hold(conv_got)
    conv_pieces = (conv_w, conv_got, core_swap(conv_got))
    d_kv, my_kv, give_kv, d_relative, d_queries, d_bias_u, d_bias_v = attend_back(
        queries, key_value, relative, vectors, probs, d_attended, ints(core)
    )
    both_kv = (my_kv, core_swap(give_kv))
    both_q, both_rel = both(d_queries), both(d_relative)

    compact, comp_normed = compress(oldest, conv_pieces, vectors, thirds_c)
    comp_pair = dot(comp_normed, kv_whole).astype(bf16)
    compressed_next = jnp.concatenate([compressed[T // 3 :], compact], axis=0)
    near = flows(
        [
            ("x", [(both_normed, 0, KEYS, both_kv, True)]),
            (
                "z",
                [
                    (both_normed, 2, T, both_q, False),
                    ((sinus_table,), 0, KEYS, both_rel, False),
                ],
            ),
        ]
    )
    onward(large, cuts)
    loss, d_ck, d_cv = reconstruct(queries, key_value, comp_pair, none)
    recon_loss = jnp.sum(loss) / (T * D)
    d_compact, d_conv_b = compress_back(d_ck, d_cv, kv_whole, compact, vectors, thirds_d)
    ring_got = exchange(d_compact, "x", (1, 3))
    sends = gate([f.send for f in near], d_compact)
    for f, send in zip(near, sends):
        f.send = send
    start(near)
    line.hold(*sends)
    turn(large, cuts)
    d_tokens, d_ln1_g, d_ln1_b = first_norm_back(
        d_kv, d_queries, kv_whole, q_whole, compressed, memory, tokens, vectors, d_residual,
        thirds_d,
    )
    (ring_got,) = gate((ring_got,), d_ln1_g)
    onward(large, cuts)
    ring_pair = jnp.concatenate([d_compact, ring_got])
    pair_got = exchange(ring_pair, "x", (3, 1))
    compact_ring = jnp.concatenate([ring_pair, pair_got])
    compact_twin = core_swap(compact_ring)
    onward(near, cuts)
    line.expect(1, *[f.last for f in near])
    line.hold(pair_got)
    early = Finish(large, [], cuts)
    conv = Flow("x", None, conv_grad(old_ring, old_twin, compact_ring, compact_twin, cuts))
    early.second(none)
    late_flows = [*near, conv]
    turn(late_flows, cuts)
    early_sums = early.gather(none)
    onward(late_flows, cuts)

    total = jnp.concatenate(
        [d_ln1_g, d_ln1_b, d_bias_u, d_bias_v, d_ln2_g, d_ln2_b, d_b_out, d_conv_b]
        + [d_b_in]
    )
    total = jnp.concatenate(
        [
            total[:8].reshape(8, 2, STEP).transpose(1, 0, 2),
            total[8:].reshape(2, 4, STEP),
            jnp.zeros((2, 4, STEP), f32),
        ],
        axis=1,
    )
    late = Finish(late_flows, [total], cuts)
    late.second(none)
    late_sums = late.gather(none, early_sums)

    g_out, g_in, g_o = widen(
        early_sums, [(FF // 2, D, "x"), (D // 2, FF, "z"), (D // 2, D, "z")], none
    )
    g_kv, g_q, g_r, g_conv = widen(
        late_sums,
        [(D // 2, 2 * D, "x"), (D // 2, D, "z"), (D // 2, D, "z"), (3 * D // 2, D, "x")],
        none,
    )
    half = jnp.sum(late_sums[:, 224:236].astype(f32), axis=0)
    t_ln1_g, t_ln1_b, t_bu, t_bv, t_ln2_g, t_ln2_b, t_bout, t_convb = [half[i] for i in range(8)]
    t_bin = half[8:].reshape(-1)
    return (
        mixed_out[None],
        compressed_next[None],
        recon_loss[None],
        d_tokens[None],
        t_ln1_g,
        t_ln1_b,
        g_q,
        g_kv,
        g_r,
        t_bu,
        t_bv,
        g_o,
        t_ln2_g,
        t_ln2_b,
        g_in,
        t_bin,
        g_out,
        t_bout,
        g_conv,
        t_convb,
    )


def solution(mesh):
    fine = Mesh(mesh.devices.reshape(2, 4, 4, 2, 2), AXES)
    stream = P(AXES, None, None)
    vec, mat = P("yl"), P("yl", None)
    weights = (vec, vec, mat, mat, mat, vec, vec, mat, vec, vec, mat, vec, mat, vec, mat, vec)
    return jax.shard_map(
        per_device,
        mesh=fine,
        in_specs=(stream,) * 4 + weights,
        out_specs=(stream, stream, P(AXES), stream) + weights,
        check_vma=False,
    )
```

```python
import jax
import jax.numpy as jnp
from jax import lax
from jax.experimental import pallas as pl
from jax.experimental.pallas import tpu as pltpu
from jax.sharding import Mesh, PartitionSpec as P

H = 8
HD = 128
D = 1024
T = 192
KEYS = 576
PAD = 640
FF = 4096
FACTOR = HD ** (-0.5)
f32 = jnp.float32
bf16 = jnp.bfloat16
AXES = ("yh", "x", "z", "c", "yl")
RING = {"x": ("x", "c"), "z": ("z", "c"), "y": ("yh", "c", "yl")}


def sinusoid(key_count, model_dim):
    distance = (key_count - 1 - jnp.arange(key_count)).astype(f32)
    inverse = 1.0 / 10000.0 ** (jnp.arange(0, model_dim, 2).astype(f32) / model_dim)
    angles = distance[:, None] * inverse[None, :]
    return jnp.concatenate([jnp.sin(angles), jnp.cos(angles)], axis=-1)


def dot(a, b):
    return jnp.dot(a, b, preferred_element_type=f32)


def dot_t(a, b):
    return lax.dot_general(a, b, (((1,), (1,)), ((), ())), preferred_element_type=f32)


def t_dot(a, b):
    return lax.dot_general(a, b, (((0,), (0,)), ((), ())), preferred_element_type=f32)


class Line:
    def __init__(self):
        self.held, self.due = [], {}

    def hold(self, *values):
        self.held += values

    def expect(self, gap, *values):
        self.due.setdefault(gap, []).extend(values)

    def ran(self, result):
        self.held = [result, *self.due.get(1, [])]
        self.due = {gap - 1: values for gap, values in self.due.items() if gap > 1}

    def later(self, value):
        return lax.optimization_barrier((value, *self.held))[0] if self.held else value


line = Line()


def call(kernel, out, grid, in_specs, out_specs, scalars, args, scratch=()):
    held, n = line.held, len(args)

    def body(s, *refs):
        kernel(s, *refs[:n], *refs[n + len(held) :])

    result = pl.pallas_call(
        body,
        out_shape=out,
        grid_spec=pltpu.PrefetchScalarGridSpec(
            num_scalar_prefetch=1,
            grid=grid,
            in_specs=list(in_specs) + [pl.BlockSpec(memory_space=pl.ANY)] * len(held),
            out_specs=out_specs,
            scratch_shapes=list(scratch),
        ),
        compiler_params=pltpu.CompilerParams(vmem_limit_bytes=56 << 20),
    )(scalars, *args, *held)
    line.ran(jax.tree.leaves(result)[0])
    return result


def gate(values, *after):
    n = len(values)
    anywhere = pl.BlockSpec(memory_space=pl.ANY)
    return pl.pallas_call(
        lambda *refs: None,
        out_shape=[jax.ShapeDtypeStruct(v.shape, v.dtype) for v in values],
        in_specs=[anywhere] * (n + len(after)),
        out_specs=[anywhere] * n,
        input_output_aliases={i: i for i in range(n)},
    )(*values, *after)


def whole(a):
    zeros = (0,) * a.ndim
    return pl.BlockSpec(a.shape, lambda *_: zeros)


def shape(dims, dtype):
    return jax.ShapeDtypeStruct(dims, dtype)


def at(offset):
    return pl.multiple_of(offset, 128)


def center_scale(v):
    mid = v - jnp.mean(v, axis=-1, keepdims=True)
    r = lax.rsqrt(jnp.mean(mid * mid, axis=-1, keepdims=True) + 1e-5)
    return mid * r, r


def norm_back(xhat, r, g, dn):
    gd = dn * g
    return r * (
        gd
        - jnp.mean(gd, axis=-1, keepdims=True)
        - xhat * jnp.mean(gd * xhat, axis=-1, keepdims=True)
    )


def softmax(s):
    e = jnp.exp(s - jnp.max(s, axis=-1, keepdims=True))
    return e / jnp.sum(e, axis=-1, keepdims=True)


(LN1_G, LN1_B, BIAS_U, BIAS_V, LN2_G, LN2_B, B_OUT, CONV_B) = range(8)


def row(ref, i):
    return ref[i : i + 1, :]


def pack(vectors, w_in, w_out, scalars):
    n_in, n_out = (w.shape[0] // 32 for w in (w_in, w_out))
    chunks = FF // D
    rows = n_out + n_in * chunks
    half = D // 2

    def kernel(_, *refs):
        wi, wo, piece, flat = refs[-4:]
        flat[...] = jnp.zeros_like(flat)
        for i, ref in enumerate(refs[:8]):
            flat[i : i + 1, :half] = ref[...].astype(f32).reshape(1, half)
        flat[8 : 8 + FF // 2 // D, :] = refs[8][...].astype(f32).reshape(FF // 2 // D, D)
        piece[:n_out, :] = wo[...]
        for i in range(chunks):
            piece[n_out + i * n_in : n_out + (i + 1) * n_in, :] = wi[:, i * D : (i + 1) * D]
        piece[rows:, :] = flat[...].astype(bf16)

    out = shape((rows + 16, D), bf16)
    return call(
        kernel,
        out,
        (1,),
        [whole(v) for v in vectors]
        + [
            pl.BlockSpec((w.shape[0] // 32, w.shape[1]), lambda j, s: (s[0], 0))
            for w in (w_in, w_out)
        ],
        whole(out),
        scalars,
        (*vectors, w_in, w_out),
        [pltpu.VMEM((16, D), f32)],
    )


def half_rows(w, scalars):
    n = w.shape[0] // 2

    def kernel(_, w, out):
        out[...] = w[...]

    out = shape((n, w.shape[1]), w.dtype)
    spec = pl.BlockSpec((n, w.shape[1]), lambda j, s: (s[0], 0))
    return call(kernel, out, (1,), [spec], whole(out), scalars, (w,))


def pack_rows(w_kv, w_q, w_r, w_o, scalars):
    n = w_q.shape[0] // 2

    def kernel(_, kv, q, r, o, kv_out, out, o_out):
        kv_out[...] = kv[...]
        out[0] = q[...]
        out[1] = r[...]
        o_out[...] = o[...]

    args = (w_kv, w_q, w_r, w_o)
    out = (shape((n, 2 * D), bf16), shape((2, n, D), bf16), shape((n, D), bf16))
    return call(
        kernel,
        out,
        (1,),
        [pl.BlockSpec((w.shape[0] // 2, w.shape[1]), lambda j, s: (s[0], 0)) for w in args],
        [whole(o) for o in out],
        scalars,
        args,
    )


def unpack(mine, theirs, scalars):
    half = D // 2
    at_row = mine.shape[0] // 16 - 1
    tail = pl.BlockSpec((16, D), lambda j, s: (at_row, 0))

    def kernel(s, mine, theirs, vectors, b_in):
        a, b = mine[...].astype(f32), theirs[...].astype(f32)
        low = jnp.where(s[0] == 0, a, b)
        high = jnp.where(s[0] == 0, b, a)
        vectors[:, :half] = low[:8, :half]
        vectors[:, half:] = high[:8, :half]
        rows = FF // 2 // D
        b_in[:rows] = low[8 : 8 + rows]
        b_in[rows:] = high[8 : 8 + rows]

    out = (shape((8, D), f32), shape((FF // D, D), f32))
    return call(
        kernel, out, (1,), [tail, tail], [whole(o) for o in out], scalars, (mine, theirs)
    )


def relative_columns(x, s, widths):
    parts = [x[:, pl.ds(at(s[i]), width)] for i, width in enumerate(widths)]
    return jnp.concatenate(parts, axis=1)


def natural_columns(out, x, s, widths):
    start = 0
    for i, width in enumerate(widths):
        out[:, pl.ds(at(s[i]), width)] = x[:, start : start + width]
        start += width


THIRDS = (D // 2, D // 4, D // 4)


def first_norm(compressed, memory, tokens, vectors, offsets):
    def kernel(s, comp, mem, tok, vec, out, out_rel, old, old_quarters):
        gain, bias = row(vec, LN1_G), row(vec, LN1_B)

        def part(ref, base):
            for i in range(0, T, 32):
                xhat, r = center_scale(ref[i : i + 32, :].astype(f32))
                out[base + i : base + i + 32, :] = (xhat * gain + bias).astype(bf16)

        part(comp, 0)
        part(mem, T)
        part(tok, 2 * T)
        out_rel[...] = relative_columns(out, s, THIRDS)
        line_of = lax.broadcasted_iota(jnp.int32, (T // 3, T), 0)
        col = lax.broadcasted_iota(jnp.int32, (T // 3, T), 1)
        low = mem[...].astype(bf16)
        for tap in range(3):
            take = jnp.where(col == 3 * line_of + tap, 1.0, 0.0).astype(bf16)
            old[:, tap * D : (tap + 1) * D] = dot(take, low).astype(bf16)
        width = 3 * D // 8
        for q in range(4):
            for y in range(2):
                begin = y * 3 * D // 2 + q * width
                old_quarters[q, :, y * width : (y + 1) * width] = old[:, begin : begin + width]

    args = (compressed, memory, tokens, vectors)
    out = (
        shape((KEYS, D), bf16),
        shape((KEYS, D), bf16),
        shape((T // 3, 3 * D), bf16),
        shape((4, T // 3, 3 * D // 4), bf16),
    )
    return call(
        kernel, out, (1,), [whole(a) for a in args], [whole(o) for o in out], offsets, args
    )


def head(n, rows, row_block=0, first=0):
    return pl.BlockSpec((rows, n * HD), lambda h, s: (row_block, first // n + h))


def columns_of(n):
    return [slice(i * HD, (i + 1) * HD) for i in range(n)]


def attend(queries, key_value, relative, vectors, none):
    n = 2

    def kernel(_, q, k, v, rel, vec, probs, out):
        pad = jnp.zeros((PAD - KEYS, HD), bf16)
        i = lax.broadcasted_iota(jnp.int32, (T, PAD), 0)
        j = lax.broadcasted_iota(jnp.int32, (T, PAD), 1)
        seen = j <= i + (KEYS - T)
        cuts = columns_of(n)
        content = [((q[:, c] + vec[BIAS_U : BIAS_U + 1, c]) * FACTOR).astype(bf16) for c in cuts]
        located = [((q[:, c] + vec[BIAS_V : BIAS_V + 1, c]) * FACTOR).astype(bf16) for c in cuts]
        raw = [
            dot_t(x, jnp.concatenate([rel[:, c], pad], axis=0)) for x, c in zip(located, cuts)
        ]
        near = [dot_t(x, jnp.concatenate([k[:, c], pad], axis=0)) for x, c in zip(content, cuts)]
        raw = [pltpu.roll(x, PAD - T + 1, 1, stride=1, stride_axis=0) for x in raw]
        p = [softmax(jnp.where(seen, a + b, -1e30)) for a, b in zip(near, raw)]
        for h, c in enumerate(cuts):
            probs[h] = p[h]
            value = jnp.concatenate([v[:, c], pad], axis=0)
            out[:, c] = dot(p[h].astype(bf16), value).astype(bf16)

    return call(
        kernel,
        (shape((H, T, PAD), f32), shape((T, D), bf16)),
        (H // n,),
        [head(n, T), head(n, KEYS), head(n, KEYS, 0, H), head(n, KEYS), head(n, 8)],
        [pl.BlockSpec((n, T, PAD), lambda h, s: (h, 0, 0)), head(n, T)],
        none,
        (queries, key_value, key_value, relative, vectors),
    )


def attend_back(queries, key_value, relative, vectors, probs, d_attended, scalars):
    n = 2

    def kernel(s, q, k, v, rel, vec, probs, d_att, d_kv, mine, give, d_rel, d_q, d_bu, d_bv):
        pad = jnp.zeros((PAD - KEYS, HD), bf16)
        i = lax.broadcasted_iota(jnp.int32, (T, T), 0)
        j = lax.broadcasted_iota(jnp.int32, (T, T), 1)
        flip = jnp.where(i + j == T - 1, 1.0, 0.0).astype(bf16)
        cuts = columns_of(n)
        content = [((q[:, c] + vec[BIAS_U : BIAS_U + 1, c]) * FACTOR).astype(bf16) for c in cuts]
        located = [((q[:, c] + vec[BIAS_V : BIAS_V + 1, c]) * FACTOR).astype(bf16) for c in cuts]
        da = [d_att[:, c] for c in cuts]
        d_p = [dot_t(x, jnp.concatenate([v[:, c], pad], axis=0)) for x, c in zip(da, cuts)]
        d_v = [t_dot(probs[h].astype(bf16), x)[:KEYS].astype(bf16) for h, x in enumerate(da)]
        d_s = []
        for h, x in enumerate(d_p):
            p = probs[h]
            d_s.append((p * (x - jnp.sum(p * x, axis=-1, keepdims=True))).astype(bf16))
        d_raw = [dot(flip, x) for x in d_s]
        d_c = [
            dot(x, jnp.concatenate([k[:, c], pad], axis=0)) * FACTOR for x, c in zip(d_s, cuts)
        ]
        d_k = [t_dot(x, y)[:KEYS].astype(bf16) for x, y in zip(d_s, content)]
        d_raw = [pltpu.roll(x, 0, 1, stride=1, stride_axis=0).astype(bf16) for x in d_raw]
        d_raw = [dot(flip, x).astype(bf16) for x in d_raw]
        d_l = [
            dot(x, jnp.concatenate([rel[:, c], pad], axis=0)) * FACTOR for x, c in zip(d_raw, cuts)
        ]
        for h, c in enumerate(cuts):
            d_rel[:, c] = t_dot(d_raw[h], located[h])[:KEYS].astype(bf16)
            d_kv[0, :, c] = d_k[h]
            d_kv[1, :, c] = d_v[h]
            mine[:, c] = jnp.where(s[0] == 0, d_k[h], d_v[h])
            give[:, c] = jnp.where(s[0] == 0, d_v[h], d_k[h])
            d_q[:, c] = (d_c[h] + d_l[h]).astype(bf16)
            d_bu[:, c] = jnp.sum(d_c[h], axis=0, keepdims=True)
            d_bv[:, c] = jnp.sum(d_l[h], axis=0, keepdims=True)

    return call(
        kernel,
        (shape((2, KEYS, D), bf16),)
        + (shape((KEYS, D), bf16),) * 3
        + (shape((T, D), bf16), shape((1, D), f32), shape((1, D), f32)),
        (H // n,),
        [
            head(n, T),
            head(n, KEYS),
            head(n, KEYS, 0, H),
            head(n, KEYS),
            head(n, 8),
            pl.BlockSpec((n, T, PAD), lambda h, s: (h, 0, 0)),
            head(n, T),
        ],
        [
            pl.BlockSpec((2, KEYS, n * HD), lambda h, s: (0, 0, h)),
            head(n, KEYS),
            head(n, KEYS),
            head(n, KEYS),
            head(n, T),
            head(n, 1),
            head(n, 1),
        ],
        scalars,
        (queries, key_value, key_value, relative, vectors, probs, d_attended),
    )


def out_and_norm(attended, w_o, tokens, vectors, offsets):
    def kernel(s, att, w, tok, vec, res, n2, n2_rel):
        total = tok[...].astype(f32) + dot(relative_columns(att, s, THIRDS), w[...])
        res[...] = total
        xhat, r = center_scale(total)
        n2[...] = (xhat * row(vec, LN2_G) + row(vec, LN2_B)).astype(bf16)
        other = at(D // 2 - s[0])
        n2_rel[:, : D // 2] = n2[:, pl.ds(at(s[0]), D // 2)]
        n2_rel[:, D // 2 :] = n2[:, pl.ds(other, D // 2)]

    args = (attended, w_o, tokens, vectors)
    out = (shape((T, D), f32), shape((T, D), bf16), shape((T, D), bf16))
    return call(
        kernel, out, (1,), [whole(a) for a in args], [whole(o) for o in out], offsets, args
    )


STEP = 512
UNITS = 1024
HALF = FF // 2 // UNITS


def feed_forward(n2_rel, residual, cotangent, w_in, w_out, spread, b_in, vectors, scalars):
    n_in = w_in.shape[0] // 32
    n_out = w_out.shape[0] // 32
    skip = n_out // n_in
    per = UNITS // n_out
    K_NORM = 0.7978845608028654

    def natural(j, s):
        return lax.rem(j + s[0] * HALF, 2 * HALF)

    def kernel(s, n2, res, cot, wi0, wi1, wo0, wo1, bi, vec, hid, dpre, mixed, dn2, dbi, acc, back):
        j = pl.program_id(0)
        n = natural(j, s)

        @pl.when(j == 0)
        def _():
            acc[...] = jnp.zeros_like(acc)
            back[...] = jnp.zeros_like(back)

        wo = jnp.where(j < HALF, wo0[...], wo1[...].reshape(UNITS, D))
        win = jnp.concatenate([wi0[...], wi1[...].reshape(D // 2, UNITS)], axis=0)
        pre = dot(n2[...], win) + bi[pl.ds(n, 1), :]
        d_hidden = dot_t(cot[...], wo)
        square = pre * pre
        t = jnp.tanh(K_NORM * pre * (1.0 + 0.044715 * square))
        gate_ = 0.5 * (1.0 + t)
        hidden = (pre * gate_).astype(bf16)
        slope = gate_ + (0.5 * K_NORM) * pre * (1.0 - t * t) * (1.0 + (3 * 0.044715) * square)
        d_pre = (d_hidden * slope).astype(bf16)
        hid[...] = hidden
        dpre[...] = d_pre
        dbi[pl.ds(n, 1), :] = jnp.sum(d_pre.astype(f32), axis=0, keepdims=True)
        acc[...] += dot(hidden, wo)
        back[...] += dot_t(d_pre, win)

        @pl.when(j == 2 * HALF - 1)
        def _():
            mixed[...] = (res[...] + acc[...] + row(vec, B_OUT)).astype(bf16)
            dn2[:, pl.ds(at(s[0] * (D // 2)), D // 2)] = back[:, : D // 2]
            dn2[:, pl.ds(at((1 - s[0]) * (D // 2)), D // 2)] = back[:, D // 2 :]

    out = (
        shape((T, FF), bf16),
        shape((T, FF), bf16),
        shape((T, D), bf16),
        shape((T, D), f32),
        shape((2 * HALF, UNITS), f32),
    )
    by_unit = pl.BlockSpec((T, UNITS), lambda j, s: (0, natural(j, s)))
    return call(
        kernel,
        out,
        (2 * HALF,),
        [
            whole(n2_rel),
            whole(residual),
            whole(cotangent),
            pl.BlockSpec((D // 2, UNITS), lambda j, s: (0, natural(j, s))),
            pl.BlockSpec((32, n_in, UNITS), lambda j, s: (0, skip + natural(j, s), 0)),
            pl.BlockSpec((UNITS, D), lambda j, s: (jnp.minimum(j, HALF - 1), 0)),
            pl.BlockSpec(
                (per, n_out, D), lambda j, s: (jnp.maximum(j - HALF, 0), 0, 0)
            ),
            whole(b_in),
            whole(vectors),
        ],
        [by_unit, by_unit, whole(out[2]), whole(out[3]), whole(out[4])],
        scalars,
        (n2_rel, residual, cotangent, w_in, spread, w_out, spread, b_in, vectors),
        [pltpu.VMEM((T, D), f32), pltpu.VMEM((T, D), f32)],
    )


def second_norm_back(cotangent, d_n2, residual, vectors, w_o, offsets):
    def kernel(s, cot, dn, res, vec, w, d_res, d_br, d_att, dg, db, dbo):
        xhat, r = center_scale(res[...])
        dn, wide = dn[...], cot[...].astype(f32)
        dg[...] = jnp.sum(dn * xhat, axis=0, keepdims=True)
        db[...] = jnp.sum(dn, axis=0, keepdims=True)
        dbo[...] = jnp.sum(wide, axis=0, keepdims=True)
        total = wide + norm_back(xhat, r, row(vec, LN2_G), dn)
        d_res[...] = total
        low = total.astype(bf16)
        d_br[...] = low
        natural_columns(d_att, dot_t(low, w[...]).astype(bf16), s, THIRDS)

    args = (cotangent, d_n2, residual, vectors, w_o)
    out = (
        shape((T, D), f32),
        shape((T, D), bf16),
        shape((T, D), bf16),
        shape((1, D), f32),
        shape((1, D), f32),
        shape((1, D), f32),
    )
    return call(
        kernel, out, (1,), [whole(a) for a in args], [whole(o) for o in out], offsets, args
    )


def first_norm_back(d_kv, d_q, w_kv, w_q, compressed, memory, tokens, vectors, d_res, offsets):
    steps = 4
    wide, slim = 2 * D // steps, D // steps

    def kernel(s, dkv, dq, kw, qw, comp, mem, tok, vec, dres, dtok, dg, db, acc, nat, xh, rs):
        j = pl.program_id(0)

        def product(start):
            value = dot_t(dkv[0], kw[...])
            if start:
                acc[...] = value
            else:
                acc[...] += value
            acc[2 * T :, :] += dot_t(dq[...], qw[...])

        for block, ref in enumerate((comp, mem, tok)):

            @pl.when(j == block)
            def _(block=block, ref=ref):
                product(block == 0)
                for i in range(0, T, 32):
                    xhat, r = center_scale(ref[i : i + 32, :].astype(f32))
                    xh[block * T + i : block * T + i + 32, :] = xhat
                    if block == 2:
                        rs[i : i + 32, :] = jnp.broadcast_to(r, (32, HD))

        @pl.when(j == steps - 1)
        def _():
            product(False)
            natural_columns(nat, acc, s, THIRDS)
            gain = row(vec, LN1_G)
            sum_g = jnp.zeros((8, D), f32)
            sum_b = jnp.zeros((8, D), f32)
            for i in range(0, KEYS, 32):
                dn, xhat = nat[i : i + 32, :], xh[i : i + 32, :]
                both = dn * xhat
                sum_g += (both[:8] + both[8:16]) + (both[16:24] + both[24:])
                sum_b += (dn[:8] + dn[8:16]) + (dn[16:24] + dn[24:])
                if i >= 2 * T:
                    k = i - 2 * T
                    r = rs[k : k + 32, :1]
                    dtok[k : k + 32, :] = dres[k : k + 32, :] + norm_back(xhat, r, gain, dn)
            dg[...] = jnp.sum(sum_g, axis=0, keepdims=True)
            db[...] = jnp.sum(sum_b, axis=0, keepdims=True)

    rest = (compressed, memory, tokens, vectors, d_res)
    out = (shape((T, D), f32), shape((1, D), f32), shape((1, D), f32))
    return call(
        kernel,
        out,
        (steps,),
        [
            pl.BlockSpec((1, KEYS, wide), lambda j, s: (j // (steps // 2), 0, lax.rem(j, steps // 2))),
            pl.BlockSpec((T, slim), lambda j, s: (0, j)),
            pl.BlockSpec((D, wide), lambda j, s: (0, j)),
            pl.BlockSpec((D, slim), lambda j, s: (0, j)),
        ]
        + [whole(a) for a in rest],
        [whole(o) for o in out],
        offsets,
        (d_kv, d_q, w_kv, w_q, *rest),
        [pltpu.VMEM((KEYS, D), f32)] * 3 + [pltpu.VMEM((T, HD), f32)],
    )


def compress(oldest, pieces, vectors, offsets):
    block = 256
    rows = T // 3

    def kernel(s, x, w0, w1, w2, vec, compact, normed, x_rel, natural):
        j = pl.program_id(0)

        @pl.when(j == 0)
        def _():
            x_rel[...] = relative_columns(x, s, (3 * D // 2, 3 * D // 4, 3 * D // 4))

        w = jnp.concatenate([w0[...], w1[...], w2[...]], axis=0)
        here = pl.ds(at(j * block), block)
        compact[:, here] = dot(x_rel[...], w) + vec[CONV_B : CONV_B + 1, here]

        @pl.when(j == D // block - 1)
        def _():
            xhat, r = center_scale(compact[...])
            natural[...] = (xhat * row(vec, LN1_G) + row(vec, LN1_B)).astype(bf16)
            start = 0
            for i, width in enumerate(THIRDS):
                normed[:, start : start + width] = natural[:, pl.ds(at(s[3 + i]), width)]
                start += width

    out = (shape((rows, D), f32), shape((rows, D), bf16))
    return call(
        kernel,
        out,
        (D // block,),
        [whole(oldest)]
        + [pl.BlockSpec((w.shape[0], block), lambda j, s: (0, j)) for w in pieces]
        + [whole(vectors)],
        [whole(o) for o in out],
        offsets,
        (oldest, *pieces, vectors),
        [pltpu.VMEM((rows, 3 * D), bf16), pltpu.VMEM((rows, D), bf16)],
    )


def reconstruct(queries, key_value, comp_pair, none):
    rows = T // 3
    n = 4

    def kernel(_, q, k, v, ck, cv, loss, dck, dcv):
        cuts = columns_of(n)
        asking = [(q[:, c] * FACTOR).astype(bf16) for c in cuts]
        far = [dot_t(x, k[:, c]) for x, c in zip(asking, cuts)]
        near = [dot_t(x, ck[:, c]) for x, c in zip(asking, cuts)]
        p = [softmax(x).astype(bf16) for x in far]
        gp = [softmax(x) for x in near]
        low = [x.astype(bf16) for x in gp]
        miss = [dot(p[h], v[:, c]) - dot(low[h], cv[:, c]) for h, c in enumerate(cuts)]
        total = sum(jnp.sum(x * x, axis=0, keepdims=True) for x in miss)
        d_guess = [((-2.0 / (T * D)) * x).astype(bf16) for x in miss]
        d_gp = [dot_t(x, cv[:, c]) for x, c in zip(d_guess, cuts)]
        d_gs = [
            (x * (y - jnp.sum(x * y, axis=-1, keepdims=True))).astype(bf16)
            for x, y in zip(gp, d_gp)
        ]
        for h, c in enumerate(cuts):
            dcv[:, c] = t_dot(low[h], d_guess[h]).astype(bf16)
            dck[:, c] = t_dot(d_gs[h], asking[h]).astype(bf16)

        @pl.when(pl.program_id(0) == 0)
        def _():
            loss[...] = total

        @pl.when(pl.program_id(0) > 0)
        def _():
            loss[...] += total

    return call(
        kernel,
        (shape((1, HD), f32), shape((rows, D), bf16), shape((rows, D), bf16)),
        (H // n,),
        [head(n, T), head(n, T, 1), head(n, T, 1, H), head(n, rows), head(n, rows, 0, H)],
        [pl.BlockSpec((1, HD), lambda h, s: (0, 0)), head(n, rows), head(n, rows)],
        none,
        (queries, key_value, key_value, comp_pair, comp_pair),
    )


def compress_back(dck, dcv, w_kv, compact, vectors, offsets):
    rows = T // 3

    def kernel(s, dck, dcv, w, compact, vec, d_compact, d_bias, dn):
        back = dot_t(jnp.concatenate([dck[...], dcv[...]], axis=1), w[...])
        natural_columns(dn, back, s, THIRDS)
        xhat, r = center_scale(compact[...])
        low = norm_back(xhat, r, row(vec, LN1_G), dn[...]).astype(bf16)
        d_compact[...] = low
        d_bias[...] = jnp.sum(low.astype(f32), axis=0, keepdims=True)

    args = (dck, dcv, w_kv, compact, vectors)
    out = (shape((rows, D), bf16), shape((1, D), f32))
    return call(
        kernel,
        out,
        (1,),
        [whole(a) for a in args],
        [whole(o) for o in out],
        offsets,
        args,
        [pltpu.VMEM((rows, D), f32)],
    )


def weight_grads(groups, scalars):
    in_specs, args, outs, out_specs, layout, scratch = [], [], [], [], [], []
    for ring, jobs in groups:
        first = 1 if ring == "x" else 5
        block = jobs[0][0][0].shape[1] // 8
        plan = []
        for xs, row_block, rows, dys, ready in jobs:
            width = dys[0].shape[1] // (1 if ready else 2)
            plan.append((width, rows, len(xs)))
            for x in xs:
                for y in range(2):
                    in_specs.append(
                        pl.BlockSpec(
                            (rows, block),
                            lambda q, s, r=row_block, f=first, y=y: (r, y * 4 + s[f + q]),
                        )
                    )
                    args.append(x)
            for dy in dys:
                in_specs.append(
                    pl.BlockSpec((rows, width), lambda q, s, r=ready: (0, 0 if r else s[0]))
                )
                args.append(dy)
            scratch.append(pltpu.VMEM((rows * len(xs), width), bf16))
        dims = (1, 2, block, sum(p[0] for p in plan))
        outs += [shape((2, *dims[1:]), bf16)] * 2
        out_specs += [
            pl.BlockSpec(dims, lambda q, s: (jnp.minimum(q, 1), 0, 0, 0)),
            pl.BlockSpec(dims, lambda q, s: (jnp.maximum(q - 2, 0), 0, 0, 0)),
        ]
        layout.append(plan)
    n_in, n_out = len(in_specs), len(outs)

    def kernel(s, *refs):
        ins, results, joined = refs[:n_in], refs[n_in : n_in + n_out], refs[n_in + n_out :]
        q = pl.program_id(0)

        @pl.when(q == 0)
        def _():
            place, k = 0, 0
            for plan in layout:
                for _, rows, n in plan:
                    da, db = ins[place + 2 * n], ins[place + 2 * n + 1]
                    if n == 2:
                        joined[k][:rows, :] = da[...]
                        joined[k][rows:, :] = db[...]
                    else:
                        joined[k][...] = (da[...].astype(f32) + db[...].astype(f32)).astype(bf16)
                    place += 2 * n + 2
                    k += 1

        place, k = 0, 0
        for i, plan in enumerate(layout):
            send, keep = results[2 * i : 2 * i + 2]
            block = send.shape[2]
            start = 0
            for width, rows, n in plan:
                x = jnp.concatenate([r[...] for r in ins[place : place + 2]], axis=1)
                if n == 2:
                    other = jnp.concatenate([r[...] for r in ins[place + 2 : place + 4]], axis=1)
                    x = jnp.concatenate([x, other], axis=0)
                value = t_dot(x, joined[k][...]).astype(bf16).reshape(2, block, width)
                cut = slice(start, start + width)
                send[0, :, :, cut] = jnp.where(q < 2, value, send[0, :, :, cut])
                keep[0, :, :, cut] = value
                start += width
                place += 2 * n + 2
                k += 1

    flat = call(kernel, tuple(outs), (4,), in_specs, out_specs, scalars, args, scratch)
    return [(flat[2 * i], flat[2 * i + 1]) for i in range(len(groups))]


def conv_grad(x, x_twin, dy, dy_twin, scalars):
    rows, columns = x.shape[1] // 2, D // 2

    def kernel(s, xa, xb, da, db, out):
        both = jnp.concatenate([xa[...], xb[...]], axis=0)
        total = t_dot(both, jnp.concatenate([da[...], db[...]], axis=0))
        out[...] = total.reshape(2, rows, columns)

    half = pl.BlockSpec((dy.shape[0], columns), lambda j, s: (0, s[0]))
    out = shape((2, rows, columns), f32)
    return call(
        kernel,
        out,
        (1,),
        [whole(x), whole(x_twin), half, half],
        whole(out),
        scalars,
        (x, x_twin, dy, dy_twin),
    )


def widen(gathered, plan, none):
    outs, specs, layout = [], [], []
    start = 0
    for rows, columns, ring in plan:
        u, chunks = rows // 16, columns // 2 // STEP
        outs.append(shape((4, 4, u, columns), f32))
        if ring == "x":
            specs.append(
                pl.BlockSpec((1, 4, u, chunks * STEP), lambda c, x, s: (x, 0, 0, c))
            )
        else:
            specs.append(
                pl.BlockSpec((4, 1, u, chunks * STEP), lambda c, x, s: (0, x, 0, c))
            )
        layout.append((start, u, chunks, ring))
        start += u * chunks

    def kernel(_, src, *results):
        for out, (start, u, chunks, ring) in zip(results, layout):
            for k in range(chunks):
                cut = slice(k * STEP, (k + 1) * STEP)
                for z in range(4):
                    value = src[z, start + k * u : start + (k + 1) * u, :].astype(f32)
                    if ring == "x":
                        out[0, z, :, cut] = value
                    else:
                        out[z, 0, :, cut] = value

    results = call(
        kernel,
        tuple(outs),
        (2, 4),
        [pl.BlockSpec((4, gathered.shape[1], STEP), lambda c, x, s: (c * 4 + x, 0, 0))],
        specs,
        none,
        (gathered,),
    )
    return [r.reshape(rows, columns) for r, (rows, columns, _) in zip(results, plan)]


def core_swap(v):
    return lax.ppermute(v, "c", [(0, 1), (1, 0)])


def pair_swap(v):
    return lax.ppermute(v, "yl", [(0, 1), (1, 0)])


def exchange(v, ring, masks):
    def flat(i, c):
        return (i // 2 * 2 + c) * 2 + i % 2 if ring == "y" else 2 * i + c

    pairs = [(flat(i, c), flat(i ^ masks[c], c)) for i in range(4) for c in range(2)]
    return lax.ppermute(v, RING[ring], pairs)


def pick(v, index, axis):
    return lax.dynamic_index_in_dim(v, index, axis, keepdims=False)


def quarters(place, core):
    first = jnp.where(core == 0, 1, 3)
    second = jnp.where(core == 0, 3, 1)
    return place, place ^ first, place ^ 2, place ^ second


class Flow:
    def __init__(self, ring, pair, done=None):
        self.ring, self.other = ring, "z" if ring == "x" else "x"
        self.before, self.result = None, done
        if done is None:
            self.send, self.keep = pair

    def start(self):
        self.got = exchange(self.send, self.ring, (1, 3))

    def sources(self):
        return [self.keep, self.got, self.last] if self.result is None else [self.result]

    def kept(self, which):
        if self.before is None:
            dims = (1, 1, *self.keep.shape[2:])
            return [pl.BlockSpec(dims, lambda y, s: (which, y, 0, 0))], [self.keep]
        return self.before(2 + which)


def onward(flows, cuts):
    in_specs, args, counts = [], [], []
    for f in flows:
        specs, arrays = f.kept(1)
        dims = (1, 1, *f.got.shape[2:])
        in_specs += specs + [pl.BlockSpec(dims, lambda y, s: (1, y, 0, 0))]
        args += arrays + [f.got]
        counts.append(len(arrays) + 1)
    out = tuple(shape(f.got.shape[1:], bf16) for f in flows)

    def kernel(_, *refs):
        k = 0
        for i, n in enumerate(counts):
            total = sum(value_of(r) for r in refs[k : k + n])
            refs[len(args) + i][...] = total.astype(bf16)
            k += n

    sums = call(
        kernel,
        out,
        (2,),
        in_specs,
        [pl.BlockSpec((1, *o.shape[1:]), lambda y, s: (y, 0, 0)) for o in out],
        cuts,
        args,
    )
    for f, v in zip(flows, sums):
        f.last = exchange(v, f.ring, (3, 1))


def value_of(ref):
    return (ref[0] if len(ref.shape) == 4 else ref[...]).astype(f32)


def turn(flows, cuts):
    in_specs, outs, out_specs, args = [], [], [], []

    counts = []
    for f in flows:
        first = 1 if f.other == "x" else 5
        arrays = f.sources()
        rows, columns = arrays[0].shape[-2] // 4, arrays[0].shape[-1]
        four = pl.BlockSpec((1, 2, rows, columns), lambda j, s, i=first: (0, 0, s[i + j], 0))
        three = pl.BlockSpec((2, rows, columns), lambda j, s, i=first: (0, s[i + j], 0))
        in_specs += [four if a.ndim == 4 else three for a in arrays]
        args += arrays
        counts.append(len(arrays))
        dims = (1, 2, rows, columns)
        outs.append(shape((2, *dims[1:]), bf16))
        out_specs.append(pl.BlockSpec(dims, lambda j, s: (j, 0, 0, 0)))

    def kernel(_, *refs):
        k = 0
        for i, n in enumerate(counts):
            total = sum(value_of(r) for r in refs[k : k + n])
            refs[len(args) + i][0] = total.astype(bf16)
            k += n

    sends = call(kernel, tuple(outs), (2,), in_specs, out_specs, cuts, args)
    for f, send in zip(flows, sends):
        f.before = halves_of(f)
        f.ring = f.other
        f.got = exchange(send, f.ring, (1, 3))


def halves_of(f):
    arrays = f.sources()
    first = 1 if f.other == "x" else 5
    rows, columns = arrays[0].shape[-2] // 4, arrays[0].shape[-1]

    def quarter(which):
        four = pl.BlockSpec((1, 1, rows, columns), lambda y, s: (0, y, s[first + which], 0))
        three = pl.BlockSpec((1, rows, columns), lambda y, s: (y, s[first + which], 0))
        return [four if a.ndim == 4 else three for a in arrays], arrays

    return quarter


def add(a, b, none):
    def kernel(_, a, b, out):
        out[...] = (a[...].astype(f32) + b[...].astype(f32)).astype(bf16)

    out = shape(a.shape, bf16)
    return call(kernel, out, (1,), [whole(a), whole(b)], whole(out), none, (a, b))


class Finish:
    def __init__(self, flows, extra, cuts):
        in_specs, args, sizes = [], [], []
        def half(spec):
            return pl.BlockSpec(
                spec.block_shape, lambda j, s: spec.index_map(lax.rem(j + s[9], 2), s)
            )

        for f in flows:
            specs, arrays = f.kept(0)
            dims = (1, 1, *f.got.shape[2:])
            specs = specs + [
                pl.BlockSpec(dims, lambda y, s: (0, y, 0, 0)),
                pl.BlockSpec((1, *f.last.shape[1:]), lambda y, s: (y, 0, 0)),
            ]
            in_specs += [half(spec) for spec in specs]
            args += arrays + [f.got, f.last]
            sizes.append((len(arrays) + 2, f.got.shape[2], f.got.shape[3] // STEP))
        for e in extra:
            in_specs.append(half(pl.BlockSpec((1, *e.shape[1:]), lambda y, s: (y, 0, 0))))
        args += extra
        rows = sum(u * n for _, u, n in sizes) + sum(e.shape[1] for e in extra)

        def kernel(_, *refs):
            send, mine = refs[-2:]
            j = pl.program_id(0)

            def put(here, value):
                @pl.when(j == 0)
                def _():
                    mine[here, :] = value

                @pl.when(j == 1)
                def _():
                    send[here, :] = value.astype(bf16)

            start, k = 0, 0
            for count, u, n in sizes:
                v = sum(value_of(r) for r in refs[k : k + count])[0]
                for i in range(n):
                    put(slice(start, start + u), v[:, i * STEP : (i + 1) * STEP])
                    start += u
                k += count
            for ref in refs[k:-2]:
                put(slice(start, start + ref.shape[1]), ref[0])
                start += ref.shape[1]

        out = (shape((rows, STEP), bf16), shape((rows, STEP), f32))
        send, self.mine = call(
            kernel, out, (2,), in_specs, [whole(o) for o in out], cuts, args
        )
        self.got = exchange(send, "y", (1, 3))

    def second(self, none):
        self.mine = add(self.mine, self.got, none)
        self.far = lax.ppermute(self.mine, "yh", [(0, 1), (1, 0)])

    def gather(self, none, *after):
        done = add(self.mine, self.far, none)
        if after:
            (done,) = gate((done,), *after)
            line.hold(done)
        return lax.all_gather(done, ("c", "x", "z"), axis=0)


def per_device(
    tokens,
    memory,
    compressed,
    cotangent,
    ln1_g,
    ln1_b,
    w_q,
    w_kv,
    w_r,
    bias_u,
    bias_v,
    w_o,
    ln2_g,
    ln2_b,
    w_in,
    b_in,
    w_out,
    b_out,
    conv_w,
    conv_b,
):
    line.held, line.due = [], {}
    tokens, memory, compressed, cotangent = tokens[0], memory[0], compressed[0], cotangent[0]
    yl, core = lax.axis_index("yl"), lax.axis_index("c")
    place = {"x": lax.axis_index("x"), "z": lax.axis_index("z")}
    none = jnp.zeros((1,), jnp.int32)
    ints = lambda *v: jnp.stack([jnp.asarray(i, jnp.int32) for i in v])

    def thirds(rows):
        half = rows // 2
        other = (1 - yl) * half
        return [yl * half, other + core * (half // 2), other + (1 - core) * (half // 2)]

    def both(v):
        return (v, core_swap(v))

    spot = (place["x"] * 4 + place["z"]) * 2 + core
    piece = pack(
        (ln1_g, ln1_b, bias_u, bias_v, ln2_g, ln2_b, b_out, conv_b, b_in),
        w_in,
        w_out,
        ints(spot),
    )
    piece_got = exchange(piece, "y", (1, 3))

    kv_part, small, o_part = pack_rows(w_kv, w_q, w_r, w_o, ints(core))
    (piece_got,) = gate((piece_got,), kv_part)
    kv_got = exchange(kv_part, "y", (1, 3))
    small_got = exchange(small, "y", (1, 3))
    o_got = exchange(o_part, "y", (1, 3))

    def joined(w, got, twin):
        return jnp.concatenate([w, got, twin], axis=0)

    spread = lax.all_gather(piece_got[:-16], ("x", "z", "c"), axis=0)
    thirds_d = ints(*thirds(D))
    thirds_c = ints(*thirds(3 * D), *thirds(D))
    sinus_table = sinusoid(KEYS, D).astype(bf16)
    sinus_rel = jnp.concatenate(
        [
            lax.dynamic_slice_in_dim(sinus_table, thirds_d[i], width, 1)
            for i, width in enumerate(THIRDS)
        ],
        axis=1,
    )
    line.hold(sinus_rel)
    vectors, b_in = unpack(piece, piece_got, ints(yl))

    normed, normed_rel, oldest, old_quarters = first_norm(compressed, memory, tokens, vectors, thirds_d)
    conv_part = half_rows(conv_w, ints(core))
    both_normed, both_cot = both(normed), both(cotangent)
    own, first, far, second = quarters(place["x"], core)
    got = exchange(
        jnp.stack([pick(old_quarters, first, 0), pick(old_quarters, far, 0)]), "x", (1, 3)
    )
    got_far = exchange(jnp.stack([pick(old_quarters, second, 0), got[1]]), "x", (3, 1))
    old_ring = jnp.concatenate([pick(old_quarters, own, 0), got[0], got_far[0], got_far[1]])
    old_twin = core_swap(old_ring)
    kv_got, small_got = gate((kv_got, small_got), normed, conv_part)
    kv_twin, small_twin = core_swap(kv_got), core_swap(small_got)
    kv_whole = joined(w_kv, kv_got, kv_twin)
    q_whole, r_whole = [
        joined(w, small_got[i], small_twin[i]) for i, w in enumerate((w_q, w_r))
    ]
    key_value = dot(normed_rel, kv_whole).astype(bf16)
    line.hold(key_value)
    queries = dot(normed_rel[2 * T :], q_whole)
    relative = dot(sinus_rel, r_whole).astype(bf16)
    (o_got,) = gate((o_got,), key_value, queries, relative)
    o_whole = joined(w_o, o_got, core_swap(o_got))
    line.hold(queries, relative)
    line.hold(got)
    probs, attended = attend(queries, key_value, relative, vectors, none)
    line.hold(both_normed[1], both_cot[1], got_far)
    residual, normed2, normed2_rel = out_and_norm(attended, o_whole, tokens, vectors, thirds_d)
    both_n2, both_att = both(normed2), both(attended)

    cuts, rels, twins = [], [], []
    for ring in ("x", "z"):
        own, first, far, second = quarters(place[ring], core)
        cuts += [first, far, own, second]
        rels.append([own, first, second, far])
        twins.append([own, second, first, far])
    cuts = ints(core, *cuts, yl)

    def flows(groups):
        pairs = weight_grads(groups, cuts)
        return [Flow(ring, pair) for (ring, _), pair in zip(groups, pairs)]

    def start(some):
        for f in some:
            f.start()

    line.hold(old_twin)
    hidden, d_pre, mixed_out, d_normed2, d_b_in = feed_forward(
        normed2_rel, residual, cotangent, w_in, w_out, spread, b_in, vectors, ints(yl)
    )
    both_hidden, both_pre = both(hidden), both(d_pre)
    conv_got = exchange(conv_part, "y", (1, 3))
    d_residual, d_branch, d_attended, d_ln2_g, d_ln2_b, d_b_out = second_norm_back(
        cotangent, d_normed2, residual, vectors, o_whole, thirds_d
    )
    both_branch = both(d_branch)
    large = flows(
        [
            ("x", [(both_hidden, 0, T, both_cot, False)]),
            ("z", [(both_n2, 0, T, both_pre, False), (both_att, 0, T, both_branch, False)]),
        ]
    )
    start(large)
    line.hold(conv_got)
    conv_pieces = (conv_w, conv_got, core_swap(conv_got))
    d_kv, my_kv, give_kv, d_relative, d_queries, d_bias_u, d_bias_v = attend_back(
        queries, key_value, relative, vectors, probs, d_attended, ints(core)
    )
    both_kv = (my_kv, core_swap(give_kv))
    both_q, both_rel = both(d_queries), both(d_relative)

    compact, comp_normed = compress(oldest, conv_pieces, vectors, thirds_c)
    comp_pair = dot(comp_normed, kv_whole).astype(bf16)
    compressed_next = jnp.concatenate([compressed[T // 3 :], compact], axis=0)
    near = flows(
        [
            ("x", [(both_normed, 0, KEYS, both_kv, True)]),
            (
                "z",
                [
                    (both_normed, 2, T, both_q, False),
                    ((sinus_table,), 0, KEYS, both_rel, False),
                ],
            ),
        ]
    )
    onward(large, cuts)
    loss, d_ck, d_cv = reconstruct(queries, key_value, comp_pair, none)
    recon_loss = jnp.sum(loss) / (T * D)
    d_compact, d_conv_b = compress_back(d_ck, d_cv, kv_whole, compact, vectors, thirds_d)
    ring_got = exchange(d_compact, "x", (1, 3))
    sends = gate([f.send for f in near], d_compact)
    for f, send in zip(near, sends):
        f.send = send
    start(near)
    line.hold(*sends)
    turn(large, cuts)
    d_tokens, d_ln1_g, d_ln1_b = first_norm_back(
        d_kv, d_queries, kv_whole, q_whole, compressed, memory, tokens, vectors, d_residual,
        thirds_d,
    )
    (ring_got,) = gate((ring_got,), d_ln1_g)
    line.hold(ring_got)
    onward(large, cuts)
    ring_pair = jnp.concatenate([d_compact, ring_got])
    pair_got = exchange(ring_pair, "x", (3, 1))
    onward(near, cuts)
    line.expect(1, *[f.last for f in near])
    early = Finish(large, [], cuts)
    early.second(none)
    (pair_got,) = gate((pair_got,), early.mine)
    compact_ring = jnp.concatenate([ring_pair, pair_got])
    compact_twin = core_swap(compact_ring)
    conv = Flow("x", None, conv_grad(old_ring, old_twin, compact_ring, compact_twin, cuts))
    early_sums = early.gather(none)
    late_flows = [*near, conv]
    turn(late_flows, cuts)
    onward(late_flows, cuts)

    total = jnp.concatenate(
        [d_ln1_g, d_ln1_b, d_bias_u, d_bias_v, d_ln2_g, d_ln2_b, d_b_out, d_conv_b]
        + [d_b_in]
    )
    total = jnp.concatenate(
        [
            total[:8].reshape(8, 2, STEP).transpose(1, 0, 2),
            total[8:].reshape(2, 4, STEP),
            jnp.zeros((2, 4, STEP), f32),
        ],
        axis=1,
    )
    late = Finish(late_flows, [total], cuts)
    late.second(none)
    late_sums = late.gather(none, early_sums)

    g_out, g_in, g_o = widen(
        early_sums, [(FF // 2, D, "x"), (D // 2, FF, "z"), (D // 2, D, "z")], none
    )
    g_kv, g_q, g_r, g_conv = widen(
        late_sums,
        [(D // 2, 2 * D, "x"), (D // 2, D, "z"), (D // 2, D, "z"), (3 * D // 2, D, "x")],
        none,
    )
    half = jnp.sum(late_sums[:, 224:236].astype(f32), axis=0)
    t_ln1_g, t_ln1_b, t_bu, t_bv, t_ln2_g, t_ln2_b, t_bout, t_convb = [half[i] for i in range(8)]
    t_bin = half[8:].reshape(-1)
    return (
        mixed_out[None],
        compressed_next[None],
        recon_loss[None],
        d_tokens[None],
        t_ln1_g,
        t_ln1_b,
        g_q,
        g_kv,
        g_r,
        t_bu,
        t_bv,
        g_o,
        t_ln2_g,
        t_ln2_b,
        g_in,
        t_bin,
        g_out,
        t_bout,
        g_conv,
        t_convb,
    )


def solution(mesh):
    fine = Mesh(mesh.devices.reshape(2, 4, 4, 2, 2), AXES)
    stream = P(AXES, None, None)
    vec, mat = P("yl"), P("yl", None)
    weights = (vec, vec, mat, mat, mat, vec, vec, mat, vec, vec, mat, vec, mat, vec, mat, vec)
    return jax.shard_map(
        per_device,
        mesh=fine,
        in_specs=(stream,) * 4 + weights,
        out_specs=(stream, stream, P(AXES), stream) + weights,
        check_vma=False,
    )
```
